32 devices in a mesh: ctx: 4 (over y, x), tp: 8 (over z, core).
Axes of the slice: x: 2, y: 2, z: 4, core: 2. Of those that a mesh axis runs over, the one named last changes fastest.
Arguments:
- hidden_input: bfloat16 [1536, 8192], P('ctx'), may hold values from -6 to 6
- output_cotangent: bfloat16 [1536, 8192], P('ctx', 'tp'), may hold values from -6 to 6
- query_projection: bfloat16 [8192, 4096], P(None, 'tp')
- key_value_projection: bfloat16 [8192, 2048], P(None, 'tp')
- output_projection: bfloat16 [4096, 8192], P('tp'), may hold values from -0.09375 to 0.09375
- adapter_qkv_down_store: bfloat16 [16, 8192, 192], P('ctx', 'tp'), may hold values from -0.0625 to 0.0625
- adapter_query_up: bfloat16 [16, 64, 4096], P('ctx', None, 'tp'), may hold values from -0.375 to 0.375
- adapter_key_value_up: bfloat16 [16, 64, 2048], P('ctx', None, 'tp'), may hold values from -0.375 to 0.375
- adapter_output_down: bfloat16 [16, 4096, 64], P('ctx', 'tp'), may hold values from -0.1875 to 0.1875
- adapter_output_up: bfloat16 [16, 64, 8192], P('ctx', None, 'tp'), may hold values from -0.75 to 0.75
- crop_token_length: int32 [4], replicated, may hold values from 1 to 1152, 1536 in all
- tenant_per_block: int32 [12], replicated, may hold values from 0 to 15, as said below
- tenant_store_row: int32 [16], replicated, may hold values from 0 to 15, as said below
Outputs:
- output: bfloat16 [1536, 8192], P('ctx', 'tp')
- hidden_input_gradient: bfloat16 [1536, 8192], P('ctx', 'tp')
- grad_down_qkv: float32 [16, 8192, 192], P('ctx', 'tp')
- grad_up_q: float32 [16, 64, 4096], P('ctx', None, 'tp')
- grad_up_kv: float32 [16, 64, 2048], P('ctx', None, 'tp')
- grad_down_o: float32 [16, 4096, 64], P('ctx', 'tp')
- grad_up_o: float32 [16, 64, 8192], P('ctx', None, 'tp')
The draws below stay inside these ranges and needn't reach their ends.
Inputs may be any that keep to these rules, and one draw needn't show every extreme that they name: A permutation: tenant t's adapters are at store row tenant_store_row[t]; rows j * 4 to (j + 1) * 4 - 1 belong to owner j. `tenant_per_block`: of the 3 blocks of one index of ctx, at most 1 name tenants of one owner, and some owner is named that often.
All inputs are finite; a program needn't handle non-finite values.
Results may differ from the reference program's by a relative error of at most 0.038.
Values may be sent and summed in bfloat16 or wider, within the bound.
No kernel may reach another device: no remote copies, remote signals or barrier semaphores. Data moves between devices by JAX's collectives and lax.ppermute only.
A program may use at most 128 MiB of HBM per device.

```python
import math
import jax
import jax.numpy as jnp
import numpy as np
from jax import lax

MODEL_WIDTH = 8192
HEAD_SIZE = 128
KEY_VALUE_HEADS = 8
QUERY_HEADS = 32
ADAPTER_RANK = 64
BLK = 128
TEN_OWN = 4
NSEG = 4
TOKENS = 1536
TENANT_COUNT = 16
TB = 3
GROUP = 4
HEAD_GROUP = 4
COL_GROUP = 1024
KV_GROUP = 256
SEG_MOST = 1152
N_TP = 8


def draw_hidden_input(key, part):
    base_values = jax.random.normal(jax.random.fold_in(key, 31), (TOKENS, MODEL_WIDTH), jnp.float32)
    return jnp.clip(base_values, -6.0, 6.0).astype(jnp.bfloat16)


def projection_normal(key, tag, array_shape):
    base_values = jax.random.normal(jax.random.fold_in(key, tag), array_shape, jnp.float32)
    return jnp.clip(base_values, -6.0, 6.0) * MODEL_WIDTH ** (-0.5)


def draw_query_projection(key, part):
    return projection_normal(key, 41, (MODEL_WIDTH, QUERY_HEADS * HEAD_SIZE)).astype(jnp.bfloat16)


def draw_key_value_projection(key, part):
    fresh_values = projection_normal(key, 42, (MODEL_WIDTH, KEY_VALUE_HEADS, 2, HEAD_SIZE))
    return fresh_values.reshape(MODEL_WIDTH, 2 * KEY_VALUE_HEADS * HEAD_SIZE).astype(jnp.bfloat16)


def store_order(key):
    return jax.random.permutation(jax.random.fold_in(key, 51), TENANT_COUNT).astype(jnp.int32)


def draw_tenant_store_row(key, part):
    return store_order(key)


def force_first(orders, picks, shard_no, target_row):
    target_owner = target_row // TEN_OWN
    order_row = orders[shard_no]
    moved = jnp.where(order_row == target_owner, order_row[0], order_row)
    moved = moved.at[0].set(target_owner)
    orders = orders.at[shard_no].set(moved)
    picks = picks.at[shard_no, 0].set(target_row % TEN_OWN)
    return (orders, picks)


def draw_tenant_per_block(key, part):
    rows_of = store_order(key)
    tenant_of_row = jnp.argsort(rows_of).astype(jnp.int32)
    shard_count = TENANT_COUNT // TEN_OWN
    shard_keys = jax.random.split(jax.random.fold_in(key, 52), shard_count)
    orders = jax.vmap(lambda key_one: jax.random.permutation(key_one, shard_count))(shard_keys).astype(jnp.int32)
    picks = jax.random.randint(jax.random.fold_in(key, 53), (shard_count, TB), 0, TEN_OWN).astype(jnp.int32)
    orders, picks = force_first(orders, picks, 0, rows_of[TENANT_COUNT - 1])
    orders, picks = force_first(orders, picks, 1, rows_of[0])
    slot_ids = jnp.arange(TB, dtype=jnp.int32) % shard_count
    owners = orders[:, slot_ids].astype(jnp.int32)
    store_rows = owners * TEN_OWN + picks
    return tenant_of_row[store_rows.reshape(-1)].astype(jnp.int32)


def steps_of(key, extent, pieces, smallest, top_value):
    level = 1.0
    for dim, shards_of in pieces:
        steps = jax.random.uniform(jax.random.fold_in(jax.random.fold_in(key, 6), dim), (shards_of,), jnp.float32, smallest / len(pieces), top_value / len(pieces))
        level = level * jnp.repeat(jnp.exp(steps), extent[dim] // shards_of).reshape((-1,) + (1,) * (len(extent) - 1 - dim))
    return level


def length_profile(amount, total, most, slope):
    portions = [(1 << 20) // math.isqrt(rank ** slope) + 1 for rank in range(2, amount + 1)]
    rest, counts = total - most - (amount - 1), [1] * (amount - 1)
    while rest > 0:
        free = [i for i in range(amount - 1) if counts[i] < most]
        mass, budget = sum([portions[i] for i in free]), rest
        for i in free:
            addition = min(most - counts[i], max(1, budget * portions[i] // mass), rest)
            counts[i] = counts[i] + addition
            rest = rest - addition
    return np.array([most] + counts)


def uneven_parts(stream_key, count, total, bound, skew):
    if count == 2:
        one = jax.random.randint(stream_key, (), max(1, total - bound), min(bound, total - 1) + 1)
        return jnp.stack([one, total - one])
    tallies = jnp.asarray(length_profile(count, total, bound, skew), jnp.int32)
    couples = (count - 1) // 2
    source_of, receiver = tallies[1:1 + 2 * couples:2], tallies[2:2 + 2 * couples:2]
    slack = jnp.minimum(source_of - 1, bound - receiver)
    passed = jax.random.randint(jax.random.fold_in(stream_key, 1), (couples,), 0, 1 << 20) % (slack + 1)
    tallies = tallies.at[1:1 + 2 * couples:2].set(source_of - passed).at[2:2 + 2 * couples:2].set(receiver + passed)
    return tallies[jax.random.permutation(jax.random.fold_in(stream_key, 2), count)]


def gaussian(rng, extent, width, limit, pieces=(), kind=jnp.bfloat16):
    result = width * jax.random.normal(rng, extent, jnp.float32)
    if pieces:
        result = result * steps_of(rng, extent, pieces, -0.22, 0.18)
    return jnp.clip(result, -limit, limit).astype(kind)


def setup_inputs(seed: int = 0) -> dict:
    streams_of = jax.random.split(jax.random.key(seed), 14)
    hidden_input = draw_hidden_input(jax.random.fold_in(streams_of[13], 71), 0)
    output_cotangent = gaussian(streams_of[1], (TOKENS, MODEL_WIDTH), 1.0, 6.0, ((0, 4), (1, 8)))
    query_projection = draw_query_projection(jax.random.fold_in(streams_of[13], 71), 0)
    key_value_projection = draw_key_value_projection(jax.random.fold_in(streams_of[13], 71), 0)
    output_projection = gaussian(streams_of[4], (QUERY_HEADS * HEAD_SIZE, MODEL_WIDTH), (QUERY_HEADS * HEAD_SIZE) ** -0.5, 0.09375, ((0, 8),))
    adapter_qkv_down_store = gaussian(streams_of[5], (TENANT_COUNT, MODEL_WIDTH, 3 * ADAPTER_RANK), MODEL_WIDTH ** -0.5, 0.0625, ((0, 4), (1, 8)))
    adapter_query_up = gaussian(streams_of[6], (TENANT_COUNT, ADAPTER_RANK, QUERY_HEADS * HEAD_SIZE), (4 * ADAPTER_RANK) ** -0.5, 0.375, ((0, 4), (2, 8)))
    adapter_key_value_up = gaussian(streams_of[7], (TENANT_COUNT, ADAPTER_RANK, 2 * KEY_VALUE_HEADS * HEAD_SIZE), (4 * ADAPTER_RANK) ** -0.5, 0.375, ((0, 4), (2, 8)))
    adapter_output_down = gaussian(streams_of[8], (TENANT_COUNT, QUERY_HEADS * HEAD_SIZE, ADAPTER_RANK), (QUERY_HEADS * HEAD_SIZE // 4) ** -0.5, 0.1875, ((0, 4), (1, 8)))
    adapter_output_up = gaussian(streams_of[9], (TENANT_COUNT, ADAPTER_RANK, MODEL_WIDTH), ADAPTER_RANK ** -0.5, 0.75, ((0, 4), (2, 8)))
    crop_token_length = uneven_parts(streams_of[10], NSEG, TOKENS, SEG_MOST, 2).astype(jnp.int32)
    tenant_per_block = draw_tenant_per_block(jax.random.fold_in(streams_of[13], 71), 0)
    tenant_store_row = draw_tenant_store_row(jax.random.fold_in(streams_of[13], 71), 0)
    return {"hidden_input": hidden_input, "output_cotangent": output_cotangent, "query_projection": query_projection, "key_value_projection": key_value_projection, "output_projection": output_projection, "adapter_qkv_down_store": adapter_qkv_down_store, "adapter_query_up": adapter_query_up, "adapter_key_value_up": adapter_key_value_up, "adapter_output_down": adapter_output_down, "adapter_output_up": adapter_output_up, "crop_token_length": crop_token_length, "tenant_per_block": tenant_per_block, "tenant_store_row": tenant_store_row}


NEG = -1.0e30
ROPE_BASE = 1000000.0


def rope_pair(positions):
    half_dim = HEAD_SIZE // 2
    exponent = jnp.arange(half_dim, dtype=jnp.float32) * (2.0 / HEAD_SIZE)
    frequency = jnp.exp(-exponent * math.log(ROPE_BASE))
    angles = positions.astype(jnp.float32)[:, None] * frequency[None, :]
    return jnp.cos(angles), jnp.sin(angles)


def rotate(values, cosine, sine_tab):
    half_dim = values.shape[-1] // 2
    first_half = values[..., :half_dim]
    second = values[..., half_dim:]
    return jnp.concatenate([first_half * cosine - second * sine_tab, second * cosine + first_half * sine_tab], axis=-1)


def rotate_back(gradient, cosine, sine_tab):
    half_dim = gradient.shape[-1] // 2
    first_half = gradient[..., :half_dim]
    second = gradient[..., half_dim:]
    return jnp.concatenate([first_half * cosine + second * sine_tab, second * cosine - first_half * sine_tab], axis=-1)


def stored(values):
    return lax.optimization_barrier(values.astype(jnp.bfloat16))


def expand_to_width(values):
    return values.astype(jnp.float32)


def reference(hidden_input, output_cotangent, query_projection, key_value_projection, output_projection, adapter_qkv_down_store, adapter_query_up, adapter_key_value_up, adapter_output_down, adapter_output_up, crop_token_length, tenant_per_block, tenant_store_row):
    rows_per_block = tenant_store_row[tenant_per_block].astype(jnp.int32)
    block_count = TOKENS // BLK
    x_blocks = expand_to_width(hidden_input).reshape(block_count, BLK, MODEL_WIDTH)
    query_key_value_down = expand_to_width(adapter_qkv_down_store[rows_per_block])
    query_up_map = expand_to_width(adapter_query_up[rows_per_block])
    key_value_up_map = expand_to_width(adapter_key_value_up[rows_per_block])
    output_down_map = expand_to_width(adapter_output_down[rows_per_block])
    output_up_map = expand_to_width(adapter_output_up[rows_per_block])

    low_in = stored(jnp.einsum('nkd,ndr->nkr', x_blocks, query_key_value_down))
    low_wide = expand_to_width(low_in)
    low_q = low_wide[..., :ADAPTER_RANK]
    low_k = low_wide[..., ADAPTER_RANK:2 * ADAPTER_RANK]
    low_v = low_wide[..., 2 * ADAPTER_RANK:]

    positions = jnp.arange(TOKENS, dtype=jnp.int32)
    cosine, sine_tab = rope_pair(positions)
    query_lin = jnp.dot(hidden_input, query_projection, preferred_element_type=jnp.float32) + jnp.einsum('nkr,nrc->nkc', low_q, query_up_map).reshape(TOKENS, QUERY_HEADS * HEAD_SIZE)
    query_rot = stored(rotate(query_lin.reshape(TOKENS, QUERY_HEADS, HEAD_SIZE), cosine[:, None, :], sine_tab[:, None, :]))
    column_ids = jnp.arange(2 * KEY_VALUE_HEADS * HEAD_SIZE, dtype=jnp.int32)
    is_value = (column_ids // HEAD_SIZE) % 2 == 1
    kv_low = jnp.where(is_value, jnp.einsum('nkr,nrc->nkc', low_v, key_value_up_map), jnp.einsum('nkr,nrc->nkc', low_k, key_value_up_map)).reshape(TOKENS, 2 * KEY_VALUE_HEADS * HEAD_SIZE)
    keyval = stored(jnp.dot(hidden_input, key_value_projection, preferred_element_type=jnp.float32) + kv_low).reshape(TOKENS, KEY_VALUE_HEADS, 2, HEAD_SIZE)
    key_rot = stored(rotate(expand_to_width(keyval[:, :, 0]), cosine[:, None, :], sine_tab[:, None, :]))
    value_all = keyval[:, :, 1]

    crop_ends = jnp.cumsum(crop_token_length).astype(jnp.int32)
    segment = jnp.sum((positions[:, None] >= crop_ends[None, :]).astype(jnp.int32), axis=1)
    allowed = (positions[None, :] <= positions[:, None]) & (segment[None, :] == segment[:, None])
    score_scale = HEAD_SIZE ** -0.5

    def scores_of(head_kv):
        queries = expand_to_width(query_rot[:, head_kv * GROUP:(head_kv + 1) * GROUP])
        raw_scores = jnp.einsum('qhd,kd->hqk', queries, expand_to_width(key_rot[:, head_kv])) * score_scale
        return jnp.where(allowed[None], raw_scores, NEG)

    head_out = []
    norms = []
    for head_kv in range(KEY_VALUE_HEADS):
        scores = scores_of(head_kv)
        row_max = jnp.max(scores, axis=2, keepdims=True)
        log_norm = row_max + jnp.log(jnp.sum(jnp.exp(scores - row_max), axis=2, keepdims=True))
        weights = expand_to_width(stored(jnp.exp(scores - log_norm)))
        head_out.append(stored(jnp.einsum('hqk,kd->qhd', weights, expand_to_width(value_all[:, head_kv]))))
        norms.append(log_norm)
    attn_out = jnp.concatenate(head_out, axis=1).reshape(TOKENS, QUERY_HEADS * HEAD_SIZE)
    out_blocks = expand_to_width(attn_out).reshape(block_count, BLK, QUERY_HEADS * HEAD_SIZE)
    lowrank_output = stored(jnp.einsum('nkc,ncr->nkr', out_blocks, output_down_map))

    group_list = jnp.arange(N_TP, dtype=jnp.int32)

    def add_heads(running, group_no):
        columns = lax.dynamic_slice_in_dim(attn_out, group_no * (HEAD_GROUP * HEAD_SIZE), HEAD_GROUP * HEAD_SIZE, 1)
        weight_rows = lax.dynamic_slice_in_dim(output_projection, group_no * (HEAD_GROUP * HEAD_SIZE), HEAD_GROUP * HEAD_SIZE, 0)
        return running + expand_to_width(stored(jnp.dot(columns, weight_rows, preferred_element_type=jnp.float32))), None

    heads_total_sum, unused = lax.scan(add_heads, jnp.zeros((TOKENS, MODEL_WIDTH), jnp.float32), group_list)
    output = (heads_total_sum + jnp.einsum('nkr,nrc->nkc', expand_to_width(lowrank_output), output_up_map).reshape(TOKENS, MODEL_WIDTH)).astype(jnp.bfloat16)

    grad_blocks = expand_to_width(output_cotangent).reshape(block_count, BLK, MODEL_WIDTH)
    low_grad_o = stored(jnp.einsum('nkc,nrc->nkr', grad_blocks, output_up_map))

    def add_columns(running, group_no):
        columns = lax.dynamic_slice_in_dim(output_cotangent, group_no * COL_GROUP, COL_GROUP, 1)
        weight_cols = lax.dynamic_slice_in_dim(output_projection, group_no * COL_GROUP, COL_GROUP, 1)
        return running + expand_to_width(stored(jnp.dot(columns, weight_cols.T, preferred_element_type=jnp.float32))), None

    grad_sum, unused = lax.scan(add_columns, jnp.zeros((TOKENS, QUERY_HEADS * HEAD_SIZE), jnp.float32), group_list)
    attention_gradient = stored(grad_sum + jnp.einsum('nkr,ncr->nkc', expand_to_width(low_grad_o), output_down_map).reshape(TOKENS, QUERY_HEADS * HEAD_SIZE))
    head_gradient = attention_gradient.reshape(TOKENS, QUERY_HEADS, HEAD_SIZE)
    out_heads = attn_out.reshape(TOKENS, QUERY_HEADS, HEAD_SIZE)

    grad_q_parts = []
    key_parts = []
    value_parts = []
    for head_kv in range(KEY_VALUE_HEADS):
        first_head = head_kv * GROUP
        end_head = first_head + GROUP
        scores = scores_of(head_kv)
        weights = jnp.exp(scores - norms[head_kv])
        weights_narrow = expand_to_width(stored(weights))
        grad_here = expand_to_width(head_gradient[:, first_head:end_head])
        grad_weights = jnp.einsum('qhd,kd->hqk', grad_here, expand_to_width(value_all[:, head_kv]))
        row_delta = jnp.sum(grad_here * expand_to_width(out_heads[:, first_head:end_head]), axis=2)
        grad_scores = expand_to_width(stored(weights * (grad_weights - row_delta.T[:, :, None])))
        grad_q_parts.append(jnp.einsum('hqk,kd->qhd', grad_scores, expand_to_width(key_rot[:, head_kv])) * score_scale)
        key_parts.append(jnp.einsum('hqk,qhd->kd', grad_scores, expand_to_width(query_rot[:, first_head:end_head])) * score_scale)
        value_parts.append(jnp.einsum('hqk,qhd->kd', weights_narrow, grad_here))
    grad_q = stored(rotate_back(jnp.concatenate(grad_q_parts, axis=1), cosine[:, None, :], sine_tab[:, None, :]).reshape(TOKENS, QUERY_HEADS * HEAD_SIZE))
    key_grad = rotate_back(jnp.stack(key_parts, axis=1), cosine[:, None, :], sine_tab[:, None, :])
    grad_kv = stored(jnp.stack([key_grad, jnp.stack(value_parts, axis=1)], axis=2).reshape(TOKENS, 2 * KEY_VALUE_HEADS * HEAD_SIZE))

    grad_q_blocks = expand_to_width(grad_q).reshape(block_count, BLK, QUERY_HEADS * HEAD_SIZE)
    grad_kv_blocks = expand_to_width(grad_kv).reshape(block_count, BLK, 2 * KEY_VALUE_HEADS * HEAD_SIZE)
    key_part = jnp.where(is_value, 0.0, grad_kv_blocks)
    value_part = jnp.where(is_value, grad_kv_blocks, 0.0)
    lowrank_gradient = stored(jnp.concatenate([
        jnp.einsum('nkc,nrc->nkr', grad_q_blocks, query_up_map),
        jnp.einsum('nkc,nrc->nkr', key_part, key_value_up_map),
        jnp.einsum('nkc,nrc->nkr', value_part, key_value_up_map)], axis=2))

    def add_inputs(running, group_no):
        query_cols = lax.dynamic_slice_in_dim(grad_q, group_no * (HEAD_GROUP * HEAD_SIZE), HEAD_GROUP * HEAD_SIZE, 1)
        query_weights = lax.dynamic_slice_in_dim(query_projection, group_no * (HEAD_GROUP * HEAD_SIZE), HEAD_GROUP * HEAD_SIZE, 1)
        keyval_cols = lax.dynamic_slice_in_dim(grad_kv, group_no * KV_GROUP, KV_GROUP, 1)
        keyval_weights = lax.dynamic_slice_in_dim(key_value_projection, group_no * KV_GROUP, KV_GROUP, 1)
        group_terms = jnp.dot(query_cols, query_weights.T, preferred_element_type=jnp.float32) + jnp.dot(keyval_cols, keyval_weights.T, preferred_element_type=jnp.float32)
        return running + expand_to_width(stored(group_terms)), None

    input_total_sum, unused = lax.scan(add_inputs, jnp.zeros((TOKENS, MODEL_WIDTH), jnp.float32), group_list)
    low_grad_wide = expand_to_width(lowrank_gradient)
    hidden_input_gradient = (input_total_sum + jnp.einsum('nkr,ndr->nkd', low_grad_wide, query_key_value_down).reshape(TOKENS, MODEL_WIDTH)).astype(jnp.bfloat16)

    grad_down_qkv = jnp.zeros((TENANT_COUNT, MODEL_WIDTH, 3 * ADAPTER_RANK), jnp.float32).at[rows_per_block].add(jnp.einsum('nkd,nkr->ndr', x_blocks, low_grad_wide))
    grad_up_q = jnp.zeros((TENANT_COUNT, ADAPTER_RANK, QUERY_HEADS * HEAD_SIZE), jnp.float32).at[rows_per_block].add(jnp.einsum('nkr,nkc->nrc', low_q, grad_q_blocks))
    grad_up_kv = jnp.zeros((TENANT_COUNT, ADAPTER_RANK, 2 * KEY_VALUE_HEADS * HEAD_SIZE), jnp.float32).at[rows_per_block].add(jnp.where(is_value, jnp.einsum('nkr,nkc->nrc', low_v, grad_kv_blocks), jnp.einsum('nkr,nkc->nrc', low_k, grad_kv_blocks)))
    grad_down_o = jnp.zeros((TENANT_COUNT, QUERY_HEADS * HEAD_SIZE, ADAPTER_RANK), jnp.float32).at[rows_per_block].add(jnp.einsum('nkc,nkr->ncr', out_blocks, expand_to_width(low_grad_o)))
    grad_up_o = jnp.zeros((TENANT_COUNT, ADAPTER_RANK, MODEL_WIDTH), jnp.float32).at[rows_per_block].add(jnp.einsum('nkr,nkc->nrc', expand_to_width(lowrank_output), grad_blocks))
    return (output, hidden_input_gradient, grad_down_qkv, grad_up_q, grad_up_kv, grad_down_o, grad_up_o)
```

```python
import functools
import math

import jax
import jax.numpy as jnp
from jax import lax
from jax.experimental import pallas as pl
from jax.experimental.pallas import tpu as pltpu
from jax.sharding import PartitionSpec as P

HEAD_SIZE = 128
KEY_VALUE_HEADS = 8
ADAPTER_RANK = 64
BLK = 128
NEG = -1e30
ROPE_BASE = 1000000.0
SCALE = HEAD_SIZE ** (-0.5)
VMEM_BYTES = 56 * 1024 * 1024

BF16 = jnp.bfloat16
F32 = jnp.float32


def params():
    return pltpu.CompilerParams(vmem_limit_bytes=VMEM_BYTES)


def cost(flops, bytes_accessed, transcendentals=0):
    return pl.CostEstimate(
        flops=int(flops), bytes_accessed=int(bytes_accessed), transcendentals=int(transcendentals)
    )


def dot_nn(a, b):
    return lax.dot_general(a, b, (((1,), (0,)), ((), ())), preferred_element_type=F32)


def dot_nt(a, b):
    return lax.dot_general(a, b, (((1,), (1,)), ((), ())), preferred_element_type=F32)


def dot_tn(a, b):
    return lax.dot_general(a, b, (((0,), (0,)), ((), ())), preferred_element_type=F32)


def swap(value, axis, mask):
    pairs = [(source, source ^ mask) for source in range(lax.axis_size(axis))]
    return lax.ppermute(value, axis, pairs)


def add_round(a, b):
    return (a.astype(F32) + b.astype(F32)).astype(BF16)


def sum_over_tp(part):
    count = lax.axis_size("tp")
    core = lax.axis_index("tp") % 2
    rows = part.shape[0] // 2
    halves = part.astype(BF16).reshape(2, rows, part.shape[1])
    mine = lax.dynamic_index_in_dim(halves, core, 0, keepdims=False)
    other = lax.dynamic_index_in_dim(halves, 1 - core, 0, keepdims=False)
    total = add_round(mine, swap(other, "tp", 1))
    mask = 2
    while mask < count:
        total = add_round(total, swap(total, "tp", mask))
        mask *= 2
    other = swap(total, "tp", 1)
    return jnp.where(
        core == 0,
        jnp.concatenate([total, other], axis=0),
        jnp.concatenate([other, total], axis=0),
    )


def rope_tables(positions):
    half_dim = HEAD_SIZE // 2
    exponent = jnp.arange(half_dim, dtype=F32) * (2.0 / HEAD_SIZE)
    frequency = jnp.exp(-exponent * math.log(ROPE_BASE))
    angles = positions.astype(F32)[:, None] * frequency[None, :]
    cosine, sine = jnp.cos(angles), jnp.sin(angles)
    return (
        jnp.concatenate([cosine, cosine], axis=1),
        jnp.concatenate([-sine, sine], axis=1),
    )


def turn(values, cosine, sine):
    return values * cosine + jnp.roll(values, HEAD_SIZE // 2, axis=1) * sine


def turn_kernel(values, cosine, sine):
    return values * cosine + pltpu.roll(values, HEAD_SIZE // 2, 1) * sine


def dense_kernel(x_ref, wq_ref, wkv_ref, q_ref, kv_ref):
    @pl.when(pl.program_id(0) == 0)
    def _():
        q_ref[...] = jnp.zeros_like(q_ref)
        kv_ref[...] = jnp.zeros_like(kv_ref)

    x = x_ref[...]
    q_ref[...] += dot_nn(x, wq_ref[...])
    kv_ref[...] += dot_nn(x, wkv_ref[...])


def dense_qkv(x, wq, wkv):
    rows, width = x.shape
    step = 1024
    cq, ckv = wq.shape[1], wkv.shape[1]
    return pl.pallas_call(
        dense_kernel,
        grid=(width // step,),
        in_specs=[
            pl.BlockSpec((rows, step), lambda i: (0, i)),
            pl.BlockSpec((step, cq), lambda i: (i, 0)),
            pl.BlockSpec((step, ckv), lambda i: (i, 0)),
        ],
        out_specs=[
            pl.BlockSpec((rows, cq), lambda i: (0, 0)),
            pl.BlockSpec((rows, ckv), lambda i: (0, 0)),
        ],
        out_shape=[
            jax.ShapeDtypeStruct((rows, cq), F32),
            jax.ShapeDtypeStruct((rows, ckv), F32),
        ],
        compiler_params=params(),
        cost_estimate=cost(2 * rows * width * (cq + ckv), 2 * width * (rows + cq + ckv)),
        name="dense_qkv",
    )(x, wq, wkv)


def low_kernel(count, tab_ref, x_ref, *refs):
    downs, out_ref = refs[:count], refs[count]
    which = tab_ref[2 + pl.program_id(0)]
    for j in range(count):

        @pl.when(which == j)
        def _(j=j):
            down = downs[j][0] if j == 0 else downs[j][...]
            out_ref[...] = dot_nn(x_ref[...], down).astype(BF16)


def low_part(table, x, store, others):
    rows = x.shape[0]
    width, cols = store.shape[1:]
    count = len(others) + 1
    return pl.pallas_call(
        functools.partial(low_kernel, count),
        grid_spec=pltpu.PrefetchScalarGridSpec(
            num_scalar_prefetch=1,
            grid=(rows // BLK,),
            in_specs=[
                pl.BlockSpec((BLK, width), lambda b, t: (b, t[0])),
                pl.BlockSpec((1, width, cols), lambda b, t: (t[1], 0, 0)),
            ]
            + [pl.BlockSpec((width, cols), lambda b, t: (0, 0))] * (count - 1),
            out_specs=pl.BlockSpec((BLK, cols), lambda b, t: (b, 0)),
        ),
        out_shape=jax.ShapeDtypeStruct((rows, cols), BF16),
        compiler_params=params(),
        cost_estimate=cost(2 * rows * width * cols, 2 * width * cols * count),
        name="low_part",
    )(table, x, store, *others)


def finish_kernel(rotate_keys, tab_ref, q_ref, kv_ref, low_ref, up_ref, cos_ref, sin_ref, qo, kvo):
    cq, ckv = q_ref.shape[1], kv_ref.shape[1]
    cosine, sine = cos_ref[...], sin_ref[...]
    low = low_ref[...]
    low_q = low[:, :ADAPTER_RANK]
    low_k = low[:, ADAPTER_RANK : 2 * ADAPTER_RANK]
    low_v = low[:, 2 * ADAPTER_RANK :]
    query = q_ref[...] + dot_nn(low_q, up_ref[0][:, :cq])
    for h in range(cq // HEAD_SIZE):
        at = slice(h * HEAD_SIZE, (h + 1) * HEAD_SIZE)
        qo[:, at] = turn_kernel(query[:, at], cosine, sine).astype(BF16)
    up_kv = up_ref[0][:, cq : cq + ckv]
    for h in range(ckv // HEAD_SIZE):
        at = slice(h * HEAD_SIZE, (h + 1) * HEAD_SIZE)
        is_value = (tab_ref[0] * (ckv // HEAD_SIZE) + h) % 2 == 1
        term = jnp.where(is_value, dot_nn(low_v, up_kv[:, at]), dot_nn(low_k, up_kv[:, at]))
        piece = (kv_ref[:, at] + term).astype(BF16)
        if rotate_keys and h % 2 == 0:
            piece = turn_kernel(piece.astype(F32), cosine, sine).astype(BF16)
        kvo[:, at] = piece


def finish_qkv(table, q_lin, kv_lin, low_in, ups, cosine, sine, rotate_keys):
    rows, cq = q_lin.shape
    ckv = kv_lin.shape[1]
    return pl.pallas_call(
        functools.partial(finish_kernel, rotate_keys),
        grid_spec=pltpu.PrefetchScalarGridSpec(
            num_scalar_prefetch=1,
            grid=(rows // BLK,),
            in_specs=[
                pl.BlockSpec((BLK, cq), lambda b, t: (b, 0)),
                pl.BlockSpec((BLK, ckv), lambda b, t: (b, 0)),
                pl.BlockSpec((BLK, low_in.shape[1]), lambda b, t: (b, 0)),
                pl.BlockSpec((1,) + ups.shape[1:], lambda b, t: (b, 0, 0)),
                pl.BlockSpec((BLK, HEAD_SIZE), lambda b, t: (b, 0)),
                pl.BlockSpec((BLK, HEAD_SIZE), lambda b, t: (b, 0)),
            ],
            out_specs=[
                pl.BlockSpec((BLK, cq), lambda b, t: (b, 0)),
                pl.BlockSpec((BLK, ckv), lambda b, t: (b, 0)),
            ],
        ),
        out_shape=[
            jax.ShapeDtypeStruct((rows, cq), BF16),
            jax.ShapeDtypeStruct((rows, ckv), BF16),
        ],
        compiler_params=params(),
        cost_estimate=cost(2 * rows * ADAPTER_RANK * (cq + 2 * ckv), 6 * rows * (cq + ckv)),
        name="finish_qkv",
    )(table, q_lin, kv_lin, low_in, ups, cosine, sine)


def masked(scores, first_ref, own, base):
    rows, cols = scores.shape
    key_pos = base + lax.broadcasted_iota(jnp.int32, (rows, cols), 0)
    allowed = key_pos >= first_ref[...]
    if own:
        allowed &= key_pos <= base + lax.broadcasted_iota(jnp.int32, (rows, cols), 1)
    return jnp.where(allowed, scores, NEG)


def chunk_on(tab_ref, k, rows):
    me = tab_ref[0]
    chunk = me ^ k
    return chunk, (chunk <= me) & ((chunk + 1) * rows > tab_ref[1])


def forward_kernel(heads, count, tab_ref, first_ref, q_ref, *refs):
    kv_refs = refs[:count]
    out_ref, norm_ref, acc, top, total = refs[count:]
    rows = q_ref.shape[0]
    for k in range(count):

        def chunk_step(k=k):
            base = (tab_ref[0] ^ k) * rows
            keys = kv_refs[k][:, :HEAD_SIZE]
            values = kv_refs[k][:, HEAD_SIZE:]
            for h in range(heads):
                at = slice(h * HEAD_SIZE, (h + 1) * HEAD_SIZE)
                scores = masked(dot_nt(keys, q_ref[:, at]), first_ref, k == 0, base)
                here = jnp.max(scores, axis=0, keepdims=True)
                if k == 0:
                    new_top = here
                else:
                    old_top = top[h : h + 1, :]
                    new_top = jnp.maximum(old_top, here)
                weights = jnp.exp((scores - new_top) * SCALE)
                here_sum = jnp.sum(weights, axis=0, keepdims=True)
                here_out = dot_tn(values, weights.astype(BF16))
                if k == 0:
                    total[h : h + 1, :] = here_sum
                    acc[h] = here_out
                else:
                    decay = jnp.exp((old_top - new_top) * SCALE)
                    total[h : h + 1, :] = total[h : h + 1, :] * decay + here_sum
                    acc[h] = acc[h] * decay + here_out
                top[h : h + 1, :] = new_top

        if k == 0:
            chunk_step()
        else:
            pl.when(chunk_on(tab_ref, k, rows)[1])(chunk_step)
    for h in range(heads):
        at = slice(h * HEAD_SIZE, (h + 1) * HEAD_SIZE)
        out_ref[:, at] = jnp.transpose(acc[h] / total[h : h + 1, :]).astype(BF16)
    norm_ref[...] = top[...] * SCALE + jnp.log(total[...])


def attention_forward(table, first, query, kvs):
    rows, cols = query.shape
    heads = cols // HEAD_SIZE
    count = len(kvs)
    smem = pl.BlockSpec(memory_space=pltpu.SMEM)
    vmem = pl.BlockSpec(memory_space=pltpu.VMEM)
    work = heads * rows * rows * count
    return pl.pallas_call(
        functools.partial(forward_kernel, heads, count),
        in_specs=[smem] + [vmem] * (2 + count),
        out_specs=[vmem] * 2,
        out_shape=[
            jax.ShapeDtypeStruct((rows, cols), BF16),
            jax.ShapeDtypeStruct((heads, rows), F32),
        ],
        scratch_shapes=[
            pltpu.VMEM((heads, HEAD_SIZE, rows), F32),
            pltpu.VMEM((heads, rows), F32),
            pltpu.VMEM((heads, rows), F32),
        ],
        compiler_params=params(),
        cost_estimate=cost(4 * work * HEAD_SIZE, 4 * rows * cols * count, work),
        name="attention_forward",
    )(table, first, query, *kvs)


def backward_kernel(
    heads, count, tab_ref, first_ref, q_ref, grad_ref, out_ref, norm_ref, cos_ref, sin_ref, *refs
):
    kv_refs = refs[:count]
    gq_ref = refs[count]
    gkv_refs = refs[count + 1 : 2 * count + 1]
    acc, delta = refs[2 * count + 1 :]
    rows = q_ref.shape[0]
    for h in range(heads):
        at = slice(h * HEAD_SIZE, (h + 1) * HEAD_SIZE)
        product = grad_ref[:, at].astype(F32) * out_ref[:, at].astype(F32)
        delta[h : h + 1, :] = jnp.sum(jnp.transpose(product), axis=0, keepdims=True)
    for k in range(count):

        def chunk_step(k=k):
            base = (tab_ref[0] ^ k) * rows
            keys = kv_refs[k][:, :HEAD_SIZE]
            values = kv_refs[k][:, HEAD_SIZE:]
            key_grad = jnp.zeros((rows, HEAD_SIZE), F32)
            value_grad = jnp.zeros((rows, HEAD_SIZE), F32)
            for h in range(heads):
                at = slice(h * HEAD_SIZE, (h + 1) * HEAD_SIZE)
                scores = masked(dot_nt(keys, q_ref[:, at]), first_ref, k == 0, base)
                weights = jnp.exp(scores * SCALE - norm_ref[h : h + 1, :])
                value_grad += dot_nn(weights.astype(BF16), grad_ref[:, at])
                grad_weights = dot_nt(values, grad_ref[:, at])
                grad_scores = (weights * (grad_weights - delta[h : h + 1, :])).astype(BF16)
                key_grad += dot_nn(grad_scores, q_ref[:, at])
                here = dot_tn(keys, grad_scores)
                if k == 0:
                    acc[h] = here
                else:
                    acc[h] += here
            gkv_refs[k][:, :HEAD_SIZE] = (key_grad * SCALE).astype(BF16)
            gkv_refs[k][:, HEAD_SIZE:] = value_grad.astype(BF16)

        if k == 0:
            chunk_step()
        else:
            on = chunk_on(tab_ref, k, rows)[1]
            pl.when(on)(chunk_step)

            @pl.when(jnp.logical_not(on))
            def _(k=k):
                gkv_refs[k][...] = jnp.zeros_like(gkv_refs[k])

    for h in range(heads):
        at = slice(h * HEAD_SIZE, (h + 1) * HEAD_SIZE)
        grad = jnp.transpose(acc[h]) * SCALE
        gq_ref[:, at] = turn_kernel(grad, cos_ref[...], -sin_ref[...]).astype(BF16)


def attention_backward(table, first, query, grad, out, norm, cosine, sine, kvs):
    rows, cols = query.shape
    heads = cols // HEAD_SIZE
    count = len(kvs)
    smem = pl.BlockSpec(memory_space=pltpu.SMEM)
    vmem = pl.BlockSpec(memory_space=pltpu.VMEM)
    work = heads * rows * rows * count
    results = pl.pallas_call(
        functools.partial(backward_kernel, heads, count),
        in_specs=[smem] + [vmem] * (7 + count),
        out_specs=[vmem] * (1 + count),
        out_shape=[jax.ShapeDtypeStruct((rows, cols), BF16)]
        + [jax.ShapeDtypeStruct((rows, 2 * HEAD_SIZE), BF16)] * count,
        scratch_shapes=[
            pltpu.VMEM((heads, HEAD_SIZE, rows), F32),
            pltpu.VMEM((heads, rows), F32),
        ],
        compiler_params=params(),
        cost_estimate=cost(10 * work * HEAD_SIZE, 8 * rows * cols * count, work),
        name="attention_backward",
    )(table, first, query, grad, out, norm, cosine, sine, *kvs)
    return results[0], list(results[1:])


def project_kernel(a_ref, w_ref, o_ref):
    o_ref[0] = dot_nn(a_ref[...], w_ref[...]).astype(BF16)


def project_out(attn, weight, groups):
    rows, depth = attn.shape
    cols = weight.shape[1] // groups
    return pl.pallas_call(
        project_kernel,
        grid=(groups,),
        in_specs=[
            pl.BlockSpec((rows, depth), lambda i: (0, 0)),
            pl.BlockSpec((depth, cols), lambda i: (0, i)),
        ],
        out_specs=pl.BlockSpec((1, rows, cols), lambda i: (i, 0, 0)),
        out_shape=jax.ShapeDtypeStruct((groups, rows, cols), BF16),
        compiler_params=params(),
        cost_estimate=cost(2 * rows * depth * cols * groups, 2 * (rows + depth) * cols * groups),
        name="project_out",
    )(attn, weight)


def grad_attn_kernel(od_at, c_ref, w_ref, lg_ref, up_ref, o_ref, acc):
    step = pl.program_id(0)

    @pl.when(step == 0)
    def _():
        acc[...] = jnp.zeros_like(acc)

    acc[...] += dot_nt(c_ref[0], w_ref[...])

    @pl.when(step == pl.num_programs(0) - 1)
    def _():
        cols = o_ref.shape[1]
        for b in range(o_ref.shape[0] // BLK):
            at = slice(b * BLK, (b + 1) * BLK)
            delta = dot_nn(lg_ref[at, :], up_ref[b][:, od_at : od_at + cols])
            o_ref[at, :] = (acc[at, :] + delta).astype(BF16)


def grad_attn(cot_all, weight, low_grad_o, ups, od_at):
    groups, rows, cols = cot_all.shape
    depth = weight.shape[0]
    return pl.pallas_call(
        functools.partial(grad_attn_kernel, od_at),
        grid=(groups,),
        in_specs=[
            pl.BlockSpec((1, rows, cols), lambda i: (i, 0, 0)),
            pl.BlockSpec((depth, cols), lambda i: (0, i)),
            pl.BlockSpec(low_grad_o.shape, lambda i: (0, 0)),
            pl.BlockSpec(ups.shape, lambda i: (0, 0, 0)),
        ],
        out_specs=pl.BlockSpec((rows, depth), lambda i: (0, 0)),
        out_shape=jax.ShapeDtypeStruct((rows, depth), BF16),
        scratch_shapes=[pltpu.VMEM((rows, depth), F32)],
        compiler_params=params(),
        cost_estimate=cost(2 * rows * depth * cols * groups, 2 * (rows + depth) * cols * groups),
        name="grad_attn",
    )(cot_all, weight, low_grad_o, ups)


def grad_input_kernel(gq_ref, gkv_ref, wq_ref, wkv_ref, o_ref):
    o_ref[0] = (dot_nt(gq_ref[...], wq_ref[...]) + dot_nt(gkv_ref[...], wkv_ref[...])).astype(BF16)


def grad_input(gq, gkv, wq, wkv, groups):
    rows, cq = gq.shape
    ckv = gkv.shape[1]
    cols = wq.shape[0] // groups
    return pl.pallas_call(
        grad_input_kernel,
        grid=(groups,),
        in_specs=[
            pl.BlockSpec((rows, cq), lambda i: (0, 0)),
            pl.BlockSpec((rows, ckv), lambda i: (0, 0)),
            pl.BlockSpec((cols, cq), lambda i: (i, 0)),
            pl.BlockSpec((cols, ckv), lambda i: (i, 0)),
        ],
        out_specs=pl.BlockSpec((1, rows, cols), lambda i: (i, 0, 0)),
        out_shape=jax.ShapeDtypeStruct((groups, rows, cols), BF16),
        compiler_params=params(),
        cost_estimate=cost(
            2 * rows * (cq + ckv) * cols * groups, 2 * (rows + cq + ckv) * cols * groups
        ),
        name="grad_input",
    )(gq, gkv, wq, wkv)


def body(
    hidden_input,
    output_cotangent,
    query_projection,
    key_value_projection,
    output_projection,
    adapter_qkv_down_store,
    adapter_query_up,
    adapter_key_value_up,
    adapter_output_down,
    adapter_output_up,
    crop_token_length,
    tenant_per_block,
    tenant_store_row,
):
    ctx_count = lax.axis_size("ctx")
    tp_count = lax.axis_size("tp")
    ctx_index = lax.axis_index("ctx")
    tp_index = lax.axis_index("tp")
    rows_dev = hidden_input.shape[0]
    head_cols = query_projection.shape[1]
    kv_cols = key_value_projection.shape[1]
    out_cols = output_cotangent.shape[1]
    width_slice = adapter_qkv_down_store.shape[1]
    tenant_owner = adapter_qkv_down_store.shape[0]
    blocks_dev = rows_dev // BLK
    pair_bits = (tp_count // KEY_VALUE_HEADS).bit_length() - 1
    groups = hidden_input.shape[1] // out_cols

    cot_all = lax.all_gather(output_cotangent, "tp", axis=0, tiled=False)

    tenant_ids = jnp.arange(tenant_store_row.shape[0], dtype=jnp.int32)
    rows_per_block = jnp.sum(
        jnp.where(tenant_per_block[:, None] == tenant_ids[None, :], tenant_store_row[None, :], 0),
        axis=1,
    )
    shard_rows = rows_per_block.reshape(ctx_count, blocks_dev)
    shard_owner = shard_rows // tenant_owner
    served = jnp.max(
        jnp.where(shard_owner == ctx_index, shard_rows - ctx_index * tenant_owner, -1), axis=1
    )
    ctx_ids = jnp.arange(ctx_count, dtype=jnp.int32)
    partner_ids = ctx_ids ^ ctx_index
    served_by = jnp.sum(
        jnp.where(partner_ids[:, None] == ctx_ids[None, :], served[None, :], 0), axis=1
    )
    source_of = (
        jnp.sum(jnp.where((ctx_ids == ctx_index)[:, None], shard_owner, 0), axis=0) ^ ctx_index
    )
    serve_row = jnp.maximum(served_by, 0)
    low_table = jnp.concatenate([jnp.stack([tp_index, serve_row[0]]), source_of]).astype(jnp.int32)

    my_pos = ctx_index * rows_dev + jnp.arange(rows_dev, dtype=jnp.int32)
    crop_ends = jnp.cumsum(crop_token_length)
    first = jnp.max(
        jnp.where(crop_ends[:, None] <= my_pos[None, :], crop_ends[:, None], 0),
        axis=0,
        keepdims=True,
    ).astype(jnp.int32)
    attn_table = jnp.stack([ctx_index, first[0, 0]]).astype(jnp.int32)
    cosine, sine = rope_tables(my_pos)

    downs = [
        swap(
            lax.dynamic_index_in_dim(adapter_qkv_down_store, serve_row[k], 0, keepdims=False),
            "ctx",
            k,
        )
        for k in range(1, ctx_count)
    ]

    def packed(k):
        def row(store):
            return lax.dynamic_index_in_dim(store, serve_row[k], 0, keepdims=False)

        return jnp.concatenate(
            [
                row(adapter_query_up),
                row(adapter_key_value_up),
                row(adapter_output_up),
                row(adapter_output_down).T,
            ],
            axis=1,
        )

    ou_at = head_cols + kv_cols
    od_at = ou_at + out_cols
    pack_all = jnp.stack(
        [packed(0)] + [swap(packed(k), "ctx", k) for k in range(1, ctx_count)], axis=0
    )
    ups = jnp.stack(
        [
            lax.dynamic_index_in_dim(pack_all, source_of[b], 0, keepdims=False)
            for b in range(blocks_dev)
        ],
        axis=0,
    )

    q_lin, kv_lin = dense_qkv(hidden_input, query_projection, key_value_projection)
    low_in = sum_over_tp(low_part(low_table, hidden_input, adapter_qkv_down_store, downs))
    query_rot, kv_local = finish_qkv(
        low_table, q_lin, kv_lin, low_in, ups, cosine, sine, pair_bits == 0
    )
    if pair_bits:
        for bit_no in range(pair_bits):
            partner = swap(kv_local, "tp", 1 << bit_no)
            is_lower = tp_index // (1 << bit_no) % 2 == 0
            kv_local = jnp.where(
                is_lower,
                jnp.concatenate([kv_local, partner], axis=1),
                jnp.concatenate([partner, kv_local], axis=1),
            )
        key_rot = turn(kv_local[:, :HEAD_SIZE].astype(F32), cosine, sine).astype(BF16)
        kv_local = jnp.concatenate([key_rot, kv_local[:, HEAD_SIZE:]], axis=1)
    kvs = [kv_local] + [swap(kv_local, "ctx", k) for k in range(1, ctx_count)]

    attn_out, log_norm = attention_forward(attn_table, first, query_rot, kvs)
    heads_sum = lax.psum_scatter(
        project_out(attn_out, output_projection, groups), "tp", scatter_dimension=0, tiled=False
    )
    out_blocks = attn_out.reshape(blocks_dev, BLK, head_cols)
    output_up = ups[:, :, ou_at : ou_at + out_cols]
    output_down_t = ups[:, :, od_at:]
    grad_blocks = output_cotangent.reshape(blocks_dev, BLK, out_cols)
    low_grad_o = sum_over_tp(
        jnp.einsum("bkc,brc->bkr", grad_blocks, output_up, preferred_element_type=F32).reshape(
            rows_dev, ADAPTER_RANK
        )
    )
    attention_gradient = grad_attn(cot_all, output_projection, low_grad_o, ups, od_at)

    grad_q, kv_parts = attention_backward(
        attn_table, first, query_rot, attention_gradient, attn_out, log_norm, cosine, sine, kvs
    )
    reduced = kv_parts[0].astype(F32)
    for k in range(1, ctx_count):
        reduced = reduced + swap(kv_parts[k], "ctx", k).astype(F32)
    reduced = jnp.concatenate(
        [turn(reduced[:, :HEAD_SIZE], cosine, -sine), reduced[:, HEAD_SIZE:]], axis=1
    )
    for bit_no in reversed(range(pair_bits)):
        half_cols = reduced.shape[1] // 2
        is_lower = tp_index // (1 << bit_no) % 2 == 0
        keep_part = jnp.where(is_lower, reduced[:, :half_cols], reduced[:, half_cols:])
        send_part = jnp.where(is_lower, reduced[:, half_cols:], reduced[:, :half_cols])
        reduced = keep_part + swap(send_part.astype(BF16), "tp", 1 << bit_no).astype(F32)
    grad_kv = reduced.astype(BF16)

    input_sum = lax.psum_scatter(
        grad_input(grad_q, grad_kv, query_projection, key_value_projection, groups),
        "tp",
        scatter_dimension=0,
        tiled=False,
    )

    low_out = sum_over_tp(
        jnp.einsum("bkc,brc->bkr", out_blocks, output_down_t, preferred_element_type=F32).reshape(
            rows_dev, ADAPTER_RANK
        )
    ).reshape(blocks_dev, BLK, ADAPTER_RANK)
    adapter_result = jnp.einsum("bkr,brc->bkc", low_out, output_up, preferred_element_type=F32)
    output = (heads_sum.astype(F32) + adapter_result.reshape(rows_dev, out_cols)).astype(BF16)

    kv_index = tp_index * kv_cols + jnp.arange(kv_cols, dtype=jnp.int32)
    is_value = kv_index // HEAD_SIZE % 2 == 1
    grad_q_blocks = grad_q.reshape(blocks_dev, BLK, head_cols)
    grad_kv_blocks = grad_kv.reshape(blocks_dev, BLK, kv_cols)
    query_up = ups[:, :, :head_cols]
    kv_up = ups[:, :, head_cols : head_cols + kv_cols]
    zero = jnp.zeros((), BF16)
    low_grad_part = jnp.concatenate(
        [
            jnp.einsum("bkc,brc->bkr", grad_q_blocks, query_up, preferred_element_type=F32),
            jnp.einsum(
                "bkc,brc->bkr",
                grad_kv_blocks,
                jnp.where(is_value, zero, kv_up),
                preferred_element_type=F32,
            ),
            jnp.einsum(
                "bkc,brc->bkr",
                grad_kv_blocks,
                jnp.where(is_value, kv_up, zero),
                preferred_element_type=F32,
            ),
        ],
        axis=2,
    )
    low_grad = sum_over_tp(low_grad_part.reshape(rows_dev, 3 * ADAPTER_RANK)).reshape(
        blocks_dev, BLK, 3 * ADAPTER_RANK
    )
    down_all = jnp.stack(
        [lax.dynamic_index_in_dim(adapter_qkv_down_store, serve_row[0], 0, keepdims=False)] + downs,
        axis=0,
    )
    down_maps = jnp.stack(
        [
            lax.dynamic_index_in_dim(down_all, source_of[b], 0, keepdims=False)
            for b in range(blocks_dev)
        ],
        axis=0,
    )
    input_delta = jnp.einsum("bkn,bjn->bkj", low_grad, down_maps, preferred_element_type=F32)
    hidden_input_gradient = (
        input_sum.astype(F32) + input_delta.reshape(rows_dev, width_slice)
    ).astype(BF16)

    low_blocks = low_in.reshape(blocks_dev, BLK, 3 * ADAPTER_RANK)
    low_q = low_blocks[..., :ADAPTER_RANK]
    low_k = low_blocks[..., ADAPTER_RANK : 2 * ADAPTER_RANK]
    low_v = low_blocks[..., 2 * ADAPTER_RANK :]
    input_slice = lax.dynamic_slice_in_dim(
        hidden_input, tp_index * width_slice, width_slice, 1
    ).reshape(blocks_dev, BLK, width_slice)
    block_down = jnp.einsum("bkw,bkr->bwr", input_slice, low_grad, preferred_element_type=F32)
    block_up_kv = jnp.where(
        is_value,
        jnp.einsum("bkr,bkc->brc", low_v, grad_kv_blocks, preferred_element_type=F32),
        jnp.einsum("bkr,bkc->brc", low_k, grad_kv_blocks, preferred_element_type=F32),
    )
    block_pack = jnp.concatenate(
        [
            jnp.einsum("bkr,bkc->brc", low_q, grad_q_blocks, preferred_element_type=F32),
            block_up_kv,
            jnp.einsum("bkr,bkc->brc", low_out, grad_blocks, preferred_element_type=F32),
            jnp.einsum(
                "bkr,bkc->brc",
                low_grad_o.reshape(blocks_dev, BLK, ADAPTER_RANK),
                out_blocks,
                preferred_element_type=F32,
            ),
        ],
        axis=2,
    )

    def returned(block_grads):
        arrived = []
        for k in range(ctx_count):
            picked = jnp.zeros(block_grads.shape[1:], BF16)
            for b in range(blocks_dev):
                picked = jnp.where(source_of[b] == k, block_grads[b].astype(BF16), picked)
            arrived.append(picked if k == 0 else swap(picked, "ctx", k))
        return arrived

    def to_store(arrived, part):
        rows = []
        for s in range(tenant_owner):
            total = jnp.where(served_by[0] == s, part(arrived[0]).astype(F32), 0.0)
            for k in range(1, ctx_count):
                total += jnp.where(served_by[k] == s, part(arrived[k]).astype(F32), 0.0)
            rows.append(total)
        return jnp.stack(rows, axis=0)

    pack_back = returned(block_pack)
    down_back = returned(block_down)
    return (
        output,
        hidden_input_gradient,
        to_store(down_back, lambda a: a),
        to_store(pack_back, lambda a: a[:, :head_cols]),
        to_store(pack_back, lambda a: a[:, head_cols:ou_at]),
        to_store(pack_back, lambda a: a[:, od_at:].T),
        to_store(pack_back, lambda a: a[:, ou_at:od_at]),
    )


def solution(mesh):
    in_specs = (
        P("ctx", None),
        P("ctx", "tp"),
        P(None, "tp"),
        P(None, "tp"),
        P("tp", None),
        P("ctx", "tp", None),
        P("ctx", None, "tp"),
        P("ctx", None, "tp"),
        P("ctx", "tp", None),
        P("ctx", None, "tp"),
        P(),
        P(),
        P(),
    )
    out_specs = (
        P("ctx", "tp"),
        P("ctx", "tp"),
        P("ctx", "tp", None),
        P("ctx", None, "tp"),
        P("ctx", None, "tp"),
        P("ctx", "tp", None),
        P("ctx", None, "tp"),
    )
    return jax.shard_map(body, mesh=mesh, in_specs=in_specs, out_specs=out_specs, check_vma=False)
```

```python
import functools
import math

import jax
import jax.numpy as jnp
from jax import lax
from jax.experimental import pallas as pl
from jax.experimental.pallas import tpu as pltpu
from jax.sharding import PartitionSpec as P

HEAD_SIZE = 128
KEY_VALUE_HEADS = 8
ADAPTER_RANK = 64
BLK = 128
NEG = -1e30
ROPE_BASE = 1000000.0
SCALE = HEAD_SIZE ** (-0.5)
VMEM_BYTES = 56 * 1024 * 1024

BF16 = jnp.bfloat16
F32 = jnp.float32


def params():
    return pltpu.CompilerParams(vmem_limit_bytes=VMEM_BYTES)


def cost(flops, bytes_accessed, transcendentals=0):
    return pl.CostEstimate(
        flops=int(flops), bytes_accessed=int(bytes_accessed), transcendentals=int(transcendentals)
    )


def dot_nn(a, b):
    return lax.dot_general(a, b, (((1,), (0,)), ((), ())), preferred_element_type=F32)


def dot_nt(a, b):
    return lax.dot_general(a, b, (((1,), (1,)), ((), ())), preferred_element_type=F32)


def dot_tn(a, b):
    return lax.dot_general(a, b, (((0,), (0,)), ((), ())), preferred_element_type=F32)


def swap(value, axis, mask):
    pairs = [(source, source ^ mask) for source in range(lax.axis_size(axis))]
    return lax.ppermute(value, axis, pairs)


def add_round(a, b):
    return (a.astype(F32) + b.astype(F32)).astype(BF16)


def rope_tables(positions):
    half_dim = HEAD_SIZE // 2
    exponent = jnp.arange(half_dim, dtype=F32) * (2.0 / HEAD_SIZE)
    frequency = jnp.exp(-exponent * math.log(ROPE_BASE))
    angles = positions.astype(F32)[:, None] * frequency[None, :]
    cosine, sine = jnp.cos(angles), jnp.sin(angles)
    return (
        jnp.concatenate([cosine, cosine], axis=1),
        jnp.concatenate([-sine, sine], axis=1),
    )


def turn(values, cosine, sine):
    return values * cosine + jnp.roll(values, HEAD_SIZE // 2, axis=1) * sine


def turn_kernel(values, cosine, sine):
    return values * cosine + pltpu.roll(values, HEAD_SIZE // 2, 1) * sine


def dense_kernel(x_ref, wq_ref, wkv_ref, q_ref, kv_ref):
    @pl.when(pl.program_id(0) == 0)
    def _():
        q_ref[...] = jnp.zeros_like(q_ref)
        kv_ref[...] = jnp.zeros_like(kv_ref)

    x = x_ref[...]
    q_ref[...] += dot_nn(x, wq_ref[...])
    kv_ref[...] += dot_nn(x, wkv_ref[...])


def dense_qkv(x, wq, wkv):
    rows, width = x.shape
    step = 2048
    cq, ckv = wq.shape[1], wkv.shape[1]
    return pl.pallas_call(
        dense_kernel,
        grid=(width // step,),
        in_specs=[
            pl.BlockSpec((rows, step), lambda i: (0, i)),
            pl.BlockSpec((step, cq), lambda i: (i, 0)),
            pl.BlockSpec((step, ckv), lambda i: (i, 0)),
        ],
        out_specs=[
            pl.BlockSpec((rows, cq), lambda i: (0, 0)),
            pl.BlockSpec((rows, ckv), lambda i: (0, 0)),
        ],
        out_shape=[
            jax.ShapeDtypeStruct((rows, cq), F32),
            jax.ShapeDtypeStruct((rows, ckv), F32),
        ],
        compiler_params=params(),
        cost_estimate=cost(2 * rows * width * (cq + ckv), 2 * width * (rows + cq + ckv)),
        name="dense_qkv",
    )(x, wq, wkv)


ENDS_AT = 2
SEND_AT = 16
SERVED_AT = 32
SOURCE_AT = 48
TABLE = 64


def serve_kernel(
    count, blocks, owned, crop_ref, tenant_ref, row_ref, down, up_q, up_kv, up_o, down_o, *outs
):
    tab = outs[0]
    firsts, lates = outs[1 : 1 + count], outs[1 + count :]
    me = lax.axis_index("ctx")
    for i in range(TABLE):
        tab[i] = 0
    tab[0] = me
    tab[1] = lax.axis_index("tp")
    end = jnp.int32(0)
    for i in range(crop_ref.shape[0]):
        end = end + crop_ref[i]
        tab[ENDS_AT + i] = end
    for b in range(blocks):
        row = row_ref[tenant_ref[me * blocks + b]]
        tab[SOURCE_AT + b] = (row // owned) ^ me
    for k in range(count):
        served = jnp.int32(-1)
        for b in range(blocks):
            row = row_ref[tenant_ref[(me ^ k) * blocks + b]]
            served = jnp.where(row // owned == me, row - me * owned, served)
        tab[SERVED_AT + k] = served
        tab[SEND_AT + k] = jnp.maximum(served, 0)
    rank, width = ADAPTER_RANK, down.shape[2]
    half, quarter = rank // 2, rank // 4
    cq, ckv = width // 2, width // 4
    for k in range(count):
        at = tab[SEND_AT + k]
        low = down.shape[1]
        firsts[k][:low, :] = down[at]
        for i in range(2):
            firsts[k][low : low + half, i * cq : (i + 1) * cq] = up_q[
                at, i * half : (i + 1) * half, :
            ]
            lates[k][rank : rank + half, i * cq : (i + 1) * cq] = down_o[
                at, i * half : (i + 1) * half, :
            ]
        for i in range(4):
            firsts[k][low + half :, i * ckv : (i + 1) * ckv] = up_kv[
                at, i * quarter : (i + 1) * quarter, :
            ]
        lates[k][:rank, :] = up_o[at]


def serve(count, blocks, crops, tenants, store_rows, down, up_q, up_kv, up_o, down_o):
    rank, width = ADAPTER_RANK, down.shape[2]
    assert up_q.shape[2] * 2 == width and up_kv.shape[2] * 4 == width
    assert up_o.shape[2] == width and down_o.shape[2] * 2 == width
    smem = pl.BlockSpec(memory_space=pltpu.SMEM)
    vmem = pl.BlockSpec(memory_space=pltpu.VMEM)
    first = jax.ShapeDtypeStruct((3 * rank + rank // 2 + rank // 4, width), BF16)
    late = jax.ShapeDtypeStruct((rank + rank // 2, width), BF16)
    results = pl.pallas_call(
        functools.partial(serve_kernel, count, blocks, down.shape[0]),
        in_specs=[smem] * 3 + [vmem] * 5,
        out_specs=[smem] + [vmem] * (2 * count),
        out_shape=[jax.ShapeDtypeStruct((TABLE,), jnp.int32)] + [first] * count + [late] * count,
        compiler_params=params(),
        name="serve",
    )(crops, tenants, store_rows, down, up_q, up_kv, up_o, down_o)
    return results[0], list(results[1 : 1 + count]), list(results[1 + count :])


def unpack_q(ref):
    rows, width = ref.shape
    value = ref[...]
    return jnp.concatenate([value[:, : width // 2], value[:, width // 2 :]], axis=0)


def unpack_kv(ref):
    rows, width = ref.shape
    value = ref[...]
    step = width // 4
    return jnp.concatenate([value[:, i * step : (i + 1) * step] for i in range(4)], axis=0)


def pick(tab_ref, block, count, step):
    for k in range(count):

        @pl.when(tab_ref[SOURCE_AT + block] == k)
        def _(k=k):
            step(k)


def split_rows(tab_ref, whole, mine, other):
    half = mine.shape[0]

    @pl.when(tab_ref[1] % 2 == 0)
    def _():
        mine[...] = whole[:half, :]
        other[...] = whole[half:, :]

    @pl.when(tab_ref[1] % 2 == 1)
    def _():
        mine[...] = whole[half:, :]
        other[...] = whole[:half, :]


def join_rows(tab_ref, mine, other, whole):
    half = mine.shape[0]

    @pl.when(tab_ref[1] % 2 == 0)
    def _():
        whole[:half, :] = mine[...]
        whole[half:, :] = other[...]

    @pl.when(tab_ref[1] % 2 == 1)
    def _():
        whole[:half, :] = other[...]
        whole[half:, :] = mine[...]


def sum_halves(mine, other, beside=None):
    total = add_round(mine, swap(other, "tp", 1))
    mask = 2
    while mask < lax.axis_size("tp"):
        arrived = swap(total, "tp", mask)
        if mask == 2 and beside is not None:
            arrived, beside = lax.optimization_barrier((arrived, beside))
        total = add_round(total, arrived)
        mask *= 2
    halves = (total, swap(total, "tp", 1))
    return halves if beside is None else (halves, beside)


def block_rows(b):
    return slice(b * BLK, (b + 1) * BLK)


def whole_spec(shape):
    return pl.BlockSpec(shape, lambda i, t: (0,) * len(shape))


def part_spec(rows, row_block, width):
    return pl.BlockSpec((rows, width), lambda i, t: (row_block, 0))


def table_call(kernel, table, operands, in_specs, shapes, scratch, name, flops=0, out_specs=None):
    moved = sum(math.prod(s.block_shape) * 2 for s in in_specs)
    moved += sum(math.prod(s.shape) * s.dtype.itemsize for s in shapes)
    return pl.pallas_call(
        kernel,
        grid_spec=pltpu.PrefetchScalarGridSpec(
            num_scalar_prefetch=1,
            grid=(1,),
            in_specs=in_specs,
            out_specs=[whole_spec(s.shape) for s in shapes],
            scratch_shapes=scratch,
        ),
        out_shape=shapes,
        compiler_params=params(),
        cost_estimate=cost(flops, moved),
        name=name,
    )(table, *operands)


def low_kernel(count, tab_ref, x_ref, *refs):
    downs = refs[:count]
    mine, other, whole = refs[count:]
    for b in range(whole.shape[0] // BLK):

        def step(k, b=b):
            whole[block_rows(b), :] = dot_nt(x_ref[block_rows(b), :], downs[k][...]).astype(BF16)

        pick(tab_ref, b, count, step)
    split_rows(tab_ref, whole, mine, other)


def low_part(table, x, firsts):
    rows, width, cols = x.shape[0], firsts[0].shape[1], 3 * ADAPTER_RANK
    half = jax.ShapeDtypeStruct((rows // 2, cols), BF16)
    return table_call(
        functools.partial(low_kernel, len(firsts)),
        table,
        [x] + firsts,
        [pl.BlockSpec((rows, width), lambda i, t: (0, t[1]))]
        + [part_spec(cols, 0, width)] * len(firsts),
        [half, half],
        [pltpu.VMEM((rows, cols), BF16)],
        "low_part",
        2 * rows * width * cols,
    )


def finish_kernel(count, rotate_keys, tab_ref, q_ref, kv_ref, mine, other, cos_ref, sin_ref, *refs):
    ups = refs[:count]
    qo, kvo, low_out, low = refs[count:]
    cq, ckv = q_ref.shape[1], kv_ref.shape[1]
    half = ADAPTER_RANK // 2
    join_rows(tab_ref, mine, other, low)
    low_out[...] = low[...]
    for b in range(q_ref.shape[0] // BLK):

        def step(k, b=b):
            at_rows = block_rows(b)
            cosine, sine = cos_ref[at_rows, :], sin_ref[at_rows, :]
            low_q = low[at_rows, :ADAPTER_RANK]
            low_k = low[at_rows, ADAPTER_RANK : 2 * ADAPTER_RANK]
            low_v = low[at_rows, 2 * ADAPTER_RANK :]
            query = q_ref[at_rows, :] + dot_nn(low_q, unpack_q(ups[k].at[:half]))
            for h in range(cq // HEAD_SIZE):
                at = slice(h * HEAD_SIZE, (h + 1) * HEAD_SIZE)
                qo[at_rows, at] = turn_kernel(query[:, at], cosine, sine).astype(BF16)
            up_kv = unpack_kv(ups[k].at[half:])
            for h in range(ckv // HEAD_SIZE):
                at = slice(h * HEAD_SIZE, (h + 1) * HEAD_SIZE)
                if rotate_keys:
                    term = dot_nn(low_v if h % 2 else low_k, up_kv[:, at])
                else:
                    is_value = (tab_ref[1] * (ckv // HEAD_SIZE) + h) % 2 == 1
                    term = jnp.where(
                        is_value, dot_nn(low_v, up_kv[:, at]), dot_nn(low_k, up_kv[:, at])
                    )
                piece = (kv_ref[at_rows, at] + term).astype(BF16)
                if rotate_keys and h % 2 == 0:
                    piece = turn_kernel(piece.astype(F32), cosine, sine).astype(BF16)
                kvo[at_rows, at] = piece

        pick(tab_ref, b, count, step)


def finish_qkv(table, q_lin, kv_lin, halves, firsts, cosine, sine, rotate_keys):
    rows, cq = q_lin.shape
    ckv = kv_lin.shape[1]
    cols, width = 3 * ADAPTER_RANK, firsts[0].shape[1]
    part = ADAPTER_RANK // 2 + ADAPTER_RANK // 4
    return table_call(
        functools.partial(finish_kernel, len(firsts), rotate_keys),
        table,
        [q_lin, kv_lin, *halves, cosine, sine] + firsts,
        [
            whole_spec((rows, cq)),
            whole_spec((rows, ckv)),
            whole_spec((rows // 2, cols)),
            whole_spec((rows // 2, cols)),
            whole_spec((rows, HEAD_SIZE)),
            whole_spec((rows, HEAD_SIZE)),
        ]
        + [part_spec(part, cols // part, width)] * len(firsts),
        [
            jax.ShapeDtypeStruct((rows, cq), BF16),
            jax.ShapeDtypeStruct((rows, ckv), BF16),
            jax.ShapeDtypeStruct((rows, cols), BF16),
        ],
        [pltpu.VMEM((rows, cols), BF16)],
        "finish_qkv",
        2 * rows * ADAPTER_RANK * (cq + 2 * ckv),
    )


def low_o_kernel(count, tab_ref, cot_ref, attn_ref, *refs):
    lates = refs[:count]
    mine, other, whole = refs[count:]
    rank = ADAPTER_RANK
    for b in range(whole.shape[0] // BLK):

        def step(k, b=b):
            at = block_rows(b)
            whole[at, :rank] = dot_nt(cot_ref[at, :], lates[k][:rank, :]).astype(BF16)
            down = unpack_q(lates[k].at[rank:])
            whole[at, rank:] = dot_nt(attn_ref[at, :], down).astype(BF16)

        pick(tab_ref, b, count, step)
    split_rows(tab_ref, whole, mine, other)


def low_o_part(table, cot, attn, lates):
    rows, width = cot.shape
    cols = 2 * ADAPTER_RANK
    half = jax.ShapeDtypeStruct((rows // 2, cols), BF16)
    return table_call(
        functools.partial(low_o_kernel, len(lates)),
        table,
        [cot, attn] + lates,
        [whole_spec(cot.shape), whole_spec(attn.shape)]
        + [whole_spec(lates[0].shape)] * len(lates),
        [half, half],
        [pltpu.VMEM((rows, cols), BF16)],
        "low_o_part",
        2 * rows * cols * width,
    )


def low_g_kernel(count, tab_ref, gq_ref, gkv_ref, *refs):
    ups = refs[:count]
    mine, other, whole = refs[count:]
    rank = ADAPTER_RANK
    ckv = gkv_ref.shape[1]
    for b in range(whole.shape[0] // BLK):

        def step(k, b=b):
            at = block_rows(b)
            up_q = unpack_q(ups[k].at[: rank // 2])
            whole[at, :rank] = dot_nt(gq_ref[at, :], up_q).astype(BF16)
            up_kv = unpack_kv(ups[k].at[rank // 2 :])
            sums = [jnp.zeros((BLK, rank), F32)] * 2
            for h in range(ckv // HEAD_SIZE):
                cols = slice(h * HEAD_SIZE, (h + 1) * HEAD_SIZE)
                term = dot_nt(gkv_ref[at, cols], up_kv[:, cols])
                is_value = (tab_ref[1] * (ckv // HEAD_SIZE) + h) % 2 == 1
                sums[0] = sums[0] + jnp.where(is_value, 0.0, term)
                sums[1] = sums[1] + jnp.where(is_value, term, 0.0)
            whole[at, rank : 2 * rank] = sums[0].astype(BF16)
            whole[at, 2 * rank :] = sums[1].astype(BF16)

        pick(tab_ref, b, count, step)
    split_rows(tab_ref, whole, mine, other)


def low_g_part(table, gq, gkv, firsts):
    rows = gq.shape[0]
    cols, width = 3 * ADAPTER_RANK, firsts[0].shape[1]
    part = ADAPTER_RANK // 2 + ADAPTER_RANK // 4
    half = jax.ShapeDtypeStruct((rows // 2, cols), BF16)
    return table_call(
        functools.partial(low_g_kernel, len(firsts)),
        table,
        [gq, gkv] + firsts,
        [whole_spec(gq.shape), whole_spec(gkv.shape)]
        + [part_spec(part, cols // part, width)] * len(firsts),
        [half, half],
        [pltpu.VMEM((rows, cols), BF16)],
        "low_g_part",
        2 * rows * width * ADAPTER_RANK,
    )


def zero_unused(tab_ref, blocks, sends):
    for k in range(len(sends)):
        used = tab_ref[SOURCE_AT] == k
        for b in range(1, blocks):
            used = used | (tab_ref[SOURCE_AT + b] == k)

        @pl.when(jnp.logical_not(used))
        def _(k=k):
            sends[k][...] = jnp.zeros_like(sends[k])


def up_grads_kernel(
    count, tab_ref, low_ref, gq_ref, gkv_ref, o_mine, o_other, cot, attn, *refs
):
    sends, low_o = refs[:count], refs[count]
    rank = ADAPTER_RANK
    join_rows(tab_ref, o_mine, o_other, low_o)
    blocks = low_o.shape[0] // BLK
    cq, ckv = gq_ref.shape[1], gkv_ref.shape[1]
    half, quarter = rank // 2, rank // 4
    late = half + quarter
    zero_unused(tab_ref, blocks, sends)
    for b in range(blocks):

        def step(k, b=b):
            at = block_rows(b)
            out = sends[k]
            up_q = dot_tn(low_ref[at, :rank], gq_ref[at, :]).astype(BF16)
            down_o = dot_tn(low_o[at, :rank], attn[at, :]).astype(BF16)
            for i in range(2):
                rows = slice(i * half, (i + 1) * half)
                cols = slice(i * cq, (i + 1) * cq)
                out[:half, cols] = up_q[rows, :]
                out[late + rank :, cols] = down_o[rows, :]
            for h in range(ckv // HEAD_SIZE):
                piece = slice(h * HEAD_SIZE, (h + 1) * HEAD_SIZE)
                is_value = (tab_ref[1] * (ckv // HEAD_SIZE) + h) % 2 == 1
                up_kv = jnp.where(
                    is_value,
                    dot_tn(low_ref[at, 2 * rank :], gkv_ref[at, piece]),
                    dot_tn(low_ref[at, rank : 2 * rank], gkv_ref[at, piece]),
                ).astype(BF16)
                for i in range(4):
                    cols = slice(i * ckv + h * HEAD_SIZE, i * ckv + (h + 1) * HEAD_SIZE)
                    out[half:late, cols] = up_kv[i * quarter : (i + 1) * quarter, :]
            out[late : late + rank, :] = dot_tn(low_o[at, rank:], cot[at, :]).astype(BF16)

        pick(tab_ref, b, count, step)


def up_grads(table, count, low_in, gq, gkv, o_halves, cot, attn):
    rows, width = cot.shape
    rank = ADAPTER_RANK
    operands = [low_in, gq, gkv, *o_halves, cot, attn]
    return list(
        table_call(
            functools.partial(up_grads_kernel, count),
            table,
            operands,
            [whole_spec(a.shape) for a in operands],
            [jax.ShapeDtypeStruct((2 * rank + rank // 4, width), BF16)] * count,
            [pltpu.VMEM((rows, 2 * rank), BF16)],
            "up_grads",
            2 * rows * width * 3 * rank,
        )
    )


def down_grads_kernel(count, tab_ref, x_ref, mine, other, *refs):
    downs, sends = refs[:count], refs[count : 2 * count]
    delta, low = refs[2 * count :]
    join_rows(tab_ref, mine, other, low)
    blocks = low.shape[0] // BLK
    zero_unused(tab_ref, blocks, sends)
    for b in range(blocks):

        def step(k, b=b):
            at = block_rows(b)
            sends[k][...] = dot_tn(low[at, :], x_ref[at, :]).astype(BF16)
            delta[at, :] = dot_nn(low[at, :], downs[k][...])

        pick(tab_ref, b, count, step)


def down_grads(table, x, halves, firsts):
    rows, cols = x.shape[0], 3 * ADAPTER_RANK
    width, count = firsts[0].shape[1], len(firsts)
    results = table_call(
        functools.partial(down_grads_kernel, count),
        table,
        [x, *halves] + firsts,
        [pl.BlockSpec((rows, width), lambda i, t: (0, t[1]))]
        + [whole_spec(halves[0].shape)] * 2
        + [part_spec(cols, 0, width)] * count,
        [jax.ShapeDtypeStruct((cols, width), BF16)] * count
        + [jax.ShapeDtypeStruct((rows, width), F32)],
        [pltpu.VMEM((rows, cols), BF16)],
        "down_grads",
        4 * rows * width * cols,
    )
    return list(results[:count]), results[count]


def store_kernel(count, tab_ref, *refs):
    downs, ups = refs[:count], refs[count : 2 * count]
    outs = refs[2 * count :]
    row = pl.program_id(0)
    for o in outs:
        o[...] = jnp.zeros_like(o)
    rank = ADAPTER_RANK
    half, quarter = rank // 2, rank // 4
    late = half + quarter
    for k in range(count):

        @pl.when(tab_ref[SERVED_AT + k] == row)
        def _(k=k):
            a = ups[k]
            outs[0][0] += downs[k][...].astype(F32)
            outs[1][0] += unpack_q(a.at[:half]).astype(F32)
            outs[2][0] += unpack_kv(a.at[half:late]).astype(F32)
            outs[3][0] += unpack_q(a.at[late + rank :]).astype(F32)
            outs[4][0] += a[late : late + rank, :].astype(F32)


def store_sums(table, downs, ups, owned):
    rank = ADAPTER_RANK
    width = downs[0].shape[1]
    shapes = [
        jax.ShapeDtypeStruct((owned, r, c), F32)
        for r, c in [
            (3 * rank, width),
            (rank, width // 2),
            (rank, width // 4),
            (rank, width // 2),
            (rank, width),
        ]
    ]
    return pl.pallas_call(
        functools.partial(store_kernel, len(downs)),
        grid_spec=pltpu.PrefetchScalarGridSpec(
            num_scalar_prefetch=1,
            grid=(owned,),
            in_specs=[pl.BlockSpec(a.shape, lambda i, t: (0, 0)) for a in downs + ups],
            out_specs=[pl.BlockSpec((1,) + s.shape[1:], lambda i, t: (i, 0, 0)) for s in shapes],
        ),
        out_shape=shapes,
        compiler_params=params(),
        name="store_sums",
    )(table, *downs, *ups)


def output_kernel(count, tab_ref, sum_ref, mine, other, *refs):
    lates = refs[:count]
    out, low = refs[count:]
    rank = ADAPTER_RANK
    join_rows(tab_ref, mine, other, low)
    for b in range(out.shape[0] // BLK):

        def step(k, b=b):
            at = block_rows(b)
            term = dot_nn(low[at, rank:], lates[k][...])
            out[at, :] = (sum_ref[at, :].astype(F32) + term).astype(BF16)

        pick(tab_ref, b, count, step)


def output_result(table, total, halves, lates):
    rows, width = total.shape
    rank = ADAPTER_RANK
    return table_call(
        functools.partial(output_kernel, len(lates)),
        table,
        [total, *halves] + lates,
        [whole_spec(total.shape)]
        + [whole_spec(halves[0].shape)] * 2
        + [part_spec(rank, 0, width)] * len(lates),
        [jax.ShapeDtypeStruct((rows, width), BF16)],
        [pltpu.VMEM((rows, 2 * rank), BF16)],
        "output_result",
        2 * rows * rank * width,
    )[0]


def crop_start(tab_ref, crops, positions):
    start = jnp.zeros_like(positions)
    for i in range(crops):
        end = tab_ref[ENDS_AT + i]
        start = jnp.where(positions >= end, end, start)
    return start


def masked(scores, first, own, base):
    rows, cols = scores.shape
    key_pos = base + lax.broadcasted_iota(jnp.int32, (rows, cols), 0)
    allowed = key_pos >= first
    if own:
        allowed &= key_pos <= base + lax.broadcasted_iota(jnp.int32, (rows, cols), 1)
    return jnp.where(allowed, scores, NEG)


def chunk_on(tab_ref, crops, k, rows):
    me = tab_ref[0]
    chunk = me ^ k
    return (chunk <= me) & ((chunk + 1) * rows > crop_start(tab_ref, crops, me * rows))


def query_starts(tab_ref, crops, rows):
    positions = tab_ref[0] * rows + lax.broadcasted_iota(jnp.int32, (1, rows), 1)
    return crop_start(tab_ref, crops, positions)


def forward_kernel(heads, count, crops, tab_ref, q_ref, *refs):
    kv_refs = refs[:count]
    out_ref, norm_ref, acc, top, total = refs[count:]
    rows = q_ref.shape[0]
    first = query_starts(tab_ref, crops, rows)
    for k in range(count):

        def chunk_step(k=k):
            base = (tab_ref[0] ^ k) * rows
            keys = kv_refs[k][:, :HEAD_SIZE]
            values = kv_refs[k][:, HEAD_SIZE:]
            for h in range(heads):
                at = slice(h * HEAD_SIZE, (h + 1) * HEAD_SIZE)
                scores = masked(dot_nt(keys, q_ref[:, at]), first, k == 0, base)
                here = jnp.max(scores, axis=0, keepdims=True)
                if k == 0:
                    new_top = here
                else:
                    old_top = top[h : h + 1, :]
                    new_top = jnp.maximum(old_top, here)
                weights = jnp.exp((scores - new_top) * SCALE)
                here_sum = jnp.sum(weights, axis=0, keepdims=True)
                here_out = dot_tn(values, weights.astype(BF16))
                if k == 0:
                    total[h : h + 1, :] = here_sum
                    acc[h] = here_out
                else:
                    decay = jnp.exp((old_top - new_top) * SCALE)
                    total[h : h + 1, :] = total[h : h + 1, :] * decay + here_sum
                    acc[h] = acc[h] * decay + here_out
                top[h : h + 1, :] = new_top

        if k == 0:
            chunk_step()
        else:
            pl.when(chunk_on(tab_ref, crops, k, rows))(chunk_step)
    for h in range(heads):
        at = slice(h * HEAD_SIZE, (h + 1) * HEAD_SIZE)
        out_ref[:, at] = jnp.transpose(acc[h] / total[h : h + 1, :]).astype(BF16)
    norm_ref[...] = top[...] * SCALE + jnp.log(total[...])


def attention_forward(table, crops, query, kvs):
    rows, cols = query.shape
    heads = cols // HEAD_SIZE
    count = len(kvs)
    smem = pl.BlockSpec(memory_space=pltpu.SMEM)
    vmem = pl.BlockSpec(memory_space=pltpu.VMEM)
    work = heads * rows * rows * count
    return pl.pallas_call(
        functools.partial(forward_kernel, heads, count, crops),
        in_specs=[smem] + [vmem] * (1 + count),
        out_specs=[vmem] * 2,
        out_shape=[
            jax.ShapeDtypeStruct((rows, cols), BF16),
            jax.ShapeDtypeStruct((heads, rows), F32),
        ],
        scratch_shapes=[
            pltpu.VMEM((heads, HEAD_SIZE, rows), F32),
            pltpu.VMEM((heads, rows), F32),
            pltpu.VMEM((heads, rows), F32),
        ],
        compiler_params=params(),
        cost_estimate=cost(4 * work * HEAD_SIZE, 4 * rows * cols * count, work),
        name="attention_forward",
    )(table, query, *kvs)


def backward_kernel(
    heads,
    count,
    crops,
    tab_ref,
    q_ref,
    dense_ref,
    mine,
    other,
    out_ref,
    norm_ref,
    cos_ref,
    sin_ref,
    *refs,
):
    kv_refs, lates = refs[:count], refs[count : 2 * count]
    gq_ref = refs[2 * count]
    gkv_refs = refs[2 * count + 1 : 3 * count + 1]
    acc, delta, low, grad_ref = refs[3 * count + 1 :]
    rows = q_ref.shape[0]
    rank = ADAPTER_RANK
    first = query_starts(tab_ref, crops, rows)
    join_rows(tab_ref, mine, other, low)
    for b in range(rows // BLK):

        def add(k, b=b):
            at = block_rows(b)
            term = dot_nn(low[at, :rank], unpack_q(lates[k].at[rank:]))
            grad_ref[at, :] = (dense_ref[at, :] + term).astype(BF16)

        pick(tab_ref, b, count, add)
    for h in range(heads):
        at = slice(h * HEAD_SIZE, (h + 1) * HEAD_SIZE)
        product = grad_ref[:, at].astype(F32) * out_ref[:, at].astype(F32)
        delta[h : h + 1, :] = jnp.sum(jnp.transpose(product), axis=0, keepdims=True)
    for k in range(count):

        def chunk_step(k=k):
            base = (tab_ref[0] ^ k) * rows
            keys = kv_refs[k][:, :HEAD_SIZE]
            values = kv_refs[k][:, HEAD_SIZE:]
            key_grad = jnp.zeros((rows, HEAD_SIZE), F32)
            value_grad = jnp.zeros((rows, HEAD_SIZE), F32)
            for h in range(heads):
                at = slice(h * HEAD_SIZE, (h + 1) * HEAD_SIZE)
                scores = masked(dot_nt(keys, q_ref[:, at]), first, k == 0, base)
                weights = jnp.exp(scores * SCALE - norm_ref[h : h + 1, :])
                value_grad += dot_nn(weights.astype(BF16), grad_ref[:, at])
                grad_weights = dot_nt(values, grad_ref[:, at])
                grad_scores = (weights * (grad_weights - delta[h : h + 1, :])).astype(BF16)
                key_grad += dot_nn(grad_scores, q_ref[:, at])
                here = dot_tn(keys, grad_scores)
                if k == 0:
                    acc[h] = here
                else:
                    acc[h] += here
            gkv_refs[k][:, :HEAD_SIZE] = (key_grad * SCALE).astype(BF16)
            gkv_refs[k][:, HEAD_SIZE:] = value_grad.astype(BF16)

        if k == 0:
            chunk_step()
        else:
            on = chunk_on(tab_ref, crops, k, rows)
            pl.when(on)(chunk_step)

            @pl.when(jnp.logical_not(on))
            def _(k=k):
                gkv_refs[k][...] = jnp.zeros_like(gkv_refs[k])

    for h in range(heads):
        at = slice(h * HEAD_SIZE, (h + 1) * HEAD_SIZE)
        grad = jnp.transpose(acc[h]) * SCALE
        gq_ref[:, at] = turn_kernel(grad, cos_ref[...], -sin_ref[...]).astype(BF16)


def attention_backward(table, crops, query, dense, halves, out, norm, cosine, sine, kvs, lates):
    rows, cols = query.shape
    heads = cols // HEAD_SIZE
    count = len(kvs)
    smem = pl.BlockSpec(memory_space=pltpu.SMEM)
    vmem = pl.BlockSpec(memory_space=pltpu.VMEM)
    work = heads * rows * rows * count
    results = pl.pallas_call(
        functools.partial(backward_kernel, heads, count, crops),
        in_specs=[smem] + [vmem] * (8 + 2 * count),
        out_specs=[vmem] * (1 + count),
        out_shape=[jax.ShapeDtypeStruct((rows, cols), BF16)]
        + [jax.ShapeDtypeStruct((rows, 2 * HEAD_SIZE), BF16)] * count,
        scratch_shapes=[
            pltpu.VMEM((heads, HEAD_SIZE, rows), F32),
            pltpu.VMEM((heads, rows), F32),
            pltpu.VMEM((rows, 2 * ADAPTER_RANK), BF16),
            pltpu.VMEM((rows, cols), BF16),
        ],
        compiler_params=params(),
        cost_estimate=cost(10 * work * HEAD_SIZE, 8 * rows * cols * count, work),
        name="attention_backward",
    )(table, query, dense, *halves, out, norm, cosine, sine, *kvs, *lates)
    return results[0], list(results[1:])


PER_STEP = 2


def project_kernel(a_ref, w_ref, o_ref):
    cols = o_ref.shape[2]
    for i in range(o_ref.shape[0]):
        o_ref[i] = dot_nn(a_ref[...], w_ref[:, i * cols : (i + 1) * cols]).astype(BF16)


def project_out(attn, weight, groups):
    rows, depth = attn.shape
    cols = weight.shape[1] // groups
    return pl.pallas_call(
        project_kernel,
        grid=(groups // PER_STEP,),
        in_specs=[
            pl.BlockSpec((rows, depth), lambda i: (0, 0)),
            pl.BlockSpec((depth, PER_STEP * cols), lambda i: (0, i)),
        ],
        out_specs=pl.BlockSpec((PER_STEP, rows, cols), lambda i: (i, 0, 0)),
        out_shape=jax.ShapeDtypeStruct((groups, rows, cols), BF16),
        compiler_params=params(),
        cost_estimate=cost(2 * rows * depth * cols * groups, 2 * (rows + depth) * cols * groups),
        name="project_out",
    )(attn, weight)


def grad_attn_kernel(c0_ref, c1_ref, w_ref, o_ref):
    step = pl.program_id(0)
    per_step, half, cols = c0_ref.shape
    for c_ref, at in ((c0_ref, slice(0, half)), (c1_ref, slice(half, 2 * half))):
        total = dot_nt(c_ref[0], w_ref[:, :cols])
        for i in range(1, per_step):
            total += dot_nt(c_ref[i], w_ref[:, i * cols : (i + 1) * cols])

        @pl.when(step == 0)
        def _(at=at, total=total):
            o_ref[at, :] = total

        @pl.when(step > 0)
        def _(at=at, total=total):
            o_ref[at, :] += total


def grad_attn(cot_first, cot_second, weight):
    groups, half, cols = cot_first.shape
    depth = weight.shape[0]
    rows = 2 * half
    return pl.pallas_call(
        grad_attn_kernel,
        grid=(groups // PER_STEP,),
        in_specs=[
            pl.BlockSpec((PER_STEP, half, cols), lambda i: (i, 0, 0)),
            pl.BlockSpec((PER_STEP, half, cols), lambda i: (i, 0, 0)),
            pl.BlockSpec((depth, PER_STEP * cols), lambda i: (0, i)),
        ],
        out_specs=pl.BlockSpec((rows, depth), lambda i: (0, 0)),
        out_shape=jax.ShapeDtypeStruct((rows, depth), F32),
        compiler_params=params(),
        cost_estimate=cost(2 * rows * depth * cols * groups, 2 * (rows + depth) * cols * groups),
        name="grad_attn",
    )(cot_first, cot_second, weight)


def grad_input_kernel(gq_ref, gkv_ref, wq_ref, wkv_ref, o_ref):
    cols = o_ref.shape[2]
    for i in range(o_ref.shape[0]):
        at = slice(i * cols, (i + 1) * cols)
        total = dot_nt(gq_ref[...], wq_ref[at, :]) + dot_nt(gkv_ref[...], wkv_ref[at, :])
        o_ref[i] = total.astype(BF16)


def grad_input(gq, gkv, wq, wkv, groups):
    rows, cq = gq.shape
    ckv = gkv.shape[1]
    cols = wq.shape[0] // groups
    return pl.pallas_call(
        grad_input_kernel,
        grid=(groups // PER_STEP,),
        in_specs=[
            pl.BlockSpec((rows, cq), lambda i: (0, 0)),
            pl.BlockSpec((rows, ckv), lambda i: (0, 0)),
            pl.BlockSpec((PER_STEP * cols, cq), lambda i: (i, 0)),
            pl.BlockSpec((PER_STEP * cols, ckv), lambda i: (i, 0)),
        ],
        out_specs=pl.BlockSpec((PER_STEP, rows, cols), lambda i: (i, 0, 0)),
        out_shape=jax.ShapeDtypeStruct((groups, rows, cols), BF16),
        compiler_params=params(),
        cost_estimate=cost(
            2 * rows * (cq + ckv) * cols * groups, 2 * (rows + cq + ckv) * cols * groups
        ),
        name="grad_input",
    )(gq, gkv, wq, wkv)


def body(
    hidden_input,
    output_cotangent,
    query_projection,
    key_value_projection,
    output_projection,
    adapter_qkv_down_store,
    adapter_query_up,
    adapter_key_value_up,
    adapter_output_down,
    adapter_output_up,
    crop_token_length,
    tenant_per_block,
    tenant_store_row,
):
    ctx_count = lax.axis_size("ctx")
    tp_count = lax.axis_size("tp")
    ctx_index = lax.axis_index("ctx")
    tp_index = lax.axis_index("tp")
    rows_dev = hidden_input.shape[0]
    out_cols = output_cotangent.shape[1]
    tenant_owner = adapter_qkv_down_store.shape[0]
    blocks_dev = rows_dev // BLK
    pair_bits = (tp_count // KEY_VALUE_HEADS).bit_length() - 1
    groups = hidden_input.shape[1] // out_cols
    crops = crop_token_length.shape[0]
    partners = range(1, ctx_count)

    half_rows = rows_dev // 2

    table, firsts, lates = serve(
        ctx_count,
        blocks_dev,
        crop_token_length,
        tenant_per_block,
        tenant_store_row,
        adapter_qkv_down_store.swapaxes(1, 2),
        adapter_query_up,
        adapter_key_value_up,
        adapter_output_up,
        adapter_output_down.swapaxes(1, 2),
    )
    table, cot_part = lax.optimization_barrier((table, output_cotangent))
    cot_first = lax.all_gather(cot_part[:half_rows], "tp", axis=0, tiled=False)
    firsts = [firsts[0]] + [swap(firsts[k], "ctx", k) for k in partners]
    my_pos = ctx_index * rows_dev + jnp.arange(rows_dev, dtype=jnp.int32)
    q_lin, kv_lin = dense_qkv(hidden_input, query_projection, key_value_projection)
    firsts, q_lin, kv_lin, tables = lax.optimization_barrier(
        (firsts, q_lin, kv_lin, rope_tables(my_pos))
    )
    cosine, sine = tables
    low_halves = low_part(table, hidden_input, firsts)
    low_halves, cot_rest = lax.optimization_barrier(
        (sum_halves(*low_halves), output_cotangent[half_rows:])
    )
    cot_second = lax.all_gather(cot_rest, "tp", axis=0, tiled=False)
    query_rot, kv_local, low_in = finish_qkv(
        table, q_lin, kv_lin, low_halves, firsts, cosine, sine, pair_bits == 0
    )
    if pair_bits:
        for bit_no in range(pair_bits):
            partner = swap(kv_local, "tp", 1 << bit_no)
            is_lower = tp_index // (1 << bit_no) % 2 == 0
            kv_local = jnp.where(
                is_lower,
                jnp.concatenate([kv_local, partner], axis=1),
                jnp.concatenate([partner, kv_local], axis=1),
            )
        key_rot = turn(kv_local[:, :HEAD_SIZE].astype(F32), cosine, sine).astype(BF16)
        kv_local = jnp.concatenate([key_rot, kv_local[:, HEAD_SIZE:]], axis=1)
    kvs = [kv_local] + [swap(kv_local, "ctx", k) for k in partners]
    kvs, lates = lax.optimization_barrier((kvs, lates))
    lates = [lates[0]] + [swap(lates[k], "ctx", k) for k in partners]

    attn_out, log_norm = attention_forward(table, crops, query_rot, kvs)
    lates, attn_out = lax.optimization_barrier((lates, attn_out))
    heads_sum = lax.psum_scatter(
        project_out(attn_out, output_projection, groups), "tp", scatter_dimension=0, tiled=False
    )
    grad_dense = grad_attn(cot_first, cot_second, output_projection)
    o_halves, grad_dense = sum_halves(
        *low_o_part(table, output_cotangent, attn_out, lates), beside=grad_dense
    )
    grad_q, kv_parts = attention_backward(
        table, crops, query_rot, grad_dense, o_halves, attn_out, log_norm, cosine, sine, kvs, lates
    )
    reduced = kv_parts[0].astype(F32)
    for k in partners:
        reduced = reduced + swap(kv_parts[k], "ctx", k).astype(F32)
    reduced = jnp.concatenate(
        [turn(reduced[:, :HEAD_SIZE], cosine, -sine), reduced[:, HEAD_SIZE:]], axis=1
    )
    for bit_no in reversed(range(pair_bits)):
        half_cols = reduced.shape[1] // 2
        is_lower = tp_index // (1 << bit_no) % 2 == 0
        keep_part = jnp.where(is_lower, reduced[:, :half_cols], reduced[:, half_cols:])
        send_part = jnp.where(is_lower, reduced[:, half_cols:], reduced[:, :half_cols])
        reduced = keep_part + swap(send_part.astype(BF16), "tp", 1 << bit_no).astype(F32)
    grad_kv = reduced.astype(BF16)

    input_sum = lax.psum_scatter(
        grad_input(grad_q, grad_kv, query_projection, key_value_projection, groups),
        "tp",
        scatter_dimension=0,
        tiled=False,
    )
    output = output_result(table, heads_sum, o_halves, lates)

    g_halves = sum_halves(*low_g_part(table, grad_q, grad_kv, firsts))
    up_sends = up_grads(
        table, ctx_count, low_in, grad_q, grad_kv, o_halves, output_cotangent, attn_out
    )
    up_back = [up_sends[0]] + [swap(up_sends[k], "ctx", k) for k in partners]
    down_sends, input_delta = down_grads(table, hidden_input, g_halves, firsts)
    down_back = [down_sends[0]] + [swap(down_sends[k], "ctx", k) for k in partners]
    down_back, output = lax.optimization_barrier((down_back, output))
    stores = store_sums(table, down_back, up_back, tenant_owner)
    input_sum, input_delta, stores = lax.optimization_barrier((input_sum, input_delta, stores))
    hidden_input_gradient = (input_sum.astype(F32) + input_delta).astype(BF16)
    return (
        output,
        hidden_input_gradient,
        stores[0].swapaxes(1, 2),
        stores[1],
        stores[2],
        stores[3].swapaxes(1, 2),
        stores[4],
    )


def solution(mesh):
    in_specs = (
        P("ctx", None),
        P("ctx", "tp"),
        P(None, "tp"),
        P(None, "tp"),
        P("tp", None),
        P("ctx", "tp", None),
        P("ctx", None, "tp"),
        P("ctx", None, "tp"),
        P("ctx", "tp", None),
        P("ctx", None, "tp"),
        P(),
        P(),
        P(),
    )
    out_specs = (
        P("ctx", "tp"),
        P("ctx", "tp"),
        P("ctx", "tp", None),
        P("ctx", None, "tp"),
        P("ctx", None, "tp"),
        P("ctx", "tp", None),
        P("ctx", None, "tp"),
    )
    return jax.shard_map(body, mesh=mesh, in_specs=in_specs, out_specs=out_specs, check_vma=False)
```

```python
import functools
import math

import jax
import jax.numpy as jnp
from jax import lax
from jax.experimental import pallas as pl
from jax.experimental.pallas import tpu as pltpu
from jax.sharding import PartitionSpec as P

HEAD_SIZE = 128
KEY_VALUE_HEADS = 8
ADAPTER_RANK = 64
BLK = 128
NEG = -1e30
ROPE_BASE = 1000000.0
SCALE = HEAD_SIZE ** (-0.5)
VMEM_BYTES = 56 * 1024 * 1024

BF16 = jnp.bfloat16
F32 = jnp.float32


def params():
    return pltpu.CompilerParams(vmem_limit_bytes=VMEM_BYTES)


def cost(flops, bytes_accessed, transcendentals=0):
    return pl.CostEstimate(
        flops=int(flops), bytes_accessed=int(bytes_accessed), transcendentals=int(transcendentals)
    )


def dot_nn(a, b):
    return lax.dot_general(a, b, (((1,), (0,)), ((), ())), preferred_element_type=F32)


def dot_nt(a, b):
    return lax.dot_general(a, b, (((1,), (1,)), ((), ())), preferred_element_type=F32)


def dot_tn(a, b):
    return lax.dot_general(a, b, (((0,), (0,)), ((), ())), preferred_element_type=F32)


def swap(value, axis, mask):
    pairs = [(source, source ^ mask) for source in range(lax.axis_size(axis))]
    return lax.ppermute(value, axis, pairs)


def add_round(a, b):
    return (a.astype(F32) + b.astype(F32)).astype(BF16)


def rope_tables(positions):
    half_dim = HEAD_SIZE // 2
    exponent = jnp.arange(half_dim, dtype=F32) * (2.0 / HEAD_SIZE)
    frequency = jnp.exp(-exponent * math.log(ROPE_BASE))
    angles = positions.astype(F32)[:, None] * frequency[None, :]
    cosine, sine = jnp.cos(angles), jnp.sin(angles)
    return (
        jnp.concatenate([cosine, cosine], axis=1),
        jnp.concatenate([-sine, sine], axis=1),
    )


def turn(values, cosine, sine):
    return values * cosine + jnp.roll(values, HEAD_SIZE // 2, axis=1) * sine


def turn_kernel(values, cosine, sine):
    return values * cosine + pltpu.roll(values, HEAD_SIZE // 2, 1) * sine


def dense_kernel(x_ref, wq_ref, wkv_ref, q_ref, kv_ref):
    @pl.when(pl.program_id(0) == 0)
    def _():
        q_ref[...] = jnp.zeros_like(q_ref)
        kv_ref[...] = jnp.zeros_like(kv_ref)

    x = x_ref[...]
    q_ref[...] += dot_nn(x, wq_ref[...])
    kv_ref[...] += dot_nn(x, wkv_ref[...])


def dense_qkv(x, wq, wkv):
    rows, width = x.shape
    step = 2048
    cq, ckv = wq.shape[1], wkv.shape[1]
    return pl.pallas_call(
        dense_kernel,
        grid=(width // step,),
        in_specs=[
            pl.BlockSpec((rows, step), lambda i: (0, i)),
            pl.BlockSpec((step, cq), lambda i: (i, 0)),
            pl.BlockSpec((step, ckv), lambda i: (i, 0)),
        ],
        out_specs=[
            pl.BlockSpec((rows, cq), lambda i: (0, 0)),
            pl.BlockSpec((rows, ckv), lambda i: (0, 0)),
        ],
        out_shape=[
            jax.ShapeDtypeStruct((rows, cq), F32),
            jax.ShapeDtypeStruct((rows, ckv), F32),
        ],
        compiler_params=params(),
        cost_estimate=cost(2 * rows * width * (cq + ckv), 2 * width * (rows + cq + ckv)),
        name="dense_qkv",
    )(x, wq, wkv)


ENDS_AT = 2
SEND_AT = 16
SERVED_AT = 32
SOURCE_AT = 48
TABLE = 64


def serve_kernel(
    count, blocks, owned, crop_ref, tenant_ref, row_ref, down, up_q, up_kv, up_o, down_o, *outs
):
    tab = outs[0]
    firsts, lates = outs[1 : 1 + count], outs[1 + count :]
    me = lax.axis_index("ctx")
    for i in range(TABLE):
        tab[i] = 0
    tab[0] = me
    tab[1] = lax.axis_index("tp")
    end = jnp.int32(0)
    for i in range(crop_ref.shape[0]):
        end = end + crop_ref[i]
        tab[ENDS_AT + i] = end
    for b in range(blocks):
        row = row_ref[tenant_ref[me * blocks + b]]
        tab[SOURCE_AT + b] = (row // owned) ^ me
    for k in range(count):
        served = jnp.int32(-1)
        for b in range(blocks):
            row = row_ref[tenant_ref[(me ^ k) * blocks + b]]
            served = jnp.where(row // owned == me, row - me * owned, served)
        tab[SERVED_AT + k] = served
        tab[SEND_AT + k] = jnp.maximum(served, 0)
    rank, width = ADAPTER_RANK, down.shape[2]
    half, quarter = rank // 2, rank // 4
    cq, ckv = width // 2, width // 4
    for k in range(count):
        at = tab[SEND_AT + k]
        low = down.shape[1]
        firsts[k][:low, :] = down[at]
        for i in range(2):
            firsts[k][low : low + half, i * cq : (i + 1) * cq] = up_q[
                at, i * half : (i + 1) * half, :
            ]
            lates[k][rank : rank + half, i * cq : (i + 1) * cq] = down_o[
                at, i * half : (i + 1) * half, :
            ]
        for i in range(4):
            firsts[k][low + half :, i * ckv : (i + 1) * ckv] = up_kv[
                at, i * quarter : (i + 1) * quarter, :
            ]
        lates[k][:rank, :] = up_o[at]


def serve(count, blocks, crops, tenants, store_rows, down, up_q, up_kv, up_o, down_o):
    rank, width = ADAPTER_RANK, down.shape[2]
    assert up_q.shape[2] * 2 == width and up_kv.shape[2] * 4 == width
    assert up_o.shape[2] == width and down_o.shape[2] * 2 == width
    smem = pl.BlockSpec(memory_space=pltpu.SMEM)
    vmem = pl.BlockSpec(memory_space=pltpu.VMEM)
    first = jax.ShapeDtypeStruct((3 * rank + rank // 2 + rank // 4, width), BF16)
    late = jax.ShapeDtypeStruct((rank + rank // 2, width), BF16)
    results = pl.pallas_call(
        functools.partial(serve_kernel, count, blocks, down.shape[0]),
        in_specs=[smem] * 3 + [vmem] * 5,
        out_specs=[smem] + [vmem] * (2 * count),
        out_shape=[jax.ShapeDtypeStruct((TABLE,), jnp.int32)] + [first] * count + [late] * count,
        compiler_params=params(),
        name="serve",
    )(crops, tenants, store_rows, down, up_q, up_kv, up_o, down_o)
    return results[0], list(results[1 : 1 + count]), list(results[1 + count :])


def unpack_q(ref):
    rows, width = ref.shape
    value = ref[...]
    return jnp.concatenate([value[:, : width // 2], value[:, width // 2 :]], axis=0)


def unpack_kv(ref):
    rows, width = ref.shape
    value = ref[...]
    step = width // 4
    return jnp.concatenate([value[:, i * step : (i + 1) * step] for i in range(4)], axis=0)


def pick(tab_ref, block, count, step):
    for k in range(count):

        @pl.when(tab_ref[SOURCE_AT + block] == k)
        def _(k=k):
            step(k)


def split_rows(tab_ref, whole, mine, other):
    half = mine.shape[0]

    @pl.when(tab_ref[1] % 2 == 0)
    def _():
        mine[...] = whole[:half, :]
        other[...] = whole[half:, :]

    @pl.when(tab_ref[1] % 2 == 1)
    def _():
        mine[...] = whole[half:, :]
        other[...] = whole[:half, :]


def join_rows(tab_ref, mine, other, whole):
    half = mine.shape[0]

    @pl.when(tab_ref[1] % 2 == 0)
    def _():
        whole[:half, :] = mine[...]
        whole[half:, :] = other[...]

    @pl.when(tab_ref[1] % 2 == 1)
    def _():
        whole[:half, :] = other[...]
        whole[half:, :] = mine[...]


def sum_halves(mine, other, beside=None):
    total = add_round(mine, swap(other, "tp", 1))
    mask = 2
    while mask < lax.axis_size("tp"):
        arrived = swap(total, "tp", mask)
        if mask == 2 and beside is not None:
            arrived, beside = lax.optimization_barrier((arrived, beside))
        total = add_round(total, arrived)
        mask *= 2
    halves = (total, swap(total, "tp", 1))
    return halves if beside is None else (halves, beside)


def block_rows(b):
    return slice(b * BLK, (b + 1) * BLK)


def whole_spec(shape):
    return pl.BlockSpec(shape, lambda i, t: (0,) * len(shape))


def part_spec(rows, row_block, width):
    return pl.BlockSpec((rows, width), lambda i, t: (row_block, 0))


def table_call(kernel, table, operands, in_specs, shapes, scratch, name, flops=0, out_specs=None):
    moved = sum(math.prod(s.block_shape) * 2 for s in in_specs)
    moved += sum(math.prod(s.shape) * s.dtype.itemsize for s in shapes)
    return pl.pallas_call(
        kernel,
        grid_spec=pltpu.PrefetchScalarGridSpec(
            num_scalar_prefetch=1,
            grid=(1,),
            in_specs=in_specs,
            out_specs=[whole_spec(s.shape) for s in shapes],
            scratch_shapes=scratch,
        ),
        out_shape=shapes,
        compiler_params=params(),
        cost_estimate=cost(flops, moved),
        name=name,
    )(table, *operands)


def low_kernel(count, tab_ref, x_ref, *refs):
    downs = refs[:count]
    mine, other, whole = refs[count:]
    for b in range(whole.shape[0] // BLK):

        def step(k, b=b):
            whole[block_rows(b), :] = dot_nt(x_ref[block_rows(b), :], downs[k][...]).astype(BF16)

        pick(tab_ref, b, count, step)
    split_rows(tab_ref, whole, mine, other)


def low_part(table, x, firsts):
    rows, width, cols = x.shape[0], firsts[0].shape[1], 3 * ADAPTER_RANK
    half = jax.ShapeDtypeStruct((rows // 2, cols), BF16)
    return table_call(
        functools.partial(low_kernel, len(firsts)),
        table,
        [x] + firsts,
        [pl.BlockSpec((rows, width), lambda i, t: (0, t[1]))]
        + [part_spec(cols, 0, width)] * len(firsts),
        [half, half],
        [pltpu.VMEM((rows, cols), BF16)],
        "low_part",
        2 * rows * width * cols,
    )


def finish_kv_kernel(count, rotate_keys, tab_ref, kv_ref, mine, other, cos_ref, sin_ref, *refs):
    ups = refs[:count]
    kvo, low = refs[count:]
    ckv = kv_ref.shape[1]
    rank = ADAPTER_RANK
    join_rows(tab_ref, mine, other, low)
    for b in range(kv_ref.shape[0] // BLK):

        def step(k, b=b):
            at_rows = block_rows(b)
            low_k = low[at_rows, rank : 2 * rank]
            low_v = low[at_rows, 2 * rank :]
            up_kv = unpack_kv(ups[k].at[rank // 2 :])
            for h in range(ckv // HEAD_SIZE):
                at = slice(h * HEAD_SIZE, (h + 1) * HEAD_SIZE)
                if rotate_keys:
                    term = dot_nn(low_v if h % 2 else low_k, up_kv[:, at])
                else:
                    is_value = (tab_ref[1] * (ckv // HEAD_SIZE) + h) % 2 == 1
                    term = jnp.where(
                        is_value, dot_nn(low_v, up_kv[:, at]), dot_nn(low_k, up_kv[:, at])
                    )
                piece = (kv_ref[at_rows, at] + term).astype(BF16)
                if rotate_keys and h % 2 == 0:
                    cosine, sine = cos_ref[at_rows, :], sin_ref[at_rows, :]
                    piece = turn_kernel(piece.astype(F32), cosine, sine).astype(BF16)
                kvo[at_rows, at] = piece

        pick(tab_ref, b, count, step)


def finish_kv(table, kv_lin, halves, firsts, cosine, sine, rotate_keys):
    rows, ckv = kv_lin.shape
    cols, width = 3 * ADAPTER_RANK, firsts[0].shape[1]
    part = ADAPTER_RANK // 2 + ADAPTER_RANK // 4
    operands = [kv_lin, *halves, cosine, sine]
    return table_call(
        functools.partial(finish_kv_kernel, len(firsts), rotate_keys),
        table,
        operands + firsts,
        [whole_spec(a.shape) for a in operands]
        + [part_spec(part, cols // part, width)] * len(firsts),
        [jax.ShapeDtypeStruct((rows, ckv), BF16), jax.ShapeDtypeStruct((rows, cols), BF16)],
        [],
        "finish_kv",
        4 * rows * ADAPTER_RANK * ckv,
    )


def finish_q_kernel(count, tab_ref, q_ref, low_ref, cos_ref, sin_ref, *refs):
    ups, qo = refs[:count], refs[count]
    cq = q_ref.shape[1]
    rank = ADAPTER_RANK
    for b in range(q_ref.shape[0] // BLK):

        def step(k, b=b):
            at_rows = block_rows(b)
            cosine, sine = cos_ref[at_rows, :], sin_ref[at_rows, :]
            up_q = unpack_q(ups[k].at[: rank // 2])
            query = q_ref[at_rows, :] + dot_nn(low_ref[at_rows, :rank], up_q)
            for h in range(cq // HEAD_SIZE):
                at = slice(h * HEAD_SIZE, (h + 1) * HEAD_SIZE)
                qo[at_rows, at] = turn_kernel(query[:, at], cosine, sine).astype(BF16)

        pick(tab_ref, b, count, step)


def finish_q(table, q_lin, low_in, firsts, cosine, sine):
    rows, cq = q_lin.shape
    cols, width = 3 * ADAPTER_RANK, firsts[0].shape[1]
    part = ADAPTER_RANK // 2 + ADAPTER_RANK // 4
    operands = [q_lin, low_in, cosine, sine]
    return table_call(
        functools.partial(finish_q_kernel, len(firsts)),
        table,
        operands + firsts,
        [whole_spec(a.shape) for a in operands]
        + [part_spec(part, cols // part, width)] * len(firsts),
        [jax.ShapeDtypeStruct((rows, cq), BF16)],
        [],
        "finish_q",
        2 * rows * ADAPTER_RANK * cq,
    )[0]


def low_o_kernel(count, tab_ref, cot_ref, attn_ref, *refs):
    lates = refs[:count]
    mine, other, whole = refs[count:]
    rank = ADAPTER_RANK
    for b in range(whole.shape[0] // BLK):

        def step(k, b=b):
            at = block_rows(b)
            whole[at, :rank] = dot_nt(cot_ref[at, :], lates[k][:rank, :]).astype(BF16)
            down = unpack_q(lates[k].at[rank:])
            whole[at, rank:] = dot_nt(attn_ref[at, :], down).astype(BF16)

        pick(tab_ref, b, count, step)
    split_rows(tab_ref, whole, mine, other)


def low_o_part(table, cot, attn, lates):
    rows, width = cot.shape
    cols = 2 * ADAPTER_RANK
    half = jax.ShapeDtypeStruct((rows // 2, cols), BF16)
    return table_call(
        functools.partial(low_o_kernel, len(lates)),
        table,
        [cot, attn] + lates,
        [whole_spec(cot.shape), whole_spec(attn.shape)]
        + [whole_spec(lates[0].shape)] * len(lates),
        [half, half],
        [pltpu.VMEM((rows, cols), BF16)],
        "low_o_part",
        2 * rows * cols * width,
    )


def low_g_kernel(count, tab_ref, gq_ref, gkv_ref, *refs):
    ups = refs[:count]
    mine, other, whole = refs[count:]
    rank = ADAPTER_RANK
    ckv = gkv_ref.shape[1]
    for b in range(whole.shape[0] // BLK):

        def step(k, b=b):
            at = block_rows(b)
            up_q = unpack_q(ups[k].at[: rank // 2])
            whole[at, :rank] = dot_nt(gq_ref[at, :], up_q).astype(BF16)
            up_kv = unpack_kv(ups[k].at[rank // 2 :])
            sums = [jnp.zeros((BLK, rank), F32)] * 2
            for h in range(ckv // HEAD_SIZE):
                cols = slice(h * HEAD_SIZE, (h + 1) * HEAD_SIZE)
                term = dot_nt(gkv_ref[at, cols], up_kv[:, cols])
                is_value = (tab_ref[1] * (ckv // HEAD_SIZE) + h) % 2 == 1
                sums[0] = sums[0] + jnp.where(is_value, 0.0, term)
                sums[1] = sums[1] + jnp.where(is_value, term, 0.0)
            whole[at, rank : 2 * rank] = sums[0].astype(BF16)
            whole[at, 2 * rank :] = sums[1].astype(BF16)

        pick(tab_ref, b, count, step)
    split_rows(tab_ref, whole, mine, other)


def low_g_part(table, gq, gkv, firsts):
    rows = gq.shape[0]
    cols, width = 3 * ADAPTER_RANK, firsts[0].shape[1]
    part = ADAPTER_RANK // 2 + ADAPTER_RANK // 4
    half = jax.ShapeDtypeStruct((rows // 2, cols), BF16)
    return table_call(
        functools.partial(low_g_kernel, len(firsts)),
        table,
        [gq, gkv] + firsts,
        [whole_spec(gq.shape), whole_spec(gkv.shape)]
        + [part_spec(part, cols // part, width)] * len(firsts),
        [half, half],
        [pltpu.VMEM((rows, cols), BF16)],
        "low_g_part",
        2 * rows * width * ADAPTER_RANK,
    )


def zero_unused(tab_ref, blocks, sends):
    for k in range(len(sends)):
        used = tab_ref[SOURCE_AT] == k
        for b in range(1, blocks):
            used = used | (tab_ref[SOURCE_AT + b] == k)

        @pl.when(jnp.logical_not(used))
        def _(k=k):
            sends[k][...] = jnp.zeros_like(sends[k])


def up_grads_kernel(
    count, tab_ref, low_ref, gq_ref, gkv_ref, o_mine, o_other, cot, attn, *refs
):
    sends, low_o = refs[:count], refs[count]
    rank = ADAPTER_RANK
    join_rows(tab_ref, o_mine, o_other, low_o)
    blocks = low_o.shape[0] // BLK
    cq, ckv = gq_ref.shape[1], gkv_ref.shape[1]
    half, quarter = rank // 2, rank // 4
    late = half + quarter
    zero_unused(tab_ref, blocks, sends)
    for b in range(blocks):

        def step(k, b=b):
            at = block_rows(b)
            out = sends[k]
            up_q = dot_tn(low_ref[at, :rank], gq_ref[at, :]).astype(BF16)
            down_o = dot_tn(low_o[at, :rank], attn[at, :]).astype(BF16)
            for i in range(2):
                rows = slice(i * half, (i + 1) * half)
                cols = slice(i * cq, (i + 1) * cq)
                out[:half, cols] = up_q[rows, :]
                out[late + rank :, cols] = down_o[rows, :]
            for h in range(ckv // HEAD_SIZE):
                piece = slice(h * HEAD_SIZE, (h + 1) * HEAD_SIZE)
                is_value = (tab_ref[1] * (ckv // HEAD_SIZE) + h) % 2 == 1
                up_kv = jnp.where(
                    is_value,
                    dot_tn(low_ref[at, 2 * rank :], gkv_ref[at, piece]),
                    dot_tn(low_ref[at, rank : 2 * rank], gkv_ref[at, piece]),
                ).astype(BF16)
                for i in range(4):
                    cols = slice(i * ckv + h * HEAD_SIZE, i * ckv + (h + 1) * HEAD_SIZE)
                    out[half:late, cols] = up_kv[i * quarter : (i + 1) * quarter, :]
            out[late : late + rank, :] = dot_tn(low_o[at, rank:], cot[at, :]).astype(BF16)

        pick(tab_ref, b, count, step)


def up_grads(table, count, low_in, gq, gkv, o_halves, cot, attn):
    rows, width = cot.shape
    rank = ADAPTER_RANK
    operands = [low_in, gq, gkv, *o_halves, cot, attn]
    return list(
        table_call(
            functools.partial(up_grads_kernel, count),
            table,
            operands,
            [whole_spec(a.shape) for a in operands],
            [jax.ShapeDtypeStruct((2 * rank + rank // 4, width), BF16)] * count,
            [pltpu.VMEM((rows, 2 * rank), BF16)],
            "up_grads",
            2 * rows * width * 3 * rank,
        )
    )


def down_grads_kernel(count, tab_ref, x_ref, mine, other, *refs):
    downs, sends = refs[:count], refs[count : 2 * count]
    delta, low = refs[2 * count :]
    join_rows(tab_ref, mine, other, low)
    blocks = low.shape[0] // BLK
    zero_unused(tab_ref, blocks, sends)
    for b in range(blocks):

        def step(k, b=b):
            at = block_rows(b)
            sends[k][...] = dot_tn(low[at, :], x_ref[at, :]).astype(BF16)
            delta[at, :] = dot_nn(low[at, :], downs[k][...])

        pick(tab_ref, b, count, step)


def down_grads(table, x, halves, firsts):
    rows, cols = x.shape[0], 3 * ADAPTER_RANK
    width, count = firsts[0].shape[1], len(firsts)
    results = table_call(
        functools.partial(down_grads_kernel, count),
        table,
        [x, *halves] + firsts,
        [pl.BlockSpec((rows, width), lambda i, t: (0, t[1]))]
        + [whole_spec(halves[0].shape)] * 2
        + [part_spec(cols, 0, width)] * count,
        [jax.ShapeDtypeStruct((cols, width), BF16)] * count
        + [jax.ShapeDtypeStruct((rows, width), F32)],
        [pltpu.VMEM((rows, cols), BF16)],
        "down_grads",
        4 * rows * width * cols,
    )
    return list(results[:count]), results[count]


def store_kernel(count, tab_ref, *refs):
    downs, ups = refs[:count], refs[count : 2 * count]
    outs = refs[2 * count :]
    row = pl.program_id(0)
    for o in outs:
        o[...] = jnp.zeros_like(o)
    rank = ADAPTER_RANK
    half, quarter = rank // 2, rank // 4
    late = half + quarter
    for k in range(count):

        @pl.when(tab_ref[SERVED_AT + k] == row)
        def _(k=k):
            a = ups[k]
            outs[0][0] += downs[k][...].astype(F32)
            outs[1][0] += unpack_q(a.at[:half]).astype(F32)
            outs[2][0] += unpack_kv(a.at[half:late]).astype(F32)
            outs[3][0] += unpack_q(a.at[late + rank :]).astype(F32)
            outs[4][0] += a[late : late + rank, :].astype(F32)


def store_sums(table, downs, ups, owned):
    rank = ADAPTER_RANK
    width = downs[0].shape[1]
    shapes = [
        jax.ShapeDtypeStruct((owned, r, c), F32)
        for r, c in [
            (3 * rank, width),
            (rank, width // 2),
            (rank, width // 4),
            (rank, width // 2),
            (rank, width),
        ]
    ]
    return pl.pallas_call(
        functools.partial(store_kernel, len(downs)),
        grid_spec=pltpu.PrefetchScalarGridSpec(
            num_scalar_prefetch=1,
            grid=(owned,),
            in_specs=[pl.BlockSpec(a.shape, lambda i, t: (0, 0)) for a in downs + ups],
            out_specs=[pl.BlockSpec((1,) + s.shape[1:], lambda i, t: (i, 0, 0)) for s in shapes],
        ),
        out_shape=shapes,
        compiler_params=params(),
        name="store_sums",
    )(table, *downs, *ups)


def output_kernel(count, tab_ref, sum_ref, mine, other, *refs):
    lates = refs[:count]
    out, low = refs[count:]
    rank = ADAPTER_RANK
    join_rows(tab_ref, mine, other, low)
    for b in range(out.shape[0] // BLK):

        def step(k, b=b):
            at = block_rows(b)
            term = dot_nn(low[at, rank:], lates[k][...])
            out[at, :] = (sum_ref[at, :].astype(F32) + term).astype(BF16)

        pick(tab_ref, b, count, step)


def output_result(table, total, halves, lates):
    rows, width = total.shape
    rank = ADAPTER_RANK
    return table_call(
        functools.partial(output_kernel, len(lates)),
        table,
        [total, *halves] + lates,
        [whole_spec(total.shape)]
        + [whole_spec(halves[0].shape)] * 2
        + [part_spec(rank, 0, width)] * len(lates),
        [jax.ShapeDtypeStruct((rows, width), BF16)],
        [pltpu.VMEM((rows, 2 * rank), BF16)],
        "output_result",
        2 * rows * rank * width,
    )[0]


def crop_start(tab_ref, crops, positions):
    start = jnp.zeros_like(positions)
    for i in range(crops):
        end = tab_ref[ENDS_AT + i]
        start = jnp.where(positions >= end, end, start)
    return start


def masked(scores, first, own, base):
    rows, cols = scores.shape
    key_pos = base + lax.broadcasted_iota(jnp.int32, (rows, cols), 0)
    allowed = key_pos >= first
    if own:
        allowed &= key_pos <= base + lax.broadcasted_iota(jnp.int32, (rows, cols), 1)
    return jnp.where(allowed, scores, NEG)


def chunk_on(tab_ref, crops, k, rows):
    me = tab_ref[0]
    chunk = me ^ k
    return (chunk <= me) & ((chunk + 1) * rows > crop_start(tab_ref, crops, me * rows))


def query_starts(tab_ref, crops, rows):
    positions = tab_ref[0] * rows + lax.broadcasted_iota(jnp.int32, (1, rows), 1)
    return crop_start(tab_ref, crops, positions)


def forward_kernel(heads, count, crops, groups, tab_ref, q_ref, *refs):
    kv_refs = refs[:count]
    w_ref, out_ref, norm_ref, y_ref, acc, top, total, w_buf, y_buf, w_sem, y_sem = refs[count:]
    rows = q_ref.shape[0]
    wide = w_ref.shape[1] // groups
    loads = []
    for g in range(groups):
        at = slice(g * wide, (g + 1) * wide)
        loads.append(pltpu.make_async_copy(w_ref.at[:, at], w_buf.at[:, at], w_sem.at[g]))
        loads[g].start()
    first = query_starts(tab_ref, crops, rows)
    for k in range(count):

        def chunk_step(k=k):
            base = (tab_ref[0] ^ k) * rows
            keys = kv_refs[k][:, :HEAD_SIZE]
            values = kv_refs[k][:, HEAD_SIZE:]
            for h in range(heads):
                at = slice(h * HEAD_SIZE, (h + 1) * HEAD_SIZE)
                scores = masked(dot_nt(keys, q_ref[:, at]), first, k == 0, base)
                here = jnp.max(scores, axis=0, keepdims=True)
                if k == 0:
                    new_top = here
                else:
                    old_top = top[h : h + 1, :]
                    new_top = jnp.maximum(old_top, here)
                weights = jnp.exp((scores - new_top) * SCALE)
                here_sum = jnp.sum(weights, axis=0, keepdims=True)
                here_out = dot_tn(values, weights.astype(BF16))
                if k == 0:
                    total[h : h + 1, :] = here_sum
                    acc[h] = here_out
                else:
                    decay = jnp.exp((old_top - new_top) * SCALE)
                    total[h : h + 1, :] = total[h : h + 1, :] * decay + here_sum
                    acc[h] = acc[h] * decay + here_out
                top[h : h + 1, :] = new_top

        if k == 0:
            chunk_step()
        else:
            pl.when(chunk_on(tab_ref, crops, k, rows))(chunk_step)
    for h in range(heads):
        at = slice(h * HEAD_SIZE, (h + 1) * HEAD_SIZE)
        out_ref[:, at] = jnp.transpose(acc[h] / total[h : h + 1, :]).astype(BF16)
    norm_ref[...] = top[...] * SCALE + jnp.log(total[...])
    stores = []
    for g in range(groups):
        slot = g % y_buf.shape[0]
        loads[g].wait()
        if g >= y_buf.shape[0]:
            stores[g - y_buf.shape[0]].wait()
        y_buf[slot] = dot_nn(out_ref[...], w_buf[:, g * wide : (g + 1) * wide]).astype(BF16)
        stores.append(pltpu.make_async_copy(y_buf.at[slot], y_ref.at[g], y_sem.at[slot]))
        stores[g].start()
    for g in range(groups - y_buf.shape[0], groups):
        stores[g].wait()


def attention_forward(table, crops, query, kvs, weight, groups):
    rows, cols = query.shape
    wide = weight.shape[1] // groups
    slots = 2
    heads = cols // HEAD_SIZE
    count = len(kvs)
    smem = pl.BlockSpec(memory_space=pltpu.SMEM)
    vmem = pl.BlockSpec(memory_space=pltpu.VMEM)
    work = heads * rows * rows * count
    return pl.pallas_call(
        functools.partial(forward_kernel, heads, count, crops, groups),
        in_specs=[smem] + [vmem] * (1 + count) + [pl.BlockSpec(memory_space=pl.ANY)],
        out_specs=[vmem] * 2 + [pl.BlockSpec(memory_space=pl.ANY)],
        out_shape=[
            jax.ShapeDtypeStruct((rows, cols), BF16),
            jax.ShapeDtypeStruct((heads, rows), F32),
            jax.ShapeDtypeStruct((groups, rows, wide), BF16),
        ],
        scratch_shapes=[
            pltpu.VMEM((heads, HEAD_SIZE, rows), F32),
            pltpu.VMEM((heads, rows), F32),
            pltpu.VMEM((heads, rows), F32),
            pltpu.VMEM(weight.shape, BF16),
            pltpu.VMEM((slots, rows, wide), BF16),
            pltpu.SemaphoreType.DMA((groups,)),
            pltpu.SemaphoreType.DMA((slots,)),
        ],
        compiler_params=params(),
        cost_estimate=cost(
            4 * work * HEAD_SIZE + 2 * rows * cols * wide * groups,
            2 * (rows + cols) * wide * groups,
            work,
        ),
        name="attention_forward",
    )(table, query, *kvs, weight)


def backward_kernel(
    heads,
    count,
    crops,
    tab_ref,
    q_ref,
    dense_ref,
    mine,
    other,
    out_ref,
    norm_ref,
    cos_ref,
    sin_ref,
    *refs,
):
    kv_refs, lates = refs[:count], refs[count : 2 * count]
    gq_ref = refs[2 * count]
    gkv_refs = refs[2 * count + 1 : 3 * count + 1]
    acc, delta, low, grad_ref = refs[3 * count + 1 :]
    rows = q_ref.shape[0]
    rank = ADAPTER_RANK
    first = query_starts(tab_ref, crops, rows)
    join_rows(tab_ref, mine, other, low)
    for b in range(rows // BLK):

        def add(k, b=b):
            at = block_rows(b)
            term = dot_nn(low[at, :rank], unpack_q(lates[k].at[rank:]))
            grad_ref[at, :] = (dense_ref[at, :] + term).astype(BF16)

        pick(tab_ref, b, count, add)
    for h in range(heads):
        at = slice(h * HEAD_SIZE, (h + 1) * HEAD_SIZE)
        product = grad_ref[:, at].astype(F32) * out_ref[:, at].astype(F32)
        delta[h : h + 1, :] = jnp.sum(jnp.transpose(product), axis=0, keepdims=True)
    for k in range(count):

        def chunk_step(k=k):
            base = (tab_ref[0] ^ k) * rows
            keys = kv_refs[k][:, :HEAD_SIZE]
            values = kv_refs[k][:, HEAD_SIZE:]
            key_grad = jnp.zeros((rows, HEAD_SIZE), F32)
            value_grad = jnp.zeros((rows, HEAD_SIZE), F32)
            for h in range(heads):
                at = slice(h * HEAD_SIZE, (h + 1) * HEAD_SIZE)
                scores = masked(dot_nt(keys, q_ref[:, at]), first, k == 0, base)
                weights = jnp.exp(scores * SCALE - norm_ref[h : h + 1, :])
                value_grad += dot_nn(weights.astype(BF16), grad_ref[:, at])
                grad_weights = dot_nt(values, grad_ref[:, at])
                grad_scores = (weights * (grad_weights - delta[h : h + 1, :])).astype(BF16)
                key_grad += dot_nn(grad_scores, q_ref[:, at])
                here = dot_tn(keys, grad_scores)
                if k == 0:
                    acc[h] = here
                else:
                    acc[h] += here
            gkv_refs[k][:, :HEAD_SIZE] = (key_grad * SCALE).astype(BF16)
            gkv_refs[k][:, HEAD_SIZE:] = value_grad.astype(BF16)

        if k == 0:
            chunk_step()
        else:
            on = chunk_on(tab_ref, crops, k, rows)
            pl.when(on)(chunk_step)

            @pl.when(jnp.logical_not(on))
            def _(k=k):
                gkv_refs[k][...] = jnp.zeros_like(gkv_refs[k])

    for h in range(heads):
        at = slice(h * HEAD_SIZE, (h + 1) * HEAD_SIZE)
        grad = jnp.transpose(acc[h]) * SCALE
        gq_ref[:, at] = turn_kernel(grad, cos_ref[...], -sin_ref[...]).astype(BF16)


def attention_backward(table, crops, query, dense, halves, out, norm, cosine, sine, kvs, lates):
    rows, cols = query.shape
    heads = cols // HEAD_SIZE
    count = len(kvs)
    smem = pl.BlockSpec(memory_space=pltpu.SMEM)
    vmem = pl.BlockSpec(memory_space=pltpu.VMEM)
    work = heads * rows * rows * count
    results = pl.pallas_call(
        functools.partial(backward_kernel, heads, count, crops),
        in_specs=[smem] + [vmem] * (8 + 2 * count),
        out_specs=[vmem] * (1 + count),
        out_shape=[jax.ShapeDtypeStruct((rows, cols), BF16)]
        + [jax.ShapeDtypeStruct((rows, 2 * HEAD_SIZE), BF16)] * count,
        scratch_shapes=[
            pltpu.VMEM((heads, HEAD_SIZE, rows), F32),
            pltpu.VMEM((heads, rows), F32),
            pltpu.VMEM((rows, 2 * ADAPTER_RANK), BF16),
            pltpu.VMEM((rows, cols), BF16),
        ],
        compiler_params=params(),
        cost_estimate=cost(10 * work * HEAD_SIZE, 8 * rows * cols * count, work),
        name="attention_backward",
    )(table, query, dense, *halves, out, norm, cosine, sine, *kvs, *lates)
    return results[0], list(results[1:])


def plane_spec(shape, first, other):
    def index(i, t):
        core = t[1] % 2
        return (2 * (first + i) + (1 - core if other else core), 0)

    return pl.BlockSpec(shape, index)


def product_kernel(terms, extra, tab_ref, *refs):
    out = refs[-1]
    total = terms(refs)
    if extra:
        total = total + refs[-1 - extra][0].astype(F32)
    out[0] = total.astype(BF16)


def product_call(table, terms, operands, make_specs, planes, shape, first, count, arrived, target):
    other = arrived is None
    in_specs = make_specs(first, other)
    arrays = list(operands)
    aliases = {}
    if not other:
        if target is not None:
            aliases = {1 + len(arrays): 0}
            arrays.append(target)
            in_specs.append(pl.BlockSpec(memory_space=pl.ANY))
        arrays.append(arrived)
        in_specs.append(pl.BlockSpec((1,) + shape, lambda i, t: (i, 0, 0)))
    start = 0 if other else first
    return pl.pallas_call(
        functools.partial(product_kernel, terms, 0 if other else 1),
        grid_spec=pltpu.PrefetchScalarGridSpec(
            num_scalar_prefetch=1,
            grid=(count,),
            in_specs=in_specs,
            out_specs=pl.BlockSpec((1,) + shape, lambda i, t: (start + i, 0, 0)),
        ),
        out_shape=jax.ShapeDtypeStruct((count if other else planes,) + shape, BF16),
        input_output_aliases=aliases,
        compiler_params=params(),
        cost_estimate=cost(
            2 * shape[0] * sum(a.shape[0] for a in operands[:1]) * shape[1] * count,
            4 * shape[0] * shape[1] * count,
        ),
        name="product",
    )(table, *arrays)


def reduced_product(table, terms, operands, make_specs, groups, shape, later):
    planes = groups // 2
    half = planes // 2
    call = functools.partial(
        product_call, table, terms, operands, make_specs, planes, shape, count=half
    )
    sent = [call(first=p * half, arrived=None, target=None) for p in range(2)]
    got = [swap(s, "tp", 1) for s in sent]
    out = call(first=0, arrived=got[0], target=None)
    out = call(first=half, arrived=got[1], target=out)
    lines = [list(range(core, groups, 2)) for core in range(2)]
    out, later = lax.optimization_barrier((out, later))
    total = lax.psum_scatter(
        out, "tp", scatter_dimension=0, axis_index_groups=lines, tiled=False
    )
    return total, later


PER_STEP = 2


def grad_attn_kernel(c0_ref, c1_ref, w_ref, o_ref):
    step = pl.program_id(0)
    per_step, first_rows, cols = c0_ref.shape
    parts = ((c0_ref, slice(0, first_rows)), (c1_ref, slice(first_rows, o_ref.shape[0])))
    for c_ref, at in parts:
        total = dot_nt(c_ref[0], w_ref[:, :cols])
        for i in range(1, per_step):
            total += dot_nt(c_ref[i], w_ref[:, i * cols : (i + 1) * cols])

        @pl.when(step == 0)
        def _(at=at, total=total):
            o_ref[at, :] = total

        @pl.when(step > 0)
        def _(at=at, total=total):
            o_ref[at, :] += total


def grad_attn(cot_first, cot_second, weight):
    groups, first_rows, cols = cot_first.shape
    depth = weight.shape[0]
    rows = first_rows + cot_second.shape[1]
    return pl.pallas_call(
        grad_attn_kernel,
        grid=(groups // PER_STEP,),
        in_specs=[
            pl.BlockSpec((PER_STEP, first_rows, cols), lambda i: (i, 0, 0)),
            pl.BlockSpec((PER_STEP, rows - first_rows, cols), lambda i: (i, 0, 0)),
            pl.BlockSpec((depth, PER_STEP * cols), lambda i: (0, i)),
        ],
        out_specs=pl.BlockSpec((rows, depth), lambda i: (0, 0)),
        out_shape=jax.ShapeDtypeStruct((rows, depth), F32),
        compiler_params=params(),
        cost_estimate=cost(2 * rows * depth * cols * groups, 2 * (rows + depth) * cols * groups),
        name="grad_attn",
    )(cot_first, cot_second, weight)


def grad_input_terms(refs):
    return dot_nt(refs[0][...], refs[2][...]) + dot_nt(refs[1][...], refs[3][...])


def grad_input(table, gq, gkv, wq, wkv, groups, later):
    rows = gq.shape[0]
    cols = wq.shape[0] // groups

    def specs(first, other):
        return [
            whole_spec(gq.shape),
            whole_spec(gkv.shape),
            plane_spec((cols, wq.shape[1]), first, other),
            plane_spec((cols, wkv.shape[1]), first, other),
        ]

    return reduced_product(
        table, grad_input_terms, [gq, gkv, wq, wkv], specs, groups, (rows, cols), later
    )


def body(
    hidden_input,
    output_cotangent,
    query_projection,
    key_value_projection,
    output_projection,
    adapter_qkv_down_store,
    adapter_query_up,
    adapter_key_value_up,
    adapter_output_down,
    adapter_output_up,
    crop_token_length,
    tenant_per_block,
    tenant_store_row,
):
    ctx_count = lax.axis_size("ctx")
    tp_count = lax.axis_size("tp")
    ctx_index = lax.axis_index("ctx")
    tp_index = lax.axis_index("tp")
    rows_dev = hidden_input.shape[0]
    out_cols = output_cotangent.shape[1]
    tenant_owner = adapter_qkv_down_store.shape[0]
    blocks_dev = rows_dev // BLK
    pair_bits = (tp_count // KEY_VALUE_HEADS).bit_length() - 1
    groups = hidden_input.shape[1] // out_cols
    crops = crop_token_length.shape[0]
    partners = range(1, ctx_count)

    first_rows = rows_dev * 7 // 12
    cot_part, crop_token_length = lax.optimization_barrier(
        (output_cotangent[:first_rows], crop_token_length)
    )
    cot_first = lax.all_gather(cot_part, "tp", axis=0, tiled=False)

    table, firsts, lates = serve(
        ctx_count,
        blocks_dev,
        crop_token_length,
        tenant_per_block,
        tenant_store_row,
        adapter_qkv_down_store.swapaxes(1, 2),
        adapter_query_up,
        adapter_key_value_up,
        adapter_output_up,
        adapter_output_down.swapaxes(1, 2),
    )
    firsts = [firsts[0]] + [swap(firsts[k], "ctx", k) for k in partners]
    my_pos = ctx_index * rows_dev + jnp.arange(rows_dev, dtype=jnp.int32)
    q_lin, kv_lin = dense_qkv(hidden_input, query_projection, key_value_projection)
    firsts, q_lin, kv_lin, tables = lax.optimization_barrier(
        (firsts, q_lin, kv_lin, rope_tables(my_pos))
    )
    cosine, sine = tables
    low_halves = low_part(table, hidden_input, firsts)
    low_halves, cot_rest = lax.optimization_barrier(
        (sum_halves(*low_halves), output_cotangent[first_rows:])
    )
    cot_second = lax.all_gather(cot_rest, "tp", axis=0, tiled=False)
    kv_local, low_in = finish_kv(
        table, kv_lin, low_halves, firsts, cosine, sine, pair_bits == 0
    )
    if pair_bits:
        for bit_no in range(pair_bits):
            partner = swap(kv_local, "tp", 1 << bit_no)
            is_lower = tp_index // (1 << bit_no) % 2 == 0
            kv_local = jnp.where(
                is_lower,
                jnp.concatenate([kv_local, partner], axis=1),
                jnp.concatenate([partner, kv_local], axis=1),
            )
        key_rot = turn(kv_local[:, :HEAD_SIZE].astype(F32), cosine, sine).astype(BF16)
        kv_local = jnp.concatenate([key_rot, kv_local[:, HEAD_SIZE:]], axis=1)
    kvs = [kv_local] + [swap(kv_local, "ctx", k) for k in partners]
    query_rot = finish_q(table, q_lin, low_in, firsts, cosine, sine)
    kvs, lates, query_rot = lax.optimization_barrier((kvs, lates, query_rot))
    lates = [lates[0]] + [swap(lates[k], "ctx", k) for k in partners]

    attn_out, log_norm, heads_part = attention_forward(
        table, crops, query_rot, kvs, output_projection, groups
    )
    heads_part, lates, attn_out, cot_first = lax.optimization_barrier(
        (heads_part, lates, attn_out, cot_first)
    )
    heads_sum = lax.psum_scatter(heads_part, "tp", scatter_dimension=0, tiled=False)
    grad_dense = grad_attn(cot_first, cot_second, output_projection)
    o_halves, grad_dense = sum_halves(
        *low_o_part(table, output_cotangent, attn_out, lates), beside=grad_dense
    )
    grad_q, kv_parts = attention_backward(
        table, crops, query_rot, grad_dense, o_halves, attn_out, log_norm, cosine, sine, kvs, lates
    )
    reduced = kv_parts[0].astype(F32)
    for k in partners:
        reduced = reduced + swap(kv_parts[k], "ctx", k).astype(F32)
    reduced = jnp.concatenate(
        [turn(reduced[:, :HEAD_SIZE], cosine, -sine), reduced[:, HEAD_SIZE:]], axis=1
    )
    for bit_no in reversed(range(pair_bits)):
        half_cols = reduced.shape[1] // 2
        is_lower = tp_index // (1 << bit_no) % 2 == 0
        keep_part = jnp.where(is_lower, reduced[:, :half_cols], reduced[:, half_cols:])
        send_part = jnp.where(is_lower, reduced[:, half_cols:], reduced[:, :half_cols])
        reduced = keep_part + swap(send_part.astype(BF16), "tp", 1 << bit_no).astype(F32)
    grad_kv = reduced.astype(BF16)

    input_sum, (grad_q, grad_kv) = grad_input(
        table,
        grad_q,
        grad_kv,
        query_projection,
        key_value_projection,
        groups,
        (grad_q, grad_kv),
    )
    output = output_result(table, heads_sum, o_halves, lates)

    g_halves = sum_halves(*low_g_part(table, grad_q, grad_kv, firsts))
    up_sends = up_grads(
        table, ctx_count, low_in, grad_q, grad_kv, o_halves, output_cotangent, attn_out
    )
    up_back = [up_sends[0]] + [swap(up_sends[k], "ctx", k) for k in partners]
    down_sends, input_delta = down_grads(table, hidden_input, g_halves, firsts)
    down_back = [down_sends[0]] + [swap(down_sends[k], "ctx", k) for k in partners]
    down_back, output = lax.optimization_barrier((down_back, output))
    stores = store_sums(table, down_back, up_back, tenant_owner)
    input_sum, input_delta, stores = lax.optimization_barrier((input_sum, input_delta, stores))
    hidden_input_gradient = (input_sum.astype(F32) + input_delta).astype(BF16)
    return (
        output,
        hidden_input_gradient,
        stores[0].swapaxes(1, 2),
        stores[1],
        stores[2],
        stores[3].swapaxes(1, 2),
        stores[4],
    )


def solution(mesh):
    in_specs = (
        P("ctx", None),
        P("ctx", "tp"),
        P(None, "tp"),
        P(None, "tp"),
        P("tp", None),
        P("ctx", "tp", None),
        P("ctx", None, "tp"),
        P("ctx", None, "tp"),
        P("ctx", "tp", None),
        P("ctx", None, "tp"),
        P(),
        P(),
        P(),
    )
    out_specs = (
        P("ctx", "tp"),
        P("ctx", "tp"),
        P("ctx", "tp", None),
        P("ctx", None, "tp"),
        P("ctx", None, "tp"),
        P("ctx", "tp", None),
        P("ctx", None, "tp"),
    )
    return jax.shard_map(body, mesh=mesh, in_specs=in_specs, out_specs=out_specs, check_vma=False)
```

```python
import functools
import math

import jax
import jax.numpy as jnp
from jax import lax
from jax.experimental import pallas as pl
from jax.experimental.pallas import tpu as pltpu
from jax.sharding import PartitionSpec as P

HEAD_SIZE = 128
KEY_VALUE_HEADS = 8
ADAPTER_RANK = 64
BLK = 128
NEG = -1e30
ROPE_BASE = 1000000.0
SCALE = HEAD_SIZE ** (-0.5)
VMEM_BYTES = 56 * 1024 * 1024

BF16 = jnp.bfloat16
F32 = jnp.float32


def params():
    return pltpu.CompilerParams(vmem_limit_bytes=VMEM_BYTES)


def cost(flops, bytes_accessed, transcendentals=0):
    return pl.CostEstimate(
        flops=int(flops), bytes_accessed=int(bytes_accessed), transcendentals=int(transcendentals)
    )


def dot_nn(a, b):
    return lax.dot_general(a, b, (((1,), (0,)), ((), ())), preferred_element_type=F32)


def dot_nt(a, b):
    return lax.dot_general(a, b, (((1,), (1,)), ((), ())), preferred_element_type=F32)


def dot_tn(a, b):
    return lax.dot_general(a, b, (((0,), (0,)), ((), ())), preferred_element_type=F32)


def swap(value, axis, mask):
    pairs = [(source, source ^ mask) for source in range(lax.axis_size(axis))]
    return lax.ppermute(value, axis, pairs)


def add_round(a, b):
    return (a.astype(F32) + b.astype(F32)).astype(BF16)


def rope_tables(positions):
    half_dim = HEAD_SIZE // 2
    exponent = jnp.arange(half_dim, dtype=F32) * (2.0 / HEAD_SIZE)
    frequency = jnp.exp(-exponent * math.log(ROPE_BASE))
    angles = positions.astype(F32)[:, None] * frequency[None, :]
    cosine, sine = jnp.cos(angles), jnp.sin(angles)
    return (
        jnp.concatenate([cosine, cosine], axis=1),
        jnp.concatenate([-sine, sine], axis=1),
    )


def turn(values, cosine, sine):
    return values * cosine + jnp.roll(values, HEAD_SIZE // 2, axis=1) * sine


def turn_kernel(values, cosine, sine):
    return values * cosine + pltpu.roll(values, HEAD_SIZE // 2, 1) * sine


def dense_kernel(x_ref, wq_ref, wkv_ref, q_ref, kv_ref):
    @pl.when(pl.program_id(0) == 0)
    def _():
        q_ref[...] = jnp.zeros_like(q_ref)
        kv_ref[...] = jnp.zeros_like(kv_ref)

    x = x_ref[...]
    q_ref[...] += dot_nn(x, wq_ref[...])
    kv_ref[...] += dot_nn(x, wkv_ref[...])


def dense_qkv(x, wq, wkv):
    rows, width = x.shape
    step = 2048
    cq, ckv = wq.shape[1], wkv.shape[1]
    return pl.pallas_call(
        dense_kernel,
        grid=(width // step,),
        in_specs=[
            pl.BlockSpec((rows, step), lambda i: (0, i)),
            pl.BlockSpec((step, cq), lambda i: (i, 0)),
            pl.BlockSpec((step, ckv), lambda i: (i, 0)),
        ],
        out_specs=[
            pl.BlockSpec((rows, cq), lambda i: (0, 0)),
            pl.BlockSpec((rows, ckv), lambda i: (0, 0)),
        ],
        out_shape=[
            jax.ShapeDtypeStruct((rows, cq), F32),
            jax.ShapeDtypeStruct((rows, ckv), F32),
        ],
        compiler_params=params(),
        cost_estimate=cost(2 * rows * width * (cq + ckv), 2 * width * (rows + cq + ckv)),
        name="dense_qkv",
    )(x, wq, wkv)


ENDS_AT = 2
SEND_AT = 16
SERVED_AT = 32
SOURCE_AT = 48
TABLE = 64


def serve_kernel(
    count, blocks, owned, crop_ref, tenant_ref, row_ref, down, up_q, up_kv, up_o, down_o, *outs
):
    tab = outs[0]
    firsts, lates = outs[1 : 1 + count], outs[1 + count :]
    me = lax.axis_index("ctx")
    for i in range(TABLE):
        tab[i] = 0
    tab[0] = me
    tab[1] = lax.axis_index("tp")
    end = jnp.int32(0)
    for i in range(crop_ref.shape[0]):
        end = end + crop_ref[i]
        tab[ENDS_AT + i] = end
    for b in range(blocks):
        row = row_ref[tenant_ref[me * blocks + b]]
        tab[SOURCE_AT + b] = (row // owned) ^ me
    for k in range(count):
        served = jnp.int32(-1)
        for b in range(blocks):
            row = row_ref[tenant_ref[(me ^ k) * blocks + b]]
            served = jnp.where(row // owned == me, row - me * owned, served)
        tab[SERVED_AT + k] = served
        tab[SEND_AT + k] = jnp.maximum(served, 0)
    rank, width = ADAPTER_RANK, down.shape[2]
    half, quarter = rank // 2, rank // 4
    cq, ckv = width // 2, width // 4
    for k in range(count):
        at = tab[SEND_AT + k]
        low = down.shape[1]
        firsts[k][:low, :] = down[at]
        for i in range(2):
            firsts[k][low : low + half, i * cq : (i + 1) * cq] = up_q[
                at, i * half : (i + 1) * half, :
            ]
            lates[k][rank : rank + half, i * cq : (i + 1) * cq] = down_o[
                at, i * half : (i + 1) * half, :
            ]
        for i in range(4):
            firsts[k][low + half :, i * ckv : (i + 1) * ckv] = up_kv[
                at, i * quarter : (i + 1) * quarter, :
            ]
        lates[k][:rank, :] = up_o[at]


def serve(count, blocks, crops, tenants, store_rows, down, up_q, up_kv, up_o, down_o):
    rank, width = ADAPTER_RANK, down.shape[2]
    assert up_q.shape[2] * 2 == width and up_kv.shape[2] * 4 == width
    assert up_o.shape[2] == width and down_o.shape[2] * 2 == width
    smem = pl.BlockSpec(memory_space=pltpu.SMEM)
    vmem = pl.BlockSpec(memory_space=pltpu.VMEM)
    first = jax.ShapeDtypeStruct((3 * rank + rank // 2 + rank // 4, width), BF16)
    late = jax.ShapeDtypeStruct((rank + rank // 2, width), BF16)
    results = pl.pallas_call(
        functools.partial(serve_kernel, count, blocks, down.shape[0]),
        in_specs=[smem] * 3 + [vmem] * 5,
        out_specs=[smem] + [vmem] * (2 * count),
        out_shape=[jax.ShapeDtypeStruct((TABLE,), jnp.int32)] + [first] * count + [late] * count,
        compiler_params=params(),
        name="serve",
    )(crops, tenants, store_rows, down, up_q, up_kv, up_o, down_o)
    return results[0], list(results[1 : 1 + count]), list(results[1 + count :])


def unpack_q(ref):
    rows, width = ref.shape
    value = ref[...]
    return jnp.concatenate([value[:, : width // 2], value[:, width // 2 :]], axis=0)


def unpack_kv(ref):
    rows, width = ref.shape
    value = ref[...]
    step = width // 4
    return jnp.concatenate([value[:, i * step : (i + 1) * step] for i in range(4)], axis=0)


def pick(tab_ref, block, count, step):
    for k in range(count):

        @pl.when(tab_ref[SOURCE_AT + block] == k)
        def _(k=k):
            step(k)


def split_rows(tab_ref, whole, mine, other):
    half = mine.shape[0]

    @pl.when(tab_ref[1] % 2 == 0)
    def _():
        mine[...] = whole[:half, :]
        other[...] = whole[half:, :]

    @pl.when(tab_ref[1] % 2 == 1)
    def _():
        mine[...] = whole[half:, :]
        other[...] = whole[:half, :]


def join_rows(tab_ref, mine, other, whole):
    half = mine.shape[0]

    @pl.when(tab_ref[1] % 2 == 0)
    def _():
        whole[:half, :] = mine[...]
        whole[half:, :] = other[...]

    @pl.when(tab_ref[1] % 2 == 1)
    def _():
        whole[:half, :] = other[...]
        whole[half:, :] = mine[...]


def sum_halves(mine, other, beside=()):
    total = add_round(mine, swap(other, "tp", 1))
    mask, done = 2, None
    beside = list(beside)
    while mask < lax.axis_size("tp"):
        arrived = swap(total, "tp", mask)
        if beside:
            done = beside.pop(0)(done)
            arrived, done = lax.optimization_barrier((arrived, done))
        total = add_round(total, arrived)
        mask *= 2
    while beside:
        done = beside.pop(0)(done)
    return (total, swap(total, "tp", 1)), done


def block_rows(b):
    return slice(b * BLK, (b + 1) * BLK)


def whole_spec(shape):
    return pl.BlockSpec(shape, lambda i, t: (0,) * len(shape))


def part_spec(rows, row_block, width):
    return pl.BlockSpec((rows, width), lambda i, t: (row_block, 0))


def table_call(kernel, table, operands, in_specs, shapes, scratch, name, flops=0, out_specs=None):
    moved = sum(math.prod(s.block_shape) * 2 for s in in_specs)
    moved += sum(math.prod(s.shape) * s.dtype.itemsize for s in shapes)
    return pl.pallas_call(
        kernel,
        grid_spec=pltpu.PrefetchScalarGridSpec(
            num_scalar_prefetch=1,
            grid=(1,),
            in_specs=in_specs,
            out_specs=[whole_spec(s.shape) for s in shapes],
            scratch_shapes=scratch,
        ),
        out_shape=shapes,
        compiler_params=params(),
        cost_estimate=cost(flops, moved),
        name=name,
    )(table, *operands)


def low_kernel(count, tab_ref, x_ref, *refs):
    downs = refs[:count]
    mine, other, whole = refs[count:]
    for b in range(whole.shape[0] // BLK):

        def step(k, b=b):
            whole[block_rows(b), :] = dot_nt(x_ref[block_rows(b), :], downs[k][...]).astype(BF16)

        pick(tab_ref, b, count, step)
    split_rows(tab_ref, whole, mine, other)


def low_part(table, x, firsts):
    rows, width, cols = x.shape[0], firsts[0].shape[1], 3 * ADAPTER_RANK
    half = jax.ShapeDtypeStruct((rows // 2, cols), BF16)
    return table_call(
        functools.partial(low_kernel, len(firsts)),
        table,
        [x] + firsts,
        [pl.BlockSpec((rows, width), lambda i, t: (0, t[1]))]
        + [part_spec(cols, 0, width)] * len(firsts),
        [half, half],
        [pltpu.VMEM((rows, cols), BF16)],
        "low_part",
        2 * rows * width * cols,
    )


def finish_kv_kernel(count, rotate_keys, tab_ref, kv_ref, mine, other, cos_ref, sin_ref, *refs):
    ups = refs[:count]
    kvo, low = refs[count:]
    ckv = kv_ref.shape[1]
    rank = ADAPTER_RANK
    join_rows(tab_ref, mine, other, low)
    for b in range(kv_ref.shape[0] // BLK):

        def step(k, b=b):
            at_rows = block_rows(b)
            low_k = low[at_rows, rank : 2 * rank]
            low_v = low[at_rows, 2 * rank :]
            up_kv = unpack_kv(ups[k].at[rank // 2 :])
            for h in range(ckv // HEAD_SIZE):
                at = slice(h * HEAD_SIZE, (h + 1) * HEAD_SIZE)
                if rotate_keys:
                    term = dot_nn(low_v if h % 2 else low_k, up_kv[:, at])
                else:
                    is_value = (tab_ref[1] * (ckv // HEAD_SIZE) + h) % 2 == 1
                    term = jnp.where(
                        is_value, dot_nn(low_v, up_kv[:, at]), dot_nn(low_k, up_kv[:, at])
                    )
                piece = (kv_ref[at_rows, at] + term).astype(BF16)
                if rotate_keys and h % 2 == 0:
                    cosine, sine = cos_ref[at_rows, :], sin_ref[at_rows, :]
                    piece = turn_kernel(piece.astype(F32), cosine, sine).astype(BF16)
                kvo[at_rows, at] = piece

        pick(tab_ref, b, count, step)


def finish_kv(table, kv_lin, halves, firsts, cosine, sine, rotate_keys):
    rows, ckv = kv_lin.shape
    cols, width = 3 * ADAPTER_RANK, firsts[0].shape[1]
    part = ADAPTER_RANK // 2 + ADAPTER_RANK // 4
    operands = [kv_lin, *halves, cosine, sine]
    return table_call(
        functools.partial(finish_kv_kernel, len(firsts), rotate_keys),
        table,
        operands + firsts,
        [whole_spec(a.shape) for a in operands]
        + [part_spec(part, cols // part, width)] * len(firsts),
        [jax.ShapeDtypeStruct((rows, ckv), BF16), jax.ShapeDtypeStruct((rows, cols), BF16)],
        [],
        "finish_kv",
        4 * rows * ADAPTER_RANK * ckv,
    )


def finish_q_kernel(count, tab_ref, q_ref, low_ref, cos_ref, sin_ref, *refs):
    ups, qo = refs[:count], refs[count]
    cq = q_ref.shape[1]
    rank = ADAPTER_RANK
    for b in range(q_ref.shape[0] // BLK):

        def step(k, b=b):
            at_rows = block_rows(b)
            cosine, sine = cos_ref[at_rows, :], sin_ref[at_rows, :]
            up_q = unpack_q(ups[k].at[: rank // 2])
            query = q_ref[at_rows, :] + dot_nn(low_ref[at_rows, :rank], up_q)
            for h in range(cq // HEAD_SIZE):
                at = slice(h * HEAD_SIZE, (h + 1) * HEAD_SIZE)
                qo[at_rows, at] = turn_kernel(query[:, at], cosine, sine).astype(BF16)

        pick(tab_ref, b, count, step)


def finish_q(table, q_lin, low_in, firsts, cosine, sine):
    rows, cq = q_lin.shape
    cols, width = 3 * ADAPTER_RANK, firsts[0].shape[1]
    part = ADAPTER_RANK // 2 + ADAPTER_RANK // 4
    operands = [q_lin, low_in, cosine, sine]
    return table_call(
        functools.partial(finish_q_kernel, len(firsts)),
        table,
        operands + firsts,
        [whole_spec(a.shape) for a in operands]
        + [part_spec(part, cols // part, width)] * len(firsts),
        [jax.ShapeDtypeStruct((rows, cq), BF16)],
        [],
        "finish_q",
        2 * rows * ADAPTER_RANK * cq,
    )[0]


def low_o_kernel(count, tab_ref, cot_ref, attn_ref, *refs):
    lates = refs[:count]
    mine, other, whole = refs[count:]
    rank = ADAPTER_RANK
    for b in range(whole.shape[0] // BLK):

        def step(k, b=b):
            at = block_rows(b)
            whole[at, :rank] = dot_nt(cot_ref[at, :], lates[k][:rank, :]).astype(BF16)
            down = unpack_q(lates[k].at[rank:])
            whole[at, rank:] = dot_nt(attn_ref[at, :], down).astype(BF16)

        pick(tab_ref, b, count, step)
    split_rows(tab_ref, whole, mine, other)


def low_o_part(table, cot, attn, lates):
    rows, width = cot.shape
    cols = 2 * ADAPTER_RANK
    half = jax.ShapeDtypeStruct((rows // 2, cols), BF16)
    return table_call(
        functools.partial(low_o_kernel, len(lates)),
        table,
        [cot, attn] + lates,
        [whole_spec(cot.shape), whole_spec(attn.shape)]
        + [whole_spec(lates[0].shape)] * len(lates),
        [half, half],
        [pltpu.VMEM((rows, cols), BF16)],
        "low_o_part",
        2 * rows * cols * width,
    )


def low_g_kernel(count, tab_ref, gq_ref, gkv_ref, *refs):
    ups = refs[:count]
    mine, other, whole = refs[count:]
    rank = ADAPTER_RANK
    ckv = gkv_ref.shape[1]
    for b in range(whole.shape[0] // BLK):

        def step(k, b=b):
            at = block_rows(b)
            up_q = unpack_q(ups[k].at[: rank // 2])
            whole[at, :rank] = dot_nt(gq_ref[at, :], up_q).astype(BF16)
            up_kv = unpack_kv(ups[k].at[rank // 2 :])
            sums = [jnp.zeros((BLK, rank), F32)] * 2
            for h in range(ckv // HEAD_SIZE):
                cols = slice(h * HEAD_SIZE, (h + 1) * HEAD_SIZE)
                term = dot_nt(gkv_ref[at, cols], up_kv[:, cols])
                is_value = (tab_ref[1] * (ckv // HEAD_SIZE) + h) % 2 == 1
                sums[0] = sums[0] + jnp.where(is_value, 0.0, term)
                sums[1] = sums[1] + jnp.where(is_value, term, 0.0)
            whole[at, rank : 2 * rank] = sums[0].astype(BF16)
            whole[at, 2 * rank :] = sums[1].astype(BF16)

        pick(tab_ref, b, count, step)
    split_rows(tab_ref, whole, mine, other)


def low_g_part(table, gq, gkv, firsts):
    rows = gq.shape[0]
    cols, width = 3 * ADAPTER_RANK, firsts[0].shape[1]
    part = ADAPTER_RANK // 2 + ADAPTER_RANK // 4
    half = jax.ShapeDtypeStruct((rows // 2, cols), BF16)
    return table_call(
        functools.partial(low_g_kernel, len(firsts)),
        table,
        [gq, gkv] + firsts,
        [whole_spec(gq.shape), whole_spec(gkv.shape)]
        + [part_spec(part, cols // part, width)] * len(firsts),
        [half, half],
        [pltpu.VMEM((rows, cols), BF16)],
        "low_g_part",
        2 * rows * width * ADAPTER_RANK,
    )


def zero_unused(tab_ref, blocks, sends):
    for k in range(len(sends)):
        used = tab_ref[SOURCE_AT] == k
        for b in range(1, blocks):
            used = used | (tab_ref[SOURCE_AT + b] == k)

        @pl.when(jnp.logical_not(used))
        def _(k=k):
            sends[k][...] = jnp.zeros_like(sends[k])


def up_grads_kernel(
    count, tab_ref, low_ref, gq_ref, gkv_ref, o_mine, o_other, cot, attn, *refs
):
    sends, low_o = refs[:count], refs[count]
    rank = ADAPTER_RANK
    join_rows(tab_ref, o_mine, o_other, low_o)
    blocks = low_o.shape[0] // BLK
    cq, ckv = gq_ref.shape[1], gkv_ref.shape[1]
    half, quarter = rank // 2, rank // 4
    late = half + quarter
    zero_unused(tab_ref, blocks, sends)
    for b in range(blocks):

        def step(k, b=b):
            at = block_rows(b)
            out = sends[k]
            up_q = dot_tn(low_ref[at, :rank], gq_ref[at, :]).astype(BF16)
            down_o = dot_tn(low_o[at, :rank], attn[at, :]).astype(BF16)
            for i in range(2):
                rows = slice(i * half, (i + 1) * half)
                cols = slice(i * cq, (i + 1) * cq)
                out[:half, cols] = up_q[rows, :]
                out[late + rank :, cols] = down_o[rows, :]
            for h in range(ckv // HEAD_SIZE):
                piece = slice(h * HEAD_SIZE, (h + 1) * HEAD_SIZE)
                is_value = (tab_ref[1] * (ckv // HEAD_SIZE) + h) % 2 == 1
                up_kv = jnp.where(
                    is_value,
                    dot_tn(low_ref[at, 2 * rank :], gkv_ref[at, piece]),
                    dot_tn(low_ref[at, rank : 2 * rank], gkv_ref[at, piece]),
                ).astype(BF16)
                for i in range(4):
                    cols = slice(i * ckv + h * HEAD_SIZE, i * ckv + (h + 1) * HEAD_SIZE)
                    out[half:late, cols] = up_kv[i * quarter : (i + 1) * quarter, :]
            out[late : late + rank, :] = dot_tn(low_o[at, rank:], cot[at, :]).astype(BF16)

        pick(tab_ref, b, count, step)


def up_grads(table, count, low_in, gq, gkv, o_halves, cot, attn):
    rows, width = cot.shape
    rank = ADAPTER_RANK
    operands = [low_in, gq, gkv, *o_halves, cot, attn]
    return list(
        table_call(
            functools.partial(up_grads_kernel, count),
            table,
            operands,
            [whole_spec(a.shape) for a in operands],
            [jax.ShapeDtypeStruct((2 * rank + rank // 4, width), BF16)] * count,
            [pltpu.VMEM((rows, 2 * rank), BF16)],
            "up_grads",
            2 * rows * width * 3 * rank,
        )
    )


def down_grads_kernel(count, tab_ref, x_ref, mine, other, *refs):
    downs, sends = refs[:count], refs[count : 2 * count]
    delta, low = refs[2 * count :]
    join_rows(tab_ref, mine, other, low)
    blocks = low.shape[0] // BLK
    zero_unused(tab_ref, blocks, sends)
    for b in range(blocks):

        def step(k, b=b):
            at = block_rows(b)
            sends[k][...] = dot_tn(low[at, :], x_ref[at, :]).astype(BF16)
            delta[at, :] = dot_nn(low[at, :], downs[k][...])

        pick(tab_ref, b, count, step)


def down_grads(table, x, halves, firsts):
    rows, cols = x.shape[0], 3 * ADAPTER_RANK
    width, count = firsts[0].shape[1], len(firsts)
    results = table_call(
        functools.partial(down_grads_kernel, count),
        table,
        [x, *halves] + firsts,
        [pl.BlockSpec((rows, width), lambda i, t: (0, t[1]))]
        + [whole_spec(halves[0].shape)] * 2
        + [part_spec(cols, 0, width)] * count,
        [jax.ShapeDtypeStruct((cols, width), BF16)] * count
        + [jax.ShapeDtypeStruct((rows, width), F32)],
        [pltpu.VMEM((rows, cols), BF16)],
        "down_grads",
        4 * rows * width * cols,
    )
    return list(results[:count]), results[count]


def store_kernel(count, tab_ref, *refs):
    downs, ups = refs[:count], refs[count : 2 * count]
    outs = refs[2 * count :]
    row = pl.program_id(0)
    for o in outs:
        o[...] = jnp.zeros_like(o)
    rank = ADAPTER_RANK
    half, quarter = rank // 2, rank // 4
    late = half + quarter
    for k in range(count):

        @pl.when(tab_ref[SERVED_AT + k] == row)
        def _(k=k):
            a = ups[k]
            outs[0][0] += downs[k][...].astype(F32)
            outs[1][0] += unpack_q(a.at[:half]).astype(F32)
            outs[2][0] += unpack_kv(a.at[half:late]).astype(F32)
            outs[3][0] += unpack_q(a.at[late + rank :]).astype(F32)
            outs[4][0] += a[late : late + rank, :].astype(F32)


def store_sums(table, downs, ups, owned):
    rank = ADAPTER_RANK
    width = downs[0].shape[1]
    shapes = [
        jax.ShapeDtypeStruct((owned, r, c), F32)
        for r, c in [
            (3 * rank, width),
            (rank, width // 2),
            (rank, width // 4),
            (rank, width // 2),
            (rank, width),
        ]
    ]
    return pl.pallas_call(
        functools.partial(store_kernel, len(downs)),
        grid_spec=pltpu.PrefetchScalarGridSpec(
            num_scalar_prefetch=1,
            grid=(owned,),
            in_specs=[pl.BlockSpec(a.shape, lambda i, t: (0, 0)) for a in downs + ups],
            out_specs=[pl.BlockSpec((1,) + s.shape[1:], lambda i, t: (i, 0, 0)) for s in shapes],
        ),
        out_shape=shapes,
        compiler_params=params(),
        name="store_sums",
    )(table, *downs, *ups)


def output_kernel(count, tab_ref, sum_ref, mine, other, *refs):
    lates = refs[:count]
    out, low = refs[count:]
    rank = ADAPTER_RANK
    join_rows(tab_ref, mine, other, low)
    for b in range(out.shape[0] // BLK):

        def step(k, b=b):
            at = block_rows(b)
            term = dot_nn(low[at, rank:], lates[k][...])
            out[at, :] = (sum_ref[at, :].astype(F32) + term).astype(BF16)

        pick(tab_ref, b, count, step)


def output_result(table, total, halves, lates):
    rows, width = total.shape
    rank = ADAPTER_RANK
    return table_call(
        functools.partial(output_kernel, len(lates)),
        table,
        [total, *halves] + lates,
        [whole_spec(total.shape)]
        + [whole_spec(halves[0].shape)] * 2
        + [part_spec(rank, 0, width)] * len(lates),
        [jax.ShapeDtypeStruct((rows, width), BF16)],
        [pltpu.VMEM((rows, 2 * rank), BF16)],
        "output_result",
        2 * rows * rank * width,
    )[0]


def crop_start(tab_ref, crops, positions):
    start = jnp.zeros_like(positions)
    for i in range(crops):
        end = tab_ref[ENDS_AT + i]
        start = jnp.where(positions >= end, end, start)
    return start


def masked(scores, first, own, base):
    rows, cols = scores.shape
    key_pos = base + lax.broadcasted_iota(jnp.int32, (rows, cols), 0)
    allowed = key_pos >= first
    if own:
        allowed &= key_pos <= base + lax.broadcasted_iota(jnp.int32, (rows, cols), 1)
    return jnp.where(allowed, scores, NEG)


def chunk_on(tab_ref, crops, k, rows):
    me = tab_ref[0]
    chunk = me ^ k
    return (chunk <= me) & ((chunk + 1) * rows > crop_start(tab_ref, crops, me * rows))


def query_starts(tab_ref, crops, rows):
    positions = tab_ref[0] * rows + lax.broadcasted_iota(jnp.int32, (1, rows), 1)
    return crop_start(tab_ref, crops, positions)


def forward_kernel(heads, count, crops, tab_ref, q_ref, *refs):
    kv_refs = refs[:count]
    out_ref, norm_ref, acc, top, total = refs[count:]
    rows = q_ref.shape[0]
    first = query_starts(tab_ref, crops, rows)
    for k in range(count):

        def chunk_step(k=k):
            base = (tab_ref[0] ^ k) * rows
            keys = kv_refs[k][:, :HEAD_SIZE]
            values = kv_refs[k][:, HEAD_SIZE:]
            for h in range(heads):
                at = slice(h * HEAD_SIZE, (h + 1) * HEAD_SIZE)
                scores = masked(dot_nt(keys, q_ref[:, at]), first, k == 0, base)
                here = jnp.max(scores, axis=0, keepdims=True)
                if k == 0:
                    new_top = here
                else:
                    old_top = top[h : h + 1, :]
                    new_top = jnp.maximum(old_top, here)
                weights = jnp.exp((scores - new_top) * SCALE)
                here_sum = jnp.sum(weights, axis=0, keepdims=True)
                here_out = dot_tn(values, weights.astype(BF16))
                if k == 0:
                    total[h : h + 1, :] = here_sum
                    acc[h] = here_out
                else:
                    decay = jnp.exp((old_top - new_top) * SCALE)
                    total[h : h + 1, :] = total[h : h + 1, :] * decay + here_sum
                    acc[h] = acc[h] * decay + here_out
                top[h : h + 1, :] = new_top

        if k == 0:
            chunk_step()
        else:
            pl.when(chunk_on(tab_ref, crops, k, rows))(chunk_step)
    for h in range(heads):
        at = slice(h * HEAD_SIZE, (h + 1) * HEAD_SIZE)
        out_ref[:, at] = jnp.transpose(acc[h] / total[h : h + 1, :]).astype(BF16)
    norm_ref[...] = top[...] * SCALE + jnp.log(total[...])


def attention_forward(table, crops, query, kvs):
    rows, cols = query.shape
    heads = cols // HEAD_SIZE
    count = len(kvs)
    smem = pl.BlockSpec(memory_space=pltpu.SMEM)
    vmem = pl.BlockSpec(memory_space=pltpu.VMEM)
    work = heads * rows * rows * count
    return pl.pallas_call(
        functools.partial(forward_kernel, heads, count, crops),
        in_specs=[smem] + [vmem] * (1 + count),
        out_specs=[vmem] * 2,
        out_shape=[
            jax.ShapeDtypeStruct((rows, cols), BF16),
            jax.ShapeDtypeStruct((heads, rows), F32),
        ],
        scratch_shapes=[
            pltpu.VMEM((heads, HEAD_SIZE, rows), F32),
            pltpu.VMEM((heads, rows), F32),
            pltpu.VMEM((heads, rows), F32),
        ],
        compiler_params=params(),
        cost_estimate=cost(4 * work * HEAD_SIZE, 4 * rows * cols * count, work),
        name="attention_forward",
    )(table, query, *kvs)


def backward_kernel(
    heads,
    count,
    crops,
    tab_ref,
    q_ref,
    dense_ref,
    mine,
    other,
    out_ref,
    norm_ref,
    cos_ref,
    sin_ref,
    *refs,
):
    kv_refs, lates = refs[:count], refs[count : 2 * count]
    gq_ref = refs[2 * count]
    gkv_refs = refs[2 * count + 1 : 3 * count + 1]
    acc, delta, low, grad_ref = refs[3 * count + 1 :]
    rows = q_ref.shape[0]
    rank = ADAPTER_RANK
    first = query_starts(tab_ref, crops, rows)
    join_rows(tab_ref, mine, other, low)
    for b in range(rows // BLK):

        def add(k, b=b):
            at = block_rows(b)
            term = dot_nn(low[at, :rank], unpack_q(lates[k].at[rank:]))
            grad_ref[at, :] = (dense_ref[at, :] + term).astype(BF16)

        pick(tab_ref, b, count, add)
    for h in range(heads):
        at = slice(h * HEAD_SIZE, (h + 1) * HEAD_SIZE)
        product = grad_ref[:, at].astype(F32) * out_ref[:, at].astype(F32)
        delta[h : h + 1, :] = jnp.sum(jnp.transpose(product), axis=0, keepdims=True)
    for k in range(count):

        def chunk_step(k=k):
            base = (tab_ref[0] ^ k) * rows
            keys = kv_refs[k][:, :HEAD_SIZE]
            values = kv_refs[k][:, HEAD_SIZE:]
            key_grad = jnp.zeros((rows, HEAD_SIZE), F32)
            value_grad = jnp.zeros((rows, HEAD_SIZE), F32)
            for h in range(heads):
                at = slice(h * HEAD_SIZE, (h + 1) * HEAD_SIZE)
                scores = masked(dot_nt(keys, q_ref[:, at]), first, k == 0, base)
                weights = jnp.exp(scores * SCALE - norm_ref[h : h + 1, :])
                value_grad += dot_nn(weights.astype(BF16), grad_ref[:, at])
                grad_weights = dot_nt(values, grad_ref[:, at])
                grad_scores = (weights * (grad_weights - delta[h : h + 1, :])).astype(BF16)
                key_grad += dot_nn(grad_scores, q_ref[:, at])
                here = dot_tn(keys, grad_scores)
                if k == 0:
                    acc[h] = here
                else:
                    acc[h] += here
            gkv_refs[k][:, :HEAD_SIZE] = (key_grad * SCALE).astype(BF16)
            gkv_refs[k][:, HEAD_SIZE:] = value_grad.astype(BF16)

        if k == 0:
            chunk_step()
        else:
            on = chunk_on(tab_ref, crops, k, rows)
            pl.when(on)(chunk_step)

            @pl.when(jnp.logical_not(on))
            def _(k=k):
                gkv_refs[k][...] = jnp.zeros_like(gkv_refs[k])

    for h in range(heads):
        at = slice(h * HEAD_SIZE, (h + 1) * HEAD_SIZE)
        grad = jnp.transpose(acc[h]) * SCALE
        gq_ref[:, at] = turn_kernel(grad, cos_ref[...], -sin_ref[...]).astype(BF16)


def attention_backward(table, crops, query, dense, halves, out, norm, cosine, sine, kvs, lates):
    rows, cols = query.shape
    heads = cols // HEAD_SIZE
    count = len(kvs)
    smem = pl.BlockSpec(memory_space=pltpu.SMEM)
    vmem = pl.BlockSpec(memory_space=pltpu.VMEM)
    work = heads * rows * rows * count
    results = pl.pallas_call(
        functools.partial(backward_kernel, heads, count, crops),
        in_specs=[smem] + [vmem] * (8 + 2 * count),
        out_specs=[vmem] * (1 + count),
        out_shape=[jax.ShapeDtypeStruct((rows, cols), BF16)]
        + [jax.ShapeDtypeStruct((rows, 2 * HEAD_SIZE), BF16)] * count,
        scratch_shapes=[
            pltpu.VMEM((heads, HEAD_SIZE, rows), F32),
            pltpu.VMEM((heads, rows), F32),
            pltpu.VMEM((rows, 2 * ADAPTER_RANK), BF16),
            pltpu.VMEM((rows, cols), BF16),
        ],
        compiler_params=params(),
        cost_estimate=cost(10 * work * HEAD_SIZE, 8 * rows * cols * count, work),
        name="attention_backward",
    )(table, query, dense, *halves, out, norm, cosine, sine, *kvs, *lates)
    return results[0], list(results[1:])


def plane_spec(shape, axis, other):
    def index(i, t):
        core = t[1] % 2
        at = 2 * i + (1 - core if other else core)
        return (0, at) if axis else (at, 0)

    return pl.BlockSpec(shape, index)


def copy_kernel(tab_ref, x_ref, o_ref):
    o_ref[...] = x_ref[...]


def pick_planes(table, weight, groups, axis):
    planes = groups // 2
    shape = list(weight.shape)
    shape[axis] //= groups
    result = list(weight.shape)
    result[axis] //= 2
    return pl.pallas_call(
        copy_kernel,
        grid_spec=pltpu.PrefetchScalarGridSpec(
            num_scalar_prefetch=1,
            grid=(planes,),
            in_specs=[plane_spec(tuple(shape), axis, True)],
            out_specs=pl.BlockSpec(
                tuple(shape), (lambda i, t: (0, i)) if axis else (lambda i, t: (i, 0))
            ),
        ),
        out_shape=jax.ShapeDtypeStruct(tuple(result), BF16),
        compiler_params=params(),
        cost_estimate=cost(0, 2 * math.prod(weight.shape)),
        name="pick_planes",
    )(table, weight)


def reduce_planes(parts, groups):
    lines = [list(range(core, groups, 2)) for core in range(2)]
    return lax.psum_scatter(parts, "tp", scatter_dimension=0, axis_index_groups=lines, tiled=False)


def project_kernel(tab_ref, a_ref, ao_ref, w_ref, wo_ref, o_ref):
    total = dot_nn(a_ref[...], w_ref[...]) + dot_nn(ao_ref[...], wo_ref[...])
    o_ref[0] = total.astype(BF16)


def project_out(table, attn, attn_other, weight, weight_other, groups):
    rows, depth = attn.shape
    cols = weight.shape[1] // groups
    planes = groups // 2
    return pl.pallas_call(
        project_kernel,
        grid_spec=pltpu.PrefetchScalarGridSpec(
            num_scalar_prefetch=1,
            grid=(planes,),
            in_specs=[
                whole_spec(attn.shape),
                whole_spec(attn.shape),
                plane_spec((depth, cols), 1, False),
                pl.BlockSpec((depth, cols), lambda i, t: (0, i)),
            ],
            out_specs=pl.BlockSpec((1, rows, cols), lambda i, t: (i, 0, 0)),
        ),
        out_shape=jax.ShapeDtypeStruct((planes, rows, cols), BF16),
        compiler_params=params(),
        cost_estimate=cost(
            2 * rows * depth * cols * groups, 2 * (rows + 2 * depth) * cols * planes
        ),
        name="project_out",
    )(table, attn, attn_other, weight, weight_other)


PER_STEP = 2


def grad_attn_kernel(c0_ref, c1_ref, w_ref, *refs):
    before, o_ref = refs[:-1], refs[-1]
    step = pl.program_id(0)
    per_step, first_rows, cols = c0_ref.shape
    parts = ((c0_ref, slice(0, first_rows)), (c1_ref, slice(first_rows, o_ref.shape[0])))
    for c_ref, at in parts:
        total = dot_nt(c_ref[0], w_ref[:, :cols])
        for i in range(1, per_step):
            total += dot_nt(c_ref[i], w_ref[:, i * cols : (i + 1) * cols])

        @pl.when(step == 0)
        def _(at=at, total=total):
            o_ref[at, :] = total + before[0][at, :] if before else total

        @pl.when(step > 0)
        def _(at=at, total=total):
            o_ref[at, :] += total


def grad_attn(cot_first, cot_second, weight, half, before=None):
    groups, first_rows, cols = cot_first.shape
    depth = weight.shape[0]
    rows = first_rows + cot_second.shape[1]
    steps = groups // PER_STEP // 2
    start = half * steps
    whole = pl.BlockSpec((rows, depth), lambda i: (0, 0))
    return pl.pallas_call(
        grad_attn_kernel,
        grid=(steps,),
        in_specs=[
            pl.BlockSpec((PER_STEP, first_rows, cols), lambda i: (start + i, 0, 0)),
            pl.BlockSpec((PER_STEP, rows - first_rows, cols), lambda i: (start + i, 0, 0)),
            pl.BlockSpec((depth, PER_STEP * cols), lambda i: (0, start + i)),
        ]
        + ([] if before is None else [whole]),
        out_specs=whole,
        out_shape=jax.ShapeDtypeStruct((rows, depth), F32),
        compiler_params=params(),
        cost_estimate=cost(rows * depth * cols * groups, (rows + depth) * cols * groups),
        name="grad_attn",
    )(cot_first, cot_second, weight, *([] if before is None else [before]))


def grad_input_kernel(tab_ref, gq, gqo, gkv, gkvo, wq, wqo, wkv, wkvo, o_ref):
    total = dot_nt(gq[...], wq[...]) + dot_nt(gqo[...], wqo[...])
    total = total + dot_nt(gkv[...], wkv[...]) + dot_nt(gkvo[...], wkvo[...])
    o_ref[0] = total.astype(BF16)


def grad_input(table, gq, gq_other, gkv, gkv_other, wq, wq_other, wkv, wkv_other, groups):
    rows, cq = gq.shape
    ckv = gkv.shape[1]
    cols = wq.shape[0] // groups
    planes = groups // 2
    return pl.pallas_call(
        grad_input_kernel,
        grid_spec=pltpu.PrefetchScalarGridSpec(
            num_scalar_prefetch=1,
            grid=(planes,),
            in_specs=[
                whole_spec(gq.shape),
                whole_spec(gq.shape),
                whole_spec(gkv.shape),
                whole_spec(gkv.shape),
                plane_spec((cols, cq), 0, False),
                pl.BlockSpec((cols, cq), lambda i, t: (i, 0)),
                plane_spec((cols, ckv), 0, False),
                pl.BlockSpec((cols, ckv), lambda i, t: (i, 0)),
            ],
            out_specs=pl.BlockSpec((1, rows, cols), lambda i, t: (i, 0, 0)),
        ),
        out_shape=jax.ShapeDtypeStruct((planes, rows, cols), BF16),
        compiler_params=params(),
        cost_estimate=cost(
            2 * rows * (cq + ckv) * cols * groups,
            2 * (rows + 2 * (cq + ckv)) * cols * planes,
        ),
        name="grad_input",
    )(table, gq, gq_other, gkv, gkv_other, wq, wq_other, wkv, wkv_other)


def body(
    hidden_input,
    output_cotangent,
    query_projection,
    key_value_projection,
    output_projection,
    adapter_qkv_down_store,
    adapter_query_up,
    adapter_key_value_up,
    adapter_output_down,
    adapter_output_up,
    crop_token_length,
    tenant_per_block,
    tenant_store_row,
):
    ctx_count = lax.axis_size("ctx")
    tp_count = lax.axis_size("tp")
    ctx_index = lax.axis_index("ctx")
    tp_index = lax.axis_index("tp")
    rows_dev = hidden_input.shape[0]
    out_cols = output_cotangent.shape[1]
    tenant_owner = adapter_qkv_down_store.shape[0]
    blocks_dev = rows_dev // BLK
    pair_bits = (tp_count // KEY_VALUE_HEADS).bit_length() - 1
    groups = hidden_input.shape[1] // out_cols
    crops = crop_token_length.shape[0]
    partners = range(1, ctx_count)

    first_rows = rows_dev * 7 // 12
    cot_part, crop_token_length = lax.optimization_barrier(
        (output_cotangent[:first_rows], crop_token_length)
    )
    cot_first = lax.all_gather(cot_part, "tp", axis=0, tiled=False)

    table, firsts, lates = serve(
        ctx_count,
        blocks_dev,
        crop_token_length,
        tenant_per_block,
        tenant_store_row,
        adapter_qkv_down_store.swapaxes(1, 2),
        adapter_query_up,
        adapter_key_value_up,
        adapter_output_up,
        adapter_output_down.swapaxes(1, 2),
    )
    firsts = [firsts[0]] + [swap(firsts[k], "ctx", k) for k in partners]
    my_pos = ctx_index * rows_dev + jnp.arange(rows_dev, dtype=jnp.int32)
    q_lin, kv_lin = dense_qkv(hidden_input, query_projection, key_value_projection)
    firsts, q_lin, kv_lin, tables = lax.optimization_barrier(
        (firsts, q_lin, kv_lin, rope_tables(my_pos))
    )
    cosine, sine = tables
    low_halves = low_part(table, hidden_input, firsts)
    low_halves, (out_pick, query_pick) = sum_halves(
        *low_halves,
        beside=[
            lambda done: pick_planes(table, output_projection, groups, 1),
            lambda done: (done, pick_planes(table, query_projection, groups, 0)),
        ],
    )
    low_halves, cot_rest = lax.optimization_barrier((low_halves, output_cotangent[first_rows:]))
    cot_second = lax.all_gather(cot_rest, "tp", axis=0, tiled=False)
    kv_local, low_in = finish_kv(
        table, kv_lin, low_halves, firsts, cosine, sine, pair_bits == 0
    )
    if pair_bits:
        for bit_no in range(pair_bits):
            partner = swap(kv_local, "tp", 1 << bit_no)
            is_lower = tp_index // (1 << bit_no) % 2 == 0
            kv_local = jnp.where(
                is_lower,
                jnp.concatenate([kv_local, partner], axis=1),
                jnp.concatenate([partner, kv_local], axis=1),
            )
        key_rot = turn(kv_local[:, :HEAD_SIZE].astype(F32), cosine, sine).astype(BF16)
        kv_local = jnp.concatenate([key_rot, kv_local[:, HEAD_SIZE:]], axis=1)
    kvs = [kv_local] + [swap(kv_local, "ctx", k) for k in partners]
    query_rot = finish_q(table, q_lin, low_in, firsts, cosine, sine)
    kv_pick = pick_planes(table, key_value_projection, groups, 0)
    kvs, lates, query_rot, kv_pick = lax.optimization_barrier((kvs, lates, query_rot, kv_pick))
    out_other, query_other, kv_other = (
        swap(pick, "tp", 1) for pick in (out_pick, query_pick, kv_pick)
    )
    lates = [lates[0]] + [swap(lates[k], "ctx", k) for k in partners]

    attn_out, log_norm = attention_forward(table, crops, query_rot, kvs)
    lates, attn_out = lax.optimization_barrier((lates, attn_out))
    heads_part = project_out(
        table, attn_out, swap(attn_out, "tp", 1), output_projection, out_other, groups
    )
    heads_part, attn_out, cot_first = lax.optimization_barrier((heads_part, attn_out, cot_first))
    heads_sum = reduce_planes(heads_part, groups)
    o_halves, grad_dense = sum_halves(
        *low_o_part(table, output_cotangent, attn_out, lates),
        beside=[
            lambda done: grad_attn(cot_first, cot_second, output_projection, 0),
            lambda done: grad_attn(cot_first, cot_second, output_projection, 1, done),
        ],
    )
    grad_q, kv_parts = attention_backward(
        table, crops, query_rot, grad_dense, o_halves, attn_out, log_norm, cosine, sine, kvs, lates
    )
    grad_q_other = swap(grad_q, "tp", 1)
    reduced = kv_parts[0].astype(F32)
    for k in partners:
        reduced = reduced + swap(kv_parts[k], "ctx", k).astype(F32)
    reduced = jnp.concatenate(
        [turn(reduced[:, :HEAD_SIZE], cosine, -sine), reduced[:, HEAD_SIZE:]], axis=1
    )
    for bit_no in reversed(range(pair_bits)):
        half_cols = reduced.shape[1] // 2
        is_lower = tp_index // (1 << bit_no) % 2 == 0
        keep_part = jnp.where(is_lower, reduced[:, :half_cols], reduced[:, half_cols:])
        send_part = jnp.where(is_lower, reduced[:, half_cols:], reduced[:, :half_cols])
        reduced = keep_part + swap(send_part.astype(BF16), "tp", 1 << bit_no).astype(F32)
    grad_kv = reduced.astype(BF16)

    input_part = grad_input(
        table,
        grad_q,
        grad_q_other,
        grad_kv,
        swap(grad_kv, "tp", 1),
        query_projection,
        query_other,
        key_value_projection,
        kv_other,
        groups,
    )
    input_part, grad_q, grad_kv = lax.optimization_barrier((input_part, grad_q, grad_kv))
    input_sum = reduce_planes(input_part, groups)

    def send_ups(done):
        return up_grads(
            table, ctx_count, low_in, grad_q, grad_kv, o_halves, output_cotangent, attn_out
        )

    g_halves, up_sends = sum_halves(
        *low_g_part(table, grad_q, grad_kv, firsts), beside=[send_ups]
    )
    up_back = [up_sends[0]] + [swap(up_sends[k], "ctx", k) for k in partners]
    output = output_result(table, heads_sum, o_halves, lates)
    g_halves, up_back, output = lax.optimization_barrier((g_halves, up_back, output))
    down_sends, input_delta = down_grads(table, hidden_input, g_halves, firsts)
    down_back = [down_sends[0]] + [swap(down_sends[k], "ctx", k) for k in partners]
    stores = store_sums(table, down_back, up_back, tenant_owner)
    input_sum, input_delta, stores = lax.optimization_barrier((input_sum, input_delta, stores))
    hidden_input_gradient = (input_sum.astype(F32) + input_delta).astype(BF16)
    return (
        output,
        hidden_input_gradient,
        stores[0].swapaxes(1, 2),
        stores[1],
        stores[2],
        stores[3].swapaxes(1, 2),
        stores[4],
    )


def solution(mesh):
    in_specs = (
        P("ctx", None),
        P("ctx", "tp"),
        P(None, "tp"),
        P(None, "tp"),
        P("tp", None),
        P("ctx", "tp", None),
        P("ctx", None, "tp"),
        P("ctx", None, "tp"),
        P("ctx", "tp", None),
        P("ctx", None, "tp"),
        P(),
        P(),
        P(),
    )
    out_specs = (
        P("ctx", "tp"),
        P("ctx", "tp"),
        P("ctx", "tp", None),
        P("ctx", None, "tp"),
        P("ctx", None, "tp"),
        P("ctx", "tp", None),
        P("ctx", None, "tp"),
    )
    return jax.shard_map(body, mesh=mesh, in_specs=in_specs, out_specs=out_specs, check_vma=False)
```

```python
import functools
import math

import jax
import jax.numpy as jnp
from jax import lax
from jax.experimental import pallas as pl
from jax.experimental.pallas import tpu as pltpu
from jax.sharding import PartitionSpec as P

HEAD_SIZE = 128
KEY_VALUE_HEADS = 8
ADAPTER_RANK = 64
BLK = 128
NEG = -1e30
ROPE_BASE = 1000000.0
SCALE = HEAD_SIZE ** (-0.5)
VMEM_BYTES = 62 * 1024 * 1024

BF16 = jnp.bfloat16
F32 = jnp.float32


def params():
    return pltpu.CompilerParams(vmem_limit_bytes=VMEM_BYTES)


def cost(flops, bytes_accessed, transcendentals=0):
    return pl.CostEstimate(
        flops=int(flops), bytes_accessed=int(bytes_accessed), transcendentals=int(transcendentals)
    )


def dot_nn(a, b):
    return lax.dot_general(a, b, (((1,), (0,)), ((), ())), preferred_element_type=F32)


def dot_nt(a, b):
    return lax.dot_general(a, b, (((1,), (1,)), ((), ())), preferred_element_type=F32)


def dot_tn(a, b):
    return lax.dot_general(a, b, (((0,), (0,)), ((), ())), preferred_element_type=F32)


def swap(value, axis, mask):
    pairs = [(source, source ^ mask) for source in range(lax.axis_size(axis))]
    return lax.ppermute(value, axis, pairs)


def add_round(a, b):
    return (a.astype(F32) + b.astype(F32)).astype(BF16)


def rope_tables(positions):
    half_dim = HEAD_SIZE // 2
    exponent = jnp.arange(half_dim, dtype=F32) * (2.0 / HEAD_SIZE)
    frequency = jnp.exp(-exponent * math.log(ROPE_BASE))
    angles = positions.astype(F32)[:, None] * frequency[None, :]
    cosine, sine = jnp.cos(angles), jnp.sin(angles)
    return (
        jnp.concatenate([cosine, cosine], axis=1),
        jnp.concatenate([-sine, sine], axis=1),
    )


def turn(values, cosine, sine):
    return values * cosine + jnp.roll(values, HEAD_SIZE // 2, axis=1) * sine


def turn_kernel(values, cosine, sine):
    return values * cosine + pltpu.roll(values, HEAD_SIZE // 2, 1) * sine


def dense_kernel(x_ref, wq_ref, wkv_ref, q_ref, kv_ref):
    @pl.when(pl.program_id(0) == 0)
    def _():
        q_ref[...] = jnp.zeros_like(q_ref)
        kv_ref[...] = jnp.zeros_like(kv_ref)

    x = x_ref[...]
    q_ref[...] += dot_nn(x, wq_ref[...])
    kv_ref[...] += dot_nn(x, wkv_ref[...])


def dense_qkv(x, wq, wkv):
    rows, width = x.shape
    step = 2048
    cq, ckv = wq.shape[1], wkv.shape[1]
    return pl.pallas_call(
        dense_kernel,
        grid=(width // step,),
        in_specs=[
            pl.BlockSpec((rows, step), lambda i: (0, i)),
            pl.BlockSpec((step, cq), lambda i: (i, 0)),
            pl.BlockSpec((step, ckv), lambda i: (i, 0)),
        ],
        out_specs=[
            pl.BlockSpec((rows, cq), lambda i: (0, 0)),
            pl.BlockSpec((rows, ckv), lambda i: (0, 0)),
        ],
        out_shape=[
            jax.ShapeDtypeStruct((rows, cq), F32),
            jax.ShapeDtypeStruct((rows, ckv), F32),
        ],
        compiler_params=params(),
        cost_estimate=cost(2 * rows * width * (cq + ckv), 2 * width * (rows + cq + ckv)),
        name="dense_qkv",
    )(x, wq, wkv)


ENDS_AT = 2
SEND_AT = 16
SERVED_AT = 32
SOURCE_AT = 48
TABLE = 64


def serve_kernel(
    count, blocks, owned, crop_ref, tenant_ref, row_ref, down, up_q, up_kv, up_o, down_o, *outs
):
    tab = outs[0]
    firsts, lates = outs[1 : 1 + count], outs[1 + count :]
    me = lax.axis_index("ctx")
    for i in range(TABLE):
        tab[i] = 0
    tab[0] = me
    tab[1] = lax.axis_index("tp")
    end = jnp.int32(0)
    for i in range(crop_ref.shape[0]):
        end = end + crop_ref[i]
        tab[ENDS_AT + i] = end
    for b in range(blocks):
        row = row_ref[tenant_ref[me * blocks + b]]
        tab[SOURCE_AT + b] = (row // owned) ^ me
    for k in range(count):
        served = jnp.int32(-1)
        for b in range(blocks):
            row = row_ref[tenant_ref[(me ^ k) * blocks + b]]
            served = jnp.where(row // owned == me, row - me * owned, served)
        tab[SERVED_AT + k] = served
        tab[SEND_AT + k] = jnp.maximum(served, 0)
    rank, width = ADAPTER_RANK, down.shape[2]
    half, quarter = rank // 2, rank // 4
    cq, ckv = width // 2, width // 4
    for k in range(count):
        at = tab[SEND_AT + k]
        low = down.shape[1]
        firsts[k][:low, :] = down[at]
        for i in range(2):
            firsts[k][low : low + half, i * cq : (i + 1) * cq] = up_q[
                at, i * half : (i + 1) * half, :
            ]
            lates[k][rank : rank + half, i * cq : (i + 1) * cq] = down_o[
                at, i * half : (i + 1) * half, :
            ]
        for i in range(4):
            firsts[k][low + half :, i * ckv : (i + 1) * ckv] = up_kv[
                at, i * quarter : (i + 1) * quarter, :
            ]
        lates[k][:rank, :] = up_o[at]


def serve(count, blocks, crops, tenants, store_rows, down, up_q, up_kv, up_o, down_o):
    rank, width = ADAPTER_RANK, down.shape[2]
    assert up_q.shape[2] * 2 == width and up_kv.shape[2] * 4 == width
    assert up_o.shape[2] == width and down_o.shape[2] * 2 == width
    smem = pl.BlockSpec(memory_space=pltpu.SMEM)
    vmem = pl.BlockSpec(memory_space=pltpu.VMEM)
    first = jax.ShapeDtypeStruct((3 * rank + rank // 2 + rank // 4, width), BF16)
    late = jax.ShapeDtypeStruct((rank + rank // 2, width), BF16)
    results = pl.pallas_call(
        functools.partial(serve_kernel, count, blocks, down.shape[0]),
        in_specs=[smem] * 3 + [vmem] * 5,
        out_specs=[smem] + [vmem] * (2 * count),
        out_shape=[jax.ShapeDtypeStruct((TABLE,), jnp.int32)] + [first] * count + [late] * count,
        compiler_params=params(),
        name="serve",
    )(crops, tenants, store_rows, down, up_q, up_kv, up_o, down_o)
    return results[0], list(results[1 : 1 + count]), list(results[1 + count :])


def unpack_q(ref):
    rows, width = ref.shape
    value = ref[...]
    return jnp.concatenate([value[:, : width // 2], value[:, width // 2 :]], axis=0)


def unpack_kv(ref):
    rows, width = ref.shape
    value = ref[...]
    step = width // 4
    return jnp.concatenate([value[:, i * step : (i + 1) * step] for i in range(4)], axis=0)


def pick(tab_ref, block, count, step):
    for k in range(count):

        @pl.when(tab_ref[SOURCE_AT + block] == k)
        def _(k=k):
            step(k)


def split_rows(tab_ref, whole, mine, other):
    half = mine.shape[0]

    @pl.when(tab_ref[1] % 2 == 0)
    def _():
        mine[...] = whole[:half, :]
        other[...] = whole[half:, :]

    @pl.when(tab_ref[1] % 2 == 1)
    def _():
        mine[...] = whole[half:, :]
        other[...] = whole[:half, :]


def join_rows(tab_ref, mine, other, whole):
    half = mine.shape[0]

    @pl.when(tab_ref[1] % 2 == 0)
    def _():
        whole[:half, :] = mine[...]
        whole[half:, :] = other[...]

    @pl.when(tab_ref[1] % 2 == 1)
    def _():
        whole[:half, :] = other[...]
        whole[half:, :] = mine[...]


def sum_halves(mine, other, beside=()):
    total = add_round(mine, swap(other, "tp", 1))
    mask, done = 2, None
    beside = list(beside)
    while mask < lax.axis_size("tp"):
        arrived = swap(total, "tp", mask)
        if beside:
            done = beside.pop(0)(done)
            arrived, done = lax.optimization_barrier((arrived, done))
        total = add_round(total, arrived)
        mask *= 2
    while beside:
        done = beside.pop(0)(done)
    return (total, swap(total, "tp", 1)), done


def block_rows(b):
    return slice(b * BLK, (b + 1) * BLK)


def whole_spec(shape):
    return pl.BlockSpec(shape, lambda i, t: (0,) * len(shape))


def part_spec(rows, row_block, width):
    return pl.BlockSpec((rows, width), lambda i, t: (row_block, 0))


def table_call(kernel, table, operands, in_specs, shapes, scratch, name, flops=0, out_specs=None):
    moved = sum(math.prod(s.block_shape) * 2 for s in in_specs)
    moved += sum(math.prod(s.shape) * s.dtype.itemsize for s in shapes)
    return pl.pallas_call(
        kernel,
        grid_spec=pltpu.PrefetchScalarGridSpec(
            num_scalar_prefetch=1,
            grid=(1,),
            in_specs=in_specs,
            out_specs=[whole_spec(s.shape) for s in shapes],
            scratch_shapes=scratch,
        ),
        out_shape=shapes,
        compiler_params=params(),
        cost_estimate=cost(flops, moved),
        name=name,
    )(table, *operands)


def low_kernel(count, tab_ref, x_ref, *refs):
    downs = refs[:count]
    mine, other, whole = refs[count:]
    for b in range(whole.shape[0] // BLK):

        def step(k, b=b):
            whole[block_rows(b), :] = dot_nt(x_ref[block_rows(b), :], downs[k][...]).astype(BF16)

        pick(tab_ref, b, count, step)
    split_rows(tab_ref, whole, mine, other)


def low_part(table, x, firsts):
    rows, width, cols = x.shape[0], firsts[0].shape[1], 3 * ADAPTER_RANK
    half = jax.ShapeDtypeStruct((rows // 2, cols), BF16)
    return table_call(
        functools.partial(low_kernel, len(firsts)),
        table,
        [x] + firsts,
        [pl.BlockSpec((rows, width), lambda i, t: (0, t[1]))]
        + [part_spec(cols, 0, width)] * len(firsts),
        [half, half],
        [pltpu.VMEM((rows, cols), BF16)],
        "low_part",
        2 * rows * width * cols,
    )


def finish_kv_kernel(count, rotate_keys, tab_ref, kv_ref, mine, other, cos_ref, sin_ref, *refs):
    ups = refs[:count]
    kvo, low = refs[count:]
    ckv = kv_ref.shape[1]
    rank = ADAPTER_RANK
    join_rows(tab_ref, mine, other, low)
    for b in range(kv_ref.shape[0] // BLK):

        def step(k, b=b):
            at_rows = block_rows(b)
            low_k = low[at_rows, rank : 2 * rank]
            low_v = low[at_rows, 2 * rank :]
            up_kv = unpack_kv(ups[k].at[rank // 2 :])
            for h in range(ckv // HEAD_SIZE):
                at = slice(h * HEAD_SIZE, (h + 1) * HEAD_SIZE)
                if rotate_keys:
                    term = dot_nn(low_v if h % 2 else low_k, up_kv[:, at])
                else:
                    is_value = (tab_ref[1] * (ckv // HEAD_SIZE) + h) % 2 == 1
                    term = jnp.where(
                        is_value, dot_nn(low_v, up_kv[:, at]), dot_nn(low_k, up_kv[:, at])
                    )
                piece = (kv_ref[at_rows, at] + term).astype(BF16)
                if rotate_keys and h % 2 == 0:
                    cosine, sine = cos_ref[at_rows, :], sin_ref[at_rows, :]
                    piece = turn_kernel(piece.astype(F32), cosine, sine).astype(BF16)
                kvo[at_rows, at] = piece

        pick(tab_ref, b, count, step)


def finish_kv(table, kv_lin, halves, firsts, cosine, sine, rotate_keys):
    rows, ckv = kv_lin.shape
    cols, width = 3 * ADAPTER_RANK, firsts[0].shape[1]
    part = ADAPTER_RANK // 2 + ADAPTER_RANK // 4
    operands = [kv_lin, *halves, cosine, sine]
    return table_call(
        functools.partial(finish_kv_kernel, len(firsts), rotate_keys),
        table,
        operands + firsts,
        [whole_spec(a.shape) for a in operands]
        + [part_spec(part, cols // part, width)] * len(firsts),
        [jax.ShapeDtypeStruct((rows, ckv), BF16), jax.ShapeDtypeStruct((rows, cols), BF16)],
        [],
        "finish_kv",
        4 * rows * ADAPTER_RANK * ckv,
    )


def finish_q_kernel(count, tab_ref, q_ref, low_ref, cos_ref, sin_ref, *refs):
    ups, qo = refs[:count], refs[count]
    cq = q_ref.shape[1]
    rank = ADAPTER_RANK
    for b in range(q_ref.shape[0] // BLK):

        def step(k, b=b):
            at_rows = block_rows(b)
            cosine, sine = cos_ref[at_rows, :], sin_ref[at_rows, :]
            up_q = unpack_q(ups[k].at[: rank // 2])
            query = q_ref[at_rows, :] + dot_nn(low_ref[at_rows, :rank], up_q)
            for h in range(cq // HEAD_SIZE):
                at = slice(h * HEAD_SIZE, (h + 1) * HEAD_SIZE)
                qo[at_rows, at] = turn_kernel(query[:, at], cosine, sine).astype(BF16)

        pick(tab_ref, b, count, step)


def finish_q(table, q_lin, low_in, firsts, cosine, sine):
    rows, cq = q_lin.shape
    cols, width = 3 * ADAPTER_RANK, firsts[0].shape[1]
    part = ADAPTER_RANK // 2 + ADAPTER_RANK // 4
    operands = [q_lin, low_in, cosine, sine]
    return table_call(
        functools.partial(finish_q_kernel, len(firsts)),
        table,
        operands + firsts,
        [whole_spec(a.shape) for a in operands]
        + [part_spec(part, cols // part, width)] * len(firsts),
        [jax.ShapeDtypeStruct((rows, cq), BF16)],
        [],
        "finish_q",
        2 * rows * ADAPTER_RANK * cq,
    )[0]


def low_o_kernel(count, tab_ref, cot_ref, attn_ref, *refs):
    lates = refs[:count]
    mine, other, whole = refs[count:]
    rank = ADAPTER_RANK
    for b in range(whole.shape[0] // BLK):

        def step(k, b=b):
            at = block_rows(b)
            whole[at, :rank] = dot_nt(cot_ref[at, :], lates[k][:rank, :]).astype(BF16)
            down = unpack_q(lates[k].at[rank:])
            whole[at, rank:] = dot_nt(attn_ref[at, :], down).astype(BF16)

        pick(tab_ref, b, count, step)
    split_rows(tab_ref, whole, mine, other)


def low_o_part(table, cot, attn, lates):
    rows, width = cot.shape
    cols = 2 * ADAPTER_RANK
    half = jax.ShapeDtypeStruct((rows // 2, cols), BF16)
    return table_call(
        functools.partial(low_o_kernel, len(lates)),
        table,
        [cot, attn] + lates,
        [whole_spec(cot.shape), whole_spec(attn.shape)]
        + [whole_spec(lates[0].shape)] * len(lates),
        [half, half],
        [pltpu.VMEM((rows, cols), BF16)],
        "low_o_part",
        2 * rows * cols * width,
    )


def low_g_kernel(count, tab_ref, gq_ref, gkv_ref, *refs):
    ups = refs[:count]
    mine, other, whole = refs[count:]
    rank = ADAPTER_RANK
    ckv = gkv_ref.shape[1]
    for b in range(whole.shape[0] // BLK):

        def step(k, b=b):
            at = block_rows(b)
            up_q = unpack_q(ups[k].at[: rank // 2])
            whole[at, :rank] = dot_nt(gq_ref[at, :], up_q).astype(BF16)
            up_kv = unpack_kv(ups[k].at[rank // 2 :])
            sums = [jnp.zeros((BLK, rank), F32)] * 2
            for h in range(ckv // HEAD_SIZE):
                cols = slice(h * HEAD_SIZE, (h + 1) * HEAD_SIZE)
                term = dot_nt(gkv_ref[at, cols], up_kv[:, cols])
                is_value = (tab_ref[1] * (ckv // HEAD_SIZE) + h) % 2 == 1
                sums[0] = sums[0] + jnp.where(is_value, 0.0, term)
                sums[1] = sums[1] + jnp.where(is_value, term, 0.0)
            whole[at, rank : 2 * rank] = sums[0].astype(BF16)
            whole[at, 2 * rank :] = sums[1].astype(BF16)

        pick(tab_ref, b, count, step)
    split_rows(tab_ref, whole, mine, other)


def low_g_part(table, gq, gkv, firsts):
    rows = gq.shape[0]
    cols, width = 3 * ADAPTER_RANK, firsts[0].shape[1]
    part = ADAPTER_RANK // 2 + ADAPTER_RANK // 4
    half = jax.ShapeDtypeStruct((rows // 2, cols), BF16)
    return table_call(
        functools.partial(low_g_kernel, len(firsts)),
        table,
        [gq, gkv] + firsts,
        [whole_spec(gq.shape), whole_spec(gkv.shape)]
        + [part_spec(part, cols // part, width)] * len(firsts),
        [half, half],
        [pltpu.VMEM((rows, cols), BF16)],
        "low_g_part",
        2 * rows * width * ADAPTER_RANK,
    )


def zero_unused(tab_ref, blocks, sends):
    for k in range(len(sends)):
        used = tab_ref[SOURCE_AT] == k
        for b in range(1, blocks):
            used = used | (tab_ref[SOURCE_AT + b] == k)

        @pl.when(jnp.logical_not(used))
        def _(k=k):
            sends[k][...] = jnp.zeros_like(sends[k])


def up_grads_kernel(
    count, tab_ref, low_ref, gq_ref, gkv_ref, o_mine, o_other, cot, attn, *refs
):
    sends, low_o = refs[:count], refs[count]
    rank = ADAPTER_RANK
    join_rows(tab_ref, o_mine, o_other, low_o)
    blocks = low_o.shape[0] // BLK
    cq, ckv = gq_ref.shape[1], gkv_ref.shape[1]
    half, quarter = rank // 2, rank // 4
    late = half + quarter
    zero_unused(tab_ref, blocks, sends)
    for b in range(blocks):

        def step(k, b=b):
            at = block_rows(b)
            out = sends[k]
            up_q = dot_tn(low_ref[at, :rank], gq_ref[at, :]).astype(BF16)
            down_o = dot_tn(low_o[at, :rank], attn[at, :]).astype(BF16)
            for i in range(2):
                rows = slice(i * half, (i + 1) * half)
                cols = slice(i * cq, (i + 1) * cq)
                out[:half, cols] = up_q[rows, :]
                out[late + rank :, cols] = down_o[rows, :]
            for h in range(ckv // HEAD_SIZE):
                piece = slice(h * HEAD_SIZE, (h + 1) * HEAD_SIZE)
                is_value = (tab_ref[1] * (ckv // HEAD_SIZE) + h) % 2 == 1
                up_kv = jnp.where(
                    is_value,
                    dot_tn(low_ref[at, 2 * rank :], gkv_ref[at, piece]),
                    dot_tn(low_ref[at, rank : 2 * rank], gkv_ref[at, piece]),
                ).astype(BF16)
                for i in range(4):
                    cols = slice(i * ckv + h * HEAD_SIZE, i * ckv + (h + 1) * HEAD_SIZE)
                    out[half:late, cols] = up_kv[i * quarter : (i + 1) * quarter, :]
            out[late : late + rank, :] = dot_tn(low_o[at, rank:], cot[at, :]).astype(BF16)

        pick(tab_ref, b, count, step)


def up_grads(table, count, low_in, gq, gkv, o_halves, cot, attn):
    rows, width = cot.shape
    rank = ADAPTER_RANK
    operands = [low_in, gq, gkv, *o_halves, cot, attn]
    return list(
        table_call(
            functools.partial(up_grads_kernel, count),
            table,
            operands,
            [whole_spec(a.shape) for a in operands],
            [jax.ShapeDtypeStruct((2 * rank + rank // 4, width), BF16)] * count,
            [pltpu.VMEM((rows, 2 * rank), BF16)],
            "up_grads",
            2 * rows * width * 3 * rank,
        )
    )


def down_grads_kernel(count, tab_ref, x_ref, mine, other, *refs):
    downs, sends = refs[:count], refs[count : 2 * count]
    delta, low = refs[2 * count :]
    join_rows(tab_ref, mine, other, low)
    blocks = low.shape[0] // BLK
    zero_unused(tab_ref, blocks, sends)
    for b in range(blocks):

        def step(k, b=b):
            at = block_rows(b)
            sends[k][...] = dot_tn(low[at, :], x_ref[at, :]).astype(BF16)
            delta[at, :] = dot_nn(low[at, :], downs[k][...]).astype(BF16)

        pick(tab_ref, b, count, step)


def down_grads(table, x, halves, firsts):
    rows, cols = x.shape[0], 3 * ADAPTER_RANK
    width, count = firsts[0].shape[1], len(firsts)
    results = table_call(
        functools.partial(down_grads_kernel, count),
        table,
        [x, *halves] + firsts,
        [pl.BlockSpec((rows, width), lambda i, t: (0, t[1]))]
        + [whole_spec(halves[0].shape)] * 2
        + [part_spec(cols, 0, width)] * count,
        [jax.ShapeDtypeStruct((cols, width), BF16)] * count
        + [jax.ShapeDtypeStruct((rows, width), BF16)],
        [pltpu.VMEM((rows, cols), BF16)],
        "down_grads",
        4 * rows * width * cols,
    )
    return list(results[:count]), results[count]


def store_kernel(count, pieces, tab_ref, *refs):
    arrived, outs = refs[:count], refs[count:]
    row = pl.program_id(0)
    for o in outs:
        o[...] = jnp.zeros_like(o)
    for k in range(count):

        @pl.when(tab_ref[SERVED_AT + k] == row)
        def _(k=k):
            for o, piece in zip(outs, pieces):
                o[0] += piece(arrived[k]).astype(F32)


def store_sums(table, arrived, owned, pieces, sizes):
    shapes = [jax.ShapeDtypeStruct((owned,) + size, F32) for size in sizes]
    return pl.pallas_call(
        functools.partial(store_kernel, len(arrived), pieces),
        grid_spec=pltpu.PrefetchScalarGridSpec(
            num_scalar_prefetch=1,
            grid=(owned,),
            in_specs=[pl.BlockSpec(a.shape, lambda i, t: (0, 0)) for a in arrived],
            out_specs=[pl.BlockSpec((1,) + s.shape[1:], lambda i, t: (i, 0, 0)) for s in shapes],
        ),
        out_shape=shapes,
        compiler_params=params(),
        name="store_sums",
    )(table, *arrived)


def store_ups(table, arrived, owned):
    rank, width = ADAPTER_RANK, arrived[0].shape[1]
    half, late = rank // 2, rank // 2 + rank // 4
    pieces = [
        lambda a: unpack_q(a.at[:half]),
        lambda a: unpack_kv(a.at[half:late]),
        lambda a: unpack_q(a.at[late + rank :]),
        lambda a: a[late : late + rank, :],
    ]
    sizes = [(rank, width // 2), (rank, width // 4), (rank, width // 2), (rank, width)]
    return store_sums(table, arrived, owned, pieces, sizes)


def store_downs(table, arrived, owned):
    return store_sums(table, arrived, owned, [lambda a: a[...]], [arrived[0].shape])[0]


def output_kernel(count, tab_ref, sum_ref, mine, other, *refs):
    lates = refs[:count]
    out, low = refs[count:]
    rank = ADAPTER_RANK
    join_rows(tab_ref, mine, other, low)
    for b in range(out.shape[0] // BLK):

        def step(k, b=b):
            at = block_rows(b)
            term = dot_nn(low[at, rank:], lates[k][...])
            out[at, :] = (sum_ref[at, :].astype(F32) + term).astype(BF16)

        pick(tab_ref, b, count, step)


def output_result(table, total, halves, lates):
    rows, width = total.shape
    rank = ADAPTER_RANK
    return table_call(
        functools.partial(output_kernel, len(lates)),
        table,
        [total, *halves] + lates,
        [whole_spec(total.shape)]
        + [whole_spec(halves[0].shape)] * 2
        + [part_spec(rank, 0, width)] * len(lates),
        [jax.ShapeDtypeStruct((rows, width), BF16)],
        [pltpu.VMEM((rows, 2 * rank), BF16)],
        "output_result",
        2 * rows * rank * width,
    )[0]


def crop_start(tab_ref, crops, positions):
    start = jnp.zeros_like(positions)
    for i in range(crops):
        end = tab_ref[ENDS_AT + i]
        start = jnp.where(positions >= end, end, start)
    return start


def masked(scores, first, own, base):
    rows, cols = scores.shape
    key_pos = base + lax.broadcasted_iota(jnp.int32, (rows, cols), 0)
    allowed = key_pos >= first
    if own:
        allowed &= key_pos <= base + lax.broadcasted_iota(jnp.int32, (rows, cols), 1)
    return jnp.where(allowed, scores, NEG)


def chunk_on(tab_ref, crops, k, rows):
    me = tab_ref[0]
    chunk = me ^ k
    return (chunk <= me) & ((chunk + 1) * rows > crop_start(tab_ref, crops, me * rows))


def query_starts(tab_ref, crops, rows):
    positions = tab_ref[0] * rows + lax.broadcasted_iota(jnp.int32, (1, rows), 1)
    return crop_start(tab_ref, crops, positions)


def forward_kernel(heads, count, crops, tab_ref, q_ref, *refs):
    kv_refs = refs[:count]
    out_ref, norm_ref, acc, top, total = refs[count:]
    rows = q_ref.shape[0]
    first = query_starts(tab_ref, crops, rows)
    for k in range(count):

        def chunk_step(k=k):
            base = (tab_ref[0] ^ k) * rows
            keys = kv_refs[k][:, :HEAD_SIZE]
            values = kv_refs[k][:, HEAD_SIZE:]
            for h in range(heads):
                at = slice(h * HEAD_SIZE, (h + 1) * HEAD_SIZE)
                scores = masked(dot_nt(keys, q_ref[:, at]), first, k == 0, base)
                here = jnp.max(scores, axis=0, keepdims=True)
                if k == 0:
                    new_top = here
                else:
                    old_top = top[h : h + 1, :]
                    new_top = jnp.maximum(old_top, here)
                weights = jnp.exp((scores - new_top) * SCALE)
                here_sum = jnp.sum(weights, axis=0, keepdims=True)
                here_out = dot_tn(values, weights.astype(BF16))
                if k == 0:
                    total[h : h + 1, :] = here_sum
                    acc[h] = here_out
                else:
                    decay = jnp.exp((old_top - new_top) * SCALE)
                    total[h : h + 1, :] = total[h : h + 1, :] * decay + here_sum
                    acc[h] = acc[h] * decay + here_out
                top[h : h + 1, :] = new_top

        if k == 0:
            chunk_step()
        else:
            pl.when(chunk_on(tab_ref, crops, k, rows))(chunk_step)
    for h in range(heads):
        at = slice(h * HEAD_SIZE, (h + 1) * HEAD_SIZE)
        out_ref[:, at] = jnp.transpose(acc[h] / total[h : h + 1, :]).astype(BF16)
    norm_ref[...] = top[...] * SCALE + jnp.log(total[...])


def attention_forward(table, crops, query, kvs):
    rows, cols = query.shape
    heads = cols // HEAD_SIZE
    count = len(kvs)
    smem = pl.BlockSpec(memory_space=pltpu.SMEM)
    vmem = pl.BlockSpec(memory_space=pltpu.VMEM)
    work = heads * rows * rows * count
    return pl.pallas_call(
        functools.partial(forward_kernel, heads, count, crops),
        in_specs=[smem] + [vmem] * (1 + count),
        out_specs=[vmem] * 2,
        out_shape=[
            jax.ShapeDtypeStruct((rows, cols), BF16),
            jax.ShapeDtypeStruct((heads, rows), F32),
        ],
        scratch_shapes=[
            pltpu.VMEM((heads, HEAD_SIZE, rows), F32),
            pltpu.VMEM((heads, rows), F32),
            pltpu.VMEM((heads, rows), F32),
        ],
        compiler_params=params(),
        cost_estimate=cost(4 * work * HEAD_SIZE, 4 * rows * cols * count, work),
        name="attention_forward",
    )(table, query, *kvs)


def backward_kernel(
    heads,
    count,
    crops,
    tab_ref,
    q_ref,
    dense_ref,
    mine,
    other,
    out_ref,
    norm_ref,
    cos_ref,
    sin_ref,
    *refs,
):
    kv_refs, lates = refs[:count], refs[count : 2 * count]
    gq_ref = refs[2 * count]
    gkv_refs = refs[2 * count + 1 : 3 * count + 1]
    acc, delta, low, grad_ref = refs[3 * count + 1 :]
    rows = q_ref.shape[0]
    rank = ADAPTER_RANK
    first = query_starts(tab_ref, crops, rows)
    join_rows(tab_ref, mine, other, low)
    for b in range(rows // BLK):

        def add(k, b=b):
            at = block_rows(b)
            term = dot_nn(low[at, :rank], unpack_q(lates[k].at[rank:]))
            grad_ref[at, :] = (dense_ref[at, :] + term).astype(BF16)

        pick(tab_ref, b, count, add)
    for h in range(heads):
        at = slice(h * HEAD_SIZE, (h + 1) * HEAD_SIZE)
        product = grad_ref[:, at].astype(F32) * out_ref[:, at].astype(F32)
        delta[h : h + 1, :] = jnp.sum(jnp.transpose(product), axis=0, keepdims=True)
    for k in range(count):

        def chunk_step(k=k):
            base = (tab_ref[0] ^ k) * rows
            keys = kv_refs[k][:, :HEAD_SIZE]
            values = kv_refs[k][:, HEAD_SIZE:]
            key_grad = jnp.zeros((rows, HEAD_SIZE), F32)
            value_grad = jnp.zeros((rows, HEAD_SIZE), F32)
            for h in range(heads):
                at = slice(h * HEAD_SIZE, (h + 1) * HEAD_SIZE)
                scores = masked(dot_nt(keys, q_ref[:, at]), first, k == 0, base)
                weights = jnp.exp(scores * SCALE - norm_ref[h : h + 1, :])
                value_grad += dot_nn(weights.astype(BF16), grad_ref[:, at])
                grad_weights = dot_nt(values, grad_ref[:, at])
                grad_scores = (weights * (grad_weights - delta[h : h + 1, :])).astype(BF16)
                key_grad += dot_nn(grad_scores, q_ref[:, at])
                here = dot_tn(keys, grad_scores)
                if k == 0:
                    acc[h] = here
                else:
                    acc[h] += here
            gkv_refs[k][:, :HEAD_SIZE] = (key_grad * SCALE).astype(BF16)
            gkv_refs[k][:, HEAD_SIZE:] = value_grad.astype(BF16)

        if k == 0:
            chunk_step()
        else:
            on = chunk_on(tab_ref, crops, k, rows)
            pl.when(on)(chunk_step)

            @pl.when(jnp.logical_not(on))
            def _(k=k):
                gkv_refs[k][...] = jnp.zeros_like(gkv_refs[k])

    for h in range(heads):
        at = slice(h * HEAD_SIZE, (h + 1) * HEAD_SIZE)
        grad = jnp.transpose(acc[h]) * SCALE
        gq_ref[:, at] = turn_kernel(grad, cos_ref[...], -sin_ref[...]).astype(BF16)


def attention_backward(table, crops, query, dense, halves, out, norm, cosine, sine, kvs, lates):
    rows, cols = query.shape
    heads = cols // HEAD_SIZE
    count = len(kvs)
    smem = pl.BlockSpec(memory_space=pltpu.SMEM)
    vmem = pl.BlockSpec(memory_space=pltpu.VMEM)
    work = heads * rows * rows * count
    results = pl.pallas_call(
        functools.partial(backward_kernel, heads, count, crops),
        in_specs=[smem] + [vmem] * (8 + 2 * count),
        out_specs=[vmem] * (1 + count),
        out_shape=[jax.ShapeDtypeStruct((rows, cols), BF16)]
        + [jax.ShapeDtypeStruct((rows, 2 * HEAD_SIZE), BF16)] * count,
        scratch_shapes=[
            pltpu.VMEM((heads, HEAD_SIZE, rows), F32),
            pltpu.VMEM((heads, rows), F32),
            pltpu.VMEM((rows, 2 * ADAPTER_RANK), BF16),
            pltpu.VMEM((rows, cols), BF16),
        ],
        compiler_params=params(),
        cost_estimate=cost(10 * work * HEAD_SIZE, 8 * rows * cols * count, work),
        name="attention_backward",
    )(table, query, dense, *halves, out, norm, cosine, sine, *kvs, *lates)
    return results[0], list(results[1:])


def plane_spec(shape, axis, other):
    def index(i, t):
        core = t[1] % 2
        at = 2 * i + (1 - core if other else core)
        return (0, at) if axis else (at, 0)

    return pl.BlockSpec(shape, index)


def pick_kernel(planes, axis, tab_ref, w_ref, o_ref, sem):
    size = w_ref.shape[axis] // planes // 2
    copies = []
    for i in range(planes):
        start = pl.multiple_of((2 * i + 1 - tab_ref[1] % 2) * size, size)
        source, target = pl.ds(start, size), pl.ds(i * size, size)
        if axis:
            copy = pltpu.make_async_copy(w_ref.at[:, source], o_ref.at[:, target], sem.at[i])
        else:
            copy = pltpu.make_async_copy(w_ref.at[source], o_ref.at[target], sem.at[i])
        copies.append(copy)
    for copy in copies:
        copy.start()
    for copy in copies:
        copy.wait()


def pick_planes(table, weight, groups, axis):
    planes = groups // 2
    result = list(weight.shape)
    result[axis] //= 2
    anywhere = pl.BlockSpec(memory_space=pl.ANY)
    return pl.pallas_call(
        functools.partial(pick_kernel, planes, axis),
        in_specs=[pl.BlockSpec(memory_space=pltpu.SMEM), anywhere],
        out_specs=anywhere,
        out_shape=jax.ShapeDtypeStruct(tuple(result), BF16),
        scratch_shapes=[pltpu.SemaphoreType.DMA((planes,))],
        compiler_params=params(),
        cost_estimate=cost(0, 2 * math.prod(weight.shape)),
        name="pick_planes",
    )(table, weight)


def reduce_planes(parts, groups):
    lines = [list(range(core, groups, 2)) for core in range(2)]
    return lax.psum_scatter(parts, "tp", scatter_dimension=0, axis_index_groups=lines, tiled=False)


def project_kernel(tab_ref, a_ref, ao_ref, w_ref, wo_ref, o_ref):
    total = dot_nn(a_ref[...], w_ref[...]) + dot_nn(ao_ref[...], wo_ref[...])
    o_ref[0] = total.astype(BF16)


def project_out(table, attn, attn_other, weight, weight_other, groups):
    rows, depth = attn.shape
    cols = weight.shape[1] // groups
    planes = groups // 2
    return pl.pallas_call(
        project_kernel,
        grid_spec=pltpu.PrefetchScalarGridSpec(
            num_scalar_prefetch=1,
            grid=(planes,),
            in_specs=[
                whole_spec(attn.shape),
                whole_spec(attn.shape),
                plane_spec((depth, cols), 1, False),
                pl.BlockSpec((depth, cols), lambda i, t: (0, i)),
            ],
            out_specs=pl.BlockSpec((1, rows, cols), lambda i, t: (i, 0, 0)),
        ),
        out_shape=jax.ShapeDtypeStruct((planes, rows, cols), BF16),
        compiler_params=params(),
        cost_estimate=cost(
            2 * rows * depth * cols * groups, 2 * (rows + 2 * depth) * cols * planes
        ),
        name="project_out",
    )(table, attn, attn_other, weight, weight_other)


PER_STEP = 2


def grad_attn_kernel(c0_ref, c1_ref, w_ref, *refs):
    before, o_ref = refs[:-1], refs[-1]
    step = pl.program_id(0)
    per_step, first_rows, cols = c0_ref.shape
    parts = ((c0_ref, slice(0, first_rows)), (c1_ref, slice(first_rows, o_ref.shape[0])))
    for c_ref, at in parts:
        total = dot_nt(c_ref[0], w_ref[:, :cols])
        for i in range(1, per_step):
            total += dot_nt(c_ref[i], w_ref[:, i * cols : (i + 1) * cols])

        @pl.when(step == 0)
        def _(at=at, total=total):
            o_ref[at, :] = total + before[0][at, :] if before else total

        @pl.when(step > 0)
        def _(at=at, total=total):
            o_ref[at, :] += total


def grad_attn(cot_first, cot_second, weight, half, before=None):
    groups, first_rows, cols = cot_first.shape
    depth = weight.shape[0]
    rows = first_rows + cot_second.shape[1]
    steps = groups // PER_STEP // 2
    start = half * steps
    whole = pl.BlockSpec((rows, depth), lambda i: (0, 0))
    return pl.pallas_call(
        grad_attn_kernel,
        grid=(steps,),
        in_specs=[
            pl.BlockSpec((PER_STEP, first_rows, cols), lambda i: (start + i, 0, 0)),
            pl.BlockSpec((PER_STEP, rows - first_rows, cols), lambda i: (start + i, 0, 0)),
            pl.BlockSpec((depth, PER_STEP * cols), lambda i: (0, start + i)),
        ]
        + ([] if before is None else [whole]),
        out_specs=whole,
        out_shape=jax.ShapeDtypeStruct((rows, depth), F32),
        compiler_params=params(),
        cost_estimate=cost(rows * depth * cols * groups, (rows + depth) * cols * groups),
        name="grad_attn",
    )(cot_first, cot_second, weight, *([] if before is None else [before]))


def grad_input_kernel(tab_ref, gq, gqo, gkv, gkvo, wq, wqo, wkv, wkvo, o_ref):
    total = dot_nt(gq[...], wq[...]) + dot_nt(gqo[...], wqo[...])
    total = total + dot_nt(gkv[...], wkv[...]) + dot_nt(gkvo[...], wkvo[...])
    o_ref[0] = total.astype(BF16)


def grad_input(table, gq, gq_other, gkv, gkv_other, wq, wq_other, wkv, wkv_other, groups):
    rows, cq = gq.shape
    ckv = gkv.shape[1]
    cols = wq.shape[0] // groups
    planes = groups // 2
    return pl.pallas_call(
        grad_input_kernel,
        grid_spec=pltpu.PrefetchScalarGridSpec(
            num_scalar_prefetch=1,
            grid=(planes,),
            in_specs=[
                whole_spec(gq.shape),
                whole_spec(gq.shape),
                whole_spec(gkv.shape),
                whole_spec(gkv.shape),
                plane_spec((cols, cq), 0, False),
                pl.BlockSpec((cols, cq), lambda i, t: (i, 0)),
                plane_spec((cols, ckv), 0, False),
                pl.BlockSpec((cols, ckv), lambda i, t: (i, 0)),
            ],
            out_specs=pl.BlockSpec((1, rows, cols), lambda i, t: (i, 0, 0)),
        ),
        out_shape=jax.ShapeDtypeStruct((planes, rows, cols), BF16),
        compiler_params=params(),
        cost_estimate=cost(
            2 * rows * (cq + ckv) * cols * groups,
            2 * (rows + 2 * (cq + ckv)) * cols * planes,
        ),
        name="grad_input",
    )(table, gq, gq_other, gkv, gkv_other, wq, wq_other, wkv, wkv_other)


def body(
    hidden_input,
    output_cotangent,
    query_projection,
    key_value_projection,
    output_projection,
    adapter_qkv_down_store,
    adapter_query_up,
    adapter_key_value_up,
    adapter_output_down,
    adapter_output_up,
    crop_token_length,
    tenant_per_block,
    tenant_store_row,
):
    ctx_count = lax.axis_size("ctx")
    tp_count = lax.axis_size("tp")
    ctx_index = lax.axis_index("ctx")
    tp_index = lax.axis_index("tp")
    rows_dev = hidden_input.shape[0]
    out_cols = output_cotangent.shape[1]
    tenant_owner = adapter_qkv_down_store.shape[0]
    blocks_dev = rows_dev // BLK
    pair_bits = (tp_count // KEY_VALUE_HEADS).bit_length() - 1
    groups = hidden_input.shape[1] // out_cols
    crops = crop_token_length.shape[0]
    partners = range(1, ctx_count)

    first_rows = rows_dev // 2

    table, firsts, lates = serve(
        ctx_count,
        blocks_dev,
        crop_token_length,
        tenant_per_block,
        tenant_store_row,
        adapter_qkv_down_store.swapaxes(1, 2),
        adapter_query_up,
        adapter_key_value_up,
        adapter_output_up,
        adapter_output_down.swapaxes(1, 2),
    )
    table, cot_early = lax.optimization_barrier((table, output_cotangent))
    cot_first = lax.all_gather(cot_early[:first_rows], "tp", axis=0, tiled=False)
    firsts = [firsts[0]] + [swap(firsts[k], "ctx", k) for k in partners]
    my_pos = ctx_index * rows_dev + jnp.arange(rows_dev, dtype=jnp.int32)
    q_lin, kv_lin = dense_qkv(hidden_input, query_projection, key_value_projection)
    out_pick = pick_planes(table, output_projection, groups, 1)
    firsts, q_lin, kv_lin, tables, out_pick = lax.optimization_barrier(
        (firsts, q_lin, kv_lin, rope_tables(my_pos), out_pick)
    )
    cosine, sine = tables
    low_halves = low_part(table, hidden_input, firsts)
    low_halves, (kv_pick, query_pick) = sum_halves(
        *low_halves,
        beside=[
            lambda done: pick_planes(table, key_value_projection, groups, 0),
            lambda done: (done, pick_planes(table, query_projection, groups, 0)),
        ],
    )
    low_halves, cot_rest = lax.optimization_barrier((low_halves, output_cotangent[first_rows:]))
    cot_second = lax.all_gather(cot_rest, "tp", axis=0, tiled=False)
    kv_local, low_in = finish_kv(
        table, kv_lin, low_halves, firsts, cosine, sine, pair_bits == 0
    )
    if pair_bits:
        for bit_no in range(pair_bits):
            partner = swap(kv_local, "tp", 1 << bit_no)
            is_lower = tp_index // (1 << bit_no) % 2 == 0
            kv_local = jnp.where(
                is_lower,
                jnp.concatenate([kv_local, partner], axis=1),
                jnp.concatenate([partner, kv_local], axis=1),
            )
        key_rot = turn(kv_local[:, :HEAD_SIZE].astype(F32), cosine, sine).astype(BF16)
        kv_local = jnp.concatenate([key_rot, kv_local[:, HEAD_SIZE:]], axis=1)
    kvs = [kv_local] + [swap(kv_local, "ctx", k) for k in partners]
    query_rot = finish_q(table, q_lin, low_in, firsts, cosine, sine)
    kvs, lates, query_rot = lax.optimization_barrier((kvs, lates, query_rot))
    out_other, query_other, kv_other = (
        swap(pick, "tp", 1) for pick in (out_pick, query_pick, kv_pick)
    )
    lates = [lates[0]] + [swap(lates[k], "ctx", k) for k in partners]

    attn_out, log_norm = attention_forward(table, crops, query_rot, kvs)
    lates, attn_out = lax.optimization_barrier((lates, attn_out))
    heads_part = project_out(
        table, attn_out, swap(attn_out, "tp", 1), output_projection, out_other, groups
    )
    heads_part, attn_out, cot_first = lax.optimization_barrier((heads_part, attn_out, cot_first))
    heads_sum = reduce_planes(heads_part, groups)
    o_halves, grad_dense = sum_halves(
        *low_o_part(table, output_cotangent, attn_out, lates),
        beside=[
            lambda done: grad_attn(cot_first, cot_second, output_projection, 0),
            lambda done: grad_attn(cot_first, cot_second, output_projection, 1, done),
        ],
    )
    grad_q, kv_parts = attention_backward(
        table, crops, query_rot, grad_dense, o_halves, attn_out, log_norm, cosine, sine, kvs, lates
    )
    grad_q_other = swap(grad_q, "tp", 1)
    reduced = kv_parts[0].astype(F32)
    for k in partners:
        reduced = reduced + swap(kv_parts[k], "ctx", k).astype(F32)
    reduced = jnp.concatenate(
        [turn(reduced[:, :HEAD_SIZE], cosine, -sine), reduced[:, HEAD_SIZE:]], axis=1
    )
    for bit_no in reversed(range(pair_bits)):
        half_cols = reduced.shape[1] // 2
        is_lower = tp_index // (1 << bit_no) % 2 == 0
        keep_part = jnp.where(is_lower, reduced[:, :half_cols], reduced[:, half_cols:])
        send_part = jnp.where(is_lower, reduced[:, half_cols:], reduced[:, :half_cols])
        reduced = keep_part + swap(send_part.astype(BF16), "tp", 1 << bit_no).astype(F32)
    grad_kv = reduced.astype(BF16)

    input_part = grad_input(
        table,
        grad_q,
        grad_q_other,
        grad_kv,
        swap(grad_kv, "tp", 1),
        query_projection,
        query_other,
        key_value_projection,
        kv_other,
        groups,
    )
    input_part, grad_q, grad_kv = lax.optimization_barrier((input_part, grad_q, grad_kv))
    input_sum = reduce_planes(input_part, groups)

    def send_ups(done):
        return up_grads(
            table, ctx_count, low_in, grad_q, grad_kv, o_halves, output_cotangent, attn_out
        )

    g_halves, (up_sends, output) = sum_halves(
        *low_g_part(table, grad_q, grad_kv, firsts),
        beside=[send_ups, lambda done: (done, output_result(table, heads_sum, o_halves, lates))],
    )
    up_back = [up_sends[0]] + [swap(up_sends[k], "ctx", k) for k in partners]
    down_sends, input_delta = down_grads(table, hidden_input, g_halves, firsts)
    down_back = [down_sends[0]] + [swap(down_sends[k], "ctx", k) for k in partners]
    up_stores = store_ups(table, up_back, tenant_owner)
    down_back, up_stores = lax.optimization_barrier((down_back, up_stores))
    down_store = store_downs(table, down_back, tenant_owner)
    input_sum, input_delta, down_store = lax.optimization_barrier(
        (input_sum, input_delta, down_store)
    )
    hidden_input_gradient = (input_sum.astype(F32) + input_delta.astype(F32)).astype(BF16)
    return (
        output,
        hidden_input_gradient,
        down_store.swapaxes(1, 2),
        up_stores[0],
        up_stores[1],
        up_stores[2].swapaxes(1, 2),
        up_stores[3],
    )


def solution(mesh):
    in_specs = (
        P("ctx", None),
        P("ctx", "tp"),
        P(None, "tp"),
        P(None, "tp"),
        P("tp", None),
        P("ctx", "tp", None),
        P("ctx", None, "tp"),
        P("ctx", None, "tp"),
        P("ctx", "tp", None),
        P("ctx", None, "tp"),
        P(),
        P(),
        P(),
    )
    out_specs = (
        P("ctx", "tp"),
        P("ctx", "tp"),
        P("ctx", "tp", None),
        P("ctx", None, "tp"),
        P("ctx", None, "tp"),
        P("ctx", "tp", None),
        P("ctx", None, "tp"),
    )
    return jax.shard_map(body, mesh=mesh, in_specs=in_specs, out_specs=out_specs, check_vma=False)
```

```python
import functools
import math

import jax
import jax.numpy as jnp
from jax import lax
from jax.experimental import pallas as pl
from jax.experimental.pallas import tpu as pltpu
from jax.sharding import PartitionSpec as P

HEAD_SIZE = 128
KEY_VALUE_HEADS = 8
ADAPTER_RANK = 64
BLK = 128
NEG = -1e30
ROPE_BASE = 1000000.0
SCALE = HEAD_SIZE ** (-0.5)
VMEM_BYTES = 62 * 1024 * 1024
SMALL_VMEM_BYTES = 16 * 1024 * 1024

BF16 = jnp.bfloat16
F32 = jnp.float32


def params(limit=VMEM_BYTES):
    return pltpu.CompilerParams(vmem_limit_bytes=limit)


def cost(flops, bytes_accessed, transcendentals=0):
    return pl.CostEstimate(
        flops=int(flops), bytes_accessed=int(bytes_accessed), transcendentals=int(transcendentals)
    )


def dot_nn(a, b):
    return lax.dot_general(a, b, (((1,), (0,)), ((), ())), preferred_element_type=F32)


def dot_nt(a, b):
    return lax.dot_general(a, b, (((1,), (1,)), ((), ())), preferred_element_type=F32)


def dot_tn(a, b):
    return lax.dot_general(a, b, (((0,), (0,)), ((), ())), preferred_element_type=F32)


def swap(value, axis, mask):
    pairs = [(source, source ^ mask) for source in range(lax.axis_size(axis))]
    return lax.ppermute(value, axis, pairs)


def add_round(a, b):
    return (a.astype(F32) + b.astype(F32)).astype(BF16)


def rope_tables(positions):
    half_dim = HEAD_SIZE // 2
    exponent = jnp.arange(half_dim, dtype=F32) * (2.0 / HEAD_SIZE)
    frequency = jnp.exp(-exponent * math.log(ROPE_BASE))
    angles = positions.astype(F32)[:, None] * frequency[None, :]
    cosine, sine = jnp.cos(angles), jnp.sin(angles)
    return (
        jnp.concatenate([cosine, cosine], axis=1),
        jnp.concatenate([-sine, sine], axis=1),
    )


def turn(values, cosine, sine):
    return values * cosine + jnp.roll(values, HEAD_SIZE // 2, axis=1) * sine


def turn_kernel(values, cosine, sine):
    return values * cosine + pltpu.roll(values, HEAD_SIZE // 2, 1) * sine


def dense_kernel(x_ref, wq_ref, wkv_ref, q_ref, kv_ref):
    @pl.when(pl.program_id(0) == 0)
    def _():
        q_ref[...] = jnp.zeros_like(q_ref)
        kv_ref[...] = jnp.zeros_like(kv_ref)

    x = x_ref[...]
    q_ref[...] += dot_nn(x, wq_ref[...])
    kv_ref[...] += dot_nn(x, wkv_ref[...])


def dense_qkv(x, wq, wkv):
    rows, width = x.shape
    step = 2048
    cq, ckv = wq.shape[1], wkv.shape[1]
    return pl.pallas_call(
        dense_kernel,
        grid=(width // step,),
        in_specs=[
            pl.BlockSpec((rows, step), lambda i: (0, i)),
            pl.BlockSpec((step, cq), lambda i: (i, 0)),
            pl.BlockSpec((step, ckv), lambda i: (i, 0)),
        ],
        out_specs=[
            pl.BlockSpec((rows, cq), lambda i: (0, 0)),
            pl.BlockSpec((rows, ckv), lambda i: (0, 0)),
        ],
        out_shape=[
            jax.ShapeDtypeStruct((rows, cq), F32),
            jax.ShapeDtypeStruct((rows, ckv), F32),
        ],
        compiler_params=params(),
        cost_estimate=cost(2 * rows * width * (cq + ckv), 2 * width * (rows + cq + ckv)),
        name="dense_qkv",
    )(x, wq, wkv)


ENDS_AT = 2
SEND_AT = 16
SERVED_AT = 32
SOURCE_AT = 48
TABLE = 64


def serve_kernel(
    count, blocks, owned, crop_ref, tenant_ref, row_ref, cot, down, up_q, up_kv, up_o, down_o, *outs
):
    tab, cots = outs[0], outs[1:3]
    firsts, lates = outs[3 : 3 + count], outs[3 + count :]
    cots[0][...] = cot[: cots[0].shape[0], :]
    cots[1][...] = cot[cots[0].shape[0] :, :]
    me = lax.axis_index("ctx")
    for i in range(TABLE):
        tab[i] = 0
    tab[0] = me
    tab[1] = lax.axis_index("tp")
    end = jnp.int32(0)
    for i in range(crop_ref.shape[0]):
        end = end + crop_ref[i]
        tab[ENDS_AT + i] = end
    for b in range(blocks):
        row = row_ref[tenant_ref[me * blocks + b]]
        tab[SOURCE_AT + b] = (row // owned) ^ me
    for k in range(count):
        served = jnp.int32(-1)
        for b in range(blocks):
            row = row_ref[tenant_ref[(me ^ k) * blocks + b]]
            served = jnp.where(row // owned == me, row - me * owned, served)
        tab[SERVED_AT + k] = served
        tab[SEND_AT + k] = jnp.maximum(served, 0)
    rank, width = ADAPTER_RANK, down.shape[2]
    half, quarter = rank // 2, rank // 4
    cq, ckv = width // 2, width // 4
    for k in range(count):
        at = tab[SEND_AT + k]
        low = down.shape[1]
        firsts[k][:low, :] = down[at]
        for i in range(2):
            firsts[k][low : low + half, i * cq : (i + 1) * cq] = up_q[
                at, i * half : (i + 1) * half, :
            ]
            lates[k][rank : rank + half, i * cq : (i + 1) * cq] = down_o[
                at, i * half : (i + 1) * half, :
            ]
        for i in range(4):
            firsts[k][low + half :, i * ckv : (i + 1) * ckv] = up_kv[
                at, i * quarter : (i + 1) * quarter, :
            ]
        lates[k][:rank, :] = up_o[at]


def serve(count, blocks, crops, tenants, store_rows, cot, down, up_q, up_kv, up_o, down_o):
    rank, width = ADAPTER_RANK, down.shape[2]
    assert up_q.shape[2] * 2 == width and up_kv.shape[2] * 4 == width
    assert up_o.shape[2] == width and down_o.shape[2] * 2 == width
    smem = pl.BlockSpec(memory_space=pltpu.SMEM)
    vmem = pl.BlockSpec(memory_space=pltpu.VMEM)
    first = jax.ShapeDtypeStruct((3 * rank + rank // 2 + rank // 4, width), BF16)
    late = jax.ShapeDtypeStruct((rank + rank // 2, width), BF16)
    results = pl.pallas_call(
        functools.partial(serve_kernel, count, blocks, down.shape[0]),
        in_specs=[smem] * 3 + [vmem] * 6,
        out_specs=[smem] + [vmem] * (2 + 2 * count),
        out_shape=[jax.ShapeDtypeStruct((TABLE,), jnp.int32)]
        + [jax.ShapeDtypeStruct((cot.shape[0] // 2, cot.shape[1]), BF16)] * 2
        + [first] * count
        + [late] * count,
        compiler_params=params(SMALL_VMEM_BYTES),
        name="serve",
    )(crops, tenants, store_rows, cot, down, up_q, up_kv, up_o, down_o)
    return results[0], results[1:3], list(results[3 : 3 + count]), list(results[3 + count :])


def unpack_q(ref):
    rows, width = ref.shape
    value = ref[...]
    return jnp.concatenate([value[:, : width // 2], value[:, width // 2 :]], axis=0)


def unpack_kv(ref):
    rows, width = ref.shape
    value = ref[...]
    step = width // 4
    return jnp.concatenate([value[:, i * step : (i + 1) * step] for i in range(4)], axis=0)


def pick(tab_ref, block, count, step):
    for k in range(count):

        @pl.when(tab_ref[SOURCE_AT + block] == k)
        def _(k=k):
            step(k)


def split_rows(tab_ref, whole, mine, other):
    half = mine.shape[0]

    @pl.when(tab_ref[1] % 2 == 0)
    def _():
        mine[...] = whole[:half, :]
        other[...] = whole[half:, :]

    @pl.when(tab_ref[1] % 2 == 1)
    def _():
        mine[...] = whole[half:, :]
        other[...] = whole[:half, :]


def join_rows(tab_ref, mine, other, whole):
    half = mine.shape[0]

    @pl.when(tab_ref[1] % 2 == 0)
    def _():
        whole[:half, :] = mine[...]
        whole[half:, :] = other[...]

    @pl.when(tab_ref[1] % 2 == 1)
    def _():
        whole[:half, :] = other[...]
        whole[half:, :] = mine[...]


def sum_halves(mine, other, beside=()):
    total = add_round(mine, swap(other, "tp", 1))
    mask, done = 2, None
    beside = list(beside)
    while mask < lax.axis_size("tp"):
        arrived = swap(total, "tp", mask)
        if beside:
            done = beside.pop(0)(done)
            arrived, done = lax.optimization_barrier((arrived, done))
        total = add_round(total, arrived)
        mask *= 2
    while beside:
        done = beside.pop(0)(done)
    return (total, swap(total, "tp", 1)), done


def block_rows(b):
    return slice(b * BLK, (b + 1) * BLK)


def whole_spec(shape):
    return pl.BlockSpec(shape, lambda i, t: (0,) * len(shape))


def table_call(kernel, table, operands, shapes, scratch, name, flops=0):
    moved = sum(math.prod(s.shape) * s.dtype.itemsize for s in operands + shapes)
    vmem = pl.BlockSpec(memory_space=pltpu.VMEM)
    return pl.pallas_call(
        kernel,
        in_specs=[pl.BlockSpec(memory_space=pltpu.SMEM)] + [vmem] * len(operands),
        out_specs=[vmem] * len(shapes),
        out_shape=shapes,
        scratch_shapes=scratch,
        compiler_params=params(SMALL_VMEM_BYTES),
        cost_estimate=cost(flops, moved),
        name=name,
    )(table, *operands)


def low_kernel(count, tab_ref, x_ref, *refs):
    downs = refs[:count]
    mine, other, whole = refs[count:]
    cols = whole.shape[1]
    for b in range(whole.shape[0] // BLK):

        def step(k, b=b):
            whole[block_rows(b), :] = dot_nt(x_ref[block_rows(b), :], downs[k][:cols, :]).astype(BF16)

        pick(tab_ref, b, count, step)
    split_rows(tab_ref, whole, mine, other)


def low_part(table, x, firsts):
    rows, width, cols = x.shape[0], firsts[0].shape[1], 3 * ADAPTER_RANK
    half = jax.ShapeDtypeStruct((rows // 2, cols), BF16)
    return table_call(
        functools.partial(low_kernel, len(firsts)),
        table,
        [x] + firsts,
        [half, half],
        [pltpu.VMEM((rows, cols), BF16)],
        "low_part",
        2 * rows * width * cols,
    )


def finish_kv_kernel(count, rotate_keys, tab_ref, kv_ref, mine, other, cos_ref, sin_ref, *refs):
    ups = refs[:count]
    kvo, low = refs[count:]
    ckv = kv_ref.shape[1]
    rank = ADAPTER_RANK
    join_rows(tab_ref, mine, other, low)
    for b in range(kv_ref.shape[0] // BLK):

        def step(k, b=b):
            at_rows = block_rows(b)
            low_k = low[at_rows, rank : 2 * rank]
            low_v = low[at_rows, 2 * rank :]
            up_kv = unpack_kv(ups[k].at[3 * rank + rank // 2 :])
            for h in range(ckv // HEAD_SIZE):
                at = slice(h * HEAD_SIZE, (h + 1) * HEAD_SIZE)
                if rotate_keys:
                    term = dot_nn(low_v if h % 2 else low_k, up_kv[:, at])
                else:
                    is_value = (tab_ref[1] * (ckv // HEAD_SIZE) + h) % 2 == 1
                    term = jnp.where(
                        is_value, dot_nn(low_v, up_kv[:, at]), dot_nn(low_k, up_kv[:, at])
                    )
                piece = (kv_ref[at_rows, at] + term).astype(BF16)
                if rotate_keys and h % 2 == 0:
                    cosine, sine = cos_ref[at_rows, :], sin_ref[at_rows, :]
                    piece = turn_kernel(piece.astype(F32), cosine, sine).astype(BF16)
                kvo[at_rows, at] = piece

        pick(tab_ref, b, count, step)


def finish_kv(table, kv_lin, halves, firsts, cosine, sine, rotate_keys):
    rows, ckv = kv_lin.shape
    cols = 3 * ADAPTER_RANK
    operands = [kv_lin, *halves, cosine, sine]
    return table_call(
        functools.partial(finish_kv_kernel, len(firsts), rotate_keys),
        table,
        operands + firsts,
        [jax.ShapeDtypeStruct((rows, ckv), BF16), jax.ShapeDtypeStruct((rows, cols), BF16)],
        [],
        "finish_kv",
        4 * rows * ADAPTER_RANK * ckv,
    )


def finish_q_kernel(count, tab_ref, q_ref, low_ref, cos_ref, sin_ref, *refs):
    ups, qo = refs[:count], refs[count]
    cq = q_ref.shape[1]
    rank = ADAPTER_RANK
    for b in range(q_ref.shape[0] // BLK):

        def step(k, b=b):
            at_rows = block_rows(b)
            cosine, sine = cos_ref[at_rows, :], sin_ref[at_rows, :]
            up_q = unpack_q(ups[k].at[3 * rank : 3 * rank + rank // 2])
            query = q_ref[at_rows, :] + dot_nn(low_ref[at_rows, :rank], up_q)
            for h in range(cq // HEAD_SIZE):
                at = slice(h * HEAD_SIZE, (h + 1) * HEAD_SIZE)
                qo[at_rows, at] = turn_kernel(query[:, at], cosine, sine).astype(BF16)

        pick(tab_ref, b, count, step)


def finish_q(table, q_lin, low_in, firsts, cosine, sine):
    rows, cq = q_lin.shape
    operands = [q_lin, low_in, cosine, sine]
    return table_call(
        functools.partial(finish_q_kernel, len(firsts)),
        table,
        operands + firsts,
        [jax.ShapeDtypeStruct((rows, cq), BF16)],
        [],
        "finish_q",
        2 * rows * ADAPTER_RANK * cq,
    )[0]


def low_o_kernel(count, tab_ref, cot_ref, attn_ref, *refs):
    lates = refs[:count]
    mine, other, whole = refs[count:]
    rank = ADAPTER_RANK
    for b in range(whole.shape[0] // BLK):

        def step(k, b=b):
            at = block_rows(b)
            whole[at, :rank] = dot_nt(cot_ref[at, :], lates[k][:rank, :]).astype(BF16)
            down = unpack_q(lates[k].at[rank:])
            whole[at, rank:] = dot_nt(attn_ref[at, :], down).astype(BF16)

        pick(tab_ref, b, count, step)
    split_rows(tab_ref, whole, mine, other)


def low_o_part(table, cot, attn, lates):
    rows, width = cot.shape
    cols = 2 * ADAPTER_RANK
    half = jax.ShapeDtypeStruct((rows // 2, cols), BF16)
    return table_call(
        functools.partial(low_o_kernel, len(lates)),
        table,
        [cot, attn] + lates,
        [half, half],
        [pltpu.VMEM((rows, cols), BF16)],
        "low_o_part",
        2 * rows * cols * width,
    )


def low_g_kernel(count, tab_ref, gq_ref, gkv_ref, *refs):
    ups = refs[:count]
    mine, other, whole = refs[count:]
    rank = ADAPTER_RANK
    ckv = gkv_ref.shape[1]
    for b in range(whole.shape[0] // BLK):

        def step(k, b=b):
            at = block_rows(b)
            up_q = unpack_q(ups[k].at[3 * rank : 3 * rank + rank // 2])
            whole[at, :rank] = dot_nt(gq_ref[at, :], up_q).astype(BF16)
            up_kv = unpack_kv(ups[k].at[3 * rank + rank // 2 :])
            sums = [jnp.zeros((BLK, rank), F32)] * 2
            for h in range(ckv // HEAD_SIZE):
                cols = slice(h * HEAD_SIZE, (h + 1) * HEAD_SIZE)
                term = dot_nt(gkv_ref[at, cols], up_kv[:, cols])
                is_value = (tab_ref[1] * (ckv // HEAD_SIZE) + h) % 2 == 1
                sums[0] = sums[0] + jnp.where(is_value, 0.0, term)
                sums[1] = sums[1] + jnp.where(is_value, term, 0.0)
            whole[at, rank : 2 * rank] = sums[0].astype(BF16)
            whole[at, 2 * rank :] = sums[1].astype(BF16)

        pick(tab_ref, b, count, step)
    split_rows(tab_ref, whole, mine, other)


def low_g_part(table, gq, gkv, firsts):
    rows = gq.shape[0]
    cols, width = 3 * ADAPTER_RANK, firsts[0].shape[1]
    half = jax.ShapeDtypeStruct((rows // 2, cols), BF16)
    return table_call(
        functools.partial(low_g_kernel, len(firsts)),
        table,
        [gq, gkv] + firsts,
        [half, half],
        [pltpu.VMEM((rows, cols), BF16)],
        "low_g_part",
        2 * rows * width * ADAPTER_RANK,
    )


def zero_unused(tab_ref, blocks, sends):
    for k in range(len(sends)):
        used = tab_ref[SOURCE_AT] == k
        for b in range(1, blocks):
            used = used | (tab_ref[SOURCE_AT + b] == k)

        @pl.when(jnp.logical_not(used))
        def _(k=k):
            sends[k][...] = jnp.zeros_like(sends[k])


def up_grads_kernel(
    count, tab_ref, low_ref, gq_ref, gkv_ref, o_mine, o_other, cot, attn, *refs
):
    sends, low_o = refs[:count], refs[count]
    rank = ADAPTER_RANK
    join_rows(tab_ref, o_mine, o_other, low_o)
    blocks = low_o.shape[0] // BLK
    cq, ckv = gq_ref.shape[1], gkv_ref.shape[1]
    half, quarter = rank // 2, rank // 4
    late = half + quarter
    zero_unused(tab_ref, blocks, sends)
    for b in range(blocks):

        def step(k, b=b):
            at = block_rows(b)
            out = sends[k]
            up_q = dot_tn(low_ref[at, :rank], gq_ref[at, :]).astype(BF16)
            down_o = dot_tn(low_o[at, :rank], attn[at, :]).astype(BF16)
            for i in range(2):
                rows = slice(i * half, (i + 1) * half)
                cols = slice(i * cq, (i + 1) * cq)
                out[:half, cols] = up_q[rows, :]
                out[late + rank :, cols] = down_o[rows, :]
            for h in range(ckv // HEAD_SIZE):
                piece = slice(h * HEAD_SIZE, (h + 1) * HEAD_SIZE)
                is_value = (tab_ref[1] * (ckv // HEAD_SIZE) + h) % 2 == 1
                up_kv = jnp.where(
                    is_value,
                    dot_tn(low_ref[at, 2 * rank :], gkv_ref[at, piece]),
                    dot_tn(low_ref[at, rank : 2 * rank], gkv_ref[at, piece]),
                ).astype(BF16)
                for i in range(4):
                    cols = slice(i * ckv + h * HEAD_SIZE, i * ckv + (h + 1) * HEAD_SIZE)
                    out[half:late, cols] = up_kv[i * quarter : (i + 1) * quarter, :]
            out[late : late + rank, :] = dot_tn(low_o[at, rank:], cot[at, :]).astype(BF16)

        pick(tab_ref, b, count, step)


def up_grads(table, count, low_in, gq, gkv, o_halves, cot, attn):
    rows, width = cot.shape
    rank = ADAPTER_RANK
    operands = [low_in, gq, gkv, *o_halves, cot, attn]
    return list(
        table_call(
            functools.partial(up_grads_kernel, count),
            table,
            operands,
            [jax.ShapeDtypeStruct((2 * rank + rank // 4, width), BF16)] * count,
            [pltpu.VMEM((rows, 2 * rank), BF16)],
            "up_grads",
            2 * rows * width * 3 * rank,
        )
    )


def down_grads_kernel(count, tab_ref, x_ref, mine, other, *refs):
    downs, sends = refs[:count], refs[count : 2 * count]
    delta, low = refs[2 * count :]
    join_rows(tab_ref, mine, other, low)
    blocks = low.shape[0] // BLK
    zero_unused(tab_ref, blocks, sends)
    for b in range(blocks):

        def step(k, b=b):
            at = block_rows(b)
            sends[k][...] = dot_tn(low[at, :], x_ref[at, :]).astype(BF16)
            delta[at, :] = dot_nn(low[at, :], downs[k][: low.shape[1], :]).astype(BF16)

        pick(tab_ref, b, count, step)


def down_grads(table, x, halves, firsts):
    rows, cols = x.shape[0], 3 * ADAPTER_RANK
    width, count = firsts[0].shape[1], len(firsts)
    results = table_call(
        functools.partial(down_grads_kernel, count),
        table,
        [x, *halves] + firsts,
        [jax.ShapeDtypeStruct((cols, width), BF16)] * count
        + [jax.ShapeDtypeStruct((rows, width), BF16)],
        [pltpu.VMEM((rows, cols), BF16)],
        "down_grads",
        4 * rows * width * cols,
    )
    return list(results[:count]), results[count]


def store_kernel(count, pieces, tab_ref, *refs):
    arrived, outs = refs[:count], refs[count:]
    row = pl.program_id(0)
    for o in outs:
        o[...] = jnp.zeros_like(o)
    for k in range(count):

        @pl.when(tab_ref[SERVED_AT + k] == row)
        def _(k=k):
            for o, piece in zip(outs, pieces):
                o[0] += piece(arrived[k]).astype(F32)


def store_sums(table, arrived, owned, pieces, sizes):
    shapes = [jax.ShapeDtypeStruct((owned,) + size, F32) for size in sizes]
    return pl.pallas_call(
        functools.partial(store_kernel, len(arrived), pieces),
        grid_spec=pltpu.PrefetchScalarGridSpec(
            num_scalar_prefetch=1,
            grid=(owned,),
            in_specs=[pl.BlockSpec(a.shape, lambda i, t: (0, 0)) for a in arrived],
            out_specs=[pl.BlockSpec((1,) + s.shape[1:], lambda i, t: (i, 0, 0)) for s in shapes],
        ),
        out_shape=shapes,
        compiler_params=params(),
        name="store_sums",
    )(table, *arrived)


def store_ups(table, arrived, owned):
    rank, width = ADAPTER_RANK, arrived[0].shape[1]
    half, late = rank // 2, rank // 2 + rank // 4
    pieces = [
        lambda a: unpack_q(a.at[:half]),
        lambda a: unpack_kv(a.at[half:late]),
        lambda a: unpack_q(a.at[late + rank :]),
        lambda a: a[late : late + rank, :],
    ]
    sizes = [(rank, width // 2), (rank, width // 4), (rank, width // 2), (rank, width)]
    return store_sums(table, arrived, owned, pieces, sizes)


def store_downs(table, arrived, owned):
    return store_sums(table, arrived, owned, [lambda a: a[...]], [arrived[0].shape])[0]


def output_kernel(count, tab_ref, sum_ref, mine, other, *refs):
    lates = refs[:count]
    out, low = refs[count:]
    rank = ADAPTER_RANK
    join_rows(tab_ref, mine, other, low)
    for b in range(out.shape[0] // BLK):

        def step(k, b=b):
            at = block_rows(b)
            term = dot_nn(low[at, rank:], lates[k][:rank, :])
            out[at, :] = (sum_ref[at, :].astype(F32) + term).astype(BF16)

        pick(tab_ref, b, count, step)


def output_result(table, total, halves, lates):
    rows, width = total.shape
    rank = ADAPTER_RANK
    return table_call(
        functools.partial(output_kernel, len(lates)),
        table,
        [total, *halves] + lates,
        [jax.ShapeDtypeStruct((rows, width), BF16)],
        [pltpu.VMEM((rows, 2 * rank), BF16)],
        "output_result",
        2 * rows * rank * width,
    )[0]


def crop_start(tab_ref, crops, positions):
    start = jnp.zeros_like(positions)
    for i in range(crops):
        end = tab_ref[ENDS_AT + i]
        start = jnp.where(positions >= end, end, start)
    return start


def masked(scores, first, own, base):
    rows, cols = scores.shape
    key_pos = base + lax.broadcasted_iota(jnp.int32, (rows, cols), 0)
    allowed = key_pos >= first
    if own:
        allowed &= key_pos <= base + lax.broadcasted_iota(jnp.int32, (rows, cols), 1)
    return jnp.where(allowed, scores, NEG)


def chunk_on(tab_ref, crops, k, rows):
    me = tab_ref[0]
    chunk = me ^ k
    return (chunk <= me) & ((chunk + 1) * rows > crop_start(tab_ref, crops, me * rows))


def query_starts(tab_ref, crops, rows):
    positions = tab_ref[0] * rows + lax.broadcasted_iota(jnp.int32, (1, rows), 1)
    return crop_start(tab_ref, crops, positions)


def forward_kernel(heads, count, crops, tab_ref, q_ref, *refs):
    kv_refs = refs[:count]
    out_ref, norm_ref, acc, top, total = refs[count:]
    rows = q_ref.shape[0]
    first = query_starts(tab_ref, crops, rows)
    for k in range(count):

        def chunk_step(k=k):
            base = (tab_ref[0] ^ k) * rows
            keys = kv_refs[k][:, :HEAD_SIZE]
            values = kv_refs[k][:, HEAD_SIZE:]
            for h in range(heads):
                at = slice(h * HEAD_SIZE, (h + 1) * HEAD_SIZE)
                scores = masked(dot_nt(keys, q_ref[:, at]), first, k == 0, base)
                here = jnp.max(scores, axis=0, keepdims=True)
                if k == 0:
                    new_top = here
                else:
                    old_top = top[h : h + 1, :]
                    new_top = jnp.maximum(old_top, here)
                weights = jnp.exp((scores - new_top) * SCALE)
                here_sum = jnp.sum(weights, axis=0, keepdims=True)
                here_out = dot_tn(values, weights.astype(BF16))
                if k == 0:
                    total[h : h + 1, :] = here_sum
                    acc[h] = here_out
                else:
                    decay = jnp.exp((old_top - new_top) * SCALE)
                    total[h : h + 1, :] = total[h : h + 1, :] * decay + here_sum
                    acc[h] = acc[h] * decay + here_out
                top[h : h + 1, :] = new_top

        if k == 0:
            chunk_step()
        else:
            pl.when(chunk_on(tab_ref, crops, k, rows))(chunk_step)
    for h in range(heads):
        at = slice(h * HEAD_SIZE, (h + 1) * HEAD_SIZE)
        out_ref[:, at] = jnp.transpose(acc[h] / total[h : h + 1, :]).astype(BF16)
    norm_ref[...] = top[...] * SCALE + jnp.log(total[...])


def attention_forward(table, crops, query, kvs):
    rows, cols = query.shape
    heads = cols // HEAD_SIZE
    count = len(kvs)
    smem = pl.BlockSpec(memory_space=pltpu.SMEM)
    vmem = pl.BlockSpec(memory_space=pltpu.VMEM)
    work = heads * rows * rows * count
    return pl.pallas_call(
        functools.partial(forward_kernel, heads, count, crops),
        in_specs=[smem] + [vmem] * (1 + count),
        out_specs=[vmem] * 2,
        out_shape=[
            jax.ShapeDtypeStruct((rows, cols), BF16),
            jax.ShapeDtypeStruct((heads, rows), F32),
        ],
        scratch_shapes=[
            pltpu.VMEM((heads, HEAD_SIZE, rows), F32),
            pltpu.VMEM((heads, rows), F32),
            pltpu.VMEM((heads, rows), F32),
        ],
        compiler_params=params(),
        cost_estimate=cost(4 * work * HEAD_SIZE, 4 * rows * cols * count, work),
        name="attention_forward",
    )(table, query, *kvs)


def backward_kernel(
    heads,
    count,
    crops,
    tab_ref,
    q_ref,
    dense_ref,
    mine,
    other,
    out_ref,
    norm_ref,
    cos_ref,
    sin_ref,
    *refs,
):
    kv_refs, lates = refs[:count], refs[count : 2 * count]
    gq_ref = refs[2 * count]
    gkv_refs = refs[2 * count + 1 : 3 * count + 1]
    acc, delta, low, grad_ref = refs[3 * count + 1 :]
    rows = q_ref.shape[0]
    rank = ADAPTER_RANK
    first = query_starts(tab_ref, crops, rows)
    join_rows(tab_ref, mine, other, low)
    for b in range(rows // BLK):

        def add(k, b=b):
            at = block_rows(b)
            term = dot_nn(low[at, :rank], unpack_q(lates[k].at[rank:]))
            grad_ref[at, :] = (dense_ref[at, :] + term).astype(BF16)

        pick(tab_ref, b, count, add)
    for h in range(heads):
        at = slice(h * HEAD_SIZE, (h + 1) * HEAD_SIZE)
        product = grad_ref[:, at].astype(F32) * out_ref[:, at].astype(F32)
        delta[h : h + 1, :] = jnp.sum(jnp.transpose(product), axis=0, keepdims=True)
    for k in range(count):

        def chunk_step(k=k):
            base = (tab_ref[0] ^ k) * rows
            keys = kv_refs[k][:, :HEAD_SIZE]
            values = kv_refs[k][:, HEAD_SIZE:]
            key_grad = jnp.zeros((rows, HEAD_SIZE), F32)
            value_grad = jnp.zeros((rows, HEAD_SIZE), F32)
            for h in range(heads):
                at = slice(h * HEAD_SIZE, (h + 1) * HEAD_SIZE)
                scores = masked(dot_nt(keys, q_ref[:, at]), first, k == 0, base)
                weights = jnp.exp(scores * SCALE - norm_ref[h : h + 1, :])
                value_grad += dot_nn(weights.astype(BF16), grad_ref[:, at])
                grad_weights = dot_nt(values, grad_ref[:, at])
                grad_scores = (weights * (grad_weights - delta[h : h + 1, :])).astype(BF16)
                key_grad += dot_nn(grad_scores, q_ref[:, at])
                here = dot_tn(keys, grad_scores)
                if k == 0:
                    acc[h] = here
                else:
                    acc[h] += here
            gkv_refs[k][:, :HEAD_SIZE] = (key_grad * SCALE).astype(BF16)
            gkv_refs[k][:, HEAD_SIZE:] = value_grad.astype(BF16)

        if k == 0:
            chunk_step()
        else:
            on = chunk_on(tab_ref, crops, k, rows)
            pl.when(on)(chunk_step)

            @pl.when(jnp.logical_not(on))
            def _(k=k):
                gkv_refs[k][...] = jnp.zeros_like(gkv_refs[k])

    for h in range(heads):
        at = slice(h * HEAD_SIZE, (h + 1) * HEAD_SIZE)
        grad = jnp.transpose(acc[h]) * SCALE
        gq_ref[:, at] = turn_kernel(grad, cos_ref[...], -sin_ref[...]).astype(BF16)


def attention_backward(table, crops, query, dense, halves, out, norm, cosine, sine, kvs, lates):
    rows, cols = query.shape
    heads = cols // HEAD_SIZE
    count = len(kvs)
    smem = pl.BlockSpec(memory_space=pltpu.SMEM)
    vmem = pl.BlockSpec(memory_space=pltpu.VMEM)
    work = heads * rows * rows * count
    results = pl.pallas_call(
        functools.partial(backward_kernel, heads, count, crops),
        in_specs=[smem] + [vmem] * (8 + 2 * count),
        out_specs=[vmem] * (1 + count),
        out_shape=[jax.ShapeDtypeStruct((rows, cols), BF16)]
        + [jax.ShapeDtypeStruct((rows, 2 * HEAD_SIZE), BF16)] * count,
        scratch_shapes=[
            pltpu.VMEM((heads, HEAD_SIZE, rows), F32),
            pltpu.VMEM((heads, rows), F32),
            pltpu.VMEM((rows, 2 * ADAPTER_RANK), BF16),
            pltpu.VMEM((rows, cols), BF16),
        ],
        compiler_params=params(),
        cost_estimate=cost(10 * work * HEAD_SIZE, 8 * rows * cols * count, work),
        name="attention_backward",
    )(table, query, dense, *halves, out, norm, cosine, sine, *kvs, *lates)
    return results[0], list(results[1:])


def plane_spec(shape, axis, other):
    def index(i, t):
        core = t[1] % 2
        at = 2 * i + (1 - core if other else core)
        return (0, at) if axis else (at, 0)

    return pl.BlockSpec(shape, index)


def pick_kernel(tab_ref, w_ref, o_ref):
    o_ref[...] = w_ref[...]


def pick_planes(table, weight, groups, axis):
    planes = groups // 2
    shape = list(weight.shape)
    shape[axis] //= groups
    result = list(weight.shape)
    result[axis] //= 2
    return pl.pallas_call(
        pick_kernel,
        grid_spec=pltpu.PrefetchScalarGridSpec(
            num_scalar_prefetch=1,
            grid=(planes,),
            in_specs=[plane_spec(tuple(shape), axis, True)],
            out_specs=pl.BlockSpec(
                tuple(shape), (lambda i, t: (0, i)) if axis else (lambda i, t: (i, 0))
            ),
        ),
        out_shape=jax.ShapeDtypeStruct(tuple(result), BF16),
        compiler_params=params(),
        cost_estimate=cost(0, 2 * math.prod(weight.shape)),
        name="pick_planes",
    )(table, weight)


def reduce_planes(parts, groups):
    lines = [list(range(core, groups, 2)) for core in range(2)]
    return lax.psum_scatter(parts, "tp", scatter_dimension=0, axis_index_groups=lines, tiled=False)


def project_kernel(tab_ref, a_ref, ao_ref, w_ref, wo_ref, o_ref):
    total = dot_nn(a_ref[...], w_ref[...]) + dot_nn(ao_ref[...], wo_ref[...])
    o_ref[0] = total.astype(BF16)


def project_out(table, attn, attn_other, weight, weight_other, groups):
    rows, depth = attn.shape
    cols = weight.shape[1] // groups
    planes = groups // 2
    return pl.pallas_call(
        project_kernel,
        grid_spec=pltpu.PrefetchScalarGridSpec(
            num_scalar_prefetch=1,
            grid=(planes,),
            in_specs=[
                whole_spec(attn.shape),
                whole_spec(attn.shape),
                plane_spec((depth, cols), 1, False),
                pl.BlockSpec((depth, cols), lambda i, t: (0, i)),
            ],
            out_specs=pl.BlockSpec((1, rows, cols), lambda i, t: (i, 0, 0)),
        ),
        out_shape=jax.ShapeDtypeStruct((planes, rows, cols), BF16),
        compiler_params=params(),
        cost_estimate=cost(
            2 * rows * depth * cols * groups, 2 * (rows + 2 * depth) * cols * planes
        ),
        name="project_out",
    )(table, attn, attn_other, weight, weight_other)


PER_STEP = 2


def grad_attn_kernel(c0_ref, c1_ref, w_ref, *refs):
    before, o_ref = refs[:-1], refs[-1]
    step = pl.program_id(0)
    per_step, first_rows, cols = c0_ref.shape
    parts = ((c0_ref, slice(0, first_rows)), (c1_ref, slice(first_rows, o_ref.shape[0])))
    for c_ref, at in parts:
        total = dot_nt(c_ref[0], w_ref[:, :cols])
        for i in range(1, per_step):
            total += dot_nt(c_ref[i], w_ref[:, i * cols : (i + 1) * cols])

        @pl.when(step == 0)
        def _(at=at, total=total):
            o_ref[at, :] = total + before[0][at, :] if before else total

        @pl.when(step > 0)
        def _(at=at, total=total):
            o_ref[at, :] += total


def grad_attn(cot_first, cot_second, weight, half, before=None):
    groups, first_rows, cols = cot_first.shape
    depth = weight.shape[0]
    rows = first_rows + cot_second.shape[1]
    steps = groups // PER_STEP // 2
    start = half * steps
    whole = pl.BlockSpec((rows, depth), lambda i: (0, 0))
    return pl.pallas_call(
        grad_attn_kernel,
        grid=(steps,),
        in_specs=[
            pl.BlockSpec((PER_STEP, first_rows, cols), lambda i: (start + i, 0, 0)),
            pl.BlockSpec((PER_STEP, rows - first_rows, cols), lambda i: (start + i, 0, 0)),
            pl.BlockSpec((depth, PER_STEP * cols), lambda i: (0, start + i)),
        ]
        + ([] if before is None else [whole]),
        out_specs=whole,
        out_shape=jax.ShapeDtypeStruct((rows, depth), F32),
        compiler_params=params(),
        cost_estimate=cost(rows * depth * cols * groups, (rows + depth) * cols * groups),
        name="grad_attn",
    )(cot_first, cot_second, weight, *([] if before is None else [before]))


def grad_input_kernel(tab_ref, gq, gqo, gkv, gkvo, wq, wqo, wkv, wkvo, o_ref):
    total = dot_nt(gq[...], wq[...]) + dot_nt(gqo[...], wqo[...])
    total = total + dot_nt(gkv[...], wkv[...]) + dot_nt(gkvo[...], wkvo[...])
    o_ref[0] = total.astype(BF16)


def grad_input(table, gq, gq_other, gkv, gkv_other, wq, wq_other, wkv, wkv_other, groups):
    rows, cq = gq.shape
    ckv = gkv.shape[1]
    cols = wq.shape[0] // groups
    planes = groups // 2
    return pl.pallas_call(
        grad_input_kernel,
        grid_spec=pltpu.PrefetchScalarGridSpec(
            num_scalar_prefetch=1,
            grid=(planes,),
            in_specs=[
                whole_spec(gq.shape),
                whole_spec(gq.shape),
                whole_spec(gkv.shape),
                whole_spec(gkv.shape),
                plane_spec((cols, cq), 0, False),
                pl.BlockSpec((cols, cq), lambda i, t: (i, 0)),
                plane_spec((cols, ckv), 0, False),
                pl.BlockSpec((cols, ckv), lambda i, t: (i, 0)),
            ],
            out_specs=pl.BlockSpec((1, rows, cols), lambda i, t: (i, 0, 0)),
        ),
        out_shape=jax.ShapeDtypeStruct((planes, rows, cols), BF16),
        compiler_params=params(),
        cost_estimate=cost(
            2 * rows * (cq + ckv) * cols * groups,
            2 * (rows + 2 * (cq + ckv)) * cols * planes,
        ),
        name="grad_input",
    )(table, gq, gq_other, gkv, gkv_other, wq, wq_other, wkv, wkv_other)


def body(
    hidden_input,
    output_cotangent,
    query_projection,
    key_value_projection,
    output_projection,
    adapter_qkv_down_store,
    adapter_query_up,
    adapter_key_value_up,
    adapter_output_down,
    adapter_output_up,
    crop_token_length,
    tenant_per_block,
    tenant_store_row,
):
    ctx_count = lax.axis_size("ctx")
    tp_count = lax.axis_size("tp")
    ctx_index = lax.axis_index("ctx")
    tp_index = lax.axis_index("tp")
    rows_dev = hidden_input.shape[0]
    out_cols = output_cotangent.shape[1]
    tenant_owner = adapter_qkv_down_store.shape[0]
    blocks_dev = rows_dev // BLK
    pair_bits = (tp_count // KEY_VALUE_HEADS).bit_length() - 1
    groups = hidden_input.shape[1] // out_cols
    crops = crop_token_length.shape[0]
    partners = range(1, ctx_count)

    x_slice = lax.dynamic_slice_in_dim(hidden_input, tp_index * out_cols, out_cols, 1)

    table, cots, firsts, lates = serve(
        ctx_count,
        blocks_dev,
        crop_token_length,
        tenant_per_block,
        tenant_store_row,
        output_cotangent,
        adapter_qkv_down_store.swapaxes(1, 2),
        adapter_query_up,
        adapter_key_value_up,
        adapter_output_up,
        adapter_output_down.swapaxes(1, 2),
    )
    cot_first = lax.all_gather(cots[0], "tp", axis=0, tiled=False)
    firsts = [firsts[0]] + [swap(firsts[k], "ctx", k) for k in partners]
    my_pos = ctx_index * rows_dev + jnp.arange(rows_dev, dtype=jnp.int32)
    q_lin, kv_lin = dense_qkv(hidden_input, query_projection, key_value_projection)
    out_pick = pick_planes(table, output_projection, groups, 1)
    firsts, q_lin, kv_lin, tables, out_pick, x_slice = lax.optimization_barrier(
        (firsts, q_lin, kv_lin, rope_tables(my_pos), out_pick, x_slice)
    )
    cosine, sine = tables
    low_halves = low_part(table, x_slice, firsts)
    low_halves, (kv_pick, query_pick) = sum_halves(
        *low_halves,
        beside=[
            lambda done: pick_planes(table, key_value_projection, groups, 0),
            lambda done: (done, pick_planes(table, query_projection, groups, 0)),
        ],
    )
    low_halves, cot_rest = lax.optimization_barrier((low_halves, cots[1]))
    cot_second = lax.all_gather(cot_rest, "tp", axis=0, tiled=False)
    kv_local, low_in = finish_kv(
        table, kv_lin, low_halves, firsts, cosine, sine, pair_bits == 0
    )
    if pair_bits:
        for bit_no in range(pair_bits):
            partner = swap(kv_local, "tp", 1 << bit_no)
            is_lower = tp_index // (1 << bit_no) % 2 == 0
            kv_local = jnp.where(
                is_lower,
                jnp.concatenate([kv_local, partner], axis=1),
                jnp.concatenate([partner, kv_local], axis=1),
            )
        key_rot = turn(kv_local[:, :HEAD_SIZE].astype(F32), cosine, sine).astype(BF16)
        kv_local = jnp.concatenate([key_rot, kv_local[:, HEAD_SIZE:]], axis=1)
    kvs = [kv_local] + [swap(kv_local, "ctx", k) for k in partners]
    query_rot = finish_q(table, q_lin, low_in, firsts, cosine, sine)
    kvs, lates, query_rot = lax.optimization_barrier((kvs, lates, query_rot))
    out_other, query_other, kv_other = (
        swap(pick, "tp", 1) for pick in (out_pick, query_pick, kv_pick)
    )
    lates = [lates[0]] + [swap(lates[k], "ctx", k) for k in partners]

    attn_out, log_norm = attention_forward(table, crops, query_rot, kvs)
    lates, attn_out = lax.optimization_barrier((lates, attn_out))
    heads_part = project_out(
        table, attn_out, swap(attn_out, "tp", 1), output_projection, out_other, groups
    )
    heads_part, attn_out, cot_first = lax.optimization_barrier((heads_part, attn_out, cot_first))
    heads_sum = reduce_planes(heads_part, groups)
    o_halves, grad_dense = sum_halves(
        *low_o_part(table, output_cotangent, attn_out, lates),
        beside=[
            lambda done: grad_attn(cot_first, cot_second, output_projection, 0),
            lambda done: grad_attn(cot_first, cot_second, output_projection, 1, done),
        ],
    )
    grad_q, kv_parts = attention_backward(
        table, crops, query_rot, grad_dense, o_halves, attn_out, log_norm, cosine, sine, kvs, lates
    )
    grad_q_other = swap(grad_q, "tp", 1)
    reduced = kv_parts[0].astype(F32)
    for k in partners:
        reduced = reduced + swap(kv_parts[k], "ctx", k).astype(F32)
    reduced = jnp.concatenate(
        [turn(reduced[:, :HEAD_SIZE], cosine, -sine), reduced[:, HEAD_SIZE:]], axis=1
    )
    for bit_no in reversed(range(pair_bits)):
        half_cols = reduced.shape[1] // 2
        is_lower = tp_index // (1 << bit_no) % 2 == 0
        keep_part = jnp.where(is_lower, reduced[:, :half_cols], reduced[:, half_cols:])
        send_part = jnp.where(is_lower, reduced[:, half_cols:], reduced[:, :half_cols])
        reduced = keep_part + swap(send_part.astype(BF16), "tp", 1 << bit_no).astype(F32)
    grad_kv = reduced.astype(BF16)

    input_part = grad_input(
        table,
        grad_q,
        grad_q_other,
        grad_kv,
        swap(grad_kv, "tp", 1),
        query_projection,
        query_other,
        key_value_projection,
        kv_other,
        groups,
    )
    input_part, grad_q, grad_kv = lax.optimization_barrier((input_part, grad_q, grad_kv))
    input_sum = reduce_planes(input_part, groups)

    def send_ups(done):
        return up_grads(
            table, ctx_count, low_in, grad_q, grad_kv, o_halves, output_cotangent, attn_out
        )

    g_halves, up_sends = sum_halves(
        *low_g_part(table, grad_q, grad_kv, firsts), beside=[send_ups]
    )
    up_back = [up_sends[0]] + [swap(up_sends[k], "ctx", k) for k in partners]
    output = output_result(table, heads_sum, o_halves, lates)
    g_halves, up_back, output = lax.optimization_barrier((g_halves, up_back, output))
    down_sends, input_delta = down_grads(table, x_slice, g_halves, firsts)
    down_back = [down_sends[0]] + [swap(down_sends[k], "ctx", k) for k in partners]
    up_stores = store_ups(table, up_back, tenant_owner)
    down_back, up_stores = lax.optimization_barrier((down_back, up_stores))
    down_store = store_downs(table, down_back, tenant_owner)
    input_sum, input_delta, down_store = lax.optimization_barrier(
        (input_sum, input_delta, down_store)
    )
    hidden_input_gradient = (input_sum.astype(F32) + input_delta.astype(F32)).astype(BF16)
    return (
        output,
        hidden_input_gradient,
        down_store.swapaxes(1, 2),
        up_stores[0],
        up_stores[1],
        up_stores[2].swapaxes(1, 2),
        up_stores[3],
    )


def solution(mesh):
    in_specs = (
        P("ctx", None),
        P("ctx", "tp"),
        P(None, "tp"),
        P(None, "tp"),
        P("tp", None),
        P("ctx", "tp", None),
        P("ctx", None, "tp"),
        P("ctx", None, "tp"),
        P("ctx", "tp", None),
        P("ctx", None, "tp"),
        P(),
        P(),
        P(),
    )
    out_specs = (
        P("ctx", "tp"),
        P("ctx", "tp"),
        P("ctx", "tp", None),
        P("ctx", None, "tp"),
        P("ctx", None, "tp"),
        P("ctx", "tp", None),
        P("ctx", None, "tp"),
    )
    return jax.shard_map(body, mesh=mesh, in_specs=in_specs, out_specs=out_specs, check_vma=False)
```

```python
import functools
import math

import jax
import jax.numpy as jnp
from jax import lax
from jax.experimental import pallas as pl
from jax.experimental.pallas import tpu as pltpu
from jax.sharding import PartitionSpec as P

HEAD_SIZE = 128
KEY_VALUE_HEADS = 8
ADAPTER_RANK = 64
BLK = 128
NEG = -1e30
ROPE_BASE = 1000000.0
SCALE = HEAD_SIZE ** (-0.5)
VMEM_BYTES = 62 * 1024 * 1024
SMALL_VMEM_BYTES = 16 * 1024 * 1024

BF16 = jnp.bfloat16
F32 = jnp.float32


def params(limit=VMEM_BYTES):
    return pltpu.CompilerParams(vmem_limit_bytes=limit)


def cost(flops, bytes_accessed, transcendentals=0):
    return pl.CostEstimate(
        flops=int(flops), bytes_accessed=int(bytes_accessed), transcendentals=int(transcendentals)
    )


def dot_nn(a, b):
    return lax.dot_general(a, b, (((1,), (0,)), ((), ())), preferred_element_type=F32)


def dot_nt(a, b):
    return lax.dot_general(a, b, (((1,), (1,)), ((), ())), preferred_element_type=F32)


def dot_tn(a, b):
    return lax.dot_general(a, b, (((0,), (0,)), ((), ())), preferred_element_type=F32)


def swap(value, axis, mask):
    pairs = [(source, source ^ mask) for source in range(lax.axis_size(axis))]
    return lax.ppermute(value, axis, pairs)


def add_round(a, b):
    return (a.astype(F32) + b.astype(F32)).astype(BF16)


def rope_tables(positions):
    half_dim = HEAD_SIZE // 2
    exponent = jnp.arange(half_dim, dtype=F32) * (2.0 / HEAD_SIZE)
    frequency = jnp.exp(-exponent * math.log(ROPE_BASE))
    angles = positions.astype(F32)[:, None] * frequency[None, :]
    cosine, sine = jnp.cos(angles), jnp.sin(angles)
    return (
        jnp.concatenate([cosine, cosine], axis=1),
        jnp.concatenate([-sine, sine], axis=1),
    )


def turn(values, cosine, sine):
    return values * cosine + jnp.roll(values, HEAD_SIZE // 2, axis=1) * sine


def turn_kernel(values, cosine, sine):
    return values * cosine + pltpu.roll(values, HEAD_SIZE // 2, 1) * sine


def dense_kernel(x_ref, wq_ref, wkv_ref, q_ref, kv_ref):
    @pl.when(pl.program_id(0) == 0)
    def _():
        q_ref[...] = jnp.zeros_like(q_ref)
        kv_ref[...] = jnp.zeros_like(kv_ref)

    x = x_ref[...]
    q_ref[...] += dot_nn(x, wq_ref[...])
    kv_ref[...] += dot_nn(x, wkv_ref[...])


def dense_qkv(x, wq, wkv):
    rows, width = x.shape
    step = 2048
    cq, ckv = wq.shape[1], wkv.shape[1]
    return pl.pallas_call(
        dense_kernel,
        grid=(width // step,),
        in_specs=[
            pl.BlockSpec((rows, step), lambda i: (0, i)),
            pl.BlockSpec((step, cq), lambda i: (i, 0)),
            pl.BlockSpec((step, ckv), lambda i: (i, 0)),
        ],
        out_specs=[
            pl.BlockSpec((rows, cq), lambda i: (0, 0)),
            pl.BlockSpec((rows, ckv), lambda i: (0, 0)),
        ],
        out_shape=[
            jax.ShapeDtypeStruct((rows, cq), F32),
            jax.ShapeDtypeStruct((rows, ckv), F32),
        ],
        compiler_params=params(),
        cost_estimate=cost(2 * rows * width * (cq + ckv), 2 * width * (rows + cq + ckv)),
        name="dense_qkv",
    )(x, wq, wkv)


ENDS_AT = 2
SEND_AT = 16
SERVED_AT = 32
SOURCE_AT = 48
TABLE = 64


def serve_kernel(
    count, blocks, owned, crop_ref, tenant_ref, row_ref, cot, down, up_q, up_kv, up_o, down_o, *outs
):
    tab, cots = outs[0], outs[1:3]
    firsts, lates = outs[3 : 3 + count], outs[3 + count :]
    cots[0][...] = cot[: cots[0].shape[0], :]
    cots[1][...] = cot[cots[0].shape[0] :, :]
    me = lax.axis_index("ctx")
    for i in range(TABLE):
        tab[i] = 0
    tab[0] = me
    tab[1] = lax.axis_index("tp")
    end = jnp.int32(0)
    for i in range(crop_ref.shape[0]):
        end = end + crop_ref[i]
        tab[ENDS_AT + i] = end
    for b in range(blocks):
        row = row_ref[tenant_ref[me * blocks + b]]
        tab[SOURCE_AT + b] = (row // owned) ^ me
    for k in range(count):
        served = jnp.int32(-1)
        for b in range(blocks):
            row = row_ref[tenant_ref[(me ^ k) * blocks + b]]
            served = jnp.where(row // owned == me, row - me * owned, served)
        tab[SERVED_AT + k] = served
        tab[SEND_AT + k] = jnp.maximum(served, 0)
    rank, width = ADAPTER_RANK, down.shape[2]
    half, quarter = rank // 2, rank // 4
    cq, ckv = width // 2, width // 4
    for k in range(count):
        at = tab[SEND_AT + k]
        low = down.shape[1]
        firsts[k][:low, :] = down[at]
        for i in range(2):
            firsts[k][low : low + half, i * cq : (i + 1) * cq] = up_q[
                at, i * half : (i + 1) * half, :
            ]
            lates[k][rank : rank + half, i * cq : (i + 1) * cq] = down_o[
                at, i * half : (i + 1) * half, :
            ]
        for i in range(4):
            firsts[k][low + half :, i * ckv : (i + 1) * ckv] = up_kv[
                at, i * quarter : (i + 1) * quarter, :
            ]
        lates[k][:rank, :] = up_o[at]


def serve(count, blocks, crops, tenants, store_rows, cot, down, up_q, up_kv, up_o, down_o):
    rank, width = ADAPTER_RANK, down.shape[2]
    assert up_q.shape[2] * 2 == width and up_kv.shape[2] * 4 == width
    assert up_o.shape[2] == width and down_o.shape[2] * 2 == width
    smem = pl.BlockSpec(memory_space=pltpu.SMEM)
    vmem = pl.BlockSpec(memory_space=pltpu.VMEM)
    first = jax.ShapeDtypeStruct((3 * rank + rank // 2 + rank // 4, width), BF16)
    late = jax.ShapeDtypeStruct((rank + rank // 2, width), BF16)
    cut = cot.shape[0] // 384 * 176
    results = pl.pallas_call(
        functools.partial(serve_kernel, count, blocks, down.shape[0]),
        in_specs=[smem] * 3 + [vmem] * 6,
        out_specs=[smem] + [vmem] * (2 + 2 * count),
        out_shape=[jax.ShapeDtypeStruct((TABLE,), jnp.int32)]
        + [jax.ShapeDtypeStruct((n, cot.shape[1]), BF16) for n in (cut, cot.shape[0] - cut)]
        + [first] * count
        + [late] * count,
        compiler_params=params(),
        name="serve",
    )(crops, tenants, store_rows, cot, down, up_q, up_kv, up_o, down_o)
    return results[0], results[1:3], list(results[3 : 3 + count]), list(results[3 + count :])


def unpack_q(ref):
    rows, width = ref.shape
    value = ref[...]
    return jnp.concatenate([value[:, : width // 2], value[:, width // 2 :]], axis=0)


def unpack_kv(ref):
    rows, width = ref.shape
    value = ref[...]
    step = width // 4
    return jnp.concatenate([value[:, i * step : (i + 1) * step] for i in range(4)], axis=0)


def pick(tab_ref, block, count, step):
    for k in range(count):

        @pl.when(tab_ref[SOURCE_AT + block] == k)
        def _(k=k):
            step(k)


def split_rows(tab_ref, whole, mine, other):
    half = mine.shape[0]

    @pl.when(tab_ref[1] % 2 == 0)
    def _():
        mine[...] = whole[:half, :]
        other[...] = whole[half:, :]

    @pl.when(tab_ref[1] % 2 == 1)
    def _():
        mine[...] = whole[half:, :]
        other[...] = whole[:half, :]


def join_rows(tab_ref, mine, other, whole):
    half = mine.shape[0]

    @pl.when(tab_ref[1] % 2 == 0)
    def _():
        whole[:half, :] = mine[...]
        whole[half:, :] = other[...]

    @pl.when(tab_ref[1] % 2 == 1)
    def _():
        whole[:half, :] = other[...]
        whole[half:, :] = mine[...]


def sum_halves(mine, other, beside=()):
    total = add_round(mine, swap(other, "tp", 1))
    mask, done = 2, None
    beside = list(beside)
    while mask < lax.axis_size("tp"):
        arrived = swap(total, "tp", mask)
        if beside:
            done = beside.pop(0)(done)
            arrived, done = lax.optimization_barrier((arrived, done))
        total = add_round(total, arrived)
        mask *= 2
    while beside:
        done = beside.pop(0)(done)
    return (total, swap(total, "tp", 1)), done


def block_rows(b):
    return slice(b * BLK, (b + 1) * BLK)


def whole_spec(shape):
    return pl.BlockSpec(shape, lambda i, t: (0,) * len(shape))


def table_call(kernel, table, operands, shapes, scratch, name, flops=0, limit=VMEM_BYTES):
    moved = sum(math.prod(s.shape) * s.dtype.itemsize for s in operands + shapes)
    vmem = pl.BlockSpec(memory_space=pltpu.VMEM)
    return pl.pallas_call(
        kernel,
        in_specs=[pl.BlockSpec(memory_space=pltpu.SMEM)] + [vmem] * len(operands),
        out_specs=[vmem] * len(shapes),
        out_shape=shapes,
        scratch_shapes=scratch,
        compiler_params=params(limit),
        cost_estimate=cost(flops, moved),
        name=name,
    )(table, *operands)


def low_kernel(count, tab_ref, x_ref, *refs):
    downs = refs[:count]
    mine, other, whole = refs[count:]
    cols = whole.shape[1]
    for b in range(whole.shape[0] // BLK):

        def step(k, b=b):
            whole[block_rows(b), :] = dot_nt(x_ref[block_rows(b), :], downs[k][:cols, :]).astype(BF16)

        pick(tab_ref, b, count, step)
    split_rows(tab_ref, whole, mine, other)


def low_part(table, x, firsts):
    rows, width, cols = x.shape[0], firsts[0].shape[1], 3 * ADAPTER_RANK
    half = jax.ShapeDtypeStruct((rows // 2, cols), BF16)
    return table_call(
        functools.partial(low_kernel, len(firsts)),
        table,
        [x] + firsts,
        [half, half],
        [pltpu.VMEM((rows, cols), BF16)],
        "low_part",
        2 * rows * width * cols,
        SMALL_VMEM_BYTES,
    )


def finish_kv_kernel(count, rotate_keys, tab_ref, kv_ref, mine, other, cos_ref, sin_ref, *refs):
    ups = refs[:count]
    kvo, low = refs[count:]
    ckv = kv_ref.shape[1]
    rank = ADAPTER_RANK
    join_rows(tab_ref, mine, other, low)
    for b in range(kv_ref.shape[0] // BLK):

        def step(k, b=b):
            at_rows = block_rows(b)
            low_k = low[at_rows, rank : 2 * rank]
            low_v = low[at_rows, 2 * rank :]
            up_kv = unpack_kv(ups[k].at[3 * rank + rank // 2 :])
            for h in range(ckv // HEAD_SIZE):
                at = slice(h * HEAD_SIZE, (h + 1) * HEAD_SIZE)
                if rotate_keys:
                    term = dot_nn(low_v if h % 2 else low_k, up_kv[:, at])
                else:
                    is_value = (tab_ref[1] * (ckv // HEAD_SIZE) + h) % 2 == 1
                    term = jnp.where(
                        is_value, dot_nn(low_v, up_kv[:, at]), dot_nn(low_k, up_kv[:, at])
                    )
                piece = (kv_ref[at_rows, at] + term).astype(BF16)
                if rotate_keys and h % 2 == 0:
                    cosine, sine = cos_ref[at_rows, :], sin_ref[at_rows, :]
                    piece = turn_kernel(piece.astype(F32), cosine, sine).astype(BF16)
                kvo[at_rows, at] = piece

        pick(tab_ref, b, count, step)


def finish_kv(table, kv_lin, halves, firsts, cosine, sine, rotate_keys):
    rows, ckv = kv_lin.shape
    cols = 3 * ADAPTER_RANK
    operands = [kv_lin, *halves, cosine, sine]
    return table_call(
        functools.partial(finish_kv_kernel, len(firsts), rotate_keys),
        table,
        operands + firsts,
        [jax.ShapeDtypeStruct((rows, ckv), BF16), jax.ShapeDtypeStruct((rows, cols), BF16)],
        [],
        "finish_kv",
        4 * rows * ADAPTER_RANK * ckv,
    )


def finish_q_kernel(count, tab_ref, q_ref, low_ref, cos_ref, sin_ref, *refs):
    ups, qo = refs[:count], refs[count]
    cq = q_ref.shape[1]
    rank = ADAPTER_RANK
    for b in range(q_ref.shape[0] // BLK):

        def step(k, b=b):
            at_rows = block_rows(b)
            cosine, sine = cos_ref[at_rows, :], sin_ref[at_rows, :]
            up_q = unpack_q(ups[k].at[3 * rank : 3 * rank + rank // 2])
            query = q_ref[at_rows, :] + dot_nn(low_ref[at_rows, :rank], up_q)
            for h in range(cq // HEAD_SIZE):
                at = slice(h * HEAD_SIZE, (h + 1) * HEAD_SIZE)
                qo[at_rows, at] = turn_kernel(query[:, at], cosine, sine).astype(BF16)

        pick(tab_ref, b, count, step)


def finish_q(table, q_lin, low_in, firsts, cosine, sine):
    rows, cq = q_lin.shape
    operands = [q_lin, low_in, cosine, sine]
    return table_call(
        functools.partial(finish_q_kernel, len(firsts)),
        table,
        operands + firsts,
        [jax.ShapeDtypeStruct((rows, cq), BF16)],
        [],
        "finish_q",
        2 * rows * ADAPTER_RANK * cq,
        SMALL_VMEM_BYTES,
    )[0]


def low_o_kernel(count, tab_ref, cot_ref, attn_ref, *refs):
    lates = refs[:count]
    mine, other, whole = refs[count:]
    rank = ADAPTER_RANK
    for b in range(whole.shape[0] // BLK):

        def step(k, b=b):
            at = block_rows(b)
            whole[at, :rank] = dot_nt(cot_ref[at, :], lates[k][:rank, :]).astype(BF16)
            down = unpack_q(lates[k].at[rank:])
            whole[at, rank:] = dot_nt(attn_ref[at, :], down).astype(BF16)

        pick(tab_ref, b, count, step)
    split_rows(tab_ref, whole, mine, other)


def low_o_part(table, cot, attn, lates):
    rows, width = cot.shape
    cols = 2 * ADAPTER_RANK
    half = jax.ShapeDtypeStruct((rows // 2, cols), BF16)
    return table_call(
        functools.partial(low_o_kernel, len(lates)),
        table,
        [cot, attn] + lates,
        [half, half],
        [pltpu.VMEM((rows, cols), BF16)],
        "low_o_part",
        2 * rows * cols * width,
        SMALL_VMEM_BYTES,
    )


def low_g_kernel(count, tab_ref, gq_ref, gkv_ref, *refs):
    ups = refs[:count]
    mine, other, whole = refs[count:]
    rank = ADAPTER_RANK
    ckv = gkv_ref.shape[1]
    for b in range(whole.shape[0] // BLK):

        def step(k, b=b):
            at = block_rows(b)
            up_q = unpack_q(ups[k].at[3 * rank : 3 * rank + rank // 2])
            whole[at, :rank] = dot_nt(gq_ref[at, :], up_q).astype(BF16)
            up_kv = unpack_kv(ups[k].at[3 * rank + rank // 2 :])
            sums = [jnp.zeros((BLK, rank), F32)] * 2
            for h in range(ckv // HEAD_SIZE):
                cols = slice(h * HEAD_SIZE, (h + 1) * HEAD_SIZE)
                term = dot_nt(gkv_ref[at, cols], up_kv[:, cols])
                is_value = (tab_ref[1] * (ckv // HEAD_SIZE) + h) % 2 == 1
                sums[0] = sums[0] + jnp.where(is_value, 0.0, term)
                sums[1] = sums[1] + jnp.where(is_value, term, 0.0)
            whole[at, rank : 2 * rank] = sums[0].astype(BF16)
            whole[at, 2 * rank :] = sums[1].astype(BF16)

        pick(tab_ref, b, count, step)
    split_rows(tab_ref, whole, mine, other)


def low_g_part(table, gq, gkv, firsts):
    rows = gq.shape[0]
    cols, width = 3 * ADAPTER_RANK, firsts[0].shape[1]
    half = jax.ShapeDtypeStruct((rows // 2, cols), BF16)
    return table_call(
        functools.partial(low_g_kernel, len(firsts)),
        table,
        [gq, gkv] + firsts,
        [half, half],
        [pltpu.VMEM((rows, cols), BF16)],
        "low_g_part",
        2 * rows * width * ADAPTER_RANK,
    )


def zero_unused(tab_ref, blocks, sends):
    for k in range(len(sends)):
        used = tab_ref[SOURCE_AT] == k
        for b in range(1, blocks):
            used = used | (tab_ref[SOURCE_AT + b] == k)

        @pl.when(jnp.logical_not(used))
        def _(k=k):
            sends[k][...] = jnp.zeros_like(sends[k])


def up_grads_kernel(
    count, tab_ref, low_ref, gq_ref, gkv_ref, o_mine, o_other, cot, attn, *refs
):
    sends, low_o = refs[:count], refs[count]
    rank = ADAPTER_RANK
    join_rows(tab_ref, o_mine, o_other, low_o)
    blocks = low_o.shape[0] // BLK
    cq, ckv = gq_ref.shape[1], gkv_ref.shape[1]
    half, quarter = rank // 2, rank // 4
    late = half + quarter
    zero_unused(tab_ref, blocks, sends)
    for b in range(blocks):

        def step(k, b=b):
            at = block_rows(b)
            out = sends[k]
            up_q = dot_tn(low_ref[at, :rank], gq_ref[at, :]).astype(BF16)
            down_o = dot_tn(low_o[at, :rank], attn[at, :]).astype(BF16)
            for i in range(2):
                rows = slice(i * half, (i + 1) * half)
                cols = slice(i * cq, (i + 1) * cq)
                out[:half, cols] = up_q[rows, :]
                out[late + rank :, cols] = down_o[rows, :]
            for h in range(ckv // HEAD_SIZE):
                piece = slice(h * HEAD_SIZE, (h + 1) * HEAD_SIZE)
                is_value = (tab_ref[1] * (ckv // HEAD_SIZE) + h) % 2 == 1
                up_kv = jnp.where(
                    is_value,
                    dot_tn(low_ref[at, 2 * rank :], gkv_ref[at, piece]),
                    dot_tn(low_ref[at, rank : 2 * rank], gkv_ref[at, piece]),
                ).astype(BF16)
                for i in range(4):
                    cols = slice(i * ckv + h * HEAD_SIZE, i * ckv + (h + 1) * HEAD_SIZE)
                    out[half:late, cols] = up_kv[i * quarter : (i + 1) * quarter, :]
            out[late : late + rank, :] = dot_tn(low_o[at, rank:], cot[at, :]).astype(BF16)

        pick(tab_ref, b, count, step)


def up_grads(table, count, low_in, gq, gkv, o_halves, cot, attn):
    rows, width = cot.shape
    rank = ADAPTER_RANK
    operands = [low_in, gq, gkv, *o_halves, cot, attn]
    return list(
        table_call(
            functools.partial(up_grads_kernel, count),
            table,
            operands,
            [jax.ShapeDtypeStruct((2 * rank + rank // 4, width), BF16)] * count,
            [pltpu.VMEM((rows, 2 * rank), BF16)],
            "up_grads",
            2 * rows * width * 3 * rank,
        )
    )


def down_grads_kernel(count, tab_ref, x_ref, mine, other, *refs):
    downs, sends = refs[:count], refs[count : 2 * count]
    delta, low = refs[2 * count :]
    join_rows(tab_ref, mine, other, low)
    blocks = low.shape[0] // BLK
    zero_unused(tab_ref, blocks, sends)
    for b in range(blocks):

        def step(k, b=b):
            at = block_rows(b)
            sends[k][...] = dot_tn(low[at, :], x_ref[at, :]).astype(BF16)
            delta[at, :] = dot_nn(low[at, :], downs[k][: low.shape[1], :]).astype(BF16)

        pick(tab_ref, b, count, step)


def down_grads(table, x, halves, firsts):
    rows, cols = x.shape[0], 3 * ADAPTER_RANK
    width, count = firsts[0].shape[1], len(firsts)
    results = table_call(
        functools.partial(down_grads_kernel, count),
        table,
        [x, *halves] + firsts,
        [jax.ShapeDtypeStruct((cols, width), BF16)] * count
        + [jax.ShapeDtypeStruct((rows, width), BF16)],
        [pltpu.VMEM((rows, cols), BF16)],
        "down_grads",
        4 * rows * width * cols,
    )
    return list(results[:count]), results[count]


def store_kernel(count, pieces, tab_ref, *refs):
    arrived, outs = refs[:count], refs[count:]
    row = pl.program_id(0)
    for o in outs:
        o[...] = jnp.zeros_like(o)
    for k in range(count):

        @pl.when(tab_ref[SERVED_AT + k] == row)
        def _(k=k):
            for o, piece in zip(outs, pieces):
                o[0] += piece(arrived[k]).astype(F32)


def store_sums(table, arrived, owned, pieces, sizes):
    shapes = [jax.ShapeDtypeStruct((owned,) + size, F32) for size in sizes]
    return pl.pallas_call(
        functools.partial(store_kernel, len(arrived), pieces),
        grid_spec=pltpu.PrefetchScalarGridSpec(
            num_scalar_prefetch=1,
            grid=(owned,),
            in_specs=[pl.BlockSpec(a.shape, lambda i, t: (0, 0)) for a in arrived],
            out_specs=[pl.BlockSpec((1,) + s.shape[1:], lambda i, t: (i, 0, 0)) for s in shapes],
        ),
        out_shape=shapes,
        compiler_params=params(),
        name="store_sums",
    )(table, *arrived)


def store_ups(table, arrived, owned):
    rank, width = ADAPTER_RANK, arrived[0].shape[1]
    half, late = rank // 2, rank // 2 + rank // 4
    pieces = [
        lambda a: unpack_q(a.at[:half]),
        lambda a: unpack_kv(a.at[half:late]),
        lambda a: unpack_q(a.at[late + rank :]),
        lambda a: a[late : late + rank, :],
    ]
    sizes = [(rank, width // 2), (rank, width // 4), (rank, width // 2), (rank, width)]
    return store_sums(table, arrived, owned, pieces, sizes)


def store_downs(table, arrived, owned):
    return store_sums(table, arrived, owned, [lambda a: a[...]], [arrived[0].shape])[0]


def output_kernel(count, tab_ref, sum_ref, mine, other, *refs):
    lates = refs[:count]
    out, low = refs[count:]
    rank = ADAPTER_RANK
    join_rows(tab_ref, mine, other, low)
    for b in range(out.shape[0] // BLK):

        def step(k, b=b):
            at = block_rows(b)
            term = dot_nn(low[at, rank:], lates[k][:rank, :])
            out[at, :] = (sum_ref[at, :].astype(F32) + term).astype(BF16)

        pick(tab_ref, b, count, step)


def output_result(table, total, halves, lates):
    rows, width = total.shape
    rank = ADAPTER_RANK
    return table_call(
        functools.partial(output_kernel, len(lates)),
        table,
        [total, *halves] + lates,
        [jax.ShapeDtypeStruct((rows, width), BF16)],
        [pltpu.VMEM((rows, 2 * rank), BF16)],
        "output_result",
        2 * rows * rank * width,
    )[0]


def crop_start(tab_ref, crops, positions):
    start = jnp.zeros_like(positions)
    for i in range(crops):
        end = tab_ref[ENDS_AT + i]
        start = jnp.where(positions >= end, end, start)
    return start


def masked(scores, first, own, base):
    rows, cols = scores.shape
    key_pos = base + lax.broadcasted_iota(jnp.int32, (rows, cols), 0)
    allowed = key_pos >= first
    if own:
        allowed &= key_pos <= base + lax.broadcasted_iota(jnp.int32, (rows, cols), 1)
    return jnp.where(allowed, scores, NEG)


def chunk_on(tab_ref, crops, k, rows):
    me = tab_ref[0]
    chunk = me ^ k
    return (chunk <= me) & ((chunk + 1) * rows > crop_start(tab_ref, crops, me * rows))


def query_starts(tab_ref, crops, rows):
    positions = tab_ref[0] * rows + lax.broadcasted_iota(jnp.int32, (1, rows), 1)
    return crop_start(tab_ref, crops, positions)


def forward_kernel(heads, count, crops, tab_ref, q_ref, *refs):
    kv_refs = refs[:count]
    out_ref, norm_ref, acc, top, total = refs[count:]
    rows = q_ref.shape[0]
    first = query_starts(tab_ref, crops, rows)
    for k in range(count):

        def chunk_step(k=k):
            base = (tab_ref[0] ^ k) * rows
            keys = kv_refs[k][:, :HEAD_SIZE]
            values = kv_refs[k][:, HEAD_SIZE:]
            for h in range(heads):
                at = slice(h * HEAD_SIZE, (h + 1) * HEAD_SIZE)
                scores = masked(dot_nt(keys, q_ref[:, at]), first, k == 0, base)
                here = jnp.max(scores, axis=0, keepdims=True)
                if k == 0:
                    new_top = here
                else:
                    old_top = top[h : h + 1, :]
                    new_top = jnp.maximum(old_top, here)
                weights = jnp.exp((scores - new_top) * SCALE)
                here_sum = jnp.sum(weights, axis=0, keepdims=True)
                here_out = dot_tn(values, weights.astype(BF16))
                if k == 0:
                    total[h : h + 1, :] = here_sum
                    acc[h] = here_out
                else:
                    decay = jnp.exp((old_top - new_top) * SCALE)
                    total[h : h + 1, :] = total[h : h + 1, :] * decay + here_sum
                    acc[h] = acc[h] * decay + here_out
                top[h : h + 1, :] = new_top

        if k == 0:
            chunk_step()
        else:
            pl.when(chunk_on(tab_ref, crops, k, rows))(chunk_step)
    for h in range(heads):
        at = slice(h * HEAD_SIZE, (h + 1) * HEAD_SIZE)
        out_ref[:, at] = jnp.transpose(acc[h] / total[h : h + 1, :]).astype(BF16)
    norm_ref[...] = top[...] * SCALE + jnp.log(total[...])


def attention_forward(table, crops, query, kvs):
    rows, cols = query.shape
    heads = cols // HEAD_SIZE
    count = len(kvs)
    smem = pl.BlockSpec(memory_space=pltpu.SMEM)
    vmem = pl.BlockSpec(memory_space=pltpu.VMEM)
    work = heads * rows * rows * count
    return pl.pallas_call(
        functools.partial(forward_kernel, heads, count, crops),
        in_specs=[smem] + [vmem] * (1 + count),
        out_specs=[vmem] * 2,
        out_shape=[
            jax.ShapeDtypeStruct((rows, cols), BF16),
            jax.ShapeDtypeStruct((heads, rows), F32),
        ],
        scratch_shapes=[
            pltpu.VMEM((heads, HEAD_SIZE, rows), F32),
            pltpu.VMEM((heads, rows), F32),
            pltpu.VMEM((heads, rows), F32),
        ],
        compiler_params=params(),
        cost_estimate=cost(4 * work * HEAD_SIZE, 4 * rows * cols * count, work),
        name="attention_forward",
    )(table, query, *kvs)


def backward_kernel(
    heads,
    count,
    crops,
    tab_ref,
    q_ref,
    dense_ref,
    mine,
    other,
    out_ref,
    norm_ref,
    cos_ref,
    sin_ref,
    *refs,
):
    kv_refs, lates = refs[:count], refs[count : 2 * count]
    gq_ref = refs[2 * count]
    gkv_refs = refs[2 * count + 1 : 3 * count + 1]
    acc, delta, low, grad_ref = refs[3 * count + 1 :]
    rows = q_ref.shape[0]
    rank = ADAPTER_RANK
    first = query_starts(tab_ref, crops, rows)
    join_rows(tab_ref, mine, other, low)
    for b in range(rows // BLK):

        def add(k, b=b):
            at = block_rows(b)
            term = dot_nn(low[at, :rank], unpack_q(lates[k].at[rank:]))
            grad_ref[at, :] = (dense_ref[at, :] + term).astype(BF16)

        pick(tab_ref, b, count, add)
    for h in range(heads):
        at = slice(h * HEAD_SIZE, (h + 1) * HEAD_SIZE)
        product = grad_ref[:, at].astype(F32) * out_ref[:, at].astype(F32)
        delta[h : h + 1, :] = jnp.sum(jnp.transpose(product), axis=0, keepdims=True)
    for k in range(count):

        def chunk_step(k=k):
            base = (tab_ref[0] ^ k) * rows
            keys = kv_refs[k][:, :HEAD_SIZE]
            values = kv_refs[k][:, HEAD_SIZE:]
            key_grad = jnp.zeros((rows, HEAD_SIZE), F32)
            value_grad = jnp.zeros((rows, HEAD_SIZE), F32)
            for h in range(heads):
                at = slice(h * HEAD_SIZE, (h + 1) * HEAD_SIZE)
                scores = masked(dot_nt(keys, q_ref[:, at]), first, k == 0, base)
                weights = jnp.exp(scores * SCALE - norm_ref[h : h + 1, :])
                value_grad += dot_nn(weights.astype(BF16), grad_ref[:, at])
                grad_weights = dot_nt(values, grad_ref[:, at])
                grad_scores = (weights * (grad_weights - delta[h : h + 1, :])).astype(BF16)
                key_grad += dot_nn(grad_scores, q_ref[:, at])
                here = dot_tn(keys, grad_scores)
                if k == 0:
                    acc[h] = here
                else:
                    acc[h] += here
            gkv_refs[k][:, :HEAD_SIZE] = (key_grad * SCALE).astype(BF16)
            gkv_refs[k][:, HEAD_SIZE:] = value_grad.astype(BF16)

        if k == 0:
            chunk_step()
        else:
            on = chunk_on(tab_ref, crops, k, rows)
            pl.when(on)(chunk_step)

            @pl.when(jnp.logical_not(on))
            def _(k=k):
                gkv_refs[k][...] = jnp.zeros_like(gkv_refs[k])

    for h in range(heads):
        at = slice(h * HEAD_SIZE, (h + 1) * HEAD_SIZE)
        grad = jnp.transpose(acc[h]) * SCALE
        gq_ref[:, at] = turn_kernel(grad, cos_ref[...], -sin_ref[...]).astype(BF16)


def attention_backward(table, crops, query, dense, halves, out, norm, cosine, sine, kvs, lates):
    rows, cols = query.shape
    heads = cols // HEAD_SIZE
    count = len(kvs)
    smem = pl.BlockSpec(memory_space=pltpu.SMEM)
    vmem = pl.BlockSpec(memory_space=pltpu.VMEM)
    work = heads * rows * rows * count
    results = pl.pallas_call(
        functools.partial(backward_kernel, heads, count, crops),
        in_specs=[smem] + [vmem] * (8 + 2 * count),
        out_specs=[vmem] * (1 + count),
        out_shape=[jax.ShapeDtypeStruct((rows, cols), BF16)]
        + [jax.ShapeDtypeStruct((rows, 2 * HEAD_SIZE), BF16)] * count,
        scratch_shapes=[
            pltpu.VMEM((heads, HEAD_SIZE, rows), F32),
            pltpu.VMEM((heads, rows), F32),
            pltpu.VMEM((rows, 2 * ADAPTER_RANK), BF16),
            pltpu.VMEM((rows, cols), BF16),
        ],
        compiler_params=params(),
        cost_estimate=cost(10 * work * HEAD_SIZE, 8 * rows * cols * count, work),
        name="attention_backward",
    )(table, query, dense, *halves, out, norm, cosine, sine, *kvs, *lates)
    return results[0], list(results[1:])


def plane_spec(shape, axis, other):
    def index(i, t):
        core = t[1] % 2
        at = 2 * i + (1 - core if other else core)
        return (0, at) if axis else (at, 0)

    return pl.BlockSpec(shape, index)


def pick_kernel(tab_ref, w_ref, o_ref):
    o_ref[...] = w_ref[...]


def pick_planes(table, weight, groups, axis):
    planes = groups // 2
    shape = list(weight.shape)
    shape[axis] //= groups
    result = list(weight.shape)
    result[axis] //= 2
    return pl.pallas_call(
        pick_kernel,
        grid_spec=pltpu.PrefetchScalarGridSpec(
            num_scalar_prefetch=1,
            grid=(planes,),
            in_specs=[plane_spec(tuple(shape), axis, True)],
            out_specs=pl.BlockSpec(
                tuple(shape), (lambda i, t: (0, i)) if axis else (lambda i, t: (i, 0))
            ),
        ),
        out_shape=jax.ShapeDtypeStruct(tuple(result), BF16),
        compiler_params=params(),
        cost_estimate=cost(0, 2 * math.prod(weight.shape)),
        name="pick_planes",
    )(table, weight)


def reduce_planes(parts, groups):
    lines = [list(range(core, groups, 2)) for core in range(2)]
    return lax.psum_scatter(parts, "tp", scatter_dimension=0, axis_index_groups=lines, tiled=False)


def project_kernel(tab_ref, a_ref, ao_ref, w_ref, wo_ref, o_ref):
    total = dot_nn(a_ref[...], w_ref[...]) + dot_nn(ao_ref[...], wo_ref[...])
    o_ref[0] = total.astype(BF16)


def project_out(table, attn, attn_other, weight, weight_other, groups):
    rows, depth = attn.shape
    cols = weight.shape[1] // groups
    planes = groups // 2
    return pl.pallas_call(
        project_kernel,
        grid_spec=pltpu.PrefetchScalarGridSpec(
            num_scalar_prefetch=1,
            grid=(planes,),
            in_specs=[
                whole_spec(attn.shape),
                whole_spec(attn.shape),
                plane_spec((depth, cols), 1, False),
                pl.BlockSpec((depth, cols), lambda i, t: (0, i)),
            ],
            out_specs=pl.BlockSpec((1, rows, cols), lambda i, t: (i, 0, 0)),
        ),
        out_shape=jax.ShapeDtypeStruct((planes, rows, cols), BF16),
        compiler_params=params(),
        cost_estimate=cost(
            2 * rows * depth * cols * groups, 2 * (rows + 2 * depth) * cols * planes
        ),
        name="project_out",
    )(table, attn, attn_other, weight, weight_other)


PER_STEP = 2


def grad_attn_kernel(c0_ref, c1_ref, w_ref, *refs):
    before, o_ref = refs[:-1], refs[-1]
    step = pl.program_id(0)
    per_step, first_rows, cols = c0_ref.shape
    parts = ((c0_ref, slice(0, first_rows)), (c1_ref, slice(first_rows, o_ref.shape[0])))
    for c_ref, at in parts:
        total = dot_nt(c_ref[0], w_ref[:, :cols])
        for i in range(1, per_step):
            total += dot_nt(c_ref[i], w_ref[:, i * cols : (i + 1) * cols])

        @pl.when(step == 0)
        def _(at=at, total=total):
            o_ref[at, :] = total + before[0][at, :] if before else total

        @pl.when(step > 0)
        def _(at=at, total=total):
            o_ref[at, :] += total


def grad_attn(cot_first, cot_second, weight, half, before=None):
    groups, first_rows, cols = cot_first.shape
    depth = weight.shape[0]
    rows = first_rows + cot_second.shape[1]
    steps = groups // PER_STEP // 2
    start = half * steps
    whole = pl.BlockSpec((rows, depth), lambda i: (0, 0))
    return pl.pallas_call(
        grad_attn_kernel,
        grid=(steps,),
        in_specs=[
            pl.BlockSpec((PER_STEP, first_rows, cols), lambda i: (start + i, 0, 0)),
            pl.BlockSpec((PER_STEP, rows - first_rows, cols), lambda i: (start + i, 0, 0)),
            pl.BlockSpec((depth, PER_STEP * cols), lambda i: (0, start + i)),
        ]
        + ([] if before is None else [whole]),
        out_specs=whole,
        out_shape=jax.ShapeDtypeStruct((rows, depth), F32),
        compiler_params=params(),
        cost_estimate=cost(rows * depth * cols * groups, (rows + depth) * cols * groups),
        name="grad_attn",
    )(cot_first, cot_second, weight, *([] if before is None else [before]))


def grad_input_kernel(tab_ref, gq, gqo, gkv, gkvo, wq, wqo, wkv, wkvo, o_ref):
    total = dot_nt(gq[...], wq[...]) + dot_nt(gqo[...], wqo[...])
    total = total + dot_nt(gkv[...], wkv[...]) + dot_nt(gkvo[...], wkvo[...])
    o_ref[0] = total.astype(BF16)


def grad_input(table, gq, gq_other, gkv, gkv_other, wq, wq_other, wkv, wkv_other, groups):
    rows, cq = gq.shape
    ckv = gkv.shape[1]
    cols = wq.shape[0] // groups
    planes = groups // 2
    return pl.pallas_call(
        grad_input_kernel,
        grid_spec=pltpu.PrefetchScalarGridSpec(
            num_scalar_prefetch=1,
            grid=(planes,),
            in_specs=[
                whole_spec(gq.shape),
                whole_spec(gq.shape),
                whole_spec(gkv.shape),
                whole_spec(gkv.shape),
                plane_spec((cols, cq), 0, False),
                pl.BlockSpec((cols, cq), lambda i, t: (i, 0)),
                plane_spec((cols, ckv), 0, False),
                pl.BlockSpec((cols, ckv), lambda i, t: (i, 0)),
            ],
            out_specs=pl.BlockSpec((1, rows, cols), lambda i, t: (i, 0, 0)),
        ),
        out_shape=jax.ShapeDtypeStruct((planes, rows, cols), BF16),
        compiler_params=params(),
        cost_estimate=cost(
            2 * rows * (cq + ckv) * cols * groups,
            2 * (rows + 2 * (cq + ckv)) * cols * planes,
        ),
        name="grad_input",
    )(table, gq, gq_other, gkv, gkv_other, wq, wq_other, wkv, wkv_other)


def body(
    hidden_input,
    output_cotangent,
    query_projection,
    key_value_projection,
    output_projection,
    adapter_qkv_down_store,
    adapter_query_up,
    adapter_key_value_up,
    adapter_output_down,
    adapter_output_up,
    crop_token_length,
    tenant_per_block,
    tenant_store_row,
):
    ctx_count = lax.axis_size("ctx")
    tp_count = lax.axis_size("tp")
    ctx_index = lax.axis_index("ctx")
    tp_index = lax.axis_index("tp")
    rows_dev = hidden_input.shape[0]
    out_cols = output_cotangent.shape[1]
    tenant_owner = adapter_qkv_down_store.shape[0]
    blocks_dev = rows_dev // BLK
    pair_bits = (tp_count // KEY_VALUE_HEADS).bit_length() - 1
    groups = hidden_input.shape[1] // out_cols
    crops = crop_token_length.shape[0]
    partners = range(1, ctx_count)

    x_slice = lax.dynamic_slice_in_dim(hidden_input, tp_index * out_cols, out_cols, 1)

    table, cots, firsts, lates = serve(
        ctx_count,
        blocks_dev,
        crop_token_length,
        tenant_per_block,
        tenant_store_row,
        output_cotangent,
        adapter_qkv_down_store.swapaxes(1, 2),
        adapter_query_up,
        adapter_key_value_up,
        adapter_output_up,
        adapter_output_down.swapaxes(1, 2),
    )
    cot_first = lax.all_gather(cots[0], "tp", axis=0, tiled=False)
    firsts = [firsts[0]] + [swap(firsts[k], "ctx", k) for k in partners]
    my_pos = ctx_index * rows_dev + jnp.arange(rows_dev, dtype=jnp.int32)
    q_lin, kv_lin = dense_qkv(hidden_input, query_projection, key_value_projection)
    out_pick = pick_planes(table, output_projection, groups, 1)
    firsts, q_lin, kv_lin, tables, out_pick, x_slice = lax.optimization_barrier(
        (firsts, q_lin, kv_lin, rope_tables(my_pos), out_pick, x_slice)
    )
    cosine, sine = tables
    low_halves = low_part(table, x_slice, firsts)
    low_halves, (kv_pick, query_pick) = sum_halves(
        *low_halves,
        beside=[
            lambda done: pick_planes(table, key_value_projection, groups, 0),
            lambda done: (done, pick_planes(table, query_projection, groups, 0)),
        ],
    )
    low_halves, cot_rest = lax.optimization_barrier((low_halves, cots[1]))
    cot_second = lax.all_gather(cot_rest, "tp", axis=0, tiled=False)
    kv_local, low_in = finish_kv(
        table, kv_lin, low_halves, firsts, cosine, sine, pair_bits == 0
    )
    if pair_bits:
        for bit_no in range(pair_bits):
            partner = swap(kv_local, "tp", 1 << bit_no)
            is_lower = tp_index // (1 << bit_no) % 2 == 0
            kv_local = jnp.where(
                is_lower,
                jnp.concatenate([kv_local, partner], axis=1),
                jnp.concatenate([partner, kv_local], axis=1),
            )
        key_rot = turn(kv_local[:, :HEAD_SIZE].astype(F32), cosine, sine).astype(BF16)
        kv_local = jnp.concatenate([key_rot, kv_local[:, HEAD_SIZE:]], axis=1)
    kvs = [kv_local] + [swap(kv_local, "ctx", k) for k in partners]
    query_rot = finish_q(table, q_lin, low_in, firsts, cosine, sine)
    kvs, lates, query_rot = lax.optimization_barrier((kvs, lates, query_rot))
    out_other, query_other, kv_other = (
        swap(pick, "tp", 1) for pick in (out_pick, query_pick, kv_pick)
    )
    lates = [lates[0]] + [swap(lates[k], "ctx", k) for k in partners]

    attn_out, log_norm = attention_forward(table, crops, query_rot, kvs)
    lates, attn_out = lax.optimization_barrier((lates, attn_out))
    heads_part = project_out(
        table, attn_out, swap(attn_out, "tp", 1), output_projection, out_other, groups
    )
    heads_part, attn_out, cot_first = lax.optimization_barrier((heads_part, attn_out, cot_first))
    heads_sum = reduce_planes(heads_part, groups)
    o_halves, grad_dense = sum_halves(
        *low_o_part(table, output_cotangent, attn_out, lates),
        beside=[
            lambda done: grad_attn(cot_first, cot_second, output_projection, 0),
            lambda done: grad_attn(cot_first, cot_second, output_projection, 1, done),
        ],
    )
    grad_q, kv_parts = attention_backward(
        table, crops, query_rot, grad_dense, o_halves, attn_out, log_norm, cosine, sine, kvs, lates
    )
    grad_q_other = swap(grad_q, "tp", 1)
    reduced = kv_parts[0].astype(F32)
    for k in partners:
        reduced = reduced + swap(kv_parts[k], "ctx", k).astype(F32)
    reduced = jnp.concatenate(
        [turn(reduced[:, :HEAD_SIZE], cosine, -sine), reduced[:, HEAD_SIZE:]], axis=1
    )
    for bit_no in reversed(range(pair_bits)):
        half_cols = reduced.shape[1] // 2
        is_lower = tp_index // (1 << bit_no) % 2 == 0
        keep_part = jnp.where(is_lower, reduced[:, :half_cols], reduced[:, half_cols:])
        send_part = jnp.where(is_lower, reduced[:, half_cols:], reduced[:, :half_cols])
        reduced = keep_part + swap(send_part.astype(BF16), "tp", 1 << bit_no).astype(F32)
    grad_kv = reduced.astype(BF16)

    input_part = grad_input(
        table,
        grad_q,
        grad_q_other,
        grad_kv,
        swap(grad_kv, "tp", 1),
        query_projection,
        query_other,
        key_value_projection,
        kv_other,
        groups,
    )
    input_part, grad_q, grad_kv = lax.optimization_barrier((input_part, grad_q, grad_kv))
    input_sum = reduce_planes(input_part, groups)

    def send_ups(done):
        return up_grads(
            table, ctx_count, low_in, grad_q, grad_kv, o_halves, output_cotangent, attn_out
        )

    g_halves, up_sends = sum_halves(
        *low_g_part(table, grad_q, grad_kv, firsts), beside=[send_ups]
    )
    up_back = [up_sends[0]] + [swap(up_sends[k], "ctx", k) for k in partners]
    output = output_result(table, heads_sum, o_halves, lates)
    g_halves, up_back, output = lax.optimization_barrier((g_halves, up_back, output))
    down_sends, input_delta = down_grads(table, x_slice, g_halves, firsts)
    down_back = [down_sends[0]] + [swap(down_sends[k], "ctx", k) for k in partners]
    up_stores = store_ups(table, up_back, tenant_owner)
    down_back, up_stores = lax.optimization_barrier((down_back, up_stores))
    down_store = store_downs(table, down_back, tenant_owner)
    input_sum, input_delta, down_store = lax.optimization_barrier(
        (input_sum, input_delta, down_store)
    )
    hidden_input_gradient = (input_sum.astype(F32) + input_delta.astype(F32)).astype(BF16)
    return (
        output,
        hidden_input_gradient,
        down_store.swapaxes(1, 2),
        up_stores[0],
        up_stores[1],
        up_stores[2].swapaxes(1, 2),
        up_stores[3],
    )


def solution(mesh):
    in_specs = (
        P("ctx", None),
        P("ctx", "tp"),
        P(None, "tp"),
        P(None, "tp"),
        P("tp", None),
        P("ctx", "tp", None),
        P("ctx", None, "tp"),
        P("ctx", None, "tp"),
        P("ctx", "tp", None),
        P("ctx", None, "tp"),
        P(),
        P(),
        P(),
    )
    out_specs = (
        P("ctx", "tp"),
        P("ctx", "tp"),
        P("ctx", "tp", None),
        P("ctx", None, "tp"),
        P("ctx", None, "tp"),
        P("ctx", "tp", None),
        P("ctx", None, "tp"),
    )
    return jax.shard_map(body, mesh=mesh, in_specs=in_specs, out_specs=out_specs, check_vma=False)
```

```python
import functools
import math

import jax
import jax.numpy as jnp
from jax import lax
from jax.experimental import pallas as pl
from jax.experimental.pallas import tpu as pltpu
from jax.sharding import PartitionSpec as P

HEAD_SIZE = 128
KEY_VALUE_HEADS = 8
ADAPTER_RANK = 64
BLK = 128
NEG = -1e30
ROPE_BASE = 1000000.0
SCALE = HEAD_SIZE ** (-0.5)
LOG2E = math.log2(math.e)
SCALE2 = SCALE * LOG2E
VMEM_BYTES = 64 * 1024 * 1024
SMALL_VMEM_BYTES = 16 * 1024 * 1024

BF16 = jnp.bfloat16
F32 = jnp.float32


def params(limit=VMEM_BYTES):
    return pltpu.CompilerParams(vmem_limit_bytes=limit)


def cost(flops, bytes_accessed, transcendentals=0):
    return pl.CostEstimate(
        flops=int(flops), bytes_accessed=int(bytes_accessed), transcendentals=int(transcendentals)
    )


def dot_nn(a, b):
    return lax.dot_general(a, b, (((1,), (0,)), ((), ())), preferred_element_type=F32)


def dot_nt(a, b):
    return lax.dot_general(a, b, (((1,), (1,)), ((), ())), preferred_element_type=F32)


def dot_tn(a, b):
    return lax.dot_general(a, b, (((0,), (0,)), ((), ())), preferred_element_type=F32)


def swap(value, axis, mask):
    pairs = [(source, source ^ mask) for source in range(lax.axis_size(axis))]
    return lax.ppermute(value, axis, pairs)


def add_round(a, b):
    return (a.astype(F32) + b.astype(F32)).astype(BF16)


def rope_tables(positions):
    half_dim = HEAD_SIZE // 2
    exponent = jnp.arange(half_dim, dtype=F32) * (2.0 / HEAD_SIZE)
    frequency = jnp.exp(-exponent * math.log(ROPE_BASE))
    angles = positions.astype(F32)[:, None] * frequency[None, :]
    cosine, sine = jnp.cos(angles), jnp.sin(angles)
    return (
        jnp.concatenate([cosine, cosine], axis=1),
        jnp.concatenate([-sine, sine], axis=1),
    )


def turn(values, cosine, sine):
    return values * cosine + jnp.roll(values, HEAD_SIZE // 2, axis=1) * sine


def turn_kernel(values, cosine, sine):
    return values * cosine + pltpu.roll(values, HEAD_SIZE // 2, 1) * sine


def dense_kernel(x_ref, wq_ref, wkv_ref, q_ref, kv_ref):
    @pl.when(pl.program_id(0) == 0)
    def _():
        q_ref[...] = jnp.zeros_like(q_ref)
        kv_ref[...] = jnp.zeros_like(kv_ref)

    x = x_ref[...]
    q_ref[...] += dot_nn(x, wq_ref[...])
    kv_ref[...] += dot_nn(x, wkv_ref[...])


def dense_qkv(x, wq, wkv):
    rows, width = x.shape
    step = 2048
    cq, ckv = wq.shape[1], wkv.shape[1]
    return pl.pallas_call(
        dense_kernel,
        grid=(width // step,),
        in_specs=[
            pl.BlockSpec((rows, step), lambda i: (0, i)),
            pl.BlockSpec((step, cq), lambda i: (i, 0)),
            pl.BlockSpec((step, ckv), lambda i: (i, 0)),
        ],
        out_specs=[
            pl.BlockSpec((rows, cq), lambda i: (0, 0)),
            pl.BlockSpec((rows, ckv), lambda i: (0, 0)),
        ],
        out_shape=[
            jax.ShapeDtypeStruct((rows, cq), F32),
            jax.ShapeDtypeStruct((rows, ckv), F32),
        ],
        compiler_params=params(),
        cost_estimate=cost(2 * rows * width * (cq + ckv), 2 * width * (rows + cq + ckv)),
        name="dense_qkv",
    )(x, wq, wkv)


ENDS_AT = 2
SEND_AT = 16
SERVED_AT = 32
SOURCE_AT = 48
TABLE = 64


def serve_kernel(
    count, blocks, owned, crop_ref, tenant_ref, row_ref, cot, down, up_q, up_kv, up_o, down_o, *outs
):
    tab, cots = outs[0], outs[1:3]
    firsts, lates = outs[3 : 3 + count], outs[3 + count :]
    cots[0][...] = cot[: cots[0].shape[0], :]
    cots[1][...] = cot[cots[0].shape[0] :, :]
    me = lax.axis_index("ctx")
    for i in range(TABLE):
        tab[i] = 0
    tab[0] = me
    tab[1] = lax.axis_index("tp")
    end = jnp.int32(0)
    for i in range(crop_ref.shape[0]):
        end = end + crop_ref[i]
        tab[ENDS_AT + i] = end
    for b in range(blocks):
        row = row_ref[tenant_ref[me * blocks + b]]
        tab[SOURCE_AT + b] = (row // owned) ^ me
    for k in range(count):
        served = jnp.int32(-1)
        for b in range(blocks):
            row = row_ref[tenant_ref[(me ^ k) * blocks + b]]
            served = jnp.where(row // owned == me, row - me * owned, served)
        tab[SERVED_AT + k] = served
        tab[SEND_AT + k] = jnp.maximum(served, 0)
    rank, width = ADAPTER_RANK, down.shape[2]
    half, quarter = rank // 2, rank // 4
    cq, ckv = width // 2, width // 4
    for k in range(count):
        at = tab[SEND_AT + k]
        low = down.shape[1]
        firsts[k][:low, :] = down[at]
        for i in range(2):
            firsts[k][low : low + half, i * cq : (i + 1) * cq] = up_q[
                at, i * half : (i + 1) * half, :
            ]
            lates[k][rank : rank + half, i * cq : (i + 1) * cq] = down_o[
                at, i * half : (i + 1) * half, :
            ]
        for i in range(4):
            firsts[k][low + half :, i * ckv : (i + 1) * ckv] = up_kv[
                at, i * quarter : (i + 1) * quarter, :
            ]
        lates[k][:rank, :] = up_o[at]


def serve(count, blocks, crops, tenants, store_rows, cot, down, up_q, up_kv, up_o, down_o):
    rank, width = ADAPTER_RANK, down.shape[2]
    assert up_q.shape[2] * 2 == width and up_kv.shape[2] * 4 == width
    assert up_o.shape[2] == width and down_o.shape[2] * 2 == width
    smem = pl.BlockSpec(memory_space=pltpu.SMEM)
    vmem = pl.BlockSpec(memory_space=pltpu.VMEM)
    first = jax.ShapeDtypeStruct((3 * rank + rank // 2 + rank // 4, width), BF16)
    late = jax.ShapeDtypeStruct((rank + rank // 2, width), BF16)
    cut = cot.shape[0] // 384 * 208
    results = pl.pallas_call(
        functools.partial(serve_kernel, count, blocks, down.shape[0]),
        in_specs=[smem] * 3 + [vmem] * 6,
        out_specs=[smem] + [vmem] * (2 + 2 * count),
        out_shape=[jax.ShapeDtypeStruct((TABLE,), jnp.int32)]
        + [jax.ShapeDtypeStruct((n, cot.shape[1]), BF16) for n in (cut, cot.shape[0] - cut)]
        + [first] * count
        + [late] * count,
        compiler_params=params(),
        name="serve",
    )(crops, tenants, store_rows, cot, down, up_q, up_kv, up_o, down_o)
    return results[0], results[1:3], list(results[3 : 3 + count]), list(results[3 + count :])


def unpack_q(ref):
    rows, width = ref.shape
    value = ref[...]
    return jnp.concatenate([value[:, : width // 2], value[:, width // 2 :]], axis=0)


def unpack_kv(ref):
    rows, width = ref.shape
    value = ref[...]
    step = width // 4
    return jnp.concatenate([value[:, i * step : (i + 1) * step] for i in range(4)], axis=0)


def pick(tab_ref, block, count, step):
    for k in range(count):

        @pl.when(tab_ref[SOURCE_AT + block] == k)
        def _(k=k):
            step(k)


def split_rows(tab_ref, whole, mine, other):
    half = mine.shape[0]

    @pl.when(tab_ref[1] % 2 == 0)
    def _():
        mine[...] = whole[:half, :]
        other[...] = whole[half:, :]

    @pl.when(tab_ref[1] % 2 == 1)
    def _():
        mine[...] = whole[half:, :]
        other[...] = whole[:half, :]


def join_rows(tab_ref, mine, other, whole):
    half = mine.shape[0]

    @pl.when(tab_ref[1] % 2 == 0)
    def _():
        whole[:half, :] = mine[...]
        whole[half:, :] = other[...]

    @pl.when(tab_ref[1] % 2 == 1)
    def _():
        whole[:half, :] = other[...]
        whole[half:, :] = mine[...]


def sum_halves(mine, other, beside=()):
    total = add_round(mine, swap(other, "tp", 1))
    mask, done = 2, None
    beside = list(beside)
    while mask < lax.axis_size("tp"):
        arrived = swap(total, "tp", mask)
        if beside:
            done = beside.pop(0)(done)
            arrived, done = lax.optimization_barrier((arrived, done))
        total = add_round(total, arrived)
        mask *= 2
    while beside:
        done = beside.pop(0)(done)
    return (total, swap(total, "tp", 1)), done


def block_rows(b):
    return slice(b * BLK, (b + 1) * BLK)


def whole_spec(shape):
    return pl.BlockSpec(shape, lambda i, t: (0,) * len(shape))


def table_call(kernel, table, operands, shapes, scratch, name, flops=0, limit=VMEM_BYTES):
    moved = sum(math.prod(s.shape) * s.dtype.itemsize for s in operands + shapes)
    vmem = pl.BlockSpec(memory_space=pltpu.VMEM)
    return pl.pallas_call(
        kernel,
        in_specs=[pl.BlockSpec(memory_space=pltpu.SMEM)] + [vmem] * len(operands),
        out_specs=[vmem] * len(shapes),
        out_shape=shapes,
        scratch_shapes=scratch,
        compiler_params=params(limit),
        cost_estimate=cost(flops, moved),
        name=name,
    )(table, *operands)


def low_kernel(count, tab_ref, x_ref, *refs):
    downs = refs[:count]
    mine, other, whole = refs[count:]
    cols = whole.shape[1]
    for b in range(whole.shape[0] // BLK):

        def step(k, b=b):
            whole[block_rows(b), :] = dot_nt(x_ref[block_rows(b), :], downs[k][:cols, :]).astype(BF16)

        pick(tab_ref, b, count, step)
    split_rows(tab_ref, whole, mine, other)


def low_part(table, x, firsts):
    rows, width, cols = x.shape[0], firsts[0].shape[1], 3 * ADAPTER_RANK
    half = jax.ShapeDtypeStruct((rows // 2, cols), BF16)
    return table_call(
        functools.partial(low_kernel, len(firsts)),
        table,
        [x] + firsts,
        [half, half],
        [pltpu.VMEM((rows, cols), BF16)],
        "low_part",
        2 * rows * width * cols,
        SMALL_VMEM_BYTES,
    )


def finish_kv_kernel(count, rotate_keys, tab_ref, kv_ref, mine, other, cos_ref, sin_ref, *refs):
    ups = refs[:count]
    kvo, low = refs[count:]
    ckv = kv_ref.shape[1]
    rank = ADAPTER_RANK
    join_rows(tab_ref, mine, other, low)
    for b in range(kv_ref.shape[0] // BLK):

        def step(k, b=b):
            at_rows = block_rows(b)
            low_k = low[at_rows, rank : 2 * rank]
            low_v = low[at_rows, 2 * rank :]
            up_kv = unpack_kv(ups[k].at[3 * rank + rank // 2 :])
            for h in range(ckv // HEAD_SIZE):
                at = slice(h * HEAD_SIZE, (h + 1) * HEAD_SIZE)
                if rotate_keys:
                    term = dot_nn(low_v if h % 2 else low_k, up_kv[:, at])
                else:
                    is_value = (tab_ref[1] * (ckv // HEAD_SIZE) + h) % 2 == 1
                    term = jnp.where(
                        is_value, dot_nn(low_v, up_kv[:, at]), dot_nn(low_k, up_kv[:, at])
                    )
                piece = (kv_ref[at_rows, at] + term).astype(BF16)
                if rotate_keys and h % 2 == 0:
                    cosine, sine = cos_ref[at_rows, :], sin_ref[at_rows, :]
                    piece = turn_kernel(piece.astype(F32), cosine, sine).astype(BF16)
                kvo[at_rows, at] = piece

        pick(tab_ref, b, count, step)


def finish_kv(table, kv_lin, halves, firsts, cosine, sine, rotate_keys):
    rows, ckv = kv_lin.shape
    cols = 3 * ADAPTER_RANK
    operands = [kv_lin, *halves, cosine, sine]
    return table_call(
        functools.partial(finish_kv_kernel, len(firsts), rotate_keys),
        table,
        operands + firsts,
        [jax.ShapeDtypeStruct((rows, ckv), BF16), jax.ShapeDtypeStruct((rows, cols), BF16)],
        [],
        "finish_kv",
        4 * rows * ADAPTER_RANK * ckv,
    )


def finish_q_kernel(count, tab_ref, q_ref, low_ref, cos_ref, sin_ref, *refs):
    ups, qo = refs[:count], refs[count]
    cq = q_ref.shape[1]
    rank = ADAPTER_RANK
    for b in range(q_ref.shape[0] // BLK):

        def step(k, b=b):
            at_rows = block_rows(b)
            cosine, sine = cos_ref[at_rows, :], sin_ref[at_rows, :]
            up_q = unpack_q(ups[k].at[3 * rank : 3 * rank + rank // 2])
            query = q_ref[at_rows, :] + dot_nn(low_ref[at_rows, :rank], up_q)
            for h in range(cq // HEAD_SIZE):
                at = slice(h * HEAD_SIZE, (h + 1) * HEAD_SIZE)
                qo[at_rows, at] = turn_kernel(query[:, at], cosine, sine).astype(BF16)

        pick(tab_ref, b, count, step)


def finish_q(table, q_lin, low_in, firsts, cosine, sine):
    rows, cq = q_lin.shape
    operands = [q_lin, low_in, cosine, sine]
    return table_call(
        functools.partial(finish_q_kernel, len(firsts)),
        table,
        operands + firsts,
        [jax.ShapeDtypeStruct((rows, cq), BF16)],
        [],
        "finish_q",
        2 * rows * ADAPTER_RANK * cq,
        SMALL_VMEM_BYTES,
    )[0]


def low_o_kernel(count, tab_ref, cot_ref, attn_ref, *refs):
    lates = refs[:count]
    mine, other, whole = refs[count:]
    rank = ADAPTER_RANK
    for b in range(whole.shape[0] // BLK):

        def step(k, b=b):
            at = block_rows(b)
            whole[at, :rank] = dot_nt(cot_ref[at, :], lates[k][:rank, :]).astype(BF16)
            down = unpack_q(lates[k].at[rank:])
            whole[at, rank:] = dot_nt(attn_ref[at, :], down).astype(BF16)

        pick(tab_ref, b, count, step)
    split_rows(tab_ref, whole, mine, other)


def low_o_part(table, cot, attn, lates):
    rows, width = cot.shape
    cols = 2 * ADAPTER_RANK
    half = jax.ShapeDtypeStruct((rows // 2, cols), BF16)
    return table_call(
        functools.partial(low_o_kernel, len(lates)),
        table,
        [cot, attn] + lates,
        [half, half],
        [pltpu.VMEM((rows, cols), BF16)],
        "low_o_part",
        2 * rows * cols * width,
        SMALL_VMEM_BYTES,
    )


def low_g_kernel(count, tab_ref, gq_ref, gkv_ref, *refs):
    ups = refs[:count]
    mine, other, whole = refs[count:]
    rank = ADAPTER_RANK
    ckv = gkv_ref.shape[1]
    for b in range(whole.shape[0] // BLK):

        def step(k, b=b):
            at = block_rows(b)
            up_q = unpack_q(ups[k].at[3 * rank : 3 * rank + rank // 2])
            whole[at, :rank] = dot_nt(gq_ref[at, :], up_q).astype(BF16)
            up_kv = unpack_kv(ups[k].at[3 * rank + rank // 2 :])
            sums = [jnp.zeros((BLK, rank), F32)] * 2
            for h in range(ckv // HEAD_SIZE):
                cols = slice(h * HEAD_SIZE, (h + 1) * HEAD_SIZE)
                term = dot_nt(gkv_ref[at, cols], up_kv[:, cols])
                is_value = (tab_ref[1] * (ckv // HEAD_SIZE) + h) % 2 == 1
                sums[0] = sums[0] + jnp.where(is_value, 0.0, term)
                sums[1] = sums[1] + jnp.where(is_value, term, 0.0)
            whole[at, rank : 2 * rank] = sums[0].astype(BF16)
            whole[at, 2 * rank :] = sums[1].astype(BF16)

        pick(tab_ref, b, count, step)
    split_rows(tab_ref, whole, mine, other)


def low_g_part(table, gq, gkv, firsts):
    rows = gq.shape[0]
    cols, width = 3 * ADAPTER_RANK, firsts[0].shape[1]
    half = jax.ShapeDtypeStruct((rows // 2, cols), BF16)
    return table_call(
        functools.partial(low_g_kernel, len(firsts)),
        table,
        [gq, gkv] + firsts,
        [half, half],
        [pltpu.VMEM((rows, cols), BF16)],
        "low_g_part",
        2 * rows * width * ADAPTER_RANK,
    )


def zero_unused(tab_ref, blocks, sends):
    for k in range(len(sends)):
        used = tab_ref[SOURCE_AT] == k
        for b in range(1, blocks):
            used = used | (tab_ref[SOURCE_AT + b] == k)

        @pl.when(jnp.logical_not(used))
        def _(k=k):
            sends[k][...] = jnp.zeros_like(sends[k])


def up_grads_kernel(
    count, tab_ref, low_ref, gq_ref, gkv_ref, o_mine, o_other, cot, attn, *refs
):
    sends, low_o = refs[:count], refs[count]
    rank = ADAPTER_RANK
    join_rows(tab_ref, o_mine, o_other, low_o)
    blocks = low_o.shape[0] // BLK
    cq, ckv = gq_ref.shape[1], gkv_ref.shape[1]
    half, quarter = rank // 2, rank // 4
    late = half + quarter
    zero_unused(tab_ref, blocks, sends)
    for b in range(blocks):

        def step(k, b=b):
            at = block_rows(b)
            out = sends[k]
            up_q = dot_tn(low_ref[at, :rank], gq_ref[at, :]).astype(BF16)
            down_o = dot_tn(low_o[at, :rank], attn[at, :]).astype(BF16)
            for i in range(2):
                rows = slice(i * half, (i + 1) * half)
                cols = slice(i * cq, (i + 1) * cq)
                out[:half, cols] = up_q[rows, :]
                out[late + rank :, cols] = down_o[rows, :]
            for h in range(ckv // HEAD_SIZE):
                piece = slice(h * HEAD_SIZE, (h + 1) * HEAD_SIZE)
                is_value = (tab_ref[1] * (ckv // HEAD_SIZE) + h) % 2 == 1
                up_kv = jnp.where(
                    is_value,
                    dot_tn(low_ref[at, 2 * rank :], gkv_ref[at, piece]),
                    dot_tn(low_ref[at, rank : 2 * rank], gkv_ref[at, piece]),
                ).astype(BF16)
                for i in range(4):
                    cols = slice(i * ckv + h * HEAD_SIZE, i * ckv + (h + 1) * HEAD_SIZE)
                    out[half:late, cols] = up_kv[i * quarter : (i + 1) * quarter, :]
            out[late : late + rank, :] = dot_tn(low_o[at, rank:], cot[at, :]).astype(BF16)

        pick(tab_ref, b, count, step)


def up_grads(table, count, low_in, gq, gkv, o_halves, cot, attn):
    rows, width = cot.shape
    rank = ADAPTER_RANK
    operands = [low_in, gq, gkv, *o_halves, cot, attn]
    return list(
        table_call(
            functools.partial(up_grads_kernel, count),
            table,
            operands,
            [jax.ShapeDtypeStruct((2 * rank + rank // 4, width), BF16)] * count,
            [pltpu.VMEM((rows, 2 * rank), BF16)],
            "up_grads",
            2 * rows * width * 3 * rank,
        )
    )


def down_grads_kernel(count, tab_ref, x_ref, mine, other, *refs):
    downs, sends = refs[:count], refs[count : 2 * count]
    delta, low = refs[2 * count :]
    join_rows(tab_ref, mine, other, low)
    blocks = low.shape[0] // BLK
    zero_unused(tab_ref, blocks, sends)
    for b in range(blocks):

        def step(k, b=b):
            at = block_rows(b)
            sends[k][...] = dot_tn(low[at, :], x_ref[at, :]).astype(BF16)
            delta[at, :] = dot_nn(low[at, :], downs[k][: low.shape[1], :]).astype(BF16)

        pick(tab_ref, b, count, step)


def down_grads(table, x, halves, firsts):
    rows, cols = x.shape[0], 3 * ADAPTER_RANK
    width, count = firsts[0].shape[1], len(firsts)
    results = table_call(
        functools.partial(down_grads_kernel, count),
        table,
        [x, *halves] + firsts,
        [jax.ShapeDtypeStruct((cols, width), BF16)] * count
        + [jax.ShapeDtypeStruct((rows, width), BF16)],
        [pltpu.VMEM((rows, cols), BF16)],
        "down_grads",
        4 * rows * width * cols,
    )
    return list(results[:count]), results[count]


def store_kernel(count, pieces, tab_ref, *refs):
    arrived, outs = refs[:count], refs[count:]
    row = pl.program_id(0)
    for o in outs:
        o[...] = jnp.zeros_like(o)
    for k in range(count):

        @pl.when(tab_ref[SERVED_AT + k] == row)
        def _(k=k):
            for o, piece in zip(outs, pieces):
                o[0] += piece(arrived[k]).astype(F32)


def store_sums(table, arrived, owned, pieces, sizes):
    shapes = [jax.ShapeDtypeStruct((owned,) + size, F32) for size in sizes]
    return pl.pallas_call(
        functools.partial(store_kernel, len(arrived), pieces),
        grid_spec=pltpu.PrefetchScalarGridSpec(
            num_scalar_prefetch=1,
            grid=(owned,),
            in_specs=[pl.BlockSpec(a.shape, lambda i, t: (0, 0)) for a in arrived],
            out_specs=[pl.BlockSpec((1,) + s.shape[1:], lambda i, t: (i, 0, 0)) for s in shapes],
        ),
        out_shape=shapes,
        compiler_params=params(),
        name="store_sums",
    )(table, *arrived)


def store_ups(table, arrived, owned):
    rank, width = ADAPTER_RANK, arrived[0].shape[1]
    half, late = rank // 2, rank // 2 + rank // 4
    pieces = [
        lambda a: unpack_q(a.at[:half]),
        lambda a: unpack_kv(a.at[half:late]),
        lambda a: unpack_q(a.at[late + rank :]),
        lambda a: a[late : late + rank, :],
    ]
    sizes = [(rank, width // 2), (rank, width // 4), (rank, width // 2), (rank, width)]
    return store_sums(table, arrived, owned, pieces, sizes)


def store_downs(table, arrived, owned):
    return store_sums(table, arrived, owned, [lambda a: a[...]], [arrived[0].shape])[0]


def output_kernel(count, tab_ref, sum_ref, mine, other, *refs):
    lates = refs[:count]
    out, low = refs[count:]
    rank = ADAPTER_RANK
    join_rows(tab_ref, mine, other, low)
    for b in range(out.shape[0] // BLK):

        def step(k, b=b):
            at = block_rows(b)
            term = dot_nn(low[at, rank:], lates[k][:rank, :])
            out[at, :] = (sum_ref[at, :].astype(F32) + term).astype(BF16)

        pick(tab_ref, b, count, step)


def output_result(table, total, halves, lates):
    rows, width = total.shape
    rank = ADAPTER_RANK
    return table_call(
        functools.partial(output_kernel, len(lates)),
        table,
        [total, *halves] + lates,
        [jax.ShapeDtypeStruct((rows, width), BF16)],
        [pltpu.VMEM((rows, 2 * rank), BF16)],
        "output_result",
        2 * rows * rank * width,
    )[0]


def crop_start(tab_ref, crops, positions):
    start = jnp.zeros_like(positions)
    for i in range(crops):
        end = tab_ref[ENDS_AT + i]
        start = jnp.where(positions >= end, end, start)
    return start


def masked(scores, first, own, base):
    rows, cols = scores.shape
    key_pos = base + lax.broadcasted_iota(jnp.int32, (rows, cols), 0)
    allowed = key_pos >= first
    if own:
        allowed &= key_pos <= base + lax.broadcasted_iota(jnp.int32, (rows, cols), 1)
    return jnp.where(allowed, scores, NEG)


def each_chunk(tab_ref, crops, k, rows, step):
    if k == 0:
        step(True)
        return
    me = tab_ref[0]
    chunk = me ^ k
    seen = (chunk <= me) & ((chunk + 1) * rows > crop_start(tab_ref, crops, me * rows))
    inside = crop_start(tab_ref, crops, (me + 1) * rows - 1) <= chunk * rows
    pl.when(seen & inside)(lambda: step(False))
    pl.when(seen & jnp.logical_not(inside))(lambda: step(True))

    return seen


def query_starts(tab_ref, crops, rows):
    positions = tab_ref[0] * rows + lax.broadcasted_iota(jnp.int32, (1, rows), 1)
    return crop_start(tab_ref, crops, positions)


def forward_kernel(heads, count, crops, tab_ref, q_ref, *refs):
    kv_refs = refs[:count]
    out_ref, norm_ref, acc, top, total = refs[count:]
    rows = q_ref.shape[0]
    first = query_starts(tab_ref, crops, rows)
    for k in range(count):

        def chunk_step(with_mask, k=k):
            base = (tab_ref[0] ^ k) * rows
            keys = kv_refs[k][:, :HEAD_SIZE]
            values = kv_refs[k][:, HEAD_SIZE:]
            for h in range(heads):
                at = slice(h * HEAD_SIZE, (h + 1) * HEAD_SIZE)
                scores = dot_nt(keys, q_ref[:, at])
                if with_mask:
                    scores = masked(scores, first, k == 0, base)
                here = jnp.max(scores, axis=0, keepdims=True)
                if k == 0:
                    new_top = here
                else:
                    old_top = top[h : h + 1, :]
                    new_top = jnp.maximum(old_top, here)
                weights = jnp.exp2(scores * SCALE2 - new_top * SCALE2)
                here_sum = jnp.sum(weights, axis=0, keepdims=True)
                here_out = dot_tn(values, weights.astype(BF16))
                if k == 0:
                    total[h : h + 1, :] = here_sum
                    acc[h] = here_out
                else:
                    decay = jnp.exp2((old_top - new_top) * SCALE2)
                    total[h : h + 1, :] = total[h : h + 1, :] * decay + here_sum
                    acc[h] = acc[h] * decay + here_out
                top[h : h + 1, :] = new_top

        each_chunk(tab_ref, crops, k, rows, chunk_step)
    for h in range(heads):
        at = slice(h * HEAD_SIZE, (h + 1) * HEAD_SIZE)
        out_ref[:, at] = jnp.transpose(acc[h] / total[h : h + 1, :]).astype(BF16)
    norm_ref[...] = top[...] * SCALE2 + jnp.log(total[...]) * LOG2E


def attention_forward(table, crops, query, kvs):
    rows, cols = query.shape
    heads = cols // HEAD_SIZE
    count = len(kvs)
    smem = pl.BlockSpec(memory_space=pltpu.SMEM)
    vmem = pl.BlockSpec(memory_space=pltpu.VMEM)
    work = heads * rows * rows * count
    return pl.pallas_call(
        functools.partial(forward_kernel, heads, count, crops),
        in_specs=[smem] + [vmem] * (1 + count),
        out_specs=[vmem] * 2,
        out_shape=[
            jax.ShapeDtypeStruct((rows, cols), BF16),
            jax.ShapeDtypeStruct((heads, rows), F32),
        ],
        scratch_shapes=[
            pltpu.VMEM((heads, HEAD_SIZE, rows), F32),
            pltpu.VMEM((heads, rows), F32),
            pltpu.VMEM((heads, rows), F32),
        ],
        compiler_params=params(),
        cost_estimate=cost(4 * work * HEAD_SIZE, 4 * rows * cols * count, work),
        name="attention_forward",
    )(table, query, *kvs)


def backward_kernel(
    heads,
    count,
    crops,
    tab_ref,
    q_ref,
    dense_ref,
    mine,
    other,
    out_ref,
    norm_ref,
    cos_ref,
    sin_ref,
    *refs,
):
    kv_refs, lates = refs[:count], refs[count : 2 * count]
    gq_ref = refs[2 * count]
    gkv_refs = refs[2 * count + 1 : 3 * count + 1]
    acc, delta, low, grad_ref = refs[3 * count + 1 :]
    rows = q_ref.shape[0]
    rank = ADAPTER_RANK
    first = query_starts(tab_ref, crops, rows)
    join_rows(tab_ref, mine, other, low)
    for b in range(rows // BLK):

        def add(k, b=b):
            at = block_rows(b)
            term = dot_nn(low[at, :rank], unpack_q(lates[k].at[rank:]))
            grad_ref[at, :] = (dense_ref[at, :] + term).astype(BF16)

        pick(tab_ref, b, count, add)
    for h in range(heads):
        at = slice(h * HEAD_SIZE, (h + 1) * HEAD_SIZE)
        product = grad_ref[:, at].astype(F32) * out_ref[:, at].astype(F32)
        delta[h : h + 1, :] = jnp.sum(jnp.transpose(product), axis=0, keepdims=True)
    for k in range(count):

        def chunk_step(with_mask, k=k):
            base = (tab_ref[0] ^ k) * rows
            keys = kv_refs[k][:, :HEAD_SIZE]
            values = kv_refs[k][:, HEAD_SIZE:]
            key_grad = jnp.zeros((rows, HEAD_SIZE), F32)
            value_grad = jnp.zeros((rows, HEAD_SIZE), F32)
            for h in range(heads):
                at = slice(h * HEAD_SIZE, (h + 1) * HEAD_SIZE)
                scores = dot_nt(keys, q_ref[:, at])
                if with_mask:
                    scores = masked(scores, first, k == 0, base)
                weights = jnp.exp2(scores * SCALE2 - norm_ref[h : h + 1, :])
                value_grad += dot_nn(weights.astype(BF16), grad_ref[:, at])
                grad_weights = dot_nt(values, grad_ref[:, at])
                grad_scores = (weights * (grad_weights - delta[h : h + 1, :])).astype(BF16)
                key_grad += dot_nn(grad_scores, q_ref[:, at])
                here = dot_tn(keys, grad_scores)
                if k == 0:
                    acc[h] = here
                else:
                    acc[h] += here
            gkv_refs[k][:, :HEAD_SIZE] = (key_grad * SCALE).astype(BF16)
            gkv_refs[k][:, HEAD_SIZE:] = value_grad.astype(BF16)

        seen = each_chunk(tab_ref, crops, k, rows, chunk_step)
        if k:

            @pl.when(jnp.logical_not(seen))
            def _(k=k):
                gkv_refs[k][...] = jnp.zeros_like(gkv_refs[k])

    for h in range(heads):
        at = slice(h * HEAD_SIZE, (h + 1) * HEAD_SIZE)
        grad = jnp.transpose(acc[h]) * SCALE
        gq_ref[:, at] = turn_kernel(grad, cos_ref[...], -sin_ref[...]).astype(BF16)


def attention_backward(table, crops, query, dense, halves, out, norm, cosine, sine, kvs, lates):
    rows, cols = query.shape
    heads = cols // HEAD_SIZE
    count = len(kvs)
    smem = pl.BlockSpec(memory_space=pltpu.SMEM)
    vmem = pl.BlockSpec(memory_space=pltpu.VMEM)
    work = heads * rows * rows * count
    results = pl.pallas_call(
        functools.partial(backward_kernel, heads, count, crops),
        in_specs=[smem] + [vmem] * (8 + 2 * count),
        out_specs=[vmem] * (1 + count),
        out_shape=[jax.ShapeDtypeStruct((rows, cols), BF16)]
        + [jax.ShapeDtypeStruct((rows, 2 * HEAD_SIZE), BF16)] * count,
        scratch_shapes=[
            pltpu.VMEM((heads, HEAD_SIZE, rows), F32),
            pltpu.VMEM((heads, rows), F32),
            pltpu.VMEM((rows, 2 * ADAPTER_RANK), BF16),
            pltpu.VMEM((rows, cols), BF16),
        ],
        compiler_params=params(),
        cost_estimate=cost(10 * work * HEAD_SIZE, 8 * rows * cols * count, work),
        name="attention_backward",
    )(table, query, dense, *halves, out, norm, cosine, sine, *kvs, *lates)
    return results[0], list(results[1:])


def plane_spec(shape, axis, other):
    def index(i, t):
        core = t[1] % 2
        at = 2 * i + (1 - core if other else core)
        return (0, at) if axis else (at, 0)

    return pl.BlockSpec(shape, index)


def pick_kernel(tab_ref, w_ref, o_ref):
    o_ref[...] = w_ref[...]


def pick_planes(table, weight, groups, axis):
    planes = groups // 2
    shape = list(weight.shape)
    shape[axis] //= groups
    result = list(weight.shape)
    result[axis] //= 2
    return pl.pallas_call(
        pick_kernel,
        grid_spec=pltpu.PrefetchScalarGridSpec(
            num_scalar_prefetch=1,
            grid=(planes,),
            in_specs=[plane_spec(tuple(shape), axis, True)],
            out_specs=pl.BlockSpec(
                tuple(shape), (lambda i, t: (0, i)) if axis else (lambda i, t: (i, 0))
            ),
        ),
        out_shape=jax.ShapeDtypeStruct(tuple(result), BF16),
        compiler_params=params(),
        cost_estimate=cost(0, 2 * math.prod(weight.shape)),
        name="pick_planes",
    )(table, weight)


def reduce_planes(parts, groups):
    lines = [list(range(core, groups, 2)) for core in range(2)]
    return lax.psum_scatter(parts, "tp", scatter_dimension=0, axis_index_groups=lines, tiled=False)


def project_kernel(tab_ref, a_ref, ao_ref, w_ref, wo_ref, o_ref):
    total = dot_nn(a_ref[...], w_ref[...]) + dot_nn(ao_ref[...], wo_ref[...])
    o_ref[0] = total.astype(BF16)


def project_out(table, attn, attn_other, weight, weight_other, groups):
    rows, depth = attn.shape
    cols = weight.shape[1] // groups
    planes = groups // 2
    return pl.pallas_call(
        project_kernel,
        grid_spec=pltpu.PrefetchScalarGridSpec(
            num_scalar_prefetch=1,
            grid=(planes,),
            in_specs=[
                whole_spec(attn.shape),
                whole_spec(attn.shape),
                plane_spec((depth, cols), 1, False),
                pl.BlockSpec((depth, cols), lambda i, t: (0, i)),
            ],
            out_specs=pl.BlockSpec((1, rows, cols), lambda i, t: (i, 0, 0)),
        ),
        out_shape=jax.ShapeDtypeStruct((planes, rows, cols), BF16),
        compiler_params=params(),
        cost_estimate=cost(
            2 * rows * depth * cols * groups, 2 * (rows + 2 * depth) * cols * planes
        ),
        name="project_out",
    )(table, attn, attn_other, weight, weight_other)


PER_STEP = 2


def grad_attn_kernel(c0_ref, c1_ref, w_ref, *refs):
    before, o_ref = refs[:-1], refs[-1]
    step = pl.program_id(0)
    per_step, first_rows, cols = c0_ref.shape
    parts = ((c0_ref, slice(0, first_rows)), (c1_ref, slice(first_rows, o_ref.shape[0])))
    for c_ref, at in parts:
        total = dot_nt(c_ref[0], w_ref[:, :cols])
        for i in range(1, per_step):
            total += dot_nt(c_ref[i], w_ref[:, i * cols : (i + 1) * cols])

        @pl.when(step == 0)
        def _(at=at, total=total):
            o_ref[at, :] = total + before[0][at, :] if before else total

        @pl.when(step > 0)
        def _(at=at, total=total):
            o_ref[at, :] += total


def grad_attn(cot_first, cot_second, weight, half, before=None):
    groups, first_rows, cols = cot_first.shape
    depth = weight.shape[0]
    rows = first_rows + cot_second.shape[1]
    steps = groups // PER_STEP // 2
    start = half * steps
    whole = pl.BlockSpec((rows, depth), lambda i: (0, 0))
    return pl.pallas_call(
        grad_attn_kernel,
        grid=(steps,),
        in_specs=[
            pl.BlockSpec((PER_STEP, first_rows, cols), lambda i: (start + i, 0, 0)),
            pl.BlockSpec((PER_STEP, rows - first_rows, cols), lambda i: (start + i, 0, 0)),
            pl.BlockSpec((depth, PER_STEP * cols), lambda i: (0, start + i)),
        ]
        + ([] if before is None else [whole]),
        out_specs=whole,
        out_shape=jax.ShapeDtypeStruct((rows, depth), F32),
        compiler_params=params(),
        cost_estimate=cost(rows * depth * cols * groups, (rows + depth) * cols * groups),
        name="grad_attn",
    )(cot_first, cot_second, weight, *([] if before is None else [before]))


def grad_input_kernel(tab_ref, gq, gqo, gkv, gkvo, wq, wqo, wkv, wkvo, o_ref):
    total = dot_nt(gq[...], wq[...]) + dot_nt(gqo[...], wqo[...])
    total = total + dot_nt(gkv[...], wkv[...]) + dot_nt(gkvo[...], wkvo[...])
    o_ref[0] = total.astype(BF16)


def grad_input(table, gq, gq_other, gkv, gkv_other, wq, wq_other, wkv, wkv_other, groups):
    rows, cq = gq.shape
    ckv = gkv.shape[1]
    cols = wq.shape[0] // groups
    planes = groups // 2
    return pl.pallas_call(
        grad_input_kernel,
        grid_spec=pltpu.PrefetchScalarGridSpec(
            num_scalar_prefetch=1,
            grid=(planes,),
            in_specs=[
                whole_spec(gq.shape),
                whole_spec(gq.shape),
                whole_spec(gkv.shape),
                whole_spec(gkv.shape),
                plane_spec((cols, cq), 0, False),
                pl.BlockSpec((cols, cq), lambda i, t: (i, 0)),
                plane_spec((cols, ckv), 0, False),
                pl.BlockSpec((cols, ckv), lambda i, t: (i, 0)),
            ],
            out_specs=pl.BlockSpec((1, rows, cols), lambda i, t: (i, 0, 0)),
        ),
        out_shape=jax.ShapeDtypeStruct((planes, rows, cols), BF16),
        compiler_params=params(),
        cost_estimate=cost(
            2 * rows * (cq + ckv) * cols * groups,
            2 * (rows + 2 * (cq + ckv)) * cols * planes,
        ),
        name="grad_input",
    )(table, gq, gq_other, gkv, gkv_other, wq, wq_other, wkv, wkv_other)


def body(
    hidden_input,
    output_cotangent,
    query_projection,
    key_value_projection,
    output_projection,
    adapter_qkv_down_store,
    adapter_query_up,
    adapter_key_value_up,
    adapter_output_down,
    adapter_output_up,
    crop_token_length,
    tenant_per_block,
    tenant_store_row,
):
    ctx_count = lax.axis_size("ctx")
    tp_count = lax.axis_size("tp")
    ctx_index = lax.axis_index("ctx")
    tp_index = lax.axis_index("tp")
    rows_dev = hidden_input.shape[0]
    out_cols = output_cotangent.shape[1]
    tenant_owner = adapter_qkv_down_store.shape[0]
    blocks_dev = rows_dev // BLK
    pair_bits = (tp_count // KEY_VALUE_HEADS).bit_length() - 1
    groups = hidden_input.shape[1] // out_cols
    crops = crop_token_length.shape[0]
    partners = range(1, ctx_count)

    x_slice = lax.dynamic_slice_in_dim(hidden_input, tp_index * out_cols, out_cols, 1)

    table, cots, firsts, lates = serve(
        ctx_count,
        blocks_dev,
        crop_token_length,
        tenant_per_block,
        tenant_store_row,
        output_cotangent,
        adapter_qkv_down_store.swapaxes(1, 2),
        adapter_query_up,
        adapter_key_value_up,
        adapter_output_up,
        adapter_output_down.swapaxes(1, 2),
    )
    cot_first = lax.all_gather(cots[0], "tp", axis=0, tiled=False)
    firsts = [firsts[0]] + [swap(firsts[k], "ctx", k) for k in partners]
    my_pos = ctx_index * rows_dev + jnp.arange(rows_dev, dtype=jnp.int32)
    q_lin, kv_lin = dense_qkv(hidden_input, query_projection, key_value_projection)
    out_pick = pick_planes(table, output_projection, groups, 1)
    firsts, q_lin, kv_lin, tables, out_pick, x_slice = lax.optimization_barrier(
        (firsts, q_lin, kv_lin, rope_tables(my_pos), out_pick, x_slice)
    )
    cosine, sine = tables
    low_halves = low_part(table, x_slice, firsts)
    low_halves, (kv_pick, query_pick) = sum_halves(
        *low_halves,
        beside=[
            lambda done: pick_planes(table, key_value_projection, groups, 0),
            lambda done: (done, pick_planes(table, query_projection, groups, 0)),
        ],
    )
    low_halves, cot_rest = lax.optimization_barrier((low_halves, cots[1]))
    cot_second = lax.all_gather(cot_rest, "tp", axis=0, tiled=False)
    kv_local, low_in = finish_kv(
        table, kv_lin, low_halves, firsts, cosine, sine, pair_bits == 0
    )
    if pair_bits:
        for bit_no in range(pair_bits):
            partner = swap(kv_local, "tp", 1 << bit_no)
            is_lower = tp_index // (1 << bit_no) % 2 == 0
            kv_local = jnp.where(
                is_lower,
                jnp.concatenate([kv_local, partner], axis=1),
                jnp.concatenate([partner, kv_local], axis=1),
            )
        key_rot = turn(kv_local[:, :HEAD_SIZE].astype(F32), cosine, sine).astype(BF16)
        kv_local = jnp.concatenate([key_rot, kv_local[:, HEAD_SIZE:]], axis=1)
    kvs = [kv_local] + [swap(kv_local, "ctx", k) for k in partners]
    query_rot = finish_q(table, q_lin, low_in, firsts, cosine, sine)
    kvs, lates, query_rot = lax.optimization_barrier((kvs, lates, query_rot))
    out_other, query_other, kv_other = (
        swap(pick, "tp", 1) for pick in (out_pick, query_pick, kv_pick)
    )
    lates = [lates[0]] + [swap(lates[k], "ctx", k) for k in partners]

    attn_out, log_norm = attention_forward(table, crops, query_rot, kvs)
    lates, attn_out = lax.optimization_barrier((lates, attn_out))
    heads_part = project_out(
        table, attn_out, swap(attn_out, "tp", 1), output_projection, out_other, groups
    )
    heads_part, attn_out, cot_first = lax.optimization_barrier((heads_part, attn_out, cot_first))
    heads_sum = reduce_planes(heads_part, groups)
    o_halves, grad_dense = sum_halves(
        *low_o_part(table, output_cotangent, attn_out, lates),
        beside=[
            lambda done: grad_attn(cot_first, cot_second, output_projection, 0),
            lambda done: grad_attn(cot_first, cot_second, output_projection, 1, done),
        ],
    )
    grad_q, kv_parts = attention_backward(
        table, crops, query_rot, grad_dense, o_halves, attn_out, log_norm, cosine, sine, kvs, lates
    )
    grad_q_other = swap(grad_q, "tp", 1)
    reduced = kv_parts[0].astype(F32)
    for k in partners:
        reduced = reduced + swap(kv_parts[k], "ctx", k).astype(F32)
    reduced = jnp.concatenate(
        [turn(reduced[:, :HEAD_SIZE], cosine, -sine), reduced[:, HEAD_SIZE:]], axis=1
    )
    for bit_no in reversed(range(pair_bits)):
        half_cols = reduced.shape[1] // 2
        is_lower = tp_index // (1 << bit_no) % 2 == 0
        keep_part = jnp.where(is_lower, reduced[:, :half_cols], reduced[:, half_cols:])
        send_part = jnp.where(is_lower, reduced[:, half_cols:], reduced[:, :half_cols])
        reduced = keep_part + swap(send_part.astype(BF16), "tp", 1 << bit_no).astype(F32)
    grad_kv = reduced.astype(BF16)

    input_part = grad_input(
        table,
        grad_q,
        grad_q_other,
        grad_kv,
        swap(grad_kv, "tp", 1),
        query_projection,
        query_other,
        key_value_projection,
        kv_other,
        groups,
    )
    input_part, grad_q, grad_kv = lax.optimization_barrier((input_part, grad_q, grad_kv))
    input_sum = reduce_planes(input_part, groups)

    def send_ups(done):
        return up_grads(
            table, ctx_count, low_in, grad_q, grad_kv, o_halves, output_cotangent, attn_out
        )

    g_halves, up_sends = sum_halves(
        *low_g_part(table, grad_q, grad_kv, firsts), beside=[send_ups]
    )
    up_back = [up_sends[0]] + [swap(up_sends[k], "ctx", k) for k in partners]
    output = output_result(table, heads_sum, o_halves, lates)
    g_halves, up_back, output = lax.optimization_barrier((g_halves, up_back, output))
    down_sends, input_delta = down_grads(table, x_slice, g_halves, firsts)
    down_back = [down_sends[0]] + [swap(down_sends[k], "ctx", k) for k in partners]
    up_stores = store_ups(table, up_back, tenant_owner)
    down_back, up_stores = lax.optimization_barrier((down_back, up_stores))
    down_store = store_downs(table, down_back, tenant_owner)
    input_sum, input_delta, down_store = lax.optimization_barrier(
        (input_sum, input_delta, down_store)
    )
    hidden_input_gradient = (input_sum.astype(F32) + input_delta.astype(F32)).astype(BF16)
    return (
        output,
        hidden_input_gradient,
        down_store.swapaxes(1, 2),
        up_stores[0],
        up_stores[1],
        up_stores[2].swapaxes(1, 2),
        up_stores[3],
    )


def solution(mesh):
    in_specs = (
        P("ctx", None),
        P("ctx", "tp"),
        P(None, "tp"),
        P(None, "tp"),
        P("tp", None),
        P("ctx", "tp", None),
        P("ctx", None, "tp"),
        P("ctx", None, "tp"),
        P("ctx", "tp", None),
        P("ctx", None, "tp"),
        P(),
        P(),
        P(),
    )
    out_specs = (
        P("ctx", "tp"),
        P("ctx", "tp"),
        P("ctx", "tp", None),
        P("ctx", None, "tp"),
        P("ctx", None, "tp"),
        P("ctx", "tp", None),
        P("ctx", None, "tp"),
    )
    return jax.shard_map(body, mesh=mesh, in_specs=in_specs, out_specs=out_specs, check_vma=False)
```

```python
import functools
import math

import jax
import jax.numpy as jnp
from jax import lax
from jax.experimental import pallas as pl
from jax.experimental.pallas import tpu as pltpu
from jax.sharding import PartitionSpec as P

HEAD_SIZE = 128
KEY_VALUE_HEADS = 8
ADAPTER_RANK = 64
BLK = 128
NEG = -1e30
ROPE_BASE = 1000000.0
SCALE = HEAD_SIZE ** (-0.5)
LOG2E = math.log2(math.e)
SCALE2 = SCALE * LOG2E
VMEM_BYTES = 62 * 1024 * 1024
SMALL_VMEM_BYTES = 16 * 1024 * 1024

BF16 = jnp.bfloat16
F32 = jnp.float32


def params(limit=VMEM_BYTES):
    return pltpu.CompilerParams(vmem_limit_bytes=limit)


def cost(flops, bytes_accessed, transcendentals=0):
    return pl.CostEstimate(
        flops=int(flops), bytes_accessed=int(bytes_accessed), transcendentals=int(transcendentals)
    )


def dot_nn(a, b):
    return lax.dot_general(a, b, (((1,), (0,)), ((), ())), preferred_element_type=F32)


def dot_nt(a, b):
    return lax.dot_general(a, b, (((1,), (1,)), ((), ())), preferred_element_type=F32)


def dot_tn(a, b):
    return lax.dot_general(a, b, (((0,), (0,)), ((), ())), preferred_element_type=F32)


def swap(value, axis, mask):
    pairs = [(source, source ^ mask) for source in range(lax.axis_size(axis))]
    return lax.ppermute(value, axis, pairs)


def add_round(a, b):
    return (a.astype(F32) + b.astype(F32)).astype(BF16)


def rope_tables(positions):
    half_dim = HEAD_SIZE // 2
    exponent = jnp.arange(half_dim, dtype=F32) * (2.0 / HEAD_SIZE)
    frequency = jnp.exp(-exponent * math.log(ROPE_BASE))
    angles = positions.astype(F32)[:, None] * frequency[None, :]
    cosine, sine = jnp.cos(angles), jnp.sin(angles)
    return (
        jnp.concatenate([cosine, cosine], axis=1),
        jnp.concatenate([-sine, sine], axis=1),
    )


def turn(values, cosine, sine):
    return values * cosine + jnp.roll(values, HEAD_SIZE // 2, axis=1) * sine


def turn_kernel(values, cosine, sine):
    return values * cosine + pltpu.roll(values, HEAD_SIZE // 2, 1) * sine


def dense_kernel(x_ref, wq_ref, wkv_ref, q_ref, kv_ref):
    @pl.when(pl.program_id(0) == 0)
    def _():
        q_ref[...] = jnp.zeros_like(q_ref)
        kv_ref[...] = jnp.zeros_like(kv_ref)

    x = x_ref[...]
    q_ref[...] += dot_nn(x, wq_ref[...])
    kv_ref[...] += dot_nn(x, wkv_ref[...])


def dense_qkv(x, wq, wkv):
    rows, width = x.shape
    step = 2048
    cq, ckv = wq.shape[1], wkv.shape[1]
    return pl.pallas_call(
        dense_kernel,
        grid=(width // step,),
        in_specs=[
            pl.BlockSpec((rows, step), lambda i: (0, i)),
            pl.BlockSpec((step, cq), lambda i: (i, 0)),
            pl.BlockSpec((step, ckv), lambda i: (i, 0)),
        ],
        out_specs=[
            pl.BlockSpec((rows, cq), lambda i: (0, 0)),
            pl.BlockSpec((rows, ckv), lambda i: (0, 0)),
        ],
        out_shape=[
            jax.ShapeDtypeStruct((rows, cq), F32),
            jax.ShapeDtypeStruct((rows, ckv), F32),
        ],
        compiler_params=params(),
        cost_estimate=cost(2 * rows * width * (cq + ckv), 2 * width * (rows + cq + ckv)),
        name="dense_qkv",
    )(x, wq, wkv)


ENDS_AT = 2
SEND_AT = 16
SERVED_AT = 32
SOURCE_AT = 48
TABLE = 64


def serve_kernel(
    count, blocks, owned, crop_ref, tenant_ref, row_ref, cot, down, up_q, up_kv, up_o, down_o, *outs
):
    tab, cots = outs[0], outs[1:3]
    firsts, lates = outs[3 : 3 + count], outs[3 + count :]
    cots[0][...] = cot[: cots[0].shape[0], :]
    cots[1][...] = cot[cots[0].shape[0] :, :]
    me = lax.axis_index("ctx")
    for i in range(TABLE):
        tab[i] = 0
    tab[0] = me
    tab[1] = lax.axis_index("tp")
    end = jnp.int32(0)
    for i in range(crop_ref.shape[0]):
        end = end + crop_ref[i]
        tab[ENDS_AT + i] = end
    for b in range(blocks):
        row = row_ref[tenant_ref[me * blocks + b]]
        tab[SOURCE_AT + b] = (row // owned) ^ me
    for k in range(count):
        served = jnp.int32(-1)
        for b in range(blocks):
            row = row_ref[tenant_ref[(me ^ k) * blocks + b]]
            served = jnp.where(row // owned == me, row - me * owned, served)
        tab[SERVED_AT + k] = served
        tab[SEND_AT + k] = jnp.maximum(served, 0)
    rank, width = ADAPTER_RANK, down.shape[2]
    half, quarter = rank // 2, rank // 4
    cq, ckv = width // 2, width // 4
    for k in range(count):
        at = tab[SEND_AT + k]
        low = down.shape[1]
        firsts[k][:low, :] = down[at]
        for i in range(2):
            firsts[k][low : low + half, i * cq : (i + 1) * cq] = up_q[
                at, i * half : (i + 1) * half, :
            ]
            lates[k][rank : rank + half, i * cq : (i + 1) * cq] = down_o[
                at, i * half : (i + 1) * half, :
            ]
        for i in range(4):
            firsts[k][low + half :, i * ckv : (i + 1) * ckv] = up_kv[
                at, i * quarter : (i + 1) * quarter, :
            ]
        lates[k][:rank, :] = up_o[at]


def serve(count, blocks, crops, tenants, store_rows, cot, down, up_q, up_kv, up_o, down_o):
    rank, width = ADAPTER_RANK, down.shape[2]
    assert up_q.shape[2] * 2 == width and up_kv.shape[2] * 4 == width
    assert up_o.shape[2] == width and down_o.shape[2] * 2 == width
    smem = pl.BlockSpec(memory_space=pltpu.SMEM)
    vmem = pl.BlockSpec(memory_space=pltpu.VMEM)
    first = jax.ShapeDtypeStruct((3 * rank + rank // 2 + rank // 4, width), BF16)
    late = jax.ShapeDtypeStruct((rank + rank // 2, width), BF16)
    cut = cot.shape[0] // 384 * 224
    results = pl.pallas_call(
        functools.partial(serve_kernel, count, blocks, down.shape[0]),
        in_specs=[smem] * 3 + [vmem] * 6,
        out_specs=[smem] + [vmem] * (2 + 2 * count),
        out_shape=[jax.ShapeDtypeStruct((TABLE,), jnp.int32)]
        + [jax.ShapeDtypeStruct((n, cot.shape[1]), BF16) for n in (cut, cot.shape[0] - cut)]
        + [first] * count
        + [late] * count,
        compiler_params=params(),
        name="serve",
    )(crops, tenants, store_rows, cot, down, up_q, up_kv, up_o, down_o)
    return results[0], results[1:3], list(results[3 : 3 + count]), list(results[3 + count :])


def unpack_q(ref):
    rows, width = ref.shape
    value = ref[...]
    return jnp.concatenate([value[:, : width // 2], value[:, width // 2 :]], axis=0)


def unpack_kv(ref):
    rows, width = ref.shape
    value = ref[...]
    step = width // 4
    return jnp.concatenate([value[:, i * step : (i + 1) * step] for i in range(4)], axis=0)


def pick(tab_ref, block, count, step):
    for k in range(count):

        @pl.when(tab_ref[SOURCE_AT + block] == k)
        def _(k=k):
            step(k)


def split_rows(tab_ref, whole, mine, other):
    half = mine.shape[0]

    @pl.when(tab_ref[1] % 2 == 0)
    def _():
        mine[...] = whole[:half, :]
        other[...] = whole[half:, :]

    @pl.when(tab_ref[1] % 2 == 1)
    def _():
        mine[...] = whole[half:, :]
        other[...] = whole[:half, :]


def join_rows(tab_ref, mine, other, whole):
    half = mine.shape[0]

    @pl.when(tab_ref[1] % 2 == 0)
    def _():
        whole[:half, :] = mine[...]
        whole[half:, :] = other[...]

    @pl.when(tab_ref[1] % 2 == 1)
    def _():
        whole[:half, :] = other[...]
        whole[half:, :] = mine[...]


def sum_halves(mine, other, beside=()):
    total = add_round(mine, swap(other, "tp", 1))
    mask, done = 2, None
    beside = list(beside)
    while mask < lax.axis_size("tp"):
        arrived = swap(total, "tp", mask)
        if beside:
            done = beside.pop(0)(done)
            arrived, done = lax.optimization_barrier((arrived, done))
        total = add_round(total, arrived)
        mask *= 2
    while beside:
        done = beside.pop(0)(done)
    return (total, swap(total, "tp", 1)), done


def block_rows(b):
    return slice(b * BLK, (b + 1) * BLK)


def whole_spec(shape):
    return pl.BlockSpec(shape, lambda i, t: (0,) * len(shape))


def table_call(kernel, table, operands, shapes, scratch, name, flops=0, limit=VMEM_BYTES):
    moved = sum(math.prod(s.shape) * s.dtype.itemsize for s in operands + shapes)
    vmem = pl.BlockSpec(memory_space=pltpu.VMEM)
    return pl.pallas_call(
        kernel,
        in_specs=[pl.BlockSpec(memory_space=pltpu.SMEM)] + [vmem] * len(operands),
        out_specs=[vmem] * len(shapes),
        out_shape=shapes,
        scratch_shapes=scratch,
        compiler_params=params(limit),
        cost_estimate=cost(flops, moved),
        name=name,
    )(table, *operands)


def low_kernel(count, tab_ref, x_ref, *refs):
    downs = refs[:count]
    mine, other, whole = refs[count:]
    cols = whole.shape[1]
    for b in range(whole.shape[0] // BLK):

        def step(k, b=b):
            whole[block_rows(b), :] = dot_nt(x_ref[block_rows(b), :], downs[k][:cols, :]).astype(BF16)

        pick(tab_ref, b, count, step)
    split_rows(tab_ref, whole, mine, other)


def low_part(table, x, firsts):
    rows, width, cols = x.shape[0], firsts[0].shape[1], 3 * ADAPTER_RANK
    half = jax.ShapeDtypeStruct((rows // 2, cols), BF16)
    return table_call(
        functools.partial(low_kernel, len(firsts)),
        table,
        [x] + firsts,
        [half, half],
        [pltpu.VMEM((rows, cols), BF16)],
        "low_part",
        2 * rows * width * cols,
        SMALL_VMEM_BYTES,
    )


def finish_kv_kernel(count, rotate_keys, tab_ref, kv_ref, mine, other, cos_ref, sin_ref, *refs):
    ups = refs[:count]
    kvo, low = refs[count:]
    ckv = kv_ref.shape[1]
    rank = ADAPTER_RANK
    join_rows(tab_ref, mine, other, low)
    for b in range(kv_ref.shape[0] // BLK):

        def step(k, b=b):
            at_rows = block_rows(b)
            low_k = low[at_rows, rank : 2 * rank]
            low_v = low[at_rows, 2 * rank :]
            up_kv = unpack_kv(ups[k].at[3 * rank + rank // 2 :])
            for h in range(ckv // HEAD_SIZE):
                at = slice(h * HEAD_SIZE, (h + 1) * HEAD_SIZE)
                if rotate_keys:
                    term = dot_nn(low_v if h % 2 else low_k, up_kv[:, at])
                else:
                    is_value = (tab_ref[1] * (ckv // HEAD_SIZE) + h) % 2 == 1
                    term = jnp.where(
                        is_value, dot_nn(low_v, up_kv[:, at]), dot_nn(low_k, up_kv[:, at])
                    )
                piece = (kv_ref[at_rows, at] + term).astype(BF16)
                if rotate_keys and h % 2 == 0:
                    cosine, sine = cos_ref[at_rows, :], sin_ref[at_rows, :]
                    piece = turn_kernel(piece.astype(F32), cosine, sine).astype(BF16)
                kvo[at_rows, at] = piece

        pick(tab_ref, b, count, step)


def finish_kv(table, kv_lin, halves, firsts, cosine, sine, rotate_keys):
    rows, ckv = kv_lin.shape
    cols = 3 * ADAPTER_RANK
    operands = [kv_lin, *halves, cosine, sine]
    return table_call(
        functools.partial(finish_kv_kernel, len(firsts), rotate_keys),
        table,
        operands + firsts,
        [jax.ShapeDtypeStruct((rows, ckv), BF16), jax.ShapeDtypeStruct((rows, cols), BF16)],
        [],
        "finish_kv",
        4 * rows * ADAPTER_RANK * ckv,
    )


def finish_q_kernel(count, tab_ref, q_ref, low_ref, cos_ref, sin_ref, *refs):
    ups, qo = refs[:count], refs[count]
    cq = q_ref.shape[1]
    rank = ADAPTER_RANK
    for b in range(q_ref.shape[0] // BLK):

        def step(k, b=b):
            at_rows = block_rows(b)
            cosine, sine = cos_ref[at_rows, :], sin_ref[at_rows, :]
            up_q = unpack_q(ups[k].at[3 * rank : 3 * rank + rank // 2])
            query = q_ref[at_rows, :] + dot_nn(low_ref[at_rows, :rank], up_q)
            for h in range(cq // HEAD_SIZE):
                at = slice(h * HEAD_SIZE, (h + 1) * HEAD_SIZE)
                qo[at_rows, at] = turn_kernel(query[:, at], cosine, sine).astype(BF16)

        pick(tab_ref, b, count, step)


def finish_q(table, q_lin, low_in, firsts, cosine, sine):
    rows, cq = q_lin.shape
    operands = [q_lin, low_in, cosine, sine]
    return table_call(
        functools.partial(finish_q_kernel, len(firsts)),
        table,
        operands + firsts,
        [jax.ShapeDtypeStruct((rows, cq), BF16)],
        [],
        "finish_q",
        2 * rows * ADAPTER_RANK * cq,
        SMALL_VMEM_BYTES,
    )[0]


def low_o_kernel(count, tab_ref, cot_ref, attn_ref, *refs):
    lates = refs[:count]
    mine, other, whole = refs[count:]
    rank = ADAPTER_RANK
    for b in range(whole.shape[0] // BLK):

        def step(k, b=b):
            at = block_rows(b)
            whole[at, :rank] = dot_nt(cot_ref[at, :], lates[k][:rank, :]).astype(BF16)
            down = unpack_q(lates[k].at[rank:])
            whole[at, rank:] = dot_nt(attn_ref[at, :], down).astype(BF16)

        pick(tab_ref, b, count, step)
    split_rows(tab_ref, whole, mine, other)


def low_o_part(table, cot, attn, lates):
    rows, width = cot.shape
    cols = 2 * ADAPTER_RANK
    half = jax.ShapeDtypeStruct((rows // 2, cols), BF16)
    return table_call(
        functools.partial(low_o_kernel, len(lates)),
        table,
        [cot, attn] + lates,
        [half, half],
        [pltpu.VMEM((rows, cols), BF16)],
        "low_o_part",
        2 * rows * cols * width,
        SMALL_VMEM_BYTES,
    )


def low_g_kernel(count, tab_ref, gq_ref, gkv_ref, *refs):
    ups = refs[:count]
    mine, other, whole = refs[count:]
    rank = ADAPTER_RANK
    ckv = gkv_ref.shape[1]
    for b in range(whole.shape[0] // BLK):

        def step(k, b=b):
            at = block_rows(b)
            up_q = unpack_q(ups[k].at[3 * rank : 3 * rank + rank // 2])
            whole[at, :rank] = dot_nt(gq_ref[at, :], up_q).astype(BF16)
            up_kv = unpack_kv(ups[k].at[3 * rank + rank // 2 :])
            sums = [jnp.zeros((BLK, rank), F32)] * 2
            for h in range(ckv // HEAD_SIZE):
                cols = slice(h * HEAD_SIZE, (h + 1) * HEAD_SIZE)
                term = dot_nt(gkv_ref[at, cols], up_kv[:, cols])
                is_value = (tab_ref[1] * (ckv // HEAD_SIZE) + h) % 2 == 1
                sums[0] = sums[0] + jnp.where(is_value, 0.0, term)
                sums[1] = sums[1] + jnp.where(is_value, term, 0.0)
            whole[at, rank : 2 * rank] = sums[0].astype(BF16)
            whole[at, 2 * rank :] = sums[1].astype(BF16)

        pick(tab_ref, b, count, step)
    split_rows(tab_ref, whole, mine, other)


def low_g_part(table, gq, gkv, firsts):
    rows = gq.shape[0]
    cols, width = 3 * ADAPTER_RANK, firsts[0].shape[1]
    half = jax.ShapeDtypeStruct((rows // 2, cols), BF16)
    return table_call(
        functools.partial(low_g_kernel, len(firsts)),
        table,
        [gq, gkv] + firsts,
        [half, half],
        [pltpu.VMEM((rows, cols), BF16)],
        "low_g_part",
        2 * rows * width * ADAPTER_RANK,
    )


def zero_unused(tab_ref, blocks, sends):
    for k in range(len(sends)):
        used = tab_ref[SOURCE_AT] == k
        for b in range(1, blocks):
            used = used | (tab_ref[SOURCE_AT + b] == k)

        @pl.when(jnp.logical_not(used))
        def _(k=k):
            sends[k][...] = jnp.zeros_like(sends[k])


def up_grads_kernel(
    count, tab_ref, low_ref, gq_ref, gkv_ref, o_mine, o_other, cot, attn, *refs
):
    sends, low_o = refs[:count], refs[count]
    rank = ADAPTER_RANK
    join_rows(tab_ref, o_mine, o_other, low_o)
    blocks = low_o.shape[0] // BLK
    cq, ckv = gq_ref.shape[1], gkv_ref.shape[1]
    half, quarter = rank // 2, rank // 4
    late = half + quarter
    zero_unused(tab_ref, blocks, sends)
    for b in range(blocks):

        def step(k, b=b):
            at = block_rows(b)
            out = sends[k]
            up_q = dot_tn(low_ref[at, :rank], gq_ref[at, :]).astype(BF16)
            down_o = dot_tn(low_o[at, :rank], attn[at, :]).astype(BF16)
            for i in range(2):
                rows = slice(i * half, (i + 1) * half)
                cols = slice(i * cq, (i + 1) * cq)
                out[:half, cols] = up_q[rows, :]
                out[late + rank :, cols] = down_o[rows, :]
            for h in range(ckv // HEAD_SIZE):
                piece = slice(h * HEAD_SIZE, (h + 1) * HEAD_SIZE)
                is_value = (tab_ref[1] * (ckv // HEAD_SIZE) + h) % 2 == 1
                up_kv = jnp.where(
                    is_value,
                    dot_tn(low_ref[at, 2 * rank :], gkv_ref[at, piece]),
                    dot_tn(low_ref[at, rank : 2 * rank], gkv_ref[at, piece]),
                ).astype(BF16)
                for i in range(4):
                    cols = slice(i * ckv + h * HEAD_SIZE, i * ckv + (h + 1) * HEAD_SIZE)
                    out[half:late, cols] = up_kv[i * quarter : (i + 1) * quarter, :]
            out[late : late + rank, :] = dot_tn(low_o[at, rank:], cot[at, :]).astype(BF16)

        pick(tab_ref, b, count, step)


def up_grads(table, count, low_in, gq, gkv, o_halves, cot, attn):
    rows, width = cot.shape
    rank = ADAPTER_RANK
    operands = [low_in, gq, gkv, *o_halves, cot, attn]
    return list(
        table_call(
            functools.partial(up_grads_kernel, count),
            table,
            operands,
            [jax.ShapeDtypeStruct((2 * rank + rank // 4, width), BF16)] * count,
            [pltpu.VMEM((rows, 2 * rank), BF16)],
            "up_grads",
            2 * rows * width * 3 * rank,
        )
    )


def down_grads_kernel(count, tab_ref, x_ref, mine, other, *refs):
    downs, sends = refs[:count], refs[count : 2 * count]
    delta, low = refs[2 * count :]
    join_rows(tab_ref, mine, other, low)
    blocks = low.shape[0] // BLK
    zero_unused(tab_ref, blocks, sends)
    for b in range(blocks):

        def step(k, b=b):
            at = block_rows(b)
            sends[k][...] = dot_tn(low[at, :], x_ref[at, :]).astype(BF16)
            delta[at, :] = dot_nn(low[at, :], downs[k][: low.shape[1], :]).astype(BF16)

        pick(tab_ref, b, count, step)


def down_grads(table, x, halves, firsts):
    rows, cols = x.shape[0], 3 * ADAPTER_RANK
    width, count = firsts[0].shape[1], len(firsts)
    results = table_call(
        functools.partial(down_grads_kernel, count),
        table,
        [x, *halves] + firsts,
        [jax.ShapeDtypeStruct((cols, width), BF16)] * count
        + [jax.ShapeDtypeStruct((rows, width), BF16)],
        [pltpu.VMEM((rows, cols), BF16)],
        "down_grads",
        4 * rows * width * cols,
    )
    return list(results[:count]), results[count]


def store_kernel(count, pieces, tab_ref, *refs):
    arrived, outs = refs[:count], refs[count:]
    row = pl.program_id(0)
    for o in outs:
        o[...] = jnp.zeros_like(o)
    for k in range(count):

        @pl.when(tab_ref[SERVED_AT + k] == row)
        def _(k=k):
            for o, piece in zip(outs, pieces):
                o[0] += piece(arrived[k]).astype(F32)


def store_sums(table, arrived, owned, pieces, sizes):
    shapes = [jax.ShapeDtypeStruct((owned,) + size, F32) for size in sizes]
    return pl.pallas_call(
        functools.partial(store_kernel, len(arrived), pieces),
        grid_spec=pltpu.PrefetchScalarGridSpec(
            num_scalar_prefetch=1,
            grid=(owned,),
            in_specs=[pl.BlockSpec(a.shape, lambda i, t: (0, 0)) for a in arrived],
            out_specs=[pl.BlockSpec((1,) + s.shape[1:], lambda i, t: (i, 0, 0)) for s in shapes],
        ),
        out_shape=shapes,
        compiler_params=params(),
        name="store_sums",
    )(table, *arrived)


def store_ups(table, arrived, owned):
    rank, width = ADAPTER_RANK, arrived[0].shape[1]
    half, late = rank // 2, rank // 2 + rank // 4
    pieces = [
        lambda a: unpack_q(a.at[:half]),
        lambda a: unpack_kv(a.at[half:late]),
        lambda a: unpack_q(a.at[late + rank :]),
        lambda a: a[late : late + rank, :],
    ]
    sizes = [(rank, width // 2), (rank, width // 4), (rank, width // 2), (rank, width)]
    return store_sums(table, arrived, owned, pieces, sizes)


def store_downs(table, arrived, owned):
    return store_sums(table, arrived, owned, [lambda a: a[...]], [arrived[0].shape])[0]


def output_kernel(count, tab_ref, sum_ref, mine, other, *refs):
    lates = refs[:count]
    out, low = refs[count:]
    rank = ADAPTER_RANK
    join_rows(tab_ref, mine, other, low)
    for b in range(out.shape[0] // BLK):

        def step(k, b=b):
            at = block_rows(b)
            term = dot_nn(low[at, rank:], lates[k][:rank, :])
            out[at, :] = (sum_ref[at, :].astype(F32) + term).astype(BF16)

        pick(tab_ref, b, count, step)


def output_result(table, total, halves, lates):
    rows, width = total.shape
    rank = ADAPTER_RANK
    return table_call(
        functools.partial(output_kernel, len(lates)),
        table,
        [total, *halves] + lates,
        [jax.ShapeDtypeStruct((rows, width), BF16)],
        [pltpu.VMEM((rows, 2 * rank), BF16)],
        "output_result",
        2 * rows * rank * width,
    )[0]


def crop_start(tab_ref, crops, positions):
    start = jnp.zeros_like(positions)
    for i in range(crops):
        end = tab_ref[ENDS_AT + i]
        start = jnp.where(positions >= end, end, start)
    return start


def masked(scores, first, own, base):
    rows, cols = scores.shape
    key_pos = base + lax.broadcasted_iota(jnp.int32, (rows, cols), 0)
    allowed = key_pos >= first
    if own:
        allowed &= key_pos <= base + lax.broadcasted_iota(jnp.int32, (rows, cols), 1)
    return jnp.where(allowed, scores, NEG)


def chunk_on(tab_ref, crops, k, rows):
    me = tab_ref[0]
    chunk = me ^ k
    return (chunk <= me) & ((chunk + 1) * rows > crop_start(tab_ref, crops, me * rows))


def query_starts(tab_ref, crops, rows):
    positions = tab_ref[0] * rows + lax.broadcasted_iota(jnp.int32, (1, rows), 1)
    return crop_start(tab_ref, crops, positions)


def forward_kernel(heads, count, crops, tab_ref, q_ref, *refs):
    kv_refs = refs[:count]
    out_ref, norm_ref, acc, top, total = refs[count:]
    rows = q_ref.shape[0]
    first = query_starts(tab_ref, crops, rows)
    for k in range(count):

        def chunk_step(k=k):
            base = (tab_ref[0] ^ k) * rows
            keys = kv_refs[k][:, :HEAD_SIZE]
            values = kv_refs[k][:, HEAD_SIZE:]
            for h in range(heads):
                at = slice(h * HEAD_SIZE, (h + 1) * HEAD_SIZE)
                scores = masked(dot_nt(keys, q_ref[:, at]), first, k == 0, base)
                here = jnp.max(scores, axis=0, keepdims=True)
                if k == 0:
                    new_top = here
                else:
                    old_top = top[h : h + 1, :]
                    new_top = jnp.maximum(old_top, here)
                weights = jnp.exp2(scores * SCALE2 - new_top * SCALE2)
                here_sum = jnp.sum(weights, axis=0, keepdims=True)
                here_out = dot_tn(values, weights.astype(BF16))
                if k == 0:
                    total[h : h + 1, :] = here_sum
                    acc[h] = here_out
                else:
                    decay = jnp.exp2((old_top - new_top) * SCALE2)
                    total[h : h + 1, :] = total[h : h + 1, :] * decay + here_sum
                    acc[h] = acc[h] * decay + here_out
                top[h : h + 1, :] = new_top

        if k == 0:
            chunk_step()
        else:
            pl.when(chunk_on(tab_ref, crops, k, rows))(chunk_step)
    for h in range(heads):
        at = slice(h * HEAD_SIZE, (h + 1) * HEAD_SIZE)
        out_ref[:, at] = jnp.transpose(acc[h] / total[h : h + 1, :]).astype(BF16)
    norm_ref[...] = top[...] * SCALE2 + jnp.log(total[...]) * LOG2E


def attention_forward(table, crops, query, kvs):
    rows, cols = query.shape
    heads = cols // HEAD_SIZE
    count = len(kvs)
    smem = pl.BlockSpec(memory_space=pltpu.SMEM)
    vmem = pl.BlockSpec(memory_space=pltpu.VMEM)
    work = heads * rows * rows * count
    return pl.pallas_call(
        functools.partial(forward_kernel, heads, count, crops),
        in_specs=[smem] + [vmem] * (1 + count),
        out_specs=[vmem] * 2,
        out_shape=[
            jax.ShapeDtypeStruct((rows, cols), BF16),
            jax.ShapeDtypeStruct((heads, rows), F32),
        ],
        scratch_shapes=[
            pltpu.VMEM((heads, HEAD_SIZE, rows), F32),
            pltpu.VMEM((heads, rows), F32),
            pltpu.VMEM((heads, rows), F32),
        ],
        compiler_params=params(),
        cost_estimate=cost(4 * work * HEAD_SIZE, 4 * rows * cols * count, work),
        name="attention_forward",
    )(table, query, *kvs)


def backward_kernel(
    heads,
    count,
    crops,
    tab_ref,
    q_ref,
    dense_ref,
    mine,
    other,
    out_ref,
    norm_ref,
    cos_ref,
    sin_ref,
    *refs,
):
    kv_refs, lates = refs[:count], refs[count : 2 * count]
    gq_ref = refs[2 * count]
    gkv_refs = refs[2 * count + 1 : 3 * count + 1]
    acc, delta, low, grad_ref = refs[3 * count + 1 :]
    rows = q_ref.shape[0]
    rank = ADAPTER_RANK
    first = query_starts(tab_ref, crops, rows)
    join_rows(tab_ref, mine, other, low)
    for b in range(rows // BLK):

        def add(k, b=b):
            at = block_rows(b)
            term = dot_nn(low[at, :rank], unpack_q(lates[k].at[rank:]))
            grad_ref[at, :] = (dense_ref[at, :] + term).astype(BF16)

        pick(tab_ref, b, count, add)
    for h in range(heads):
        at = slice(h * HEAD_SIZE, (h + 1) * HEAD_SIZE)
        product = grad_ref[:, at].astype(F32) * out_ref[:, at].astype(F32)
        delta[h : h + 1, :] = jnp.sum(jnp.transpose(product), axis=0, keepdims=True)
    for k in range(count):

        def chunk_step(k=k):
            base = (tab_ref[0] ^ k) * rows
            keys = kv_refs[k][:, :HEAD_SIZE]
            values = kv_refs[k][:, HEAD_SIZE:]
            key_grad = jnp.zeros((rows, HEAD_SIZE), F32)
            value_grad = jnp.zeros((rows, HEAD_SIZE), F32)
            for h in range(heads):
                at = slice(h * HEAD_SIZE, (h + 1) * HEAD_SIZE)
                scores = masked(dot_nt(keys, q_ref[:, at]), first, k == 0, base)
                weights = jnp.exp2(scores * SCALE2 - norm_ref[h : h + 1, :])
                value_grad += dot_nn(weights.astype(BF16), grad_ref[:, at])
                grad_weights = dot_nt(values, grad_ref[:, at])
                grad_scores = (weights * (grad_weights - delta[h : h + 1, :])).astype(BF16)
                key_grad += dot_nn(grad_scores, q_ref[:, at])
                here = dot_tn(keys, grad_scores)
                if k == 0:
                    acc[h] = here
                else:
                    acc[h] += here
            gkv_refs[k][:, :HEAD_SIZE] = (key_grad * SCALE).astype(BF16)
            gkv_refs[k][:, HEAD_SIZE:] = value_grad.astype(BF16)

        if k == 0:
            chunk_step()
        else:
            on = chunk_on(tab_ref, crops, k, rows)
            pl.when(on)(chunk_step)

            @pl.when(jnp.logical_not(on))
            def _(k=k):
                gkv_refs[k][...] = jnp.zeros_like(gkv_refs[k])

    for h in range(heads):
        at = slice(h * HEAD_SIZE, (h + 1) * HEAD_SIZE)
        grad = jnp.transpose(acc[h]) * SCALE
        gq_ref[:, at] = turn_kernel(grad, cos_ref[...], -sin_ref[...]).astype(BF16)


def attention_backward(table, crops, query, dense, halves, out, norm, cosine, sine, kvs, lates):
    rows, cols = query.shape
    heads = cols // HEAD_SIZE
    count = len(kvs)
    smem = pl.BlockSpec(memory_space=pltpu.SMEM)
    vmem = pl.BlockSpec(memory_space=pltpu.VMEM)
    work = heads * rows * rows * count
    results = pl.pallas_call(
        functools.partial(backward_kernel, heads, count, crops),
        in_specs=[smem] + [vmem] * (8 + 2 * count),
        out_specs=[vmem] * (1 + count),
        out_shape=[jax.ShapeDtypeStruct((rows, cols), BF16)]
        + [jax.ShapeDtypeStruct((rows, 2 * HEAD_SIZE), BF16)] * count,
        scratch_shapes=[
            pltpu.VMEM((heads, HEAD_SIZE, rows), F32),
            pltpu.VMEM((heads, rows), F32),
            pltpu.VMEM((rows, 2 * ADAPTER_RANK), BF16),
            pltpu.VMEM((rows, cols), BF16),
        ],
        compiler_params=params(),
        cost_estimate=cost(10 * work * HEAD_SIZE, 8 * rows * cols * count, work),
        name="attention_backward",
    )(table, query, dense, *halves, out, norm, cosine, sine, *kvs, *lates)
    return results[0], list(results[1:])


def plane_spec(shape, axis, other):
    def index(i, t):
        core = t[1] % 2
        at = 2 * i + (1 - core if other else core)
        return (0, at) if axis else (at, 0)

    return pl.BlockSpec(shape, index)


def pick_kernel(tab_ref, w_ref, o_ref):
    o_ref[...] = w_ref[...]


def pick_planes(table, weight, groups, axis):
    planes = groups // 2
    shape = list(weight.shape)
    shape[axis] //= groups
    result = list(weight.shape)
    result[axis] //= 2
    return pl.pallas_call(
        pick_kernel,
        grid_spec=pltpu.PrefetchScalarGridSpec(
            num_scalar_prefetch=1,
            grid=(planes,),
            in_specs=[plane_spec(tuple(shape), axis, True)],
            out_specs=pl.BlockSpec(
                tuple(shape), (lambda i, t: (0, i)) if axis else (lambda i, t: (i, 0))
            ),
        ),
        out_shape=jax.ShapeDtypeStruct(tuple(result), BF16),
        compiler_params=params(),
        cost_estimate=cost(0, 2 * math.prod(weight.shape)),
        name="pick_planes",
    )(table, weight)


def reduce_planes(parts, groups):
    lines = [list(range(core, groups, 2)) for core in range(2)]
    return lax.psum_scatter(parts, "tp", scatter_dimension=0, axis_index_groups=lines, tiled=False)


def project_kernel(tab_ref, a_ref, ao_ref, w_ref, wo_ref, o_ref, a_buf, w_buf, o_buf, w_sem, o_sem):
    planes, cols = o_ref.shape[0], o_ref.shape[2]
    depth = a_ref.shape[1]
    slots = o_buf.shape[0]
    loads = []
    for i in range(planes):
        start = pl.multiple_of((2 * i + tab_ref[1] % 2) * cols, cols)
        here = pltpu.make_async_copy(w_ref.at[:, pl.ds(start, cols)], w_buf.at[i, :depth], w_sem.at[i, 0])
        there = pltpu.make_async_copy(
            wo_ref.at[:, i * cols : (i + 1) * cols], w_buf.at[i, depth:], w_sem.at[i, 1]
        )
        here.start()
        there.start()
        loads.append((here, there))
    a_buf[:, :depth] = a_ref[...]
    a_buf[:, depth:] = ao_ref[...]
    stores = []
    for i in range(planes):
        slot = i % slots
        if i >= slots:
            stores[i - slots].wait()
        loads[i][0].wait()
        loads[i][1].wait()
        o_buf[slot] = dot_nn(a_buf[...], w_buf[i]).astype(BF16)
        stores.append(pltpu.make_async_copy(o_buf.at[slot], o_ref.at[i], o_sem.at[slot]))
        stores[i].start()
    for i in range(planes - slots, planes):
        stores[i].wait()


def project_out(table, attn, attn_other, weight, weight_other, groups):
    rows, depth = attn.shape
    cols = weight.shape[1] // groups
    planes = groups // 2
    vmem = pl.BlockSpec(memory_space=pltpu.VMEM)
    anywhere = pl.BlockSpec(memory_space=pl.ANY)
    return pl.pallas_call(
        project_kernel,
        in_specs=[pl.BlockSpec(memory_space=pltpu.SMEM), vmem, vmem, anywhere, anywhere],
        out_specs=anywhere,
        out_shape=jax.ShapeDtypeStruct((planes, rows, cols), BF16),
        scratch_shapes=[
            pltpu.VMEM((rows, 2 * depth), BF16),
            pltpu.VMEM((planes, 2 * depth, cols), BF16),
            pltpu.VMEM((2, rows, cols), BF16),
            pltpu.SemaphoreType.DMA((planes, 2)),
            pltpu.SemaphoreType.DMA((2,)),
        ],
        compiler_params=params(),
        cost_estimate=cost(
            2 * rows * depth * cols * groups, 2 * (rows + 2 * depth) * cols * planes
        ),
        name="project_out",
    )(table, attn, attn_other, weight, weight_other)


PER_STEP = 2


def grad_attn_kernel(c0_ref, c1_ref, w_ref, *refs):
    before, o_ref = refs[:-1], refs[-1]
    step = pl.program_id(0)
    per_step, first_rows, cols = c0_ref.shape
    parts = ((c0_ref, slice(0, first_rows)), (c1_ref, slice(first_rows, o_ref.shape[0])))
    for c_ref, at in parts:
        total = dot_nt(c_ref[0], w_ref[:, :cols])
        for i in range(1, per_step):
            total += dot_nt(c_ref[i], w_ref[:, i * cols : (i + 1) * cols])

        @pl.when(step == 0)
        def _(at=at, total=total):
            o_ref[at, :] = total + before[0][at, :] if before else total

        @pl.when(step > 0)
        def _(at=at, total=total):
            o_ref[at, :] += total


def grad_attn(cot_first, cot_second, weight, half, before=None):
    groups, first_rows, cols = cot_first.shape
    depth = weight.shape[0]
    rows = first_rows + cot_second.shape[1]
    steps = groups // PER_STEP // 2
    start = half * steps
    whole = pl.BlockSpec((rows, depth), lambda i: (0, 0))
    return pl.pallas_call(
        grad_attn_kernel,
        grid=(steps,),
        in_specs=[
            pl.BlockSpec((PER_STEP, first_rows, cols), lambda i: (start + i, 0, 0)),
            pl.BlockSpec((PER_STEP, rows - first_rows, cols), lambda i: (start + i, 0, 0)),
            pl.BlockSpec((depth, PER_STEP * cols), lambda i: (0, start + i)),
        ]
        + ([] if before is None else [whole]),
        out_specs=whole,
        out_shape=jax.ShapeDtypeStruct((rows, depth), F32),
        compiler_params=params(),
        cost_estimate=cost(rows * depth * cols * groups, (rows + depth) * cols * groups),
        name="grad_attn",
    )(cot_first, cot_second, weight, *([] if before is None else [before]))


def grad_input_kernel(tab_ref, gq, gqo, gkv, gkvo, wq, wqo, wkv, wkvo, o_ref):
    total = dot_nt(gq[...], wq[...]) + dot_nt(gqo[...], wqo[...])
    total = total + dot_nt(gkv[...], wkv[...]) + dot_nt(gkvo[...], wkvo[...])
    o_ref[0] = total.astype(BF16)


def grad_input(table, gq, gq_other, gkv, gkv_other, wq, wq_other, wkv, wkv_other, groups):
    rows, cq = gq.shape
    ckv = gkv.shape[1]
    cols = wq.shape[0] // groups
    planes = groups // 2
    return pl.pallas_call(
        grad_input_kernel,
        grid_spec=pltpu.PrefetchScalarGridSpec(
            num_scalar_prefetch=1,
            grid=(planes,),
            in_specs=[
                whole_spec(gq.shape),
                whole_spec(gq.shape),
                whole_spec(gkv.shape),
                whole_spec(gkv.shape),
                plane_spec((cols, cq), 0, False),
                pl.BlockSpec((cols, cq), lambda i, t: (i, 0)),
                plane_spec((cols, ckv), 0, False),
                pl.BlockSpec((cols, ckv), lambda i, t: (i, 0)),
            ],
            out_specs=pl.BlockSpec((1, rows, cols), lambda i, t: (i, 0, 0)),
        ),
        out_shape=jax.ShapeDtypeStruct((planes, rows, cols), BF16),
        compiler_params=params(),
        cost_estimate=cost(
            2 * rows * (cq + ckv) * cols * groups,
            2 * (rows + 2 * (cq + ckv)) * cols * planes,
        ),
        name="grad_input",
    )(table, gq, gq_other, gkv, gkv_other, wq, wq_other, wkv, wkv_other)


def body(
    hidden_input,
    output_cotangent,
    query_projection,
    key_value_projection,
    output_projection,
    adapter_qkv_down_store,
    adapter_query_up,
    adapter_key_value_up,
    adapter_output_down,
    adapter_output_up,
    crop_token_length,
    tenant_per_block,
    tenant_store_row,
):
    ctx_count = lax.axis_size("ctx")
    tp_count = lax.axis_size("tp")
    ctx_index = lax.axis_index("ctx")
    tp_index = lax.axis_index("tp")
    rows_dev = hidden_input.shape[0]
    out_cols = output_cotangent.shape[1]
    tenant_owner = adapter_qkv_down_store.shape[0]
    blocks_dev = rows_dev // BLK
    pair_bits = (tp_count // KEY_VALUE_HEADS).bit_length() - 1
    groups = hidden_input.shape[1] // out_cols
    crops = crop_token_length.shape[0]
    partners = range(1, ctx_count)

    x_slice = lax.dynamic_slice_in_dim(hidden_input, tp_index * out_cols, out_cols, 1)

    table, cots, firsts, lates = serve(
        ctx_count,
        blocks_dev,
        crop_token_length,
        tenant_per_block,
        tenant_store_row,
        output_cotangent,
        adapter_qkv_down_store.swapaxes(1, 2),
        adapter_query_up,
        adapter_key_value_up,
        adapter_output_up,
        adapter_output_down.swapaxes(1, 2),
    )
    cot_first = lax.all_gather(cots[0], "tp", axis=0, tiled=False)
    firsts = [firsts[0]] + [swap(firsts[k], "ctx", k) for k in partners]
    my_pos = ctx_index * rows_dev + jnp.arange(rows_dev, dtype=jnp.int32)
    q_lin, kv_lin = dense_qkv(hidden_input, query_projection, key_value_projection)
    out_pick = pick_planes(table, output_projection, groups, 1)
    firsts, q_lin, kv_lin, tables, out_pick, x_slice = lax.optimization_barrier(
        (firsts, q_lin, kv_lin, rope_tables(my_pos), out_pick, x_slice)
    )
    cosine, sine = tables
    low_halves = low_part(table, x_slice, firsts)
    low_halves, (kv_pick, query_pick) = sum_halves(
        *low_halves,
        beside=[
            lambda done: pick_planes(table, key_value_projection, groups, 0),
            lambda done: (done, pick_planes(table, query_projection, groups, 0)),
        ],
    )
    low_halves, cot_rest = lax.optimization_barrier((low_halves, cots[1]))
    cot_second = lax.all_gather(cot_rest, "tp", axis=0, tiled=False)
    kv_local, low_in = finish_kv(
        table, kv_lin, low_halves, firsts, cosine, sine, pair_bits == 0
    )
    if pair_bits:
        for bit_no in range(pair_bits):
            partner = swap(kv_local, "tp", 1 << bit_no)
            is_lower = tp_index // (1 << bit_no) % 2 == 0
            kv_local = jnp.where(
                is_lower,
                jnp.concatenate([kv_local, partner], axis=1),
                jnp.concatenate([partner, kv_local], axis=1),
            )
        key_rot = turn(kv_local[:, :HEAD_SIZE].astype(F32), cosine, sine).astype(BF16)
        kv_local = jnp.concatenate([key_rot, kv_local[:, HEAD_SIZE:]], axis=1)
    kvs = [kv_local] + [swap(kv_local, "ctx", k) for k in partners]
    query_rot = finish_q(table, q_lin, low_in, firsts, cosine, sine)
    kvs, lates, query_rot = lax.optimization_barrier((kvs, lates, query_rot))
    out_other, query_other, kv_other = (
        swap(pick, "tp", 1) for pick in (out_pick, query_pick, kv_pick)
    )
    lates = [lates[0]] + [swap(lates[k], "ctx", k) for k in partners]

    attn_out, log_norm = attention_forward(table, crops, query_rot, kvs)
    lates, attn_out = lax.optimization_barrier((lates, attn_out))
    heads_part = project_out(
        table, attn_out, swap(attn_out, "tp", 1), output_projection, out_other, groups
    )
    heads_part, attn_out, cot_first = lax.optimization_barrier((heads_part, attn_out, cot_first))
    heads_sum = reduce_planes(heads_part, groups)
    o_halves, grad_dense = sum_halves(
        *low_o_part(table, output_cotangent, attn_out, lates),
        beside=[
            lambda done: grad_attn(cot_first, cot_second, output_projection, 0),
            lambda done: grad_attn(cot_first, cot_second, output_projection, 1, done),
        ],
    )
    grad_q, kv_parts = attention_backward(
        table, crops, query_rot, grad_dense, o_halves, attn_out, log_norm, cosine, sine, kvs, lates
    )
    grad_q_other = swap(grad_q, "tp", 1)
    reduced = kv_parts[0].astype(F32)
    for k in partners:
        reduced = reduced + swap(kv_parts[k], "ctx", k).astype(F32)
    reduced = jnp.concatenate(
        [turn(reduced[:, :HEAD_SIZE], cosine, -sine), reduced[:, HEAD_SIZE:]], axis=1
    )
    for bit_no in reversed(range(pair_bits)):
        half_cols = reduced.shape[1] // 2
        is_lower = tp_index // (1 << bit_no) % 2 == 0
        keep_part = jnp.where(is_lower, reduced[:, :half_cols], reduced[:, half_cols:])
        send_part = jnp.where(is_lower, reduced[:, half_cols:], reduced[:, :half_cols])
        reduced = keep_part + swap(send_part.astype(BF16), "tp", 1 << bit_no).astype(F32)
    grad_kv = reduced.astype(BF16)

    input_part = grad_input(
        table,
        grad_q,
        grad_q_other,
        grad_kv,
        swap(grad_kv, "tp", 1),
        query_projection,
        query_other,
        key_value_projection,
        kv_other,
        groups,
    )
    input_part, grad_q, grad_kv = lax.optimization_barrier((input_part, grad_q, grad_kv))
    input_sum = reduce_planes(input_part, groups)

    def send_ups(done):
        return up_grads(
            table, ctx_count, low_in, grad_q, grad_kv, o_halves, output_cotangent, attn_out
        )

    g_halves, up_sends = sum_halves(
        *low_g_part(table, grad_q, grad_kv, firsts), beside=[send_ups]
    )
    up_back = [up_sends[0]] + [swap(up_sends[k], "ctx", k) for k in partners]
    output = output_result(table, heads_sum, o_halves, lates)
    g_halves, up_back, output = lax.optimization_barrier((g_halves, up_back, output))
    down_sends, input_delta = down_grads(table, x_slice, g_halves, firsts)
    down_back = [down_sends[0]] + [swap(down_sends[k], "ctx", k) for k in partners]
    up_stores = store_ups(table, up_back, tenant_owner)
    down_back, up_stores = lax.optimization_barrier((down_back, up_stores))
    down_store = store_downs(table, down_back, tenant_owner)
    input_sum, input_delta, down_store = lax.optimization_barrier(
        (input_sum, input_delta, down_store)
    )
    hidden_input_gradient = (input_sum.astype(F32) + input_delta.astype(F32)).astype(BF16)
    return (
        output,
        hidden_input_gradient,
        down_store.swapaxes(1, 2),
        up_stores[0],
        up_stores[1],
        up_stores[2].swapaxes(1, 2),
        up_stores[3],
    )


def solution(mesh):
    in_specs = (
        P("ctx", None),
        P("ctx", "tp"),
        P(None, "tp"),
        P(None, "tp"),
        P("tp", None),
        P("ctx", "tp", None),
        P("ctx", None, "tp"),
        P("ctx", None, "tp"),
        P("ctx", "tp", None),
        P("ctx", None, "tp"),
        P(),
        P(),
        P(),
    )
    out_specs = (
        P("ctx", "tp"),
        P("ctx", "tp"),
        P("ctx", "tp", None),
        P("ctx", None, "tp"),
        P("ctx", None, "tp"),
        P("ctx", "tp", None),
        P("ctx", None, "tp"),
    )
    return jax.shard_map(body, mesh=mesh, in_specs=in_specs, out_specs=out_specs, check_vma=False)
```

```python
import functools
import math

import jax
import jax.numpy as jnp
from jax import lax
from jax.experimental import pallas as pl
from jax.experimental.pallas import tpu as pltpu
from jax.sharding import PartitionSpec as P

HEAD_SIZE = 128
KEY_VALUE_HEADS = 8
ADAPTER_RANK = 64
BLK = 128
NEG = -1e30
ROPE_BASE = 1000000.0
SCALE = HEAD_SIZE ** (-0.5)
LOG2E = math.log2(math.e)
SCALE2 = SCALE * LOG2E
VMEM_BYTES = 62 * 1024 * 1024
SMALL_VMEM_BYTES = 16 * 1024 * 1024

BF16 = jnp.bfloat16
F32 = jnp.float32


def params(limit=VMEM_BYTES):
    return pltpu.CompilerParams(vmem_limit_bytes=limit)


def cost(flops, bytes_accessed, transcendentals=0):
    return pl.CostEstimate(
        flops=int(flops), bytes_accessed=int(bytes_accessed), transcendentals=int(transcendentals)
    )


def dot_nn(a, b):
    return lax.dot_general(a, b, (((1,), (0,)), ((), ())), preferred_element_type=F32)


def dot_nt(a, b):
    return lax.dot_general(a, b, (((1,), (1,)), ((), ())), preferred_element_type=F32)


def dot_tn(a, b):
    return lax.dot_general(a, b, (((0,), (0,)), ((), ())), preferred_element_type=F32)


def swap(value, axis, mask):
    pairs = [(source, source ^ mask) for source in range(lax.axis_size(axis))]
    return lax.ppermute(value, axis, pairs)


def add_round(a, b):
    return (a.astype(F32) + b.astype(F32)).astype(BF16)


def rope_tables(positions):
    half_dim = HEAD_SIZE // 2
    exponent = jnp.arange(half_dim, dtype=F32) * (2.0 / HEAD_SIZE)
    frequency = jnp.exp(-exponent * math.log(ROPE_BASE))
    angles = positions.astype(F32)[:, None] * frequency[None, :]
    cosine, sine = jnp.cos(angles), jnp.sin(angles)
    return (
        jnp.concatenate([cosine, cosine], axis=1),
        jnp.concatenate([-sine, sine], axis=1),
    )


def turn(values, cosine, sine):
    return values * cosine + jnp.roll(values, HEAD_SIZE // 2, axis=1) * sine


def turn_kernel(values, cosine, sine):
    return values * cosine + pltpu.roll(values, HEAD_SIZE // 2, 1) * sine


def dense_kernel(x_ref, wq_ref, wkv_ref, q_ref, kv_ref):
    @pl.when(pl.program_id(0) == 0)
    def _():
        q_ref[...] = jnp.zeros_like(q_ref)
        kv_ref[...] = jnp.zeros_like(kv_ref)

    x = x_ref[...]
    q_ref[...] += dot_nn(x, wq_ref[...])
    kv_ref[...] += dot_nn(x, wkv_ref[...])


def dense_qkv(x, wq, wkv):
    rows, width = x.shape
    step = 2048
    cq, ckv = wq.shape[1], wkv.shape[1]
    return pl.pallas_call(
        dense_kernel,
        grid=(width // step,),
        in_specs=[
            pl.BlockSpec((rows, step), lambda i: (0, i)),
            pl.BlockSpec((step, cq), lambda i: (i, 0)),
            pl.BlockSpec((step, ckv), lambda i: (i, 0)),
        ],
        out_specs=[
            pl.BlockSpec((rows, cq), lambda i: (0, 0)),
            pl.BlockSpec((rows, ckv), lambda i: (0, 0)),
        ],
        out_shape=[
            jax.ShapeDtypeStruct((rows, cq), F32),
            jax.ShapeDtypeStruct((rows, ckv), F32),
        ],
        compiler_params=params(),
        cost_estimate=cost(2 * rows * width * (cq + ckv), 2 * width * (rows + cq + ckv)),
        name="dense_qkv",
    )(x, wq, wkv)


ENDS_AT = 2
SEND_AT = 16
SERVED_AT = 32
SOURCE_AT = 48
TABLE = 64


def serve_kernel(
    count, blocks, owned, crop_ref, tenant_ref, row_ref, cot, down, up_q, up_kv, up_o, down_o, *outs
):
    tab, cots = outs[0], outs[1:3]
    firsts, lates = outs[3 : 3 + count], outs[3 + count :]
    cots[0][...] = cot[: cots[0].shape[0], :]
    cots[1][...] = cot[cots[0].shape[0] :, :]
    me = lax.axis_index("ctx")
    for i in range(TABLE):
        tab[i] = 0
    tab[0] = me
    tab[1] = lax.axis_index("tp")
    end = jnp.int32(0)
    for i in range(crop_ref.shape[0]):
        end = end + crop_ref[i]
        tab[ENDS_AT + i] = end
    for b in range(blocks):
        row = row_ref[tenant_ref[me * blocks + b]]
        tab[SOURCE_AT + b] = (row // owned) ^ me
    for k in range(count):
        served = jnp.int32(-1)
        for b in range(blocks):
            row = row_ref[tenant_ref[(me ^ k) * blocks + b]]
            served = jnp.where(row // owned == me, row - me * owned, served)
        tab[SERVED_AT + k] = served
        tab[SEND_AT + k] = jnp.maximum(served, 0)
    rank, width = ADAPTER_RANK, down.shape[2]
    half, quarter = rank // 2, rank // 4
    cq, ckv = width // 2, width // 4
    for k in range(count):
        at = tab[SEND_AT + k]
        low = down.shape[1]
        firsts[k][:low, :] = down[at]
        for i in range(2):
            firsts[k][low : low + half, i * cq : (i + 1) * cq] = up_q[
                at, i * half : (i + 1) * half, :
            ]
            lates[k][rank : rank + half, i * cq : (i + 1) * cq] = down_o[
                at, i * half : (i + 1) * half, :
            ]
        for i in range(4):
            firsts[k][low + half :, i * ckv : (i + 1) * ckv] = up_kv[
                at, i * quarter : (i + 1) * quarter, :
            ]
        lates[k][:rank, :] = up_o[at]


def serve(count, blocks, crops, tenants, store_rows, cot, down, up_q, up_kv, up_o, down_o):
    rank, width = ADAPTER_RANK, down.shape[2]
    assert up_q.shape[2] * 2 == width and up_kv.shape[2] * 4 == width
    assert up_o.shape[2] == width and down_o.shape[2] * 2 == width
    smem = pl.BlockSpec(memory_space=pltpu.SMEM)
    vmem = pl.BlockSpec(memory_space=pltpu.VMEM)
    first = jax.ShapeDtypeStruct((3 * rank + rank // 2 + rank // 4, width), BF16)
    late = jax.ShapeDtypeStruct((rank + rank // 2, width), BF16)
    cut = cot.shape[0] // 384 * 192
    results = pl.pallas_call(
        functools.partial(serve_kernel, count, blocks, down.shape[0]),
        in_specs=[smem] * 3 + [vmem] * 6,
        out_specs=[smem] + [vmem] * (2 + 2 * count),
        out_shape=[jax.ShapeDtypeStruct((TABLE,), jnp.int32)]
        + [jax.ShapeDtypeStruct((n, cot.shape[1]), BF16) for n in (cut, cot.shape[0] - cut)]
        + [first] * count
        + [late] * count,
        compiler_params=params(),
        name="serve",
    )(crops, tenants, store_rows, cot, down, up_q, up_kv, up_o, down_o)
    return results[0], results[1:3], list(results[3 : 3 + count]), list(results[3 + count :])


def unpack_q(ref):
    rows, width = ref.shape
    value = ref[...]
    return jnp.concatenate([value[:, : width // 2], value[:, width // 2 :]], axis=0)


def unpack_kv(ref):
    rows, width = ref.shape
    value = ref[...]
    step = width // 4
    return jnp.concatenate([value[:, i * step : (i + 1) * step] for i in range(4)], axis=0)


def pick(tab_ref, block, count, step):
    for k in range(count):

        @pl.when(tab_ref[SOURCE_AT + block] == k)
        def _(k=k):
            step(k)


def split_rows(tab_ref, whole, mine, other):
    half = mine.shape[0]

    @pl.when(tab_ref[1] % 2 == 0)
    def _():
        mine[...] = whole[:half, :]
        other[...] = whole[half:, :]

    @pl.when(tab_ref[1] % 2 == 1)
    def _():
        mine[...] = whole[half:, :]
        other[...] = whole[:half, :]


def join_rows(tab_ref, mine, other, whole):
    half = mine.shape[0]

    @pl.when(tab_ref[1] % 2 == 0)
    def _():
        whole[:half, :] = mine[...]
        whole[half:, :] = other[...]

    @pl.when(tab_ref[1] % 2 == 1)
    def _():
        whole[:half, :] = other[...]
        whole[half:, :] = mine[...]


def sum_halves(mine, other, beside=()):
    total = add_round(mine, swap(other, "tp", 1))
    mask, done = 2, None
    beside = list(beside)
    while mask < lax.axis_size("tp"):
        arrived = swap(total, "tp", mask)
        if beside:
            done = beside.pop(0)(done)
            arrived, done = lax.optimization_barrier((arrived, done))
        total = add_round(total, arrived)
        mask *= 2
    while beside:
        done = beside.pop(0)(done)
    return (total, swap(total, "tp", 1)), done


def block_rows(b):
    return slice(b * BLK, (b + 1) * BLK)


def whole_spec(shape):
    return pl.BlockSpec(shape, lambda i, t: (0,) * len(shape))


def table_call(kernel, table, operands, shapes, scratch, name, flops=0, limit=VMEM_BYTES):
    moved = sum(math.prod(s.shape) * s.dtype.itemsize for s in operands + shapes)
    vmem = pl.BlockSpec(memory_space=pltpu.VMEM)
    return pl.pallas_call(
        kernel,
        in_specs=[pl.BlockSpec(memory_space=pltpu.SMEM)] + [vmem] * len(operands),
        out_specs=[vmem] * len(shapes),
        out_shape=shapes,
        scratch_shapes=scratch,
        compiler_params=params(limit),
        cost_estimate=cost(flops, moved),
        name=name,
    )(table, *operands)


def low_kernel(count, tab_ref, x_ref, *refs):
    downs = refs[:count]
    mine, other, whole = refs[count:]
    cols = whole.shape[1]
    for b in range(whole.shape[0] // BLK):

        def step(k, b=b):
            whole[block_rows(b), :] = dot_nt(x_ref[block_rows(b), :], downs[k][:cols, :]).astype(BF16)

        pick(tab_ref, b, count, step)
    split_rows(tab_ref, whole, mine, other)


def low_part(table, x, firsts):
    rows, width, cols = x.shape[0], firsts[0].shape[1], 3 * ADAPTER_RANK
    half = jax.ShapeDtypeStruct((rows // 2, cols), BF16)
    return table_call(
        functools.partial(low_kernel, len(firsts)),
        table,
        [x] + firsts,
        [half, half],
        [pltpu.VMEM((rows, cols), BF16)],
        "low_part",
        2 * rows * width * cols,
        SMALL_VMEM_BYTES,
    )


def finish_kv_kernel(count, rotate_keys, tab_ref, kv_ref, mine, other, cos_ref, sin_ref, *refs):
    ups = refs[:count]
    kvo, low = refs[count:]
    ckv = kv_ref.shape[1]
    rank = ADAPTER_RANK
    join_rows(tab_ref, mine, other, low)
    for b in range(kv_ref.shape[0] // BLK):

        def step(k, b=b):
            at_rows = block_rows(b)
            low_k = low[at_rows, rank : 2 * rank]
            low_v = low[at_rows, 2 * rank :]
            up_kv = unpack_kv(ups[k].at[3 * rank + rank // 2 :])
            for h in range(ckv // HEAD_SIZE):
                at = slice(h * HEAD_SIZE, (h + 1) * HEAD_SIZE)
                if rotate_keys:
                    term = dot_nn(low_v if h % 2 else low_k, up_kv[:, at])
                else:
                    is_value = (tab_ref[1] * (ckv // HEAD_SIZE) + h) % 2 == 1
                    term = jnp.where(
                        is_value, dot_nn(low_v, up_kv[:, at]), dot_nn(low_k, up_kv[:, at])
                    )
                piece = (kv_ref[at_rows, at] + term).astype(BF16)
                if rotate_keys and h % 2 == 0:
                    cosine, sine = cos_ref[at_rows, :], sin_ref[at_rows, :]
                    piece = turn_kernel(piece.astype(F32), cosine, sine).astype(BF16)
                kvo[at_rows, at] = piece

        pick(tab_ref, b, count, step)


def finish_kv(table, kv_lin, halves, firsts, cosine, sine, rotate_keys):
    rows, ckv = kv_lin.shape
    cols = 3 * ADAPTER_RANK
    operands = [kv_lin, *halves, cosine, sine]
    return table_call(
        functools.partial(finish_kv_kernel, len(firsts), rotate_keys),
        table,
        operands + firsts,
        [jax.ShapeDtypeStruct((rows, ckv), BF16), jax.ShapeDtypeStruct((rows, cols), BF16)],
        [],
        "finish_kv",
        4 * rows * ADAPTER_RANK * ckv,
    )


def finish_q_kernel(count, tab_ref, q_ref, low_ref, cos_ref, sin_ref, *refs):
    ups, qo = refs[:count], refs[count]
    cq = q_ref.shape[1]
    rank = ADAPTER_RANK
    for b in range(q_ref.shape[0] // BLK):

        def step(k, b=b):
            at_rows = block_rows(b)
            cosine, sine = cos_ref[at_rows, :], sin_ref[at_rows, :]
            up_q = unpack_q(ups[k].at[3 * rank : 3 * rank + rank // 2])
            query = q_ref[at_rows, :] + dot_nn(low_ref[at_rows, :rank], up_q)
            for h in range(cq // HEAD_SIZE):
                at = slice(h * HEAD_SIZE, (h + 1) * HEAD_SIZE)
                qo[at_rows, at] = turn_kernel(query[:, at], cosine, sine).astype(BF16)

        pick(tab_ref, b, count, step)


def finish_q(table, q_lin, low_in, firsts, cosine, sine):
    rows, cq = q_lin.shape
    operands = [q_lin, low_in, cosine, sine]
    return table_call(
        functools.partial(finish_q_kernel, len(firsts)),
        table,
        operands + firsts,
        [jax.ShapeDtypeStruct((rows, cq), BF16)],
        [],
        "finish_q",
        2 * rows * ADAPTER_RANK * cq,
        SMALL_VMEM_BYTES,
    )[0]


def low_o_kernel(count, tab_ref, cot_ref, attn_ref, *refs):
    lates = refs[:count]
    mine, other, whole = refs[count:]
    rank = ADAPTER_RANK
    for b in range(whole.shape[0] // BLK):

        def step(k, b=b):
            at = block_rows(b)
            whole[at, :rank] = dot_nt(cot_ref[at, :], lates[k][:rank, :]).astype(BF16)
            down = unpack_q(lates[k].at[rank:])
            whole[at, rank:] = dot_nt(attn_ref[at, :], down).astype(BF16)

        pick(tab_ref, b, count, step)
    split_rows(tab_ref, whole, mine, other)


def low_o_part(table, cot, attn, lates):
    rows, width = cot.shape
    cols = 2 * ADAPTER_RANK
    half = jax.ShapeDtypeStruct((rows // 2, cols), BF16)
    return table_call(
        functools.partial(low_o_kernel, len(lates)),
        table,
        [cot, attn] + lates,
        [half, half],
        [pltpu.VMEM((rows, cols), BF16)],
        "low_o_part",
        2 * rows * cols * width,
        SMALL_VMEM_BYTES,
    )


def low_g_kernel(count, tab_ref, gq_ref, gkv_ref, *refs):
    ups = refs[:count]
    mine, other, whole = refs[count:]
    rank = ADAPTER_RANK
    ckv = gkv_ref.shape[1]
    for b in range(whole.shape[0] // BLK):

        def step(k, b=b):
            at = block_rows(b)
            up_q = unpack_q(ups[k].at[3 * rank : 3 * rank + rank // 2])
            whole[at, :rank] = dot_nt(gq_ref[at, :], up_q).astype(BF16)
            up_kv = unpack_kv(ups[k].at[3 * rank + rank // 2 :])
            sums = [jnp.zeros((BLK, rank), F32)] * 2
            for h in range(ckv // HEAD_SIZE):
                cols = slice(h * HEAD_SIZE, (h + 1) * HEAD_SIZE)
                term = dot_nt(gkv_ref[at, cols], up_kv[:, cols])
                is_value = (tab_ref[1] * (ckv // HEAD_SIZE) + h) % 2 == 1
                sums[0] = sums[0] + jnp.where(is_value, 0.0, term)
                sums[1] = sums[1] + jnp.where(is_value, term, 0.0)
            whole[at, rank : 2 * rank] = sums[0].astype(BF16)
            whole[at, 2 * rank :] = sums[1].astype(BF16)

        pick(tab_ref, b, count, step)
    split_rows(tab_ref, whole, mine, other)


def low_g_part(table, gq, gkv, firsts):
    rows = gq.shape[0]
    cols, width = 3 * ADAPTER_RANK, firsts[0].shape[1]
    half = jax.ShapeDtypeStruct((rows // 2, cols), BF16)
    return table_call(
        functools.partial(low_g_kernel, len(firsts)),
        table,
        [gq, gkv] + firsts,
        [half, half],
        [pltpu.VMEM((rows, cols), BF16)],
        "low_g_part",
        2 * rows * width * ADAPTER_RANK,
    )


def zero_unused(tab_ref, blocks, sends):
    for k in range(len(sends)):
        used = tab_ref[SOURCE_AT] == k
        for b in range(1, blocks):
            used = used | (tab_ref[SOURCE_AT + b] == k)

        @pl.when(jnp.logical_not(used))
        def _(k=k):
            sends[k][...] = jnp.zeros_like(sends[k])


def up_grads_kernel(
    count, tab_ref, low_ref, gq_ref, gkv_ref, o_mine, o_other, cot, attn, *refs
):
    sends, low_o = refs[:count], refs[count]
    rank = ADAPTER_RANK
    join_rows(tab_ref, o_mine, o_other, low_o)
    blocks = low_o.shape[0] // BLK
    cq, ckv = gq_ref.shape[1], gkv_ref.shape[1]
    half, quarter = rank // 2, rank // 4
    late = half + quarter
    zero_unused(tab_ref, blocks, sends)
    for b in range(blocks):

        def step(k, b=b):
            at = block_rows(b)
            out = sends[k]
            up_q = dot_tn(low_ref[at, :rank], gq_ref[at, :]).astype(BF16)
            down_o = dot_tn(low_o[at, :rank], attn[at, :]).astype(BF16)
            for i in range(2):
                rows = slice(i * half, (i + 1) * half)
                cols = slice(i * cq, (i + 1) * cq)
                out[:half, cols] = up_q[rows, :]
                out[late + rank :, cols] = down_o[rows, :]
            for h in range(ckv // HEAD_SIZE):
                piece = slice(h * HEAD_SIZE, (h + 1) * HEAD_SIZE)
                is_value = (tab_ref[1] * (ckv // HEAD_SIZE) + h) % 2 == 1
                up_kv = jnp.where(
                    is_value,
                    dot_tn(low_ref[at, 2 * rank :], gkv_ref[at, piece]),
                    dot_tn(low_ref[at, rank : 2 * rank], gkv_ref[at, piece]),
                ).astype(BF16)
                for i in range(4):
                    cols = slice(i * ckv + h * HEAD_SIZE, i * ckv + (h + 1) * HEAD_SIZE)
                    out[half:late, cols] = up_kv[i * quarter : (i + 1) * quarter, :]
            out[late : late + rank, :] = dot_tn(low_o[at, rank:], cot[at, :]).astype(BF16)

        pick(tab_ref, b, count, step)


def up_grads(table, count, low_in, gq, gkv, o_halves, cot, attn):
    rows, width = cot.shape
    rank = ADAPTER_RANK
    operands = [low_in, gq, gkv, *o_halves, cot, attn]
    return list(
        table_call(
            functools.partial(up_grads_kernel, count),
            table,
            operands,
            [jax.ShapeDtypeStruct((2 * rank + rank // 4, width), BF16)] * count,
            [pltpu.VMEM((rows, 2 * rank), BF16)],
            "up_grads",
            2 * rows * width * 3 * rank,
        )
    )


def down_grads_kernel(count, tab_ref, x_ref, mine, other, *refs):
    downs, sends = refs[:count], refs[count : 2 * count]
    delta, low = refs[2 * count :]
    join_rows(tab_ref, mine, other, low)
    blocks = low.shape[0] // BLK
    zero_unused(tab_ref, blocks, sends)
    for b in range(blocks):

        def step(k, b=b):
            at = block_rows(b)
            sends[k][...] = dot_tn(low[at, :], x_ref[at, :]).astype(BF16)
            delta[at, :] = dot_nn(low[at, :], downs[k][: low.shape[1], :]).astype(BF16)

        pick(tab_ref, b, count, step)


def down_grads(table, x, halves, firsts):
    rows, cols = x.shape[0], 3 * ADAPTER_RANK
    width, count = firsts[0].shape[1], len(firsts)
    results = table_call(
        functools.partial(down_grads_kernel, count),
        table,
        [x, *halves] + firsts,
        [jax.ShapeDtypeStruct((cols, width), BF16)] * count
        + [jax.ShapeDtypeStruct((rows, width), BF16)],
        [pltpu.VMEM((rows, cols), BF16)],
        "down_grads",
        4 * rows * width * cols,
    )
    return list(results[:count]), results[count]


def store_kernel(count, pieces, tab_ref, *refs):
    arrived, outs = refs[:count], refs[count:]
    row = pl.program_id(0)
    for o in outs:
        o[...] = jnp.zeros_like(o)
    for k in range(count):

        @pl.when(tab_ref[SERVED_AT + k] == row)
        def _(k=k):
            for o, piece in zip(outs, pieces):
                o[0] += piece(arrived[k]).astype(F32)


def store_sums(table, arrived, owned, pieces, sizes):
    shapes = [jax.ShapeDtypeStruct((owned,) + size, F32) for size in sizes]
    return pl.pallas_call(
        functools.partial(store_kernel, len(arrived), pieces),
        grid_spec=pltpu.PrefetchScalarGridSpec(
            num_scalar_prefetch=1,
            grid=(owned,),
            in_specs=[pl.BlockSpec(a.shape, lambda i, t: (0, 0)) for a in arrived],
            out_specs=[pl.BlockSpec((1,) + s.shape[1:], lambda i, t: (i, 0, 0)) for s in shapes],
        ),
        out_shape=shapes,
        compiler_params=params(),
        name="store_sums",
    )(table, *arrived)


def store_ups(table, arrived, owned):
    rank, width = ADAPTER_RANK, arrived[0].shape[1]
    half, late = rank // 2, rank // 2 + rank // 4
    pieces = [
        lambda a: unpack_q(a.at[:half]),
        lambda a: unpack_kv(a.at[half:late]),
        lambda a: unpack_q(a.at[late + rank :]),
        lambda a: a[late : late + rank, :],
    ]
    sizes = [(rank, width // 2), (rank, width // 4), (rank, width // 2), (rank, width)]
    return store_sums(table, arrived, owned, pieces, sizes)


def store_downs(table, arrived, owned):
    return store_sums(table, arrived, owned, [lambda a: a[...]], [arrived[0].shape])[0]


def output_kernel(count, tab_ref, sum_ref, mine, other, *refs):
    lates = refs[:count]
    out, low = refs[count:]
    rank = ADAPTER_RANK
    join_rows(tab_ref, mine, other, low)
    for b in range(out.shape[0] // BLK):

        def step(k, b=b):
            at = block_rows(b)
            term = dot_nn(low[at, rank:], lates[k][:rank, :])
            out[at, :] = (sum_ref[at, :].astype(F32) + term).astype(BF16)

        pick(tab_ref, b, count, step)


def output_result(table, total, halves, lates):
    rows, width = total.shape
    rank = ADAPTER_RANK
    return table_call(
        functools.partial(output_kernel, len(lates)),
        table,
        [total, *halves] + lates,
        [jax.ShapeDtypeStruct((rows, width), BF16)],
        [pltpu.VMEM((rows, 2 * rank), BF16)],
        "output_result",
        2 * rows * rank * width,
    )[0]


def crop_start(tab_ref, crops, positions):
    start = jnp.zeros_like(positions)
    for i in range(crops):
        end = tab_ref[ENDS_AT + i]
        start = jnp.where(positions >= end, end, start)
    return start


def masked(scores, first, own, base):
    rows, cols = scores.shape
    key_pos = base + lax.broadcasted_iota(jnp.int32, (rows, cols), 0)
    allowed = key_pos >= first
    if own:
        allowed &= key_pos <= base + lax.broadcasted_iota(jnp.int32, (rows, cols), 1)
    return jnp.where(allowed, scores, NEG)


def chunk_on(tab_ref, crops, k, rows):
    me = tab_ref[0]
    chunk = me ^ k
    return (chunk <= me) & ((chunk + 1) * rows > crop_start(tab_ref, crops, me * rows))


def query_starts(tab_ref, crops, rows):
    positions = tab_ref[0] * rows + lax.broadcasted_iota(jnp.int32, (1, rows), 1)
    return crop_start(tab_ref, crops, positions)


def forward_kernel(heads, count, crops, tab_ref, q_ref, *refs):
    kv_refs = refs[:count]
    out_ref, norm_ref, acc, top, total = refs[count:]
    rows = q_ref.shape[0]
    first = query_starts(tab_ref, crops, rows)
    for k in range(count):

        def chunk_step(k=k):
            base = (tab_ref[0] ^ k) * rows
            keys = kv_refs[k][:, :HEAD_SIZE]
            values = kv_refs[k][:, HEAD_SIZE:]
            for h in range(heads):
                at = slice(h * HEAD_SIZE, (h + 1) * HEAD_SIZE)
                scores = masked(dot_nt(keys, q_ref[:, at]), first, k == 0, base)
                here = jnp.max(scores, axis=0, keepdims=True)
                if k == 0:
                    new_top = here
                else:
                    old_top = top[h : h + 1, :]
                    new_top = jnp.maximum(old_top, here)
                weights = jnp.exp2(scores * SCALE2 - new_top * SCALE2)
                here_sum = jnp.sum(weights, axis=0, keepdims=True)
                here_out = dot_tn(values, weights.astype(BF16))
                if k == 0:
                    total[h : h + 1, :] = here_sum
                    acc[h] = here_out
                else:
                    decay = jnp.exp2((old_top - new_top) * SCALE2)
                    total[h : h + 1, :] = total[h : h + 1, :] * decay + here_sum
                    acc[h] = acc[h] * decay + here_out
                top[h : h + 1, :] = new_top

        if k == 0:
            chunk_step()
        else:
            pl.when(chunk_on(tab_ref, crops, k, rows))(chunk_step)
    for h in range(heads):
        at = slice(h * HEAD_SIZE, (h + 1) * HEAD_SIZE)
        out_ref[:, at] = jnp.transpose(acc[h] / total[h : h + 1, :]).astype(BF16)
    norm_ref[...] = top[...] * SCALE2 + jnp.log(total[...]) * LOG2E


def attention_forward(table, crops, query, kvs):
    rows, cols = query.shape
    heads = cols // HEAD_SIZE
    count = len(kvs)
    smem = pl.BlockSpec(memory_space=pltpu.SMEM)
    vmem = pl.BlockSpec(memory_space=pltpu.VMEM)
    work = heads * rows * rows * count
    return pl.pallas_call(
        functools.partial(forward_kernel, heads, count, crops),
        in_specs=[smem] + [vmem] * (1 + count),
        out_specs=[vmem] * 2,
        out_shape=[
            jax.ShapeDtypeStruct((rows, cols), BF16),
            jax.ShapeDtypeStruct((heads, rows), F32),
        ],
        scratch_shapes=[
            pltpu.VMEM((heads, HEAD_SIZE, rows), F32),
            pltpu.VMEM((heads, rows), F32),
            pltpu.VMEM((heads, rows), F32),
        ],
        compiler_params=params(),
        cost_estimate=cost(4 * work * HEAD_SIZE, 4 * rows * cols * count, work),
        name="attention_forward",
    )(table, query, *kvs)


def backward_kernel(
    heads,
    count,
    crops,
    tab_ref,
    q_ref,
    dense_ref,
    mine,
    other,
    out_ref,
    norm_ref,
    cos_ref,
    sin_ref,
    *refs,
):
    kv_refs, lates = refs[:count], refs[count : 2 * count]
    gq_ref = refs[2 * count]
    gkv_refs = refs[2 * count + 1 : 3 * count + 1]
    acc, delta, low, grad_ref = refs[3 * count + 1 :]
    rows = q_ref.shape[0]
    rank = ADAPTER_RANK
    first = query_starts(tab_ref, crops, rows)
    join_rows(tab_ref, mine, other, low)
    for b in range(rows // BLK):

        def add(k, b=b):
            at = block_rows(b)
            term = dot_nn(low[at, :rank], unpack_q(lates[k].at[rank:]))
            grad_ref[at, :] = (dense_ref[at, :] + term).astype(BF16)

        pick(tab_ref, b, count, add)
    for h in range(heads):
        at = slice(h * HEAD_SIZE, (h + 1) * HEAD_SIZE)
        product = grad_ref[:, at].astype(F32) * out_ref[:, at].astype(F32)
        delta[h : h + 1, :] = jnp.sum(jnp.transpose(product), axis=0, keepdims=True)
    for k in range(count):

        def chunk_step(k=k):
            base = (tab_ref[0] ^ k) * rows
            keys = kv_refs[k][:, :HEAD_SIZE]
            values = kv_refs[k][:, HEAD_SIZE:]
            key_grad = jnp.zeros((rows, HEAD_SIZE), F32)
            value_grad = jnp.zeros((rows, HEAD_SIZE), F32)
            for h in range(heads):
                at = slice(h * HEAD_SIZE, (h + 1) * HEAD_SIZE)
                scores = masked(dot_nt(keys, q_ref[:, at]), first, k == 0, base)
                weights = jnp.exp2(scores * SCALE2 - norm_ref[h : h + 1, :])
                value_grad += dot_nn(weights.astype(BF16), grad_ref[:, at])
                grad_weights = dot_nt(values, grad_ref[:, at])
                grad_scores = (weights * (grad_weights - delta[h : h + 1, :])).astype(BF16)
                key_grad += dot_nn(grad_scores, q_ref[:, at])
                here = dot_tn(keys, grad_scores)
                if k == 0:
                    acc[h] = here
                else:
                    acc[h] += here
            gkv_refs[k][:, :HEAD_SIZE] = (key_grad * SCALE).astype(BF16)
            gkv_refs[k][:, HEAD_SIZE:] = value_grad.astype(BF16)

        if k == 0:
            chunk_step()
        else:
            on = chunk_on(tab_ref, crops, k, rows)
            pl.when(on)(chunk_step)

            @pl.when(jnp.logical_not(on))
            def _(k=k):
                gkv_refs[k][...] = jnp.zeros_like(gkv_refs[k])

    for h in range(heads):
        at = slice(h * HEAD_SIZE, (h + 1) * HEAD_SIZE)
        grad = jnp.transpose(acc[h]) * SCALE
        gq_ref[:, at] = turn_kernel(grad, cos_ref[...], -sin_ref[...]).astype(BF16)


def attention_backward(table, crops, query, dense, halves, out, norm, cosine, sine, kvs, lates):
    rows, cols = query.shape
    heads = cols // HEAD_SIZE
    count = len(kvs)
    smem = pl.BlockSpec(memory_space=pltpu.SMEM)
    vmem = pl.BlockSpec(memory_space=pltpu.VMEM)
    work = heads * rows * rows * count
    results = pl.pallas_call(
        functools.partial(backward_kernel, heads, count, crops),
        in_specs=[smem] + [vmem] * (8 + 2 * count),
        out_specs=[vmem] * (1 + count),
        out_shape=[jax.ShapeDtypeStruct((rows, cols), BF16)]
        + [jax.ShapeDtypeStruct((rows, 2 * HEAD_SIZE), BF16)] * count,
        scratch_shapes=[
            pltpu.VMEM((heads, HEAD_SIZE, rows), F32),
            pltpu.VMEM((heads, rows), F32),
            pltpu.VMEM((rows, 2 * ADAPTER_RANK), BF16),
            pltpu.VMEM((rows, cols), BF16),
        ],
        compiler_params=params(),
        cost_estimate=cost(10 * work * HEAD_SIZE, 8 * rows * cols * count, work),
        name="attention_backward",
    )(table, query, dense, *halves, out, norm, cosine, sine, *kvs, *lates)
    return results[0], list(results[1:])


def plane_spec(shape, axis, other):
    def index(i, t):
        core = t[1] % 2
        at = 2 * i + (1 - core if other else core)
        return (0, at) if axis else (at, 0)

    return pl.BlockSpec(shape, index)


def pick_kernel(tab_ref, w_ref, o_ref):
    o_ref[...] = w_ref[...]


def pick_planes(table, weight, groups, axis):
    planes = groups // 2
    shape = list(weight.shape)
    shape[axis] //= groups
    result = list(weight.shape)
    result[axis] //= 2
    return pl.pallas_call(
        pick_kernel,
        grid_spec=pltpu.PrefetchScalarGridSpec(
            num_scalar_prefetch=1,
            grid=(planes,),
            in_specs=[plane_spec(tuple(shape), axis, True)],
            out_specs=pl.BlockSpec(
                tuple(shape), (lambda i, t: (0, i)) if axis else (lambda i, t: (i, 0))
            ),
        ),
        out_shape=jax.ShapeDtypeStruct(tuple(result), BF16),
        compiler_params=params(),
        cost_estimate=cost(0, 2 * math.prod(weight.shape)),
        name="pick_planes",
    )(table, weight)


def reduce_planes(parts, groups):
    lines = [list(range(core, groups, 2)) for core in range(2)]
    return lax.psum_scatter(parts, "tp", scatter_dimension=0, axis_index_groups=lines, tiled=False)


def project_kernel(
    tab_ref, a_ref, ao_ref, w_ref, wo_ref, o_ref, a_buf, w_buf, o_buf, a_sem, w_sem, o_sem
):
    planes, cols = o_ref.shape[0], o_ref.shape[2]
    depth = a_ref.shape[1]
    slots = o_buf.shape[0]
    terms = [
        pltpu.make_async_copy(a_ref, a_buf.at[:, :depth], a_sem.at[0]),
        pltpu.make_async_copy(ao_ref, a_buf.at[:, depth:], a_sem.at[1]),
    ]
    for term in terms:
        term.start()
    loads = []
    for i in range(planes):
        start = pl.multiple_of((2 * i + tab_ref[1] % 2) * cols, cols)
        here = pltpu.make_async_copy(w_ref.at[:, pl.ds(start, cols)], w_buf.at[i, :depth], w_sem.at[i, 0])
        there = pltpu.make_async_copy(
            wo_ref.at[:, i * cols : (i + 1) * cols], w_buf.at[i, depth:], w_sem.at[i, 1]
        )
        here.start()
        there.start()
        loads.append((here, there))
    for term in terms:
        term.wait()
    stores = []
    for i in range(planes):
        slot = i % slots
        if i >= slots:
            stores[i - slots].wait()
        loads[i][0].wait()
        loads[i][1].wait()
        o_buf[slot] = dot_nn(a_buf[...], w_buf[i]).astype(BF16)
        stores.append(pltpu.make_async_copy(o_buf.at[slot], o_ref.at[i], o_sem.at[slot]))
        stores[i].start()
    for i in range(planes - slots, planes):
        stores[i].wait()


def project_out(table, attn, attn_other, weight, weight_other, groups):
    rows, depth = attn.shape
    cols = weight.shape[1] // groups
    planes = groups // 2
    anywhere = pl.BlockSpec(memory_space=pl.ANY)
    return pl.pallas_call(
        project_kernel,
        in_specs=[pl.BlockSpec(memory_space=pltpu.SMEM)] + [anywhere] * 4,
        out_specs=anywhere,
        out_shape=jax.ShapeDtypeStruct((planes, rows, cols), BF16),
        scratch_shapes=[
            pltpu.VMEM((rows, 2 * depth), BF16),
            pltpu.VMEM((planes, 2 * depth, cols), BF16),
            pltpu.VMEM((2, rows, cols), BF16),
            pltpu.SemaphoreType.DMA((2,)),
            pltpu.SemaphoreType.DMA((planes, 2)),
            pltpu.SemaphoreType.DMA((2,)),
        ],
        compiler_params=params(),
        cost_estimate=cost(
            2 * rows * depth * cols * groups, 2 * (rows + 2 * depth) * cols * planes
        ),
        name="project_out",
    )(table, attn, attn_other, weight, weight_other)


PER_STEP = 2


def grad_attn_kernel(c0_ref, c1_ref, w_ref, *refs):
    before, o_ref = refs[:-1], refs[-1]
    step = pl.program_id(0)
    per_step, first_rows, cols = c0_ref.shape
    parts = ((c0_ref, slice(0, first_rows)), (c1_ref, slice(first_rows, o_ref.shape[0])))
    for c_ref, at in parts:
        total = dot_nt(c_ref[0], w_ref[:, :cols])
        for i in range(1, per_step):
            total += dot_nt(c_ref[i], w_ref[:, i * cols : (i + 1) * cols])

        @pl.when(step == 0)
        def _(at=at, total=total):
            o_ref[at, :] = total + before[0][at, :] if before else total

        @pl.when(step > 0)
        def _(at=at, total=total):
            o_ref[at, :] += total


def grad_attn(cot_first, cot_second, weight, half, before=None):
    groups, first_rows, cols = cot_first.shape
    depth = weight.shape[0]
    rows = first_rows + cot_second.shape[1]
    steps = groups // PER_STEP // 2
    start = half * steps
    whole = pl.BlockSpec((rows, depth), lambda i: (0, 0))
    return pl.pallas_call(
        grad_attn_kernel,
        grid=(steps,),
        in_specs=[
            pl.BlockSpec((PER_STEP, first_rows, cols), lambda i: (start + i, 0, 0)),
            pl.BlockSpec((PER_STEP, rows - first_rows, cols), lambda i: (start + i, 0, 0)),
            pl.BlockSpec((depth, PER_STEP * cols), lambda i: (0, start + i)),
        ]
        + ([] if before is None else [whole]),
        out_specs=whole,
        out_shape=jax.ShapeDtypeStruct((rows, depth), F32),
        compiler_params=params(),
        cost_estimate=cost(rows * depth * cols * groups, (rows + depth) * cols * groups),
        name="grad_attn",
    )(cot_first, cot_second, weight, *([] if before is None else [before]))


def grad_input_kernel(tab_ref, gq, gqo, gkv, gkvo, wq, wqo, wkv, wkvo, o_ref):
    total = dot_nt(gq[...], wq[...]) + dot_nt(gqo[...], wqo[...])
    total = total + dot_nt(gkv[...], wkv[...]) + dot_nt(gkvo[...], wkvo[...])
    o_ref[0] = total.astype(BF16)


def grad_input(table, gq, gq_other, gkv, gkv_other, wq, wq_other, wkv, wkv_other, groups):
    rows, cq = gq.shape
    ckv = gkv.shape[1]
    cols = wq.shape[0] // groups
    planes = groups // 2
    return pl.pallas_call(
        grad_input_kernel,
        grid_spec=pltpu.PrefetchScalarGridSpec(
            num_scalar_prefetch=1,
            grid=(planes,),
            in_specs=[
                whole_spec(gq.shape),
                whole_spec(gq.shape),
                whole_spec(gkv.shape),
                whole_spec(gkv.shape),
                plane_spec((cols, cq), 0, False),
                pl.BlockSpec((cols, cq), lambda i, t: (i, 0)),
                plane_spec((cols, ckv), 0, False),
                pl.BlockSpec((cols, ckv), lambda i, t: (i, 0)),
            ],
            out_specs=pl.BlockSpec((1, rows, cols), lambda i, t: (i, 0, 0)),
        ),
        out_shape=jax.ShapeDtypeStruct((planes, rows, cols), BF16),
        compiler_params=params(),
        cost_estimate=cost(
            2 * rows * (cq + ckv) * cols * groups,
            2 * (rows + 2 * (cq + ckv)) * cols * planes,
        ),
        name="grad_input",
    )(table, gq, gq_other, gkv, gkv_other, wq, wq_other, wkv, wkv_other)


def body(
    hidden_input,
    output_cotangent,
    query_projection,
    key_value_projection,
    output_projection,
    adapter_qkv_down_store,
    adapter_query_up,
    adapter_key_value_up,
    adapter_output_down,
    adapter_output_up,
    crop_token_length,
    tenant_per_block,
    tenant_store_row,
):
    ctx_count = lax.axis_size("ctx")
    tp_count = lax.axis_size("tp")
    ctx_index = lax.axis_index("ctx")
    tp_index = lax.axis_index("tp")
    rows_dev = hidden_input.shape[0]
    out_cols = output_cotangent.shape[1]
    tenant_owner = adapter_qkv_down_store.shape[0]
    blocks_dev = rows_dev // BLK
    pair_bits = (tp_count // KEY_VALUE_HEADS).bit_length() - 1
    groups = hidden_input.shape[1] // out_cols
    crops = crop_token_length.shape[0]
    partners = range(1, ctx_count)

    x_slice = lax.dynamic_slice_in_dim(hidden_input, tp_index * out_cols, out_cols, 1)

    table, cots, firsts, lates = serve(
        ctx_count,
        blocks_dev,
        crop_token_length,
        tenant_per_block,
        tenant_store_row,
        output_cotangent,
        adapter_qkv_down_store.swapaxes(1, 2),
        adapter_query_up,
        adapter_key_value_up,
        adapter_output_up,
        adapter_output_down.swapaxes(1, 2),
    )
    cot_first = lax.all_gather(cots[0], "tp", axis=0, tiled=False)
    firsts = [firsts[0]] + [swap(firsts[k], "ctx", k) for k in partners]
    my_pos = ctx_index * rows_dev + jnp.arange(rows_dev, dtype=jnp.int32)
    q_lin, kv_lin = dense_qkv(hidden_input, query_projection, key_value_projection)
    out_pick = pick_planes(table, output_projection, groups, 1)
    firsts, q_lin, kv_lin, tables, out_pick, x_slice = lax.optimization_barrier(
        (firsts, q_lin, kv_lin, rope_tables(my_pos), out_pick, x_slice)
    )
    cosine, sine = tables
    low_halves = low_part(table, x_slice, firsts)
    low_halves, (kv_pick, query_pick, cot_rest) = sum_halves(
        *low_halves,
        beside=[
            lambda done: pick_planes(table, key_value_projection, groups, 0),
            lambda done: (done, pick_planes(table, query_projection, groups, 0), cots[1]),
        ],
    )
    cot_second = lax.all_gather(cot_rest, "tp", axis=0, tiled=False)
    kv_local, low_in = finish_kv(
        table, kv_lin, low_halves, firsts, cosine, sine, pair_bits == 0
    )
    if pair_bits:
        for bit_no in range(pair_bits):
            partner = swap(kv_local, "tp", 1 << bit_no)
            is_lower = tp_index // (1 << bit_no) % 2 == 0
            kv_local = jnp.where(
                is_lower,
                jnp.concatenate([kv_local, partner], axis=1),
                jnp.concatenate([partner, kv_local], axis=1),
            )
        key_rot = turn(kv_local[:, :HEAD_SIZE].astype(F32), cosine, sine).astype(BF16)
        kv_local = jnp.concatenate([key_rot, kv_local[:, HEAD_SIZE:]], axis=1)
    kvs = [kv_local] + [swap(kv_local, "ctx", k) for k in partners]
    query_rot = finish_q(table, q_lin, low_in, firsts, cosine, sine)
    kvs, lates, query_rot = lax.optimization_barrier((kvs, lates, query_rot))
    out_other, query_other, kv_other = (
        swap(pick, "tp", 1) for pick in (out_pick, query_pick, kv_pick)
    )
    lates = [lates[0]] + [swap(lates[k], "ctx", k) for k in partners]

    attn_out, log_norm = attention_forward(table, crops, query_rot, kvs)
    lates, attn_out = lax.optimization_barrier((lates, attn_out))
    heads_part = project_out(
        table, attn_out, swap(attn_out, "tp", 1), output_projection, out_other, groups
    )
    heads_part, attn_out, cot_first = lax.optimization_barrier((heads_part, attn_out, cot_first))
    heads_sum = reduce_planes(heads_part, groups)
    o_halves, grad_dense = sum_halves(
        *low_o_part(table, output_cotangent, attn_out, lates),
        beside=[
            lambda done: grad_attn(cot_first, cot_second, output_projection, 0),
            lambda done: grad_attn(cot_first, cot_second, output_projection, 1, done),
        ],
    )
    grad_q, kv_parts = attention_backward(
        table, crops, query_rot, grad_dense, o_halves, attn_out, log_norm, cosine, sine, kvs, lates
    )
    grad_q_other = swap(grad_q, "tp", 1)
    reduced = kv_parts[0].astype(F32)
    for k in partners:
        reduced = reduced + swap(kv_parts[k], "ctx", k).astype(F32)
    reduced = jnp.concatenate(
        [turn(reduced[:, :HEAD_SIZE], cosine, -sine), reduced[:, HEAD_SIZE:]], axis=1
    )
    for bit_no in reversed(range(pair_bits)):
        half_cols = reduced.shape[1] // 2
        is_lower = tp_index // (1 << bit_no) % 2 == 0
        keep_part = jnp.where(is_lower, reduced[:, :half_cols], reduced[:, half_cols:])
        send_part = jnp.where(is_lower, reduced[:, half_cols:], reduced[:, :half_cols])
        reduced = keep_part + swap(send_part.astype(BF16), "tp", 1 << bit_no).astype(F32)
    grad_kv = reduced.astype(BF16)

    input_part = grad_input(
        table,
        grad_q,
        grad_q_other,
        grad_kv,
        swap(grad_kv, "tp", 1),
        query_projection,
        query_other,
        key_value_projection,
        kv_other,
        groups,
    )
    input_part, grad_q, grad_kv = lax.optimization_barrier((input_part, grad_q, grad_kv))
    input_sum = reduce_planes(input_part, groups)

    def send_ups(done):
        return up_grads(
            table, ctx_count, low_in, grad_q, grad_kv, o_halves, output_cotangent, attn_out
        )

    g_halves, up_sends = sum_halves(
        *low_g_part(table, grad_q, grad_kv, firsts), beside=[send_ups]
    )
    up_back = [up_sends[0]] + [swap(up_sends[k], "ctx", k) for k in partners]
    output = output_result(table, heads_sum, o_halves, lates)
    g_halves, up_back, output = lax.optimization_barrier((g_halves, up_back, output))
    down_sends, input_delta = down_grads(table, x_slice, g_halves, firsts)
    down_back = [down_sends[0]] + [swap(down_sends[k], "ctx", k) for k in partners]
    up_stores = store_ups(table, up_back, tenant_owner)
    down_back, up_stores = lax.optimization_barrier((down_back, up_stores))
    down_store = store_downs(table, down_back, tenant_owner)
    input_sum, input_delta, down_store = lax.optimization_barrier(
        (input_sum, input_delta, down_store)
    )
    hidden_input_gradient = (input_sum.astype(F32) + input_delta.astype(F32)).astype(BF16)
    return (
        output,
        hidden_input_gradient,
        down_store.swapaxes(1, 2),
        up_stores[0],
        up_stores[1],
        up_stores[2].swapaxes(1, 2),
        up_stores[3],
    )


def solution(mesh):
    in_specs = (
        P("ctx", None),
        P("ctx", "tp"),
        P(None, "tp"),
        P(None, "tp"),
        P("tp", None),
        P("ctx", "tp", None),
        P("ctx", None, "tp"),
        P("ctx", None, "tp"),
        P("ctx", "tp", None),
        P("ctx", None, "tp"),
        P(),
        P(),
        P(),
    )
    out_specs = (
        P("ctx", "tp"),
        P("ctx", "tp"),
        P("ctx", "tp", None),
        P("ctx", None, "tp"),
        P("ctx", None, "tp"),
        P("ctx", "tp", None),
        P("ctx", None, "tp"),
    )
    return jax.shard_map(body, mesh=mesh, in_specs=in_specs, out_specs=out_specs, check_vma=False)
```

```python
import functools
import math

import jax
import jax.numpy as jnp
from jax import lax
from jax.experimental import pallas as pl
from jax.experimental.pallas import tpu as pltpu
from jax.sharding import PartitionSpec as P

HEAD_SIZE = 128
KEY_VALUE_HEADS = 8
ADAPTER_RANK = 64
BLK = 128
NEG = -1e30
ROPE_BASE = 1000000.0
SCALE = HEAD_SIZE ** (-0.5)
LOG2E = math.log2(math.e)
SCALE2 = SCALE * LOG2E
VMEM_BYTES = 62 * 1024 * 1024
SMALL_VMEM_BYTES = 16 * 1024 * 1024

BF16 = jnp.bfloat16
F32 = jnp.float32


def params(limit=VMEM_BYTES):
    return pltpu.CompilerParams(vmem_limit_bytes=limit)


def cost(flops, bytes_accessed, transcendentals=0):
    return pl.CostEstimate(
        flops=int(flops), bytes_accessed=int(bytes_accessed), transcendentals=int(transcendentals)
    )


def dot_nn(a, b):
    return lax.dot_general(a, b, (((1,), (0,)), ((), ())), preferred_element_type=F32)


def dot_nt(a, b):
    return lax.dot_general(a, b, (((1,), (1,)), ((), ())), preferred_element_type=F32)


def dot_tn(a, b):
    return lax.dot_general(a, b, (((0,), (0,)), ((), ())), preferred_element_type=F32)


def swap(value, axis, mask):
    pairs = [(source, source ^ mask) for source in range(lax.axis_size(axis))]
    return lax.ppermute(value, axis, pairs)


def add_round(a, b):
    return (a.astype(F32) + b.astype(F32)).astype(BF16)


def rope_tables(positions):
    half_dim = HEAD_SIZE // 2
    exponent = jnp.arange(half_dim, dtype=F32) * (2.0 / HEAD_SIZE)
    frequency = jnp.exp(-exponent * math.log(ROPE_BASE))
    angles = positions.astype(F32)[:, None] * frequency[None, :]
    cosine, sine = jnp.cos(angles), jnp.sin(angles)
    return (
        jnp.concatenate([cosine, cosine], axis=1),
        jnp.concatenate([-sine, sine], axis=1),
    )


def turn(values, cosine, sine):
    return values * cosine + jnp.roll(values, HEAD_SIZE // 2, axis=1) * sine


def turn_kernel(values, cosine, sine):
    return values * cosine + pltpu.roll(values, HEAD_SIZE // 2, 1) * sine


def dense_kernel(x_ref, wq_ref, wkv_ref, q_ref, kv_ref):
    @pl.when(pl.program_id(0) == 0)
    def _():
        q_ref[...] = jnp.zeros_like(q_ref)
        kv_ref[...] = jnp.zeros_like(kv_ref)

    x = x_ref[...]
    q_ref[...] += dot_nn(x, wq_ref[...])
    kv_ref[...] += dot_nn(x, wkv_ref[...])


def dense_qkv(x, wq, wkv):
    rows, width = x.shape
    step = 2048
    cq, ckv = wq.shape[1], wkv.shape[1]
    return pl.pallas_call(
        dense_kernel,
        grid=(width // step,),
        in_specs=[
            pl.BlockSpec((rows, step), lambda i: (0, i)),
            pl.BlockSpec((step, cq), lambda i: (i, 0)),
            pl.BlockSpec((step, ckv), lambda i: (i, 0)),
        ],
        out_specs=[
            pl.BlockSpec((rows, cq), lambda i: (0, 0)),
            pl.BlockSpec((rows, ckv), lambda i: (0, 0)),
        ],
        out_shape=[
            jax.ShapeDtypeStruct((rows, cq), F32),
            jax.ShapeDtypeStruct((rows, ckv), F32),
        ],
        compiler_params=params(),
        cost_estimate=cost(2 * rows * width * (cq + ckv), 2 * width * (rows + cq + ckv)),
        name="dense_qkv",
    )(x, wq, wkv)


ENDS_AT = 2
SEND_AT = 16
SERVED_AT = 32
SOURCE_AT = 48
TABLE = 64


def serve_kernel(
    count, blocks, owned, crop_ref, tenant_ref, row_ref, cot, down, up_q, up_kv, up_o, down_o, *outs
):
    tab, cots = outs[0], outs[1:3]
    firsts, lates = outs[3 : 3 + count], outs[3 + count :]
    cots[0][...] = cot[: cots[0].shape[0], :]
    cots[1][...] = cot[cots[0].shape[0] :, :]
    me = lax.axis_index("ctx")
    for i in range(TABLE):
        tab[i] = 0
    tab[0] = me
    tab[1] = lax.axis_index("tp")
    end = jnp.int32(0)
    for i in range(crop_ref.shape[0]):
        end = end + crop_ref[i]
        tab[ENDS_AT + i] = end
    for b in range(blocks):
        row = row_ref[tenant_ref[me * blocks + b]]
        tab[SOURCE_AT + b] = (row // owned) ^ me
    for k in range(count):
        served = jnp.int32(-1)
        for b in range(blocks):
            row = row_ref[tenant_ref[(me ^ k) * blocks + b]]
            served = jnp.where(row // owned == me, row - me * owned, served)
        tab[SERVED_AT + k] = served
        tab[SEND_AT + k] = jnp.maximum(served, 0)
    rank, width = ADAPTER_RANK, down.shape[2]
    half, quarter = rank // 2, rank // 4
    cq, ckv = width // 2, width // 4
    for k in range(count):
        at = tab[SEND_AT + k]
        low = down.shape[1]
        firsts[k][:low, :] = down[at]
        for i in range(2):
            firsts[k][low : low + half, i * cq : (i + 1) * cq] = up_q[
                at, i * half : (i + 1) * half, :
            ]
            lates[k][rank : rank + half, i * cq : (i + 1) * cq] = down_o[
                at, i * half : (i + 1) * half, :
            ]
        for i in range(4):
            firsts[k][low + half :, i * ckv : (i + 1) * ckv] = up_kv[
                at, i * quarter : (i + 1) * quarter, :
            ]
        lates[k][:rank, :] = up_o[at]


def serve(count, blocks, crops, tenants, store_rows, cot, down, up_q, up_kv, up_o, down_o):
    rank, width = ADAPTER_RANK, down.shape[2]
    assert up_q.shape[2] * 2 == width and up_kv.shape[2] * 4 == width
    assert up_o.shape[2] == width and down_o.shape[2] * 2 == width
    smem = pl.BlockSpec(memory_space=pltpu.SMEM)
    vmem = pl.BlockSpec(memory_space=pltpu.VMEM)
    first = jax.ShapeDtypeStruct((3 * rank + rank // 2 + rank // 4, width), BF16)
    late = jax.ShapeDtypeStruct((rank + rank // 2, width), BF16)
    cut = cot.shape[0] // 384 * 192
    results = pl.pallas_call(
        functools.partial(serve_kernel, count, blocks, down.shape[0]),
        in_specs=[smem] * 3 + [vmem] * 6,
        out_specs=[smem] + [vmem] * (2 + 2 * count),
        out_shape=[jax.ShapeDtypeStruct((TABLE,), jnp.int32)]
        + [jax.ShapeDtypeStruct((n, cot.shape[1]), BF16) for n in (cut, cot.shape[0] - cut)]
        + [first] * count
        + [late] * count,
        compiler_params=params(),
        name="serve",
    )(crops, tenants, store_rows, cot, down, up_q, up_kv, up_o, down_o)
    return results[0], results[1:3], list(results[3 : 3 + count]), list(results[3 + count :])


def unpack_q(ref):
    rows, width = ref.shape
    value = ref[...]
    return jnp.concatenate([value[:, : width // 2], value[:, width // 2 :]], axis=0)


def unpack_kv(ref):
    rows, width = ref.shape
    value = ref[...]
    step = width // 4
    return jnp.concatenate([value[:, i * step : (i + 1) * step] for i in range(4)], axis=0)


def pick(tab_ref, block, count, step):
    for k in range(count):

        @pl.when(tab_ref[SOURCE_AT + block] == k)
        def _(k=k):
            step(k)


def split_rows(tab_ref, whole, mine, other):
    half = mine.shape[0]

    @pl.when(tab_ref[1] % 2 == 0)
    def _():
        mine[...] = whole[:half, :]
        other[...] = whole[half:, :]

    @pl.when(tab_ref[1] % 2 == 1)
    def _():
        mine[...] = whole[half:, :]
        other[...] = whole[:half, :]


def join_rows(tab_ref, mine, other, whole):
    half = mine.shape[0]

    @pl.when(tab_ref[1] % 2 == 0)
    def _():
        whole[:half, :] = mine[...]
        whole[half:, :] = other[...]

    @pl.when(tab_ref[1] % 2 == 1)
    def _():
        whole[:half, :] = other[...]
        whole[half:, :] = mine[...]


def sum_halves(mine, other, beside=()):
    total = add_round(mine, swap(other, "tp", 1))
    mask, done = 2, None
    beside = list(beside)
    while mask < lax.axis_size("tp"):
        arrived = swap(total, "tp", mask)
        if beside:
            done = beside.pop(0)(done)
            arrived, done = lax.optimization_barrier((arrived, done))
        total = add_round(total, arrived)
        mask *= 2
    while beside:
        done = beside.pop(0)(done)
    return (total, swap(total, "tp", 1)), done


def block_rows(b):
    return slice(b * BLK, (b + 1) * BLK)


def whole_spec(shape):
    return pl.BlockSpec(shape, lambda i, t: (0,) * len(shape))


def table_call(kernel, table, operands, shapes, scratch, name, flops=0, limit=VMEM_BYTES):
    moved = sum(math.prod(s.shape) * s.dtype.itemsize for s in operands + shapes)
    vmem = pl.BlockSpec(memory_space=pltpu.VMEM)
    return pl.pallas_call(
        kernel,
        in_specs=[pl.BlockSpec(memory_space=pltpu.SMEM)] + [vmem] * len(operands),
        out_specs=[vmem] * len(shapes),
        out_shape=shapes,
        scratch_shapes=scratch,
        compiler_params=params(limit),
        cost_estimate=cost(flops, moved),
        name=name,
    )(table, *operands)


def low_kernel(count, tab_ref, x_ref, *refs):
    downs = refs[:count]
    mine, other, whole = refs[count:]
    cols = whole.shape[1]
    for b in range(whole.shape[0] // BLK):

        def step(k, b=b):
            whole[block_rows(b), :] = dot_nt(x_ref[block_rows(b), :], downs[k][:cols, :]).astype(BF16)

        pick(tab_ref, b, count, step)
    split_rows(tab_ref, whole, mine, other)


def low_part(table, x, firsts):
    rows, width, cols = x.shape[0], firsts[0].shape[1], 3 * ADAPTER_RANK
    half = jax.ShapeDtypeStruct((rows // 2, cols), BF16)
    return table_call(
        functools.partial(low_kernel, len(firsts)),
        table,
        [x] + firsts,
        [half, half],
        [pltpu.VMEM((rows, cols), BF16)],
        "low_part",
        2 * rows * width * cols,
        SMALL_VMEM_BYTES,
    )


def finish_kv_kernel(count, rotate_keys, tab_ref, kv_ref, mine, other, cos_ref, sin_ref, *refs):
    ups = refs[:count]
    kvo, low = refs[count:]
    ckv = kv_ref.shape[1]
    rank = ADAPTER_RANK
    join_rows(tab_ref, mine, other, low)
    for b in range(kv_ref.shape[0] // BLK):

        def step(k, b=b):
            at_rows = block_rows(b)
            low_k = low[at_rows, rank : 2 * rank]
            low_v = low[at_rows, 2 * rank :]
            up_kv = unpack_kv(ups[k].at[3 * rank + rank // 2 :])
            for h in range(ckv // HEAD_SIZE):
                at = slice(h * HEAD_SIZE, (h + 1) * HEAD_SIZE)
                if rotate_keys:
                    term = dot_nn(low_v if h % 2 else low_k, up_kv[:, at])
                else:
                    is_value = (tab_ref[1] * (ckv // HEAD_SIZE) + h) % 2 == 1
                    term = jnp.where(
                        is_value, dot_nn(low_v, up_kv[:, at]), dot_nn(low_k, up_kv[:, at])
                    )
                piece = (kv_ref[at_rows, at] + term).astype(BF16)
                if rotate_keys and h % 2 == 0:
                    cosine, sine = cos_ref[at_rows, :], sin_ref[at_rows, :]
                    piece = turn_kernel(piece.astype(F32), cosine, sine).astype(BF16)
                kvo[at_rows, at] = piece

        pick(tab_ref, b, count, step)


def finish_kv(table, kv_lin, halves, firsts, cosine, sine, rotate_keys):
    rows, ckv = kv_lin.shape
    cols = 3 * ADAPTER_RANK
    operands = [kv_lin, *halves, cosine, sine]
    return table_call(
        functools.partial(finish_kv_kernel, len(firsts), rotate_keys),
        table,
        operands + firsts,
        [jax.ShapeDtypeStruct((rows, ckv), BF16), jax.ShapeDtypeStruct((rows, cols), BF16)],
        [],
        "finish_kv",
        4 * rows * ADAPTER_RANK * ckv,
    )


def finish_q_kernel(count, tab_ref, q_ref, low_ref, cos_ref, sin_ref, *refs):
    ups, qo = refs[:count], refs[count]
    cq = q_ref.shape[1]
    rank = ADAPTER_RANK
    for b in range(q_ref.shape[0] // BLK):

        def step(k, b=b):
            at_rows = block_rows(b)
            cosine, sine = cos_ref[at_rows, :], sin_ref[at_rows, :]
            up_q = unpack_q(ups[k].at[3 * rank : 3 * rank + rank // 2])
            query = q_ref[at_rows, :] + dot_nn(low_ref[at_rows, :rank], up_q)
            for h in range(cq // HEAD_SIZE):
                at = slice(h * HEAD_SIZE, (h + 1) * HEAD_SIZE)
                qo[at_rows, at] = turn_kernel(query[:, at], cosine, sine).astype(BF16)

        pick(tab_ref, b, count, step)


def finish_q(table, q_lin, low_in, firsts, cosine, sine):
    rows, cq = q_lin.shape
    operands = [q_lin, low_in, cosine, sine]
    return table_call(
        functools.partial(finish_q_kernel, len(firsts)),
        table,
        operands + firsts,
        [jax.ShapeDtypeStruct((rows, cq), BF16)],
        [],
        "finish_q",
        2 * rows * ADAPTER_RANK * cq,
        SMALL_VMEM_BYTES,
    )[0]


def low_o_kernel(count, tab_ref, cot_ref, attn_ref, *refs):
    lates = refs[:count]
    mine, other, whole = refs[count:]
    rank = ADAPTER_RANK
    for b in range(whole.shape[0] // BLK):

        def step(k, b=b):
            at = block_rows(b)
            whole[at, :rank] = dot_nt(cot_ref[at, :], lates[k][:rank, :]).astype(BF16)
            down = unpack_q(lates[k].at[rank:])
            whole[at, rank:] = dot_nt(attn_ref[at, :], down).astype(BF16)

        pick(tab_ref, b, count, step)
    split_rows(tab_ref, whole, mine, other)


def low_o_part(table, cot, attn, lates):
    rows, width = cot.shape
    cols = 2 * ADAPTER_RANK
    half = jax.ShapeDtypeStruct((rows // 2, cols), BF16)
    return table_call(
        functools.partial(low_o_kernel, len(lates)),
        table,
        [cot, attn] + lates,
        [half, half],
        [pltpu.VMEM((rows, cols), BF16)],
        "low_o_part",
        2 * rows * cols * width,
        SMALL_VMEM_BYTES,
    )


def low_g_kernel(count, tab_ref, gq_ref, gkv_ref, *refs):
    ups = refs[:count]
    mine, other, whole = refs[count:]
    rank = ADAPTER_RANK
    ckv = gkv_ref.shape[1]
    for b in range(whole.shape[0] // BLK):

        def step(k, b=b):
            at = block_rows(b)
            up_q = unpack_q(ups[k].at[3 * rank : 3 * rank + rank // 2])
            whole[at, :rank] = dot_nt(gq_ref[at, :], up_q).astype(BF16)
            up_kv = unpack_kv(ups[k].at[3 * rank + rank // 2 :])
            sums = [jnp.zeros((BLK, rank), F32)] * 2
            for h in range(ckv // HEAD_SIZE):
                cols = slice(h * HEAD_SIZE, (h + 1) * HEAD_SIZE)
                term = dot_nt(gkv_ref[at, cols], up_kv[:, cols])
                is_value = (tab_ref[1] * (ckv // HEAD_SIZE) + h) % 2 == 1
                sums[0] = sums[0] + jnp.where(is_value, 0.0, term)
                sums[1] = sums[1] + jnp.where(is_value, term, 0.0)
            whole[at, rank : 2 * rank] = sums[0].astype(BF16)
            whole[at, 2 * rank :] = sums[1].astype(BF16)

        pick(tab_ref, b, count, step)
    split_rows(tab_ref, whole, mine, other)


def low_g_part(table, gq, gkv, firsts):
    rows = gq.shape[0]
    cols, width = 3 * ADAPTER_RANK, firsts[0].shape[1]
    half = jax.ShapeDtypeStruct((rows // 2, cols), BF16)
    return table_call(
        functools.partial(low_g_kernel, len(firsts)),
        table,
        [gq, gkv] + firsts,
        [half, half],
        [pltpu.VMEM((rows, cols), BF16)],
        "low_g_part",
        2 * rows * width * ADAPTER_RANK,
    )


def zero_unused(tab_ref, blocks, sends):
    for k in range(len(sends)):
        used = tab_ref[SOURCE_AT] == k
        for b in range(1, blocks):
            used = used | (tab_ref[SOURCE_AT + b] == k)

        @pl.when(jnp.logical_not(used))
        def _(k=k):
            sends[k][...] = jnp.zeros_like(sends[k])


def up_grads_kernel(
    count, tab_ref, low_ref, gq_ref, gkv_ref, o_mine, o_other, cot, attn, *refs
):
    sends, low_o = refs[:count], refs[count]
    rank = ADAPTER_RANK
    join_rows(tab_ref, o_mine, o_other, low_o)
    blocks = low_o.shape[0] // BLK
    cq, ckv = gq_ref.shape[1], gkv_ref.shape[1]
    half, quarter = rank // 2, rank // 4
    late = half + quarter
    zero_unused(tab_ref, blocks, sends)
    for b in range(blocks):

        def step(k, b=b):
            at = block_rows(b)
            out = sends[k]
            up_q = dot_tn(low_ref[at, :rank], gq_ref[at, :]).astype(BF16)
            down_o = dot_tn(low_o[at, :rank], attn[at, :]).astype(BF16)
            for i in range(2):
                rows = slice(i * half, (i + 1) * half)
                cols = slice(i * cq, (i + 1) * cq)
                out[:half, cols] = up_q[rows, :]
                out[late + rank :, cols] = down_o[rows, :]
            for h in range(ckv // HEAD_SIZE):
                piece = slice(h * HEAD_SIZE, (h + 1) * HEAD_SIZE)
                is_value = (tab_ref[1] * (ckv // HEAD_SIZE) + h) % 2 == 1
                up_kv = jnp.where(
                    is_value,
                    dot_tn(low_ref[at, 2 * rank :], gkv_ref[at, piece]),
                    dot_tn(low_ref[at, rank : 2 * rank], gkv_ref[at, piece]),
                ).astype(BF16)
                for i in range(4):
                    cols = slice(i * ckv + h * HEAD_SIZE, i * ckv + (h + 1) * HEAD_SIZE)
                    out[half:late, cols] = up_kv[i * quarter : (i + 1) * quarter, :]
            out[late : late + rank, :] = dot_tn(low_o[at, rank:], cot[at, :]).astype(BF16)

        pick(tab_ref, b, count, step)


def up_grads(table, count, low_in, gq, gkv, o_halves, cot, attn):
    rows, width = cot.shape
    rank = ADAPTER_RANK
    operands = [low_in, gq, gkv, *o_halves, cot, attn]
    return list(
        table_call(
            functools.partial(up_grads_kernel, count),
            table,
            operands,
            [jax.ShapeDtypeStruct((2 * rank + rank // 4, width), BF16)] * count,
            [pltpu.VMEM((rows, 2 * rank), BF16)],
            "up_grads",
            2 * rows * width * 3 * rank,
        )
    )


def down_grads_kernel(count, tab_ref, x_ref, mine, other, *refs):
    downs, sends = refs[:count], refs[count : 2 * count]
    delta, low = refs[2 * count :]
    join_rows(tab_ref, mine, other, low)
    blocks = low.shape[0] // BLK
    zero_unused(tab_ref, blocks, sends)
    for b in range(blocks):

        def step(k, b=b):
            at = block_rows(b)
            sends[k][...] = dot_tn(low[at, :], x_ref[at, :]).astype(BF16)
            delta[at, :] = dot_nn(low[at, :], downs[k][: low.shape[1], :]).astype(BF16)

        pick(tab_ref, b, count, step)


def down_grads(table, x, halves, firsts):
    rows, cols = x.shape[0], 3 * ADAPTER_RANK
    width, count = firsts[0].shape[1], len(firsts)
    results = table_call(
        functools.partial(down_grads_kernel, count),
        table,
        [x, *halves] + firsts,
        [jax.ShapeDtypeStruct((cols, width), BF16)] * count
        + [jax.ShapeDtypeStruct((rows, width), BF16)],
        [pltpu.VMEM((rows, cols), BF16)],
        "down_grads",
        4 * rows * width * cols,
    )
    return list(results[:count]), results[count]


def store_kernel(count, pieces, tab_ref, *refs):
    arrived, outs = refs[:count], refs[count:]
    row = pl.program_id(0)
    for o in outs:
        o[...] = jnp.zeros_like(o)
    for k in range(count):

        @pl.when(tab_ref[SERVED_AT + k] == row)
        def _(k=k):
            for o, piece in zip(outs, pieces):
                o[0] += piece(arrived[k]).astype(F32)


def store_sums(table, arrived, owned, pieces, sizes):
    shapes = [jax.ShapeDtypeStruct((owned,) + size, F32) for size in sizes]
    return pl.pallas_call(
        functools.partial(store_kernel, len(arrived), pieces),
        grid_spec=pltpu.PrefetchScalarGridSpec(
            num_scalar_prefetch=1,
            grid=(owned,),
            in_specs=[pl.BlockSpec(a.shape, lambda i, t: (0, 0)) for a in arrived],
            out_specs=[pl.BlockSpec((1,) + s.shape[1:], lambda i, t: (i, 0, 0)) for s in shapes],
        ),
        out_shape=shapes,
        compiler_params=params(),
        name="store_sums",
    )(table, *arrived)


def store_ups(table, arrived, owned):
    rank, width = ADAPTER_RANK, arrived[0].shape[1]
    half, late = rank // 2, rank // 2 + rank // 4
    pieces = [
        lambda a: unpack_q(a.at[:half]),
        lambda a: unpack_kv(a.at[half:late]),
        lambda a: unpack_q(a.at[late + rank :]),
        lambda a: a[late : late + rank, :],
    ]
    sizes = [(rank, width // 2), (rank, width // 4), (rank, width // 2), (rank, width)]
    return store_sums(table, arrived, owned, pieces, sizes)


def store_downs(table, arrived, owned):
    return store_sums(table, arrived, owned, [lambda a: a[...]], [arrived[0].shape])[0]


def output_kernel(count, tab_ref, sum_ref, mine, other, *refs):
    lates = refs[:count]
    out, low = refs[count:]
    rank = ADAPTER_RANK
    join_rows(tab_ref, mine, other, low)
    for b in range(out.shape[0] // BLK):

        def step(k, b=b):
            at = block_rows(b)
            term = dot_nn(low[at, rank:], lates[k][:rank, :])
            out[at, :] = (sum_ref[at, :].astype(F32) + term).astype(BF16)

        pick(tab_ref, b, count, step)


def output_result(table, total, halves, lates):
    rows, width = total.shape
    rank = ADAPTER_RANK
    return table_call(
        functools.partial(output_kernel, len(lates)),
        table,
        [total, *halves] + lates,
        [jax.ShapeDtypeStruct((rows, width), BF16)],
        [pltpu.VMEM((rows, 2 * rank), BF16)],
        "output_result",
        2 * rows * rank * width,
    )[0]


def crop_start(tab_ref, crops, positions):
    start = jnp.zeros_like(positions)
    for i in range(crops):
        end = tab_ref[ENDS_AT + i]
        start = jnp.where(positions >= end, end, start)
    return start


def masked(scores, first, own, base):
    rows, cols = scores.shape
    key_pos = base + lax.broadcasted_iota(jnp.int32, (rows, cols), 0)
    allowed = key_pos >= first
    if own:
        allowed &= key_pos <= base + lax.broadcasted_iota(jnp.int32, (rows, cols), 1)
    return jnp.where(allowed, scores, NEG)


def chunk_on(tab_ref, crops, k, rows):
    me = tab_ref[0]
    chunk = me ^ k
    return (chunk <= me) & ((chunk + 1) * rows > crop_start(tab_ref, crops, me * rows))


def query_starts(tab_ref, crops, rows):
    positions = tab_ref[0] * rows + lax.broadcasted_iota(jnp.int32, (1, rows), 1)
    return crop_start(tab_ref, crops, positions)


def forward_kernel(heads, count, crops, tab_ref, q_ref, *refs):
    kv_refs = refs[:count]
    out_ref, norm_ref, acc, top, total = refs[count:]
    rows = q_ref.shape[0]
    first = query_starts(tab_ref, crops, rows)
    for k in range(count):

        def chunk_step(k=k):
            base = (tab_ref[0] ^ k) * rows
            keys = kv_refs[k][:, :HEAD_SIZE]
            values = kv_refs[k][:, HEAD_SIZE:]
            for h in range(heads):
                at = slice(h * HEAD_SIZE, (h + 1) * HEAD_SIZE)
                scores = masked(dot_nt(keys, q_ref[:, at]), first, k == 0, base)
                here = jnp.max(scores, axis=0, keepdims=True)
                if k == 0:
                    new_top = here
                else:
                    old_top = top[h : h + 1, :]
                    new_top = jnp.maximum(old_top, here)
                weights = jnp.exp2(scores * SCALE2 - new_top * SCALE2)
                here_sum = jnp.sum(weights, axis=0, keepdims=True)
                here_out = dot_tn(values, weights.astype(BF16))
                if k == 0:
                    total[h : h + 1, :] = here_sum
                    acc[h] = here_out
                else:
                    decay = jnp.exp2((old_top - new_top) * SCALE2)
                    total[h : h + 1, :] = total[h : h + 1, :] * decay + here_sum
                    acc[h] = acc[h] * decay + here_out
                top[h : h + 1, :] = new_top

        if k == 0:
            chunk_step()
        else:
            pl.when(chunk_on(tab_ref, crops, k, rows))(chunk_step)
    for h in range(heads):
        at = slice(h * HEAD_SIZE, (h + 1) * HEAD_SIZE)
        out_ref[:, at] = jnp.transpose(acc[h] / total[h : h + 1, :]).astype(BF16)
    norm_ref[...] = top[...] * SCALE2 + jnp.log(total[...]) * LOG2E


def attention_forward(table, crops, query, kvs):
    rows, cols = query.shape
    heads = cols // HEAD_SIZE
    count = len(kvs)
    smem = pl.BlockSpec(memory_space=pltpu.SMEM)
    vmem = pl.BlockSpec(memory_space=pltpu.VMEM)
    work = heads * rows * rows * count
    return pl.pallas_call(
        functools.partial(forward_kernel, heads, count, crops),
        in_specs=[smem] + [vmem] * (1 + count),
        out_specs=[vmem] * 2,
        out_shape=[
            jax.ShapeDtypeStruct((rows, cols), BF16),
            jax.ShapeDtypeStruct((heads, rows), F32),
        ],
        scratch_shapes=[
            pltpu.VMEM((heads, HEAD_SIZE, rows), F32),
            pltpu.VMEM((heads, rows), F32),
            pltpu.VMEM((heads, rows), F32),
        ],
        compiler_params=params(),
        cost_estimate=cost(4 * work * HEAD_SIZE, 4 * rows * cols * count, work),
        name="attention_forward",
    )(table, query, *kvs)


def backward_kernel(
    heads,
    count,
    crops,
    tab_ref,
    q_ref,
    dense_ref,
    mine,
    other,
    out_ref,
    norm_ref,
    cos_ref,
    sin_ref,
    *refs,
):
    kv_refs, lates = refs[:count], refs[count : 2 * count]
    gq_ref = refs[2 * count]
    gkv_refs = refs[2 * count + 1 : 3 * count + 1]
    acc, delta, low, grad_ref = refs[3 * count + 1 :]
    rows = q_ref.shape[0]
    rank = ADAPTER_RANK
    first = query_starts(tab_ref, crops, rows)
    join_rows(tab_ref, mine, other, low)
    for b in range(rows // BLK):

        def add(k, b=b):
            at = block_rows(b)
            term = dot_nn(low[at, :rank], unpack_q(lates[k].at[rank:]))
            grad_ref[at, :] = (dense_ref[at, :] + term).astype(BF16)

        pick(tab_ref, b, count, add)
    for h in range(heads):
        at = slice(h * HEAD_SIZE, (h + 1) * HEAD_SIZE)
        product = grad_ref[:, at].astype(F32) * out_ref[:, at].astype(F32)
        delta[h : h + 1, :] = jnp.sum(jnp.transpose(product), axis=0, keepdims=True)
    for k in range(count):

        def chunk_step(k=k):
            base = (tab_ref[0] ^ k) * rows
            keys = kv_refs[k][:, :HEAD_SIZE]
            values = kv_refs[k][:, HEAD_SIZE:]
            key_grad = jnp.zeros((rows, HEAD_SIZE), F32)
            value_grad = jnp.zeros((rows, HEAD_SIZE), F32)
            for h in range(heads):
                at = slice(h * HEAD_SIZE, (h + 1) * HEAD_SIZE)
                scores = masked(dot_nt(keys, q_ref[:, at]), first, k == 0, base)
                weights = jnp.exp2(scores * SCALE2 - norm_ref[h : h + 1, :])
                value_grad += dot_nn(weights.astype(BF16), grad_ref[:, at])
                grad_weights = dot_nt(values, grad_ref[:, at])
                grad_scores = (weights * (grad_weights - delta[h : h + 1, :])).astype(BF16)
                key_grad += dot_nn(grad_scores, q_ref[:, at])
                here = dot_tn(keys, grad_scores)
                if k == 0:
                    acc[h] = here
                else:
                    acc[h] += here
            gkv_refs[k][:, :HEAD_SIZE] = (key_grad * SCALE).astype(BF16)
            gkv_refs[k][:, HEAD_SIZE:] = value_grad.astype(BF16)

        if k == 0:
            chunk_step()
        else:
            on = chunk_on(tab_ref, crops, k, rows)
            pl.when(on)(chunk_step)

            @pl.when(jnp.logical_not(on))
            def _(k=k):
                gkv_refs[k][...] = jnp.zeros_like(gkv_refs[k])

    for h in range(heads):
        at = slice(h * HEAD_SIZE, (h + 1) * HEAD_SIZE)
        grad = jnp.transpose(acc[h]) * SCALE
        gq_ref[:, at] = turn_kernel(grad, cos_ref[...], -sin_ref[...]).astype(BF16)


def attention_backward(table, crops, query, dense, halves, out, norm, cosine, sine, kvs, lates):
    rows, cols = query.shape
    heads = cols // HEAD_SIZE
    count = len(kvs)
    smem = pl.BlockSpec(memory_space=pltpu.SMEM)
    vmem = pl.BlockSpec(memory_space=pltpu.VMEM)
    work = heads * rows * rows * count
    results = pl.pallas_call(
        functools.partial(backward_kernel, heads, count, crops),
        in_specs=[smem] + [vmem] * (8 + 2 * count),
        out_specs=[vmem] * (1 + count),
        out_shape=[jax.ShapeDtypeStruct((rows, cols), BF16)]
        + [jax.ShapeDtypeStruct((rows, 2 * HEAD_SIZE), BF16)] * count,
        scratch_shapes=[
            pltpu.VMEM((heads, HEAD_SIZE, rows), F32),
            pltpu.VMEM((heads, rows), F32),
            pltpu.VMEM((rows, 2 * ADAPTER_RANK), BF16),
            pltpu.VMEM((rows, cols), BF16),
        ],
        compiler_params=params(),
        cost_estimate=cost(10 * work * HEAD_SIZE, 8 * rows * cols * count, work),
        name="attention_backward",
    )(table, query, dense, *halves, out, norm, cosine, sine, *kvs, *lates)
    return results[0], list(results[1:])


def plane_spec(shape, axis, other):
    def index(i, t):
        core = t[1] % 2
        at = 2 * i + (1 - core if other else core)
        return (0, at) if axis else (at, 0)

    return pl.BlockSpec(shape, index)


def pick_kernel(tab_ref, w_ref, o_ref):
    o_ref[...] = w_ref[...]


def pick_planes(table, weight, groups, axis):
    planes = groups // 2
    shape = list(weight.shape)
    shape[axis] //= groups
    result = list(weight.shape)
    result[axis] //= 2
    return pl.pallas_call(
        pick_kernel,
        grid_spec=pltpu.PrefetchScalarGridSpec(
            num_scalar_prefetch=1,
            grid=(planes,),
            in_specs=[plane_spec(tuple(shape), axis, True)],
            out_specs=pl.BlockSpec(
                tuple(shape), (lambda i, t: (0, i)) if axis else (lambda i, t: (i, 0))
            ),
        ),
        out_shape=jax.ShapeDtypeStruct(tuple(result), BF16),
        compiler_params=params(),
        cost_estimate=cost(0, 2 * math.prod(weight.shape)),
        name="pick_planes",
    )(table, weight)


def reduce_planes(parts, groups):
    lines = [list(range(core, groups, 2)) for core in range(2)]
    return lax.psum_scatter(parts, "tp", scatter_dimension=0, axis_index_groups=lines, tiled=False)


def project_kernel(tab_ref, a_ref, ao_ref, w_ref, wo_ref, o_ref, a_buf, w_buf, o_buf, w_sem, o_sem):
    planes, cols = o_ref.shape[0], o_ref.shape[2]
    depth = a_ref.shape[1]
    slots = o_buf.shape[0]
    loads = []
    for i in range(planes):
        start = pl.multiple_of((2 * i + tab_ref[1] % 2) * cols, cols)
        here = pltpu.make_async_copy(w_ref.at[:, pl.ds(start, cols)], w_buf.at[i, :depth], w_sem.at[i, 0])
        there = pltpu.make_async_copy(
            wo_ref.at[:, i * cols : (i + 1) * cols], w_buf.at[i, depth:], w_sem.at[i, 1]
        )
        here.start()
        there.start()
        loads.append((here, there))
    a_buf[:, :depth] = a_ref[...]
    a_buf[:, depth:] = ao_ref[...]
    stores = []
    for i in range(planes):
        slot = i % slots
        if i >= slots:
            stores[i - slots].wait()
        loads[i][0].wait()
        loads[i][1].wait()
        o_buf[slot] = dot_nn(a_buf[...], w_buf[i]).astype(BF16)
        stores.append(pltpu.make_async_copy(o_buf.at[slot], o_ref.at[i], o_sem.at[slot]))
        stores[i].start()
    for i in range(planes - slots, planes):
        stores[i].wait()


def project_out(table, attn, attn_other, weight, weight_other, groups):
    rows, depth = attn.shape
    cols = weight.shape[1] // groups
    planes = groups // 2
    vmem = pl.BlockSpec(memory_space=pltpu.VMEM)
    anywhere = pl.BlockSpec(memory_space=pl.ANY)
    return pl.pallas_call(
        project_kernel,
        in_specs=[pl.BlockSpec(memory_space=pltpu.SMEM), vmem, vmem, anywhere, anywhere],
        out_specs=anywhere,
        out_shape=jax.ShapeDtypeStruct((planes, rows, cols), BF16),
        scratch_shapes=[
            pltpu.VMEM((rows, 2 * depth), BF16),
            pltpu.VMEM((planes, 2 * depth, cols), BF16),
            pltpu.VMEM((2, rows, cols), BF16),
            pltpu.SemaphoreType.DMA((planes, 2)),
            pltpu.SemaphoreType.DMA((2,)),
        ],
        compiler_params=params(),
        cost_estimate=cost(
            2 * rows * depth * cols * groups, 2 * (rows + 2 * depth) * cols * planes
        ),
        name="project_out",
    )(table, attn, attn_other, weight, weight_other)


PER_STEP = 2


def grad_attn_kernel(c0_ref, c1_ref, w_ref, *refs):
    before, o_ref = refs[:-1], refs[-1]
    step = pl.program_id(0)
    per_step, first_rows, cols = c0_ref.shape
    parts = ((c0_ref, slice(0, first_rows)), (c1_ref, slice(first_rows, o_ref.shape[0])))
    for c_ref, at in parts:
        total = dot_nt(c_ref[0], w_ref[:, :cols])
        for i in range(1, per_step):
            total += dot_nt(c_ref[i], w_ref[:, i * cols : (i + 1) * cols])

        @pl.when(step == 0)
        def _(at=at, total=total):
            o_ref[at, :] = total + before[0][at, :] if before else total

        @pl.when(step > 0)
        def _(at=at, total=total):
            o_ref[at, :] += total


def grad_attn(cot_first, cot_second, weight, half, before=None):
    groups, first_rows, cols = cot_first.shape
    depth = weight.shape[0]
    rows = first_rows + cot_second.shape[1]
    steps = groups // PER_STEP // 2
    start = half * steps
    whole = pl.BlockSpec((rows, depth), lambda i: (0, 0))
    return pl.pallas_call(
        grad_attn_kernel,
        grid=(steps,),
        in_specs=[
            pl.BlockSpec((PER_STEP, first_rows, cols), lambda i: (start + i, 0, 0)),
            pl.BlockSpec((PER_STEP, rows - first_rows, cols), lambda i: (start + i, 0, 0)),
            pl.BlockSpec((depth, PER_STEP * cols), lambda i: (0, start + i)),
        ]
        + ([] if before is None else [whole]),
        out_specs=whole,
        out_shape=jax.ShapeDtypeStruct((rows, depth), F32),
        compiler_params=params(),
        cost_estimate=cost(rows * depth * cols * groups, (rows + depth) * cols * groups),
        name="grad_attn",
    )(cot_first, cot_second, weight, *([] if before is None else [before]))


def grad_input_kernel(tab_ref, gq, gqo, gkv, gkvo, wq, wqo, wkv, wkvo, o_ref):
    total = dot_nt(gq[...], wq[...]) + dot_nt(gqo[...], wqo[...])
    total = total + dot_nt(gkv[...], wkv[...]) + dot_nt(gkvo[...], wkvo[...])
    o_ref[0] = total.astype(BF16)


def grad_input(table, gq, gq_other, gkv, gkv_other, wq, wq_other, wkv, wkv_other, groups):
    rows, cq = gq.shape
    ckv = gkv.shape[1]
    cols = wq.shape[0] // groups
    planes = groups // 2
    return pl.pallas_call(
        grad_input_kernel,
        grid_spec=pltpu.PrefetchScalarGridSpec(
            num_scalar_prefetch=1,
            grid=(planes,),
            in_specs=[
                whole_spec(gq.shape),
                whole_spec(gq.shape),
                whole_spec(gkv.shape),
                whole_spec(gkv.shape),
                plane_spec((cols, cq), 0, False),
                pl.BlockSpec((cols, cq), lambda i, t: (i, 0)),
                plane_spec((cols, ckv), 0, False),
                pl.BlockSpec((cols, ckv), lambda i, t: (i, 0)),
            ],
            out_specs=pl.BlockSpec((1, rows, cols), lambda i, t: (i, 0, 0)),
        ),
        out_shape=jax.ShapeDtypeStruct((planes, rows, cols), BF16),
        compiler_params=params(),
        cost_estimate=cost(
            2 * rows * (cq + ckv) * cols * groups,
            2 * (rows + 2 * (cq + ckv)) * cols * planes,
        ),
        name="grad_input",
    )(table, gq, gq_other, gkv, gkv_other, wq, wq_other, wkv, wkv_other)


def body(
    hidden_input,
    output_cotangent,
    query_projection,
    key_value_projection,
    output_projection,
    adapter_qkv_down_store,
    adapter_query_up,
    adapter_key_value_up,
    adapter_output_down,
    adapter_output_up,
    crop_token_length,
    tenant_per_block,
    tenant_store_row,
):
    ctx_count = lax.axis_size("ctx")
    tp_count = lax.axis_size("tp")
    ctx_index = lax.axis_index("ctx")
    tp_index = lax.axis_index("tp")
    rows_dev = hidden_input.shape[0]
    out_cols = output_cotangent.shape[1]
    tenant_owner = adapter_qkv_down_store.shape[0]
    blocks_dev = rows_dev // BLK
    pair_bits = (tp_count // KEY_VALUE_HEADS).bit_length() - 1
    groups = hidden_input.shape[1] // out_cols
    crops = crop_token_length.shape[0]
    partners = range(1, ctx_count)

    x_slice = lax.dynamic_slice_in_dim(hidden_input, tp_index * out_cols, out_cols, 1)

    table, cots, firsts, lates = serve(
        ctx_count,
        blocks_dev,
        crop_token_length,
        tenant_per_block,
        tenant_store_row,
        output_cotangent,
        adapter_qkv_down_store.swapaxes(1, 2),
        adapter_query_up,
        adapter_key_value_up,
        adapter_output_up,
        adapter_output_down.swapaxes(1, 2),
    )
    cot_first = lax.all_gather(cots[0], "tp", axis=0, tiled=False)
    firsts = [firsts[0]] + [swap(firsts[k], "ctx", k) for k in partners]
    my_pos = ctx_index * rows_dev + jnp.arange(rows_dev, dtype=jnp.int32)
    q_lin, kv_lin = dense_qkv(hidden_input, query_projection, key_value_projection)
    out_pick = pick_planes(table, output_projection, groups, 1)
    firsts, q_lin, kv_lin, tables, out_pick, x_slice = lax.optimization_barrier(
        (firsts, q_lin, kv_lin, rope_tables(my_pos), out_pick, x_slice)
    )
    cosine, sine = tables
    low_halves = low_part(table, x_slice, firsts)
    low_halves, (kv_pick, query_pick, cot_rest) = sum_halves(
        *low_halves,
        beside=[
            lambda done: pick_planes(table, key_value_projection, groups, 0),
            lambda done: (done, pick_planes(table, query_projection, groups, 0), cots[1]),
        ],
    )
    cot_second = lax.all_gather(cot_rest, "tp", axis=0, tiled=False)
    low_halves, kv_pick, query_pick = lax.optimization_barrier((low_halves, kv_pick, query_pick))
    kv_local, low_in = finish_kv(
        table, kv_lin, low_halves, firsts, cosine, sine, pair_bits == 0
    )
    if pair_bits:
        for bit_no in range(pair_bits):
            partner = swap(kv_local, "tp", 1 << bit_no)
            is_lower = tp_index // (1 << bit_no) % 2 == 0
            kv_local = jnp.where(
                is_lower,
                jnp.concatenate([kv_local, partner], axis=1),
                jnp.concatenate([partner, kv_local], axis=1),
            )
        key_rot = turn(kv_local[:, :HEAD_SIZE].astype(F32), cosine, sine).astype(BF16)
        kv_local = jnp.concatenate([key_rot, kv_local[:, HEAD_SIZE:]], axis=1)
    kvs = [kv_local] + [swap(kv_local, "ctx", k) for k in partners]
    query_rot = finish_q(table, q_lin, low_in, firsts, cosine, sine)
    kvs, lates, query_rot = lax.optimization_barrier((kvs, lates, query_rot))
    out_other, query_other, kv_other = (
        swap(pick, "tp", 1) for pick in (out_pick, query_pick, kv_pick)
    )
    lates = [lates[0]] + [swap(lates[k], "ctx", k) for k in partners]

    attn_out, log_norm = attention_forward(table, crops, query_rot, kvs)
    lates, attn_out = lax.optimization_barrier((lates, attn_out))
    heads_part = project_out(
        table, attn_out, swap(attn_out, "tp", 1), output_projection, out_other, groups
    )
    heads_part, attn_out, cot_first = lax.optimization_barrier((heads_part, attn_out, cot_first))
    heads_sum = reduce_planes(heads_part, groups)
    o_halves, grad_dense = sum_halves(
        *low_o_part(table, output_cotangent, attn_out, lates),
        beside=[
            lambda done: grad_attn(cot_first, cot_second, output_projection, 0),
            lambda done: grad_attn(cot_first, cot_second, output_projection, 1, done),
        ],
    )
    grad_q, kv_parts = attention_backward(
        table, crops, query_rot, grad_dense, o_halves, attn_out, log_norm, cosine, sine, kvs, lates
    )
    grad_q_other = swap(grad_q, "tp", 1)
    reduced = kv_parts[0].astype(F32)
    for k in partners:
        reduced = reduced + swap(kv_parts[k], "ctx", k).astype(F32)
    reduced = jnp.concatenate(
        [turn(reduced[:, :HEAD_SIZE], cosine, -sine), reduced[:, HEAD_SIZE:]], axis=1
    )
    for bit_no in reversed(range(pair_bits)):
        half_cols = reduced.shape[1] // 2
        is_lower = tp_index // (1 << bit_no) % 2 == 0
        keep_part = jnp.where(is_lower, reduced[:, :half_cols], reduced[:, half_cols:])
        send_part = jnp.where(is_lower, reduced[:, half_cols:], reduced[:, :half_cols])
        reduced = keep_part + swap(send_part.astype(BF16), "tp", 1 << bit_no).astype(F32)
    grad_kv = reduced.astype(BF16)

    input_part = grad_input(
        table,
        grad_q,
        grad_q_other,
        grad_kv,
        swap(grad_kv, "tp", 1),
        query_projection,
        query_other,
        key_value_projection,
        kv_other,
        groups,
    )
    input_part, grad_q, grad_kv = lax.optimization_barrier((input_part, grad_q, grad_kv))
    input_sum = reduce_planes(input_part, groups)

    def send_ups(done):
        return up_grads(
            table, ctx_count, low_in, grad_q, grad_kv, o_halves, output_cotangent, attn_out
        )

    g_halves, up_sends = sum_halves(
        *low_g_part(table, grad_q, grad_kv, firsts), beside=[send_ups]
    )
    up_back = [up_sends[0]] + [swap(up_sends[k], "ctx", k) for k in partners]
    output = output_result(table, heads_sum, o_halves, lates)
    g_halves, up_back, output = lax.optimization_barrier((g_halves, up_back, output))
    down_sends, input_delta = down_grads(table, x_slice, g_halves, firsts)
    down_back = [down_sends[0]] + [swap(down_sends[k], "ctx", k) for k in partners]
    up_stores = store_ups(table, up_back, tenant_owner)
    down_back, up_stores = lax.optimization_barrier((down_back, up_stores))
    down_store = store_downs(table, down_back, tenant_owner)
    input_sum, input_delta, down_store = lax.optimization_barrier(
        (input_sum, input_delta, down_store)
    )
    hidden_input_gradient = (input_sum.astype(F32) + input_delta.astype(F32)).astype(BF16)
    return (
        output,
        hidden_input_gradient,
        down_store.swapaxes(1, 2),
        up_stores[0],
        up_stores[1],
        up_stores[2].swapaxes(1, 2),
        up_stores[3],
    )


def solution(mesh):
    in_specs = (
        P("ctx", None),
        P("ctx", "tp"),
        P(None, "tp"),
        P(None, "tp"),
        P("tp", None),
        P("ctx", "tp", None),
        P("ctx", None, "tp"),
        P("ctx", None, "tp"),
        P("ctx", "tp", None),
        P("ctx", None, "tp"),
        P(),
        P(),
        P(),
    )
    out_specs = (
        P("ctx", "tp"),
        P("ctx", "tp"),
        P("ctx", "tp", None),
        P("ctx", None, "tp"),
        P("ctx", None, "tp"),
        P("ctx", "tp", None),
        P("ctx", None, "tp"),
    )
    return jax.shard_map(body, mesh=mesh, in_specs=in_specs, out_specs=out_specs, check_vma=False)
```
